32 devices in a mesh: dp: 4 (over z), row: 4 (over y, x), col: 2 (over core).
Axes of the slice: x: 2, y: 2, z: 4, core: 2. Of those that a mesh axis runs over, the one named last changes fastest.
Arguments:
- tokens: bfloat16 [4096, 768], P(('dp', 'row', 'col')), may hold values from -6 to 6
- lengths: int32 [32, 2], P(('dp', 'row', 'col')), may hold values from 16 to 64, as said below
- routes: int32 [4096, 2], P(('dp', 'row', 'col')), may hold values from 0 to 7, all different within a row; in each aligned block of 128 rows (0 to 127, 128 to 255, ...) at most 32 rows name the same one
- prev_logits: float32 [4096, 8], P(('dp', 'row', 'col')), may hold values from -4 to 4
- cotangent: bfloat16 [4096, 768], P(('dp', 'row', 'col')), may hold values from -6 to 6
- w_qkv: float32 [768, 2304], P(('dp', 'row', 'col')), may hold values from -0.21875 to 0.21875
- w_out: float32 [768, 768], P(('dp', 'row', 'col')), may hold values from -0.75 to 0.75
- route_w: float32 [768, 12], P(('dp', 'row', 'col')), may hold values from -0.109375 to 0.109375
- gains: float32 [2, 768], P(None, ('dp', 'row', 'col')), may hold values from 0.1 to 1.9
- const_vec: float32 [2, 768], P(None, ('dp', 'row', 'col')), may hold values from -4 to 4
- stat_qkv: float32 [768, 2304], P(('dp', 'row', 'col')), may hold values from 2048 to 8192
- stat_out: float32 [768, 768], P(('dp', 'row', 'col')), may hold values from 204 to 819
- stat_route: float32 [768, 12], P(('dp', 'row', 'col')), may hold values from 163 to 655
- stat_gains: float32 [2, 768], P(None, ('dp', 'row', 'col')), may hold values from 4096 to 16384
- stat_const: float32 [2, 768], P(None, ('dp', 'row', 'col')), may hold values from 163 to 655
- w_gate_up: float32 [4, 768, 2, 2048], P('dp', 'row', None, 'col'), may hold values from -0.21875 to 0.21875
- w_down: float32 [4, 2048, 768], P('dp', 'col', 'row'), may hold values from -0.125 to 0.125
- left_gu: float32 [4, 2, 768, 768], P('dp', None, ('row', 'col')), as said below
- right_gu: float32 [4, 2, 2048, 2048], P('dp', None, ('row', 'col')), as said below
- left_down: float32 [4, 2048, 2048], P('dp', ('row', 'col')), as said below
- right_down: float32 [4, 768, 768], P('dp', ('row', 'col')), as said below
- left_root_gu: float32 [4, 2, 768, 768], P('dp', None, 'row'), as said below
- right_root_gu: float32 [4, 2, 2048, 2048], P('dp', None, 'col'), as said below
- left_root_down: float32 [4, 2048, 2048], P('dp', 'col'), as said below
- right_root_down: float32 [4, 768, 768], P('dp', 'row'), as said below
Outputs:
- out: bfloat16 [4096, 768], P(('dp', 'row', 'col'))
- grad_tokens: float32 [4096, 768], P(('dp', 'row', 'col'))
- grad_qkv: float32 [768, 2304], P(('dp', 'row', 'col'))
- moment_qkv: float32 [768, 2304], P(('dp', 'row', 'col'))
- new_qkv: float32 [768, 2304], P(('dp', 'row', 'col'))
- grad_attn_out: float32 [768, 768], P(('dp', 'row', 'col'))
- moment_attn_out: float32 [768, 768], P(('dp', 'row', 'col'))
- new_attn_out: float32 [768, 768], P(('dp', 'row', 'col'))
- grad_route: float32 [768, 12], P(('dp', 'row', 'col'))
- moment_route: float32 [768, 12], P(('dp', 'row', 'col'))
- new_route: float32 [768, 12], P(('dp', 'row', 'col'))
- grad_gains: float32 [2, 768], P(None, ('dp', 'row', 'col'))
- moment_gains: float32 [2, 768], P(None, ('dp', 'row', 'col'))
- new_gains: float32 [2, 768], P(None, ('dp', 'row', 'col'))
- grad_const: float32 [2, 768], P(None, ('dp', 'row', 'col'))
- moment_const: float32 [2, 768], P(None, ('dp', 'row', 'col'))
- new_const: float32 [2, 768], P(None, ('dp', 'row', 'col'))
- grad_gate_up: float32 [4, 768, 2, 2048], P('dp', 'row', None, 'col')
- grad_down: float32 [4, 2048, 768], P('dp', 'col', 'row')
- new_left_gu: float32 [4, 2, 768, 768], P('dp', None, ('row', 'col'))
- new_right_gu: float32 [4, 2, 2048, 2048], P('dp', None, ('row', 'col'))
- new_left_down: float32 [4, 2048, 2048], P('dp', ('row', 'col'))
- new_right_down: float32 [4, 768, 768], P('dp', ('row', 'col'))
- new_gate_up: float32 [4, 768, 2, 2048], P('dp', 'row', None, 'col')
- new_down: float32 [4, 2048, 768], P('dp', 'col', 'row')
The draws below stay inside these ranges and needn't reach their ends.
Inputs may be any that keep to these rules, and one draw needn't show every extreme that they name: Each device's lengths sum to at most 128; some device holds a sequence of exactly 64. `routes`: A token's two experts differ. Among the rows of one device no expert is named more than 32 times, a bound that some block reaches. `left_gu`: each matrix is symmetric. `right_gu`: each matrix is symmetric. `left_down`: each matrix is symmetric. `right_down`: each matrix is symmetric. `left_root_gu`: each matrix is symmetric. `right_root_gu`: each matrix is symmetric. `left_root_down`: each matrix is symmetric. `right_root_down`: each matrix is symmetric.
All inputs are finite; a program needn't handle non-finite values.
Results may differ from the reference program's by a relative error of at most 0.017.
The reference program's roundings to bfloat16 on the way count: a program that leaves them out, or rounds other values in their place, can miss the bound.
Values may be sent and summed in bfloat16 or wider, within the bound.
A program may use at most 256 MiB of HBM per device.

```python
import math
import jax
import jax.numpy as jnp
import numpy as np
from jax import lax

D = 768
HEADS = 12
HEAD = 64
FF = 2048
NSEQ = 2
TOK_DEV = 128
EXPERTS = 4
E_ALL = 8
SEQ_MAX = 64
CAP = 32
TOKENS = 4096
N_DP = 4
N_ROW = 4
N_COL = 2


def symmetric_draw(key, leading_shape, matrix_order, diag_scale, diag_spread, off_scale):
    key_diag, key_off = jax.random.split(key)
    full_shape = tuple(leading_shape) + (matrix_order, matrix_order)
    noise_field = jax.random.truncated_normal(key_off, -4.0, 4.0, full_shape, jnp.float32)
    noise_field = (noise_field + jnp.swapaxes(noise_field, -1, -2)) * 0.7071067811865476
    log_factor = jax.random.uniform(key_diag, tuple(leading_shape) + (matrix_order,), jnp.float32, 0.0, 1.0)
    diagonal = diag_scale * jnp.exp(log_factor * jnp.log(jnp.float32(diag_spread)))
    on_diagonal = jnp.arange(matrix_order)[:, None] == jnp.arange(matrix_order)[None, :]
    return jnp.where(on_diagonal, diagonal[..., :, None], off_scale * noise_field).astype(jnp.float32)


def root_scale(weight_spread, grad_square):
    return (weight_spread / grad_square ** 0.5) ** 0.5


def draw_lengths(key, part):
    key = jax.random.fold_in(key, 1)
    key_len, key_row = jax.random.split(key)
    device_count = N_DP * N_ROW * N_COL
    drawn = jax.random.randint(key_len, (device_count, NSEQ), SEQ_MAX // 4, SEQ_MAX + 1, dtype=jnp.int32)
    picked_row = jax.random.randint(key_row, (), 0, device_count, dtype=jnp.int32)
    row_ids = jnp.arange(device_count, dtype=jnp.int32)[:, None]
    col_ids = jnp.arange(NSEQ, dtype=jnp.int32)[None, :]
    return jnp.where((row_ids == picked_row) & (col_ids == 0), SEQ_MAX, drawn).astype(jnp.int32)


def draw_left_gu(key, part):
    key = jax.random.fold_in(key, 2)
    grad_square = 0.002 * TOKENS
    return symmetric_draw(key, (EXPERTS, 2), D, FF * grad_square, 4.0, FF ** 0.5 * grad_square)


def draw_right_gu(key, part):
    key = jax.random.fold_in(key, 3)
    grad_square = 0.002 * TOKENS
    return symmetric_draw(key, (EXPERTS, 2), FF, D * grad_square, 4.0, D ** 0.5 * grad_square)


def draw_left_down(key, part):
    key = jax.random.fold_in(key, 4)
    grad_square = 0.004 * TOKENS
    return symmetric_draw(key, (EXPERTS,), FF, D * grad_square, 4.0, D ** 0.5 * grad_square)


def draw_right_down(key, part):
    key = jax.random.fold_in(key, 5)
    grad_square = 0.004 * TOKENS
    return symmetric_draw(key, (EXPERTS,), D, FF * grad_square, 4.0, FF ** 0.5 * grad_square)


def draw_left_root_gu(key, part):
    key = jax.random.fold_in(key, 6)
    factor = root_scale(D ** (-0.5), 0.002 * TOKENS)
    return symmetric_draw(key, (EXPERTS, 2), D, factor, 2.0, 0.3 * factor / D ** 0.5)


def draw_right_root_gu(key, part):
    key = jax.random.fold_in(key, 7)
    factor = root_scale(D ** (-0.5), 0.002 * TOKENS)
    return symmetric_draw(key, (EXPERTS, 2), FF, factor, 2.0, 0.3 * factor / FF ** 0.5)


def draw_left_root_down(key, part):
    key = jax.random.fold_in(key, 8)
    factor = root_scale(FF ** (-0.5), 0.004 * TOKENS)
    return symmetric_draw(key, (EXPERTS,), FF, factor, 2.0, 0.3 * factor / FF ** 0.5)


def draw_right_root_down(key, part):
    key = jax.random.fold_in(key, 9)
    factor = root_scale(FF ** (-0.5), 0.004 * TOKENS)
    return symmetric_draw(key, (EXPERTS,), D, factor, 2.0, 0.3 * factor / D ** 0.5)


def levels(stream_key, shape, cuts, smallest, largest):
    def one(axis_at, parts):
        steps = jax.random.uniform(jax.random.fold_in(jax.random.fold_in(stream_key, 6), axis_at), (parts,), jnp.float32, smallest / len(cuts), largest / len(cuts))
        return jnp.repeat(jnp.exp(steps), shape[axis_at] // parts).reshape((-1,) + (1,) * (len(shape) - axis_at - 1))

    loudness = one(*cuts[0])
    for cut in cuts[1:]:
        loudness = loudness * one(*cut)
    return loudness


def deal_out(own_key, own, number, rows, amount, top, limit, skew):
    order = jax.random.permutation(own_key, amount)
    packed, common = load_shares(amount, rows * top, limit, skew, True), load_shares(amount, rows * top, limit, skew, False)
    places = jnp.arange(amount)

    def named(sizes, rotation):
        used = int((sizes > 0).sum())
        fixed = max(1, used // 4)
        passed = fixed + (places - fixed + rotation * (used - fixed)) % max(1, amount - fixed)
        return jnp.zeros((amount,), jnp.int32).at[order[jnp.where(places < fixed, places, passed)]].set(jnp.asarray(sizes, jnp.int32))

    sizes = jnp.where(number % 4 == 0, named(packed, number // 4), named(common, number - number // 4 - 1))
    mixed = jax.random.permutation(jax.random.fold_in(own, 3), amount)
    donor, sink = mixed[0:amount // 2 * 2:2], mixed[1:amount // 2 * 2:2]
    room = jnp.minimum(sizes[donor] - 1, limit - sizes[sink]) // 2
    room = jnp.where((donor == order[0]) | (sink == order[0]) | (sizes[sink] == 0), 0, jnp.maximum(room, 0))
    passed = jax.random.randint(jax.random.fold_in(own, 4), (amount // 2,), 0, 1 << 20) % (room + 1)
    sizes = sizes.at[donor].add(-passed).at[sink].add(passed)
    labels = jnp.searchsorted(jnp.cumsum(sizes), jnp.arange(rows * top), side="right").astype(jnp.int32)
    grid = labels.reshape(top, rows).T
    grid = grid[jax.random.permutation(jax.random.fold_in(own, 1), rows)]
    rotation = jax.random.randint(jax.random.fold_in(own, 2), (rows, 1), 0, top)
    return jnp.take_along_axis(grid, (jnp.arange(top)[None, :] + rotation) % top, axis=1)


def load_shares(number_of, total, limit, skew, full):
    portions = [(1 << 20) // math.isqrt(grade ** skew) + 1 for grade in range(1, number_of + 1)]
    largest = limit if full else min(limit, max(-(-total // number_of), total * portions[0] // sum(portions)))
    least = 1 if total - largest >= number_of - 1 else 0
    given, surplus = [largest] + [least] * (number_of - 1), total - largest - least * (number_of - 1)
    while surplus > 0:
        free = [i for i in range(1, number_of) if given[i] < largest] or [i for i in range(1, number_of) if given[i] < limit]
        whole, budget = sum([portions[i] for i in free]), surplus
        for i in free:
            more = min(limit - given[i], max(1, budget * portions[i] // whole), surplus)
            given[i] = given[i] + more
            surplus = surplus - more
    return np.array(given)


def scatter_about(rng, shape, scale, bound, cuts=(), held_as=jnp.bfloat16):
    array = scale * jax.random.normal(rng, shape, jnp.float32)
    if cuts:
        array = array * levels(rng, shape, cuts, -0.22, 0.18)
    return jnp.clip(array, -bound, bound).astype(held_as)


def setup_inputs(seed: int = 0) -> dict:
    streams_of = jax.random.split(jax.random.key(seed), 26)
    tokens = scatter_about(streams_of[0], (TOKENS, D), 1.0, 6.0, ((0, 32),))
    lengths = draw_lengths(jax.random.fold_in(streams_of[25], 71), 0)
    routes_keys = jax.random.split(jax.random.fold_in(streams_of[2], 1), TOKENS // TOK_DEV)
    routes_turns = jax.random.permutation(jax.random.fold_in(streams_of[2], 3), TOKENS // TOK_DEV)
    routes = jax.vmap(lambda own, number: deal_out(jax.random.fold_in(streams_of[2], 2), own, number, TOK_DEV, E_ALL, 2, CAP, 1))(routes_keys, routes_turns).reshape((TOKENS, 2))
    prev_logits = scatter_about(streams_of[3], (TOKENS, E_ALL), 1.0, 4.0, ((0, 32),), jnp.float32)
    cotangent = scatter_about(streams_of[4], (TOKENS, D), 1.0, 6.0, ((0, 32),))
    w_qkv = scatter_about(streams_of[5], (D, 3 * D), D ** -0.5, 0.21875, ((0, 32),), jnp.float32)
    w_out = scatter_about(streams_of[6], (D, D), HEAD ** -0.5, 0.75, ((0, 32),), jnp.float32)
    route_w = scatter_about(streams_of[7], (D, E_ALL + 4), (4 * D) ** -0.5, 0.109375, ((0, 32),), jnp.float32)
    gains = jnp.clip(1.0 + 0.18 * jax.random.normal(streams_of[8], (2, D), jnp.float32), 0.1, 1.9)
    const_vec = scatter_about(streams_of[9], (2, D), 1.0, 4.0, ((1, 32),), jnp.float32)
    stat_qkv = jnp.clip(jnp.exp(math.log(8192.0) - 1.3862944 * jax.random.uniform(streams_of[10], (D, 3 * D), jnp.float32) ** levels(streams_of[10], (D, 3 * D), ((0, 32),), -0.2, 0.2)), 2048.0, 8192.0)
    stat_out = jnp.clip(jnp.exp(math.log(819.0) - 1.3899641 * jax.random.uniform(streams_of[11], (D, D), jnp.float32) ** levels(streams_of[11], (D, D), ((0, 32),), -0.2, 0.2)), 204.0, 819.0)
    stat_route = jnp.clip(jnp.exp(math.log(655.0) - 1.390885 * jax.random.uniform(streams_of[12], (D, E_ALL + 4), jnp.float32) ** levels(streams_of[12], (D, E_ALL + 4), ((0, 32),), -0.2, 0.2)), 163.0, 655.0)
    stat_gains = jnp.clip(jnp.exp(math.log(16384.0) - 1.3862944 * jax.random.uniform(streams_of[13], (2, D), jnp.float32) ** levels(streams_of[13], (2, D), ((1, 32),), -0.2, 0.2)), 4096.0, 16384.0)
    stat_const = jnp.clip(jnp.exp(math.log(655.0) - 1.390885 * jax.random.uniform(streams_of[14], (2, D), jnp.float32) ** levels(streams_of[14], (2, D), ((1, 32),), -0.2, 0.2)), 163.0, 655.0)
    w_gate_up = scatter_about(streams_of[15], (EXPERTS, D, 2, FF), D ** -0.5, 0.21875, ((0, 4), (1, 4), (3, 2)), jnp.float32)
    w_down = scatter_about(streams_of[16], (EXPERTS, FF, D), FF ** -0.5, 0.125, ((0, 4), (1, 2), (2, 4)), jnp.float32)
    left_gu = draw_left_gu(jax.random.fold_in(streams_of[25], 71), 0)
    right_gu = draw_right_gu(jax.random.fold_in(streams_of[25], 71), 0)
    left_down = draw_left_down(jax.random.fold_in(streams_of[25], 71), 0)
    right_down = draw_right_down(jax.random.fold_in(streams_of[25], 71), 0)
    left_root_gu = draw_left_root_gu(jax.random.fold_in(streams_of[25], 71), 0)
    right_root_gu = draw_right_root_gu(jax.random.fold_in(streams_of[25], 71), 0)
    left_root_down = draw_left_root_down(jax.random.fold_in(streams_of[25], 71), 0)
    right_root_down = draw_right_root_down(jax.random.fold_in(streams_of[25], 71), 0)
    return {"tokens": tokens, "lengths": lengths, "routes": routes, "prev_logits": prev_logits, "cotangent": cotangent, "w_qkv": w_qkv, "w_out": w_out, "route_w": route_w, "gains": gains, "const_vec": const_vec, "stat_qkv": stat_qkv, "stat_out": stat_out, "stat_route": stat_route, "stat_gains": stat_gains, "stat_const": stat_const, "w_gate_up": w_gate_up, "w_down": w_down, "left_gu": left_gu, "right_gu": right_gu, "left_down": left_down, "right_down": right_down, "left_root_gu": left_root_gu, "right_root_gu": right_root_gu, "left_root_down": left_root_down, "right_root_down": right_root_down}


@jax.custom_vjp
def low(v):
    return lax.optimization_barrier(v.astype(jnp.bfloat16)).astype(jnp.float32)

@jax.custom_vjp
def low_back(v):
    return v

def low_keep(v):
    return (low(v), None)

def low_pass(kept, grad):
    return (grad,)

def back_keep(v):
    return (v, None)

def back_low(kept, grad):
    return (low(grad),)
low.defvjp(low_keep, low_pass)
low_back.defvjp(back_keep, back_low)
NORM_EPS = 1e-06
HIGH_PREC = lax.Precision.HIGHEST
SHAMPOO_RATE = 0.5

def norm_apply(values, gain_vec):
    norm_scale = lax.rsqrt(lax.optimization_barrier(jnp.mean(values * values, axis=-1, keepdims=True)) + NORM_EPS)
    return values * norm_scale * gain_vec

def slot_tables(route_rows, num_ffn, capacity, total_experts):
    flat_routes = route_rows.reshape(-1)
    one_hot = (flat_routes[:, None] == jnp.arange(total_experts, dtype=jnp.int32)[None, :]).astype(jnp.int32)
    earlier = (jnp.cumsum(one_hot, axis=0) - one_hot).astype(jnp.int32)
    slot_index = lax.optimization_barrier(jnp.sum(earlier * one_hot, axis=1)).astype(jnp.int32)
    is_ffn = flat_routes < num_ffn
    target = jnp.where(is_ffn, flat_routes, num_ffn).astype(jnp.int32)
    token_index = (jnp.arange(flat_routes.shape[0], dtype=jnp.int32) // 2).astype(jnp.int32)
    token_of = jnp.zeros((num_ffn, capacity), jnp.int32).at[target, slot_index].set(token_index, mode='drop')
    filled = jnp.zeros((num_ffn, capacity), jnp.float32).at[target, slot_index].set(1.0, mode='drop')
    where_in = jnp.where(is_ffn, flat_routes * capacity + slot_index, 0).astype(jnp.int32)
    return (token_of, filled, where_in, is_ffn, target, slot_index)

def block_forward(weights, x_rows, length_row, route_rows, prev_rows):
    w_qkv, w_out, route_w, gains, const_vec, w_gate_up, w_down = weights
    row_count = x_rows.shape[0]
    positions = jnp.arange(row_count, dtype=jnp.int32)
    seq_ends = jnp.cumsum(length_row).astype(jnp.int32)
    doc_index = lax.optimization_barrier(jnp.sum((positions[:, None] >= seq_ends[None, :]).astype(jnp.int32), axis=1)).astype(jnp.int32)
    valid_rows = (doc_index < NSEQ).astype(jnp.float32)[:, None]
    allowed = (doc_index[:, None] == doc_index[None, :]) & (positions[:, None] >= positions[None, :])
    h_one = low(norm_apply(x_rows, gains[0]))
    qkv_rows = low_back(low(jnp.dot(h_one, w_qkv, precision=HIGH_PREC))).reshape(row_count, 3, HEADS, HEAD)
    queries, key_heads, values = (qkv_rows[:, 0], qkv_rows[:, 1], qkv_rows[:, 2])
    scores = low_back(jnp.einsum('qhd,khd->hqk', queries, key_heads, precision=HIGH_PREC) * HEAD ** (-0.5))
    scores = jnp.where(allowed[None], scores, -1e+30)
    top_score = lax.optimization_barrier(jnp.max(scores, axis=-1, keepdims=True))
    exp_scores = jnp.exp(scores - top_score)
    softmax_probs = exp_scores / lax.optimization_barrier(jnp.sum(exp_scores, axis=-1, keepdims=True))
    mixed_heads = jnp.einsum('hqk,khd->qhd', low(softmax_probs), values, precision=HIGH_PREC).reshape(row_count, D)
    mixed_heads = low_back(low(mixed_heads))
    attn_out = low_back(jnp.dot(mixed_heads, w_out, precision=HIGH_PREC))
    first_sum = x_rows + valid_rows * attn_out
    h_two = norm_apply(first_sum, gains[1])
    h_two_low = low(h_two)
    logits_all = low_back(jnp.dot(h_two_low, route_w, precision=HIGH_PREC))
    logits = logits_all[:, :E_ALL] + prev_rows
    chosen = jnp.take_along_axis(logits, route_rows, axis=1)
    gate_weights = jax.nn.softmax(chosen, axis=-1)
    const_mix = jax.nn.softmax(logits_all[:, E_ALL:].reshape(row_count, 2, 2), axis=-1)
    token_of, filled, where_in, is_ffn, target, slot_index = slot_tables(route_rows, EXPERTS, CAP, E_ALL)
    sent_rows = low_back(h_two_low[token_of] * filled[:, :, None])
    pre_act = low_back(jnp.einsum('ecd,edf->ecf', sent_rows, w_gate_up.reshape(EXPERTS, D, 2 * FF), precision=HIGH_PREC))
    hidden = low(jax.nn.silu(pre_act[:, :, :FF]) * pre_act[:, :, FF:])
    expert_out = low_back(low(jnp.einsum('ecf,efd->ecd', hidden, w_down, precision=HIGH_PREC)))
    picked = expert_out.reshape(EXPERTS * CAP, D)[where_in] * is_ffn.astype(jnp.float32)[:, None]
    picked = picked.reshape(row_count, 2, D)
    copy_sel = (route_rows == EXPERTS + 1).astype(jnp.float32)
    const_sel = (route_rows[:, :, None] == EXPERTS + 2 + jnp.arange(2, dtype=jnp.int32)[None, None, :]).astype(jnp.float32)
    const_out = const_mix[:, :, 0:1] * h_two[:, None, :] + const_mix[:, :, 1:2] * const_vec[None, :, :]
    outputs = picked + copy_sel[:, :, None] * h_two[:, None, :] + jnp.einsum('tkc,tcd->tkd', const_sel, const_out, precision=HIGH_PREC)
    moe_out = valid_rows * lax.optimization_barrier(jnp.sum(gate_weights[:, :, None] * outputs, axis=1))
    return first_sum + moe_out

def diag_update(weight, grad, state, rate):
    new_state = 0.5 * state + 0.5 * grad * grad
    return (new_state, weight - rate * grad / (jnp.sqrt(new_state) + 1e-08))

def reference(tokens, lengths, routes, prev_logits, cotangent, w_qkv, w_out, route_w, gains, const_vec, stat_qkv, stat_out, stat_route, stat_gains, stat_const, w_gate_up, w_down, left_gu, right_gu, left_down, right_down, left_root_gu, right_root_gu, left_root_down, right_root_down):
    block_count = lengths.shape[0]

    def forward(x_all, *masters):
        rounded = tuple((low(weight) for weight in masters))

        def one_block(pieces):
            return block_forward(rounded, *pieces)
        pieces = (x_all.reshape(block_count, TOK_DEV, D), lengths, routes.reshape(block_count, TOK_DEV, 2), prev_logits.reshape(block_count, TOK_DEV, E_ALL))
        return lax.map(jax.checkpoint(one_block), pieces).reshape(block_count * TOK_DEV, D)
    masters = (w_qkv, w_out, route_w, gains, const_vec, w_gate_up, w_down)
    out_full, pull_back = jax.vjp(forward, tokens.astype(jnp.float32), *masters)
    grads = pull_back(cotangent.astype(jnp.float32))
    grad_tokens = grads[0]
    grad_qkv, grad_attn_out, grad_route, grad_gains, grad_const, grad_gate_up, grad_down = grads[1:]
    moment_qkv, new_qkv = diag_update(w_qkv, grad_qkv, stat_qkv, D ** (-0.5))
    moment_attn_out, new_attn_out = diag_update(w_out, grad_attn_out, stat_out, HEAD ** (-0.5))
    moment_route, new_route = diag_update(route_w, grad_route, stat_route, (4 * D) ** (-0.5))
    moment_gains, new_gains = diag_update(gains, grad_gains, stat_gains, 0.3)
    moment_const, new_const = diag_update(const_vec, grad_const, stat_const, 0.5)
    gu_mats = jnp.transpose(grad_gate_up, (0, 2, 1, 3))
    new_left_gu = 0.5 * left_gu + 0.5 * jnp.einsum('emif,emjf->emij', gu_mats, gu_mats, precision=HIGH_PREC)
    new_right_gu = 0.5 * right_gu + 0.5 * jnp.einsum('emdi,emdj->emij', gu_mats, gu_mats, precision=HIGH_PREC)
    gu_step = jnp.einsum('emid,emdf->emif', left_root_gu, gu_mats, precision=HIGH_PREC)
    gu_step = jnp.einsum('emif,emfj->emij', gu_step, right_root_gu, precision=HIGH_PREC)
    new_gate_up = w_gate_up - SHAMPOO_RATE * jnp.transpose(gu_step, (0, 2, 1, 3))
    new_left_down = 0.5 * left_down + 0.5 * jnp.einsum('eif,ejf->eij', grad_down, grad_down, precision=HIGH_PREC)
    new_right_down = 0.5 * right_down + 0.5 * jnp.einsum('efi,efj->eij', grad_down, grad_down, precision=HIGH_PREC)
    down_step = jnp.einsum('eif,efd->eid', left_root_down, grad_down, precision=HIGH_PREC)
    down_step = jnp.einsum('eid,edj->eij', down_step, right_root_down, precision=HIGH_PREC)
    new_down = w_down - SHAMPOO_RATE * down_step
    return (out_full.astype(jnp.bfloat16), grad_tokens, grad_qkv, moment_qkv, new_qkv, grad_attn_out, moment_attn_out, new_attn_out, grad_route, moment_route, new_route, grad_gains, moment_gains, new_gains, grad_const, moment_const, new_const, grad_gate_up, grad_down, new_left_gu, new_right_gu, new_left_down, new_right_down, new_gate_up, new_down)
```

```python
import functools

import jax
import jax.numpy as jnp
from jax import lax
from jax.experimental import pallas as pl
from jax.experimental.pallas import tpu as pltpu
from jax.sharding import PartitionSpec as P

D = 768
HEADS = 12
HEAD = 64
CAP = 32
LANES = 128


NORM_EPS = 1e-06
SHAMPOO_RATE = 0.5
MESH = pl.DeviceIdType.MESH
VMEM_BYTES = 56 * 2**20


def flip(index, bit):
    return index + bit * (1 - 2 * ((index // bit) % 2))


def flip_all(index, mask, bits):
    for dim in range(bits):
        if mask & (1 << dim):
            index = flip(index, 1 << dim)
    return index


def mesh_sizes():
    return tuple(lax.axis_size(name) for name in ("dp", "row", "col"))


def bits_of(count):
    bits = count.bit_length() - 1
    assert 1 << bits == count
    return bits


def greet(over_dp, dims, place):
    n_dp, n_row, n_col = dims
    d, r, c = place
    peers = []
    if over_dp:
        peers += [((d + j) % n_dp, r, c) for j in range(1, n_dp)]
    peers += [(d, flip(r, 1 << dim), c) for dim in range(bits_of(n_row))]
    peers += [(d, r, (c + i) % n_col) for i in range(1, n_col)]
    barrier = pltpu.get_barrier_semaphore()
    for peer in peers:
        pl.semaphore_signal(barrier, inc=1, device_id=peer, device_id_type=MESH)
    pl.semaphore_wait(barrier, len(peers))


def remote(src, dst, send_sem, recv_sem, device):
    return pltpu.make_async_remote_copy(
        src_ref=src,
        dst_ref=dst,
        send_sem=send_sem,
        recv_sem=recv_sem,
        device_id=device,
        device_id_type=MESH,
    )


def spread_blocks(dims, place, chunks, over_dp, own, dp_source, slot, sems):
    n_dp, n_row, n_col = dims
    d, r, c = place
    bits = bits_of(n_row)
    dp_send, dp_recv, row_send, row_recv, col_send, col_recv, own_sem = sems
    sent = []

    def block(j, x):
        return slot(c, j, flip_all(r, x, bits))

    def to_row(j, src, x, bit):
        copy = remote(
            src,
            block(j, x),
            row_send.at[j, x ^ bit],
            row_recv.at[j, x ^ bit],
            (d, flip(r, bit), c),
        )
        copy.start()
        sent.append(copy)

    def to_cols(j, src, x):
        for i in range(1, n_col):
            copy = remote(
                src,
                block(j, x),
                col_send.at[j, x, i],
                col_recv.at[j, x, i],
                (d, r, (c + i) % n_col),
            )
            copy.start()
            sent.append(copy)

    def order(j):
        return [1 << ((j + s) % bits) for s in range(bits)]

    locals_ = []

    def start(j):
        if over_dp and j > 0:
            src = block(j, 0)
            remote(src, src, dp_send.at[j], dp_recv.at[j], (d, r, c)).wait_recv()
        else:
            src = own(j)
            keep = pltpu.make_async_copy(src, block(j, 0), own_sem.at[j])
            keep.start()
            locals_.append(keep)
        for bit in order(j):
            to_row(j, src, 0, bit)
        to_cols(j, src, 0)

    start(0)
    if over_dp:
        for j in range(1, n_dp):
            peer = (d + j) % n_dp
            copy = remote(
                dp_source(peer),
                slot(c, ("from", d), r),
                dp_send.at[j],
                dp_recv.at[j],
                (peer, r, c),
            )
            copy.start()
            sent.append(copy)
    for j in range(chunks):
        if j + 1 < chunks:
            start(j + 1)
        have = [0]
        dim_order = order(j)
        for s, bit in enumerate(dim_order):
            new = [x ^ bit for x in have]
            for x in new:
                ref = block(j, x)
                remote(ref, ref, row_send.at[j, x], row_recv.at[j, x], (d, r, c)).wait_recv()
                for later in dim_order[s + 1 :]:
                    to_row(j, ref, x, later)
                to_cols(j, ref, x)
            have += new
    for j in range(chunks):
        for x in range(n_row):
            for i in range(1, n_col):
                ref = slot((c + n_col - i) % n_col, j, flip_all(r, x, bits))
                remote(ref, ref, col_send.at[j, x, i], col_recv.at[j, x, i], (d, r, c)).wait_recv()
    for copy in sent:
        copy.wait_send()
    for copy in locals_:
        copy.wait()


def spread_sems(dims, chunks):
    n_dp, n_row, n_col = dims
    dma = pltpu.SemaphoreType.DMA
    return [
        dma((n_dp,)),
        dma((n_dp,)),
        dma((chunks, n_row)),
        dma((chunks, n_row)),
        dma((chunks, n_row, n_col)),
        dma((chunks, n_row, n_col)),
        dma((chunks,)),
    ]


def axis_place():
    return tuple(lax.axis_index(name) for name in ("dp", "row", "col"))


def param_gather_kernel(dims, shard_ref, out_ref, swap_ref, block_ref, swap_send, swap_recv, *sems):
    n_dp, n_row, n_col = dims
    place = axis_place()
    d, r, c = place
    rows = shard_ref.shape[1]
    greet(True, dims, place)
    copies = []
    for i in range(1, n_col):
        other = (c + i) % n_col
        copy = remote(
            shard_ref.at[other], swap_ref.at[c], swap_send.at[i], swap_recv.at[i], (d, r, other)
        )
        copy.start()
        copies.append(copy)
    swap_ref[pl.ds(c, 1)] = shard_ref[pl.ds(c, 1)]
    for copy in copies:
        copy.wait()
    for i in range(n_col):
        block_ref[i * rows : (i + 1) * rows, :] = swap_ref[i]
    low_ref = sems[-1]
    low_ref[...] = block_ref[...].astype(jnp.bfloat16)

    def slot(col, j, b):
        k = j[1] if isinstance(j, tuple) else (d + n_dp - j) % n_dp
        return out_ref.at[col, k, b]

    spread_blocks(
        dims, place, n_dp, True, lambda j: low_ref, lambda k: low_ref, slot, sems[:-1]
    )


def param_gather(shard, dims):
    n_dp, n_row, n_col = dims
    _, rows, width = shard.shape
    dma = pltpu.SemaphoreType.DMA
    return pl.pallas_call(
        functools.partial(param_gather_kernel, dims),
        out_shape=jax.ShapeDtypeStruct((n_col, n_dp, n_row, n_col * rows, width), jnp.bfloat16),
        in_specs=[pl.BlockSpec(memory_space=pltpu.VMEM)],
        out_specs=pl.BlockSpec(memory_space=pl.ANY),
        scratch_shapes=[
            pltpu.VMEM((n_col, rows, width), jnp.float32),
            pltpu.VMEM((n_col * rows, width), jnp.float32),
            dma((n_col,)),
            dma((n_col,)),
            *spread_sems(dims, n_dp),
            pltpu.VMEM((n_col * rows, width), jnp.bfloat16),
        ],
        compiler_params=pltpu.CompilerParams(
            collective_id=0, has_side_effects=True, vmem_limit_bytes=VMEM_BYTES
        ),
        name="param_gather",
    )(shard)


def token_gather_kernel(dims, src_ref, out_ref, *sems):
    n_dp, n_row, n_col = dims
    place = axis_place()
    d = place[0]
    greet(True, dims, place)

    def slot(col, j, b):
        k = j[1] if isinstance(j, tuple) else (d + n_dp - j) % n_dp
        return out_ref.at[col, k, b]

    spread_blocks(
        dims,
        place,
        n_dp,
        True,
        lambda j: src_ref.at[d],
        lambda k: src_ref.at[k],
        slot,
        sems,
    )


def token_gather(rows, dims):
    n_dp, n_row, n_col = dims
    _, slots, width = rows.shape
    return pl.pallas_call(
        functools.partial(token_gather_kernel, dims),
        out_shape=jax.ShapeDtypeStruct((n_col, n_dp, n_row, slots, width), rows.dtype),
        in_specs=[pl.BlockSpec(memory_space=pl.ANY)],
        out_specs=pl.BlockSpec(memory_space=pl.ANY),
        scratch_shapes=spread_sems(dims, n_dp),
        compiler_params=pltpu.CompilerParams(
            collective_id=1, has_side_effects=True, vmem_limit_bytes=VMEM_BYTES
        ),
        name="token_gather",
    )(rows)


def plane_gather_kernel(dims, src_ref, out_ref, *sems):
    place = axis_place()
    greet(False, dims, place)
    spread_blocks(
        dims,
        place,
        src_ref.shape[0],
        False,
        lambda j: src_ref.at[j],
        None,
        lambda col, j, b: out_ref.at[col, b, j],
        sems,
    )


def plane_gather(parts, dims):
    n_dp, n_row, n_col = dims
    chunks, rows, width = parts.shape
    return pl.pallas_call(
        functools.partial(plane_gather_kernel, dims),
        out_shape=jax.ShapeDtypeStruct((n_col, n_row, chunks, rows, width), parts.dtype),
        in_specs=[pl.BlockSpec(memory_space=pl.ANY)],
        out_specs=pl.BlockSpec(memory_space=pl.ANY),
        scratch_shapes=spread_sems(dims, chunks),
        compiler_params=pltpu.CompilerParams(
            collective_id=2, has_side_effects=True, vmem_limit_bytes=VMEM_BYTES
        ),
        name="plane_gather",
    )(parts)


def add_low(left, right):
    return (left.astype(jnp.float32) + right.astype(jnp.float32)).astype(jnp.bfloat16)


def reduce_blocks(dims, place, part_ref, bufs, sems, deliver):
    n_dp, n_row, n_col = dims
    d, r, c = place
    bits = bits_of(n_row)
    mine_ref, col_ref, row_ref = bufs
    mine_sem, col_send, col_recv, row_send, row_recv = sems
    steps = list(range(1, n_dp)) + [0]
    sent = []
    held = []
    for t, j in enumerate(steps):
        k = (d + j) % n_dp
        for i in range(1, n_col):
            other = (c + i) % n_col
            copy = remote(
                part_ref.at[other, k],
                col_ref.at[t, i - 1],
                col_send.at[t, i],
                col_recv.at[t, i],
                (d, r, other),
            )
            copy.start()
            sent.append(copy)
        keep = pltpu.make_async_copy(part_ref.at[c, k], mine_ref.at[t], mine_sem.at[t])
        keep.start()
        held.append(keep)

    def order(t):
        return [1 << ((t + s) % bits) for s in range(bits)]

    def send_half(t, s):
        dim_order = order(t)
        bit = dim_order[s]
        before = sum(dim_order[:s])
        for x in range(n_row):
            if not x & before and x & bit:
                copy = remote(
                    mine_ref.at[t, flip_all(r, x, bits)],
                    row_ref.at[t, x ^ bit, s],
                    row_send.at[t, x ^ bit, s],
                    row_recv.at[t, x ^ bit, s],
                    (d, flip(r, bit), c),
                )
                copy.start()
                sent.append(copy)

    def stage_col(t):
        held[t].wait()
        for i in range(1, n_col):
            ref = col_ref.at[t, i - 1]
            remote(ref, ref, col_send.at[t, i], col_recv.at[t, i], (d, r, c)).wait_recv()

        @pl.loop(0, n_row)
        def _(b):
            total = mine_ref[t, b].astype(jnp.float32)
            for i in range(1, n_col):
                total = total + col_ref[t, i - 1, b].astype(jnp.float32)
            mine_ref[t, b] = total.astype(jnp.bfloat16)

        send_half(t, 0)

    def stage_row(t, s):
        dim_order = order(t)
        before = sum(dim_order[: s + 1])
        for y in range(n_row):
            if not y & before:
                ref = row_ref.at[t, y, s]
                remote(
                    ref, ref, row_send.at[t, y, s], row_recv.at[t, y, s], (d, r, c)
                ).wait_recv()
                b = flip_all(r, y, bits)
                mine_ref[t, b] = add_low(mine_ref[t, b], row_ref[t, y, s])
        if s + 1 < bits:
            send_half(t, s + 1)
        else:
            deliver(t, steps[t], mine_ref.at[t, r])

    for tick in range(n_dp + bits):
        for s in reversed(range(bits)):
            t = tick - 1 - s
            if 0 <= t < n_dp:
                stage_row(t, s)
        if tick < n_dp:
            stage_col(tick)
    return sent


def reduce_scratch(dims, rows, width):
    n_dp, n_row, n_col = dims
    bits = bits_of(n_row)
    dma = pltpu.SemaphoreType.DMA
    low = jnp.bfloat16
    return [
        pltpu.VMEM((n_dp, n_row, rows, width), low),
        pltpu.VMEM((n_dp, max(1, n_col - 1), n_row, rows, width), low),
        pltpu.VMEM((n_dp, n_row // 2, bits, rows, width), low)
        if n_row == 2
        else pltpu.VMEM((n_dp, n_row, bits, rows, width), low),
        dma((n_dp,)),
        dma((n_dp, n_col)),
        dma((n_dp, n_col)),
        dma((n_dp, n_row, bits)),
        dma((n_dp, n_row, bits)),
    ]


def token_reduce_kernel(dims, part_ref, out_ref, *scratch):
    n_dp, n_row, n_col = dims
    place = axis_place()
    d, r, c = place
    dp_send, dp_recv, own_sem = scratch[8:]
    greet(True, dims, place)
    late = []

    def deliver(t, j, block):
        if j == 0:
            keep = pltpu.make_async_copy(block, out_ref.at[d], own_sem)
            keep.start()
            late.append(keep.wait)
        else:
            copy = remote(
                block, out_ref.at[d], dp_send.at[j], dp_recv.at[j], ((d + j) % n_dp, r, c)
            )
            copy.start()
            late.append(copy.wait_send)

    sent = reduce_blocks(dims, place, part_ref, scratch[:3], scratch[3:8], deliver)
    for j in range(1, n_dp):
        ref = out_ref.at[(d + n_dp - j) % n_dp]
        remote(ref, ref, dp_send.at[j], dp_recv.at[j], (d, r, c)).wait_recv()
    for copy in sent:
        copy.wait_send()
    for wait in late:
        wait()


def token_reduce(parts, dims):
    n_dp = dims[0]
    slots, width = parts.shape[3:]
    dma = pltpu.SemaphoreType.DMA
    return pl.pallas_call(
        functools.partial(token_reduce_kernel, dims),
        out_shape=jax.ShapeDtypeStruct((n_dp, slots, width), jnp.bfloat16),
        in_specs=[pl.BlockSpec(memory_space=pl.ANY)],
        out_specs=pl.BlockSpec(memory_space=pl.ANY),
        scratch_shapes=[*reduce_scratch(dims, slots, width), dma((n_dp,)), dma((n_dp,)), dma],
        compiler_params=pltpu.CompilerParams(
            collective_id=3, has_side_effects=True, vmem_limit_bytes=VMEM_BYTES
        ),
        name="token_reduce",
    )(parts)


def param_reduce_kernel(dims, part_ref, out_ref, *scratch):
    n_dp, n_row, n_col = dims
    place = axis_place()
    d, r, c = place
    dp_send, dp_recv, dp_ref, swap_send, swap_recv, swap_ref, sum_ref = scratch[8:]
    rows = out_ref.shape[1]
    greet(True, dims, place)
    late = []
    kept = []

    def deliver(t, j, block):
        if j == 0:
            kept.append(block)
        else:
            copy = remote(
                block, dp_ref.at[j], dp_send.at[j], dp_recv.at[j], ((d + j) % n_dp, r, c)
            )
            copy.start()
            late.append(copy)

    sent = reduce_blocks(dims, place, part_ref, scratch[:3], scratch[3:8], deliver)
    total = kept[0][...].astype(jnp.float32)
    for j in range(1, n_dp):
        ref = dp_ref.at[j]
        remote(ref, ref, dp_send.at[j], dp_recv.at[j], (d, r, c)).wait_recv()
        total = total + dp_ref[j].astype(jnp.float32)
    sum_ref[...] = total
    for i in range(n_col):
        swap_ref[i] = sum_ref[i * rows : (i + 1) * rows, :]
    for i in range(1, n_col):
        other = (c + i) % n_col
        copy = remote(
            swap_ref.at[other], out_ref.at[c], swap_send.at[i], swap_recv.at[i], (d, r, other)
        )
        copy.start()
        late.append(copy)
    out_ref[pl.ds(c, 1)] = swap_ref[pl.ds(c, 1)]
    for i in range(1, n_col):
        ref = out_ref.at[(c + n_col - i) % n_col]
        remote(ref, ref, swap_send.at[i], swap_recv.at[i], (d, r, c)).wait_recv()
    for copy in sent:
        copy.wait_send()
    for copy in late:
        copy.wait_send()


def param_reduce(parts, dims):
    n_dp, n_row, n_col = dims
    block_rows, width = parts.shape[3:]
    rows = block_rows // n_col
    dma = pltpu.SemaphoreType.DMA
    return pl.pallas_call(
        functools.partial(param_reduce_kernel, dims),
        out_shape=jax.ShapeDtypeStruct((n_col, rows, width), jnp.float32),
        in_specs=[pl.BlockSpec(memory_space=pl.ANY)],
        out_specs=pl.BlockSpec(memory_space=pltpu.VMEM),
        scratch_shapes=[
            *reduce_scratch(dims, block_rows, width),
            dma((n_dp,)),
            dma((n_dp,)),
            pltpu.VMEM((n_dp, block_rows, width), jnp.bfloat16),
            dma((n_col,)),
            dma((n_col,)),
            pltpu.VMEM((n_col, rows, width), jnp.float32),
            pltpu.VMEM((block_rows, width), jnp.float32),
        ],
        compiler_params=pltpu.CompilerParams(
            collective_id=4, has_side_effects=True, vmem_limit_bytes=VMEM_BYTES
        ),
        name="param_reduce",
    )(parts)


def norm_forward(values, gain_vec):
    norm_scale = lax.rsqrt(jnp.mean(values * values, axis=-1, keepdims=True) + NORM_EPS)
    normed = values * norm_scale
    return (normed * gain_vec, normed, norm_scale)


def norm_backward(grad_out, normed, norm_scale, gain_vec):
    grad_normed = grad_out * gain_vec
    inner_mean = jnp.mean(grad_normed * normed, axis=-1, keepdims=True)
    return (norm_scale * (grad_normed - normed * inner_mean), jnp.sum(grad_out * normed, axis=0))


def attention_probs(queries, key_heads, allowed):
    scores = jnp.einsum(
        "qhd,khd->hqk", queries, key_heads, preferred_element_type=jnp.float32
    ) * HEAD ** (-0.5)
    scores = jnp.where(allowed[None], scores, -1e30)
    top_score = jnp.max(scores, axis=-1, keepdims=True)
    exp_scores = jnp.exp(scores - top_score)
    return exp_scores / jnp.sum(exp_scores, axis=-1, keepdims=True)


def diag_update(weight, grad, state, rate):
    new_state = 0.5 * state + 0.5 * grad * grad
    return (new_state, weight - rate * grad / (jnp.sqrt(new_state) + 1e-08))


def dot(left, right, dims=(((1,), (0,)), ((), ()))):
    return lax.dot_general(left, right, dims, preferred_element_type=jnp.float32)


NT = (((1,), (1,)), ((), ()))
TN = (((0,), (0,)), ((), ()))


def body(
    tokens,
    lengths,
    routes,
    prev_logits,
    cotangent,
    w_qkv,
    w_out,
    route_w,
    gains,
    const_vec,
    stat_qkv,
    stat_out,
    stat_route,
    stat_gains,
    stat_const,
    w_gate_up,
    w_down,
    left_gu,
    right_gu,
    left_down,
    right_down,
    left_root_gu,
    right_root_gu,
    left_root_down,
    right_root_down,
):
    dims = mesh_sizes()
    n_dp, n_row, n_col = dims
    low = jnp.bfloat16
    row_total = tokens.shape[0]
    total_experts = prev_logits.shape[1]
    num_ffn = total_experts - 4
    seq_count = lengths.shape[1]
    shard_rows = w_qkv.shape[0]
    wide_qkv = w_qkv.shape[1] // n_col
    wide_out = w_out.shape[1] // n_col
    route_cols = route_w.shape[1]
    wide = wide_qkv + wide_out + LANES

    def by_col(matrix):
        return matrix.reshape(matrix.shape[0], n_col, -1).transpose(1, 0, 2)

    def small_block(route_part, gain_part, const_part):
        together = jnp.concatenate([route_part, gain_part.T, const_part.T], axis=1)
        return jnp.pad(together, ((0, 0), (0, LANES - together.shape[1])))

    small = small_block(route_w, gains, const_vec)
    shard = jnp.concatenate(
        [by_col(w_qkv), by_col(w_out), jnp.broadcast_to(small[None], (n_col, shard_rows, LANES))],
        axis=2,
    )
    whole = param_gather(shard, dims).reshape(n_col, D, wide)
    full_qkv = [whole[i, :, :wide_qkv] for i in range(n_col)]
    full_out = [whole[i, :, wide_qkv : wide_qkv + wide_out] for i in range(n_col)]
    full_small = whole[0, :, wide_qkv + wide_out :]
    full_route = full_small[:, :route_cols]
    row_vectors = full_small[:, route_cols : route_cols + 4].T.astype(jnp.float32)
    gain_one, gain_two, const_rows = row_vectors[0], row_vectors[1], row_vectors[2:4]

    row_depth = w_gate_up.shape[1]
    col_width = w_gate_up.shape[3]
    slice_wide = col_width // n_row
    gu_slices = w_gate_up[0].astype(low).reshape(row_depth, 2, n_row, slice_wide)
    gu_slices = gu_slices.transpose(2, 0, 1, 3)
    gu_own = lax.all_to_all(gu_slices, "row", split_axis=0, concat_axis=0, tiled=True)
    gu_own = gu_own.reshape(n_row * row_depth, 2 * slice_wide)
    down_slices = w_down[0].astype(low).reshape(n_row, slice_wide, row_depth)
    down_own = lax.all_to_all(down_slices, "row", split_axis=0, concat_axis=0, tiled=True)
    down_own = down_own.transpose(1, 0, 2).reshape(slice_wide, n_row * row_depth)

    positions = jnp.arange(row_total, dtype=jnp.int32)
    seq_ends = jnp.cumsum(lengths[0])
    doc_index = jnp.sum((positions[:, None] >= seq_ends[None, :]).astype(jnp.int32), axis=1)
    valid_rows = (doc_index < seq_count).astype(jnp.float32)[:, None]
    allowed = (doc_index[:, None] == doc_index[None, :]) & (
        positions[:, None] >= positions[None, :]
    )
    inputs = tokens.astype(jnp.float32)
    h_one, normed_one, scale_one = norm_forward(inputs, gain_one)
    h_one_low = h_one.astype(low)
    qkv_rows = jnp.concatenate([dot(h_one_low, part) for part in full_qkv], axis=1).astype(low)
    qkv_rows = qkv_rows.reshape(row_total, 3, HEADS, HEAD)
    queries, key_heads, values = (qkv_rows[:, 0], qkv_rows[:, 1], qkv_rows[:, 2])
    softmax_probs = attention_probs(queries, key_heads, allowed)
    probs_low = softmax_probs.astype(low)
    mixed_heads = jnp.einsum("hqk,khd->qhd", probs_low, values, preferred_element_type=jnp.float32)
    mixed_heads = mixed_heads.reshape(row_total, D).astype(low)
    attn_out = jnp.concatenate([dot(mixed_heads, part) for part in full_out], axis=1)
    first_sum = inputs + valid_rows * attn_out
    h_two, normed_two, scale_two = norm_forward(first_sum, gain_two)
    h_two_low = h_two.astype(low)
    logits_all = dot(h_two_low, full_route)
    logits = logits_all[:, :total_experts] + prev_logits
    pick_table = (
        routes[:, :, None] == jnp.arange(total_experts, dtype=jnp.int32)[None, None, :]
    ).astype(jnp.float32)
    chosen = jnp.sum(pick_table * logits[:, None, :], axis=-1)
    gate_weights = jax.nn.softmax(chosen, axis=-1)
    const_mix = jax.nn.softmax(logits_all[:, total_experts:].reshape(row_total, 2, 2), axis=-1)

    earlier = dot(
        (positions[:, None] > positions[None, :]).astype(low),
        jnp.sum(pick_table, axis=1).astype(low),
    )
    slot_index = jnp.sum(earlier[:, None, :] * pick_table, axis=-1).astype(jnp.int32)
    where_in = jnp.where(routes < num_ffn, routes * CAP + slot_index, -1)
    slot_ids = jnp.arange(num_ffn * CAP, dtype=jnp.int32)
    place_first = where_in[:, 0:1] == slot_ids[None, :]
    place_second = where_in[:, 1:2] == slot_ids[None, :]
    place_both = (place_first | place_second).astype(low)
    slot_gate = jnp.sum(
        place_first.astype(jnp.float32) * gate_weights[:, 0:1]
        + place_second.astype(jnp.float32) * gate_weights[:, 1:2],
        axis=0,
    )
    grad_y = cotangent.astype(jnp.float32) * valid_rows
    sent_rows = dot(place_both, h_two_low, TN).astype(low)
    grad_made = (slot_gate[:, None] * dot(place_both, grad_y.astype(low), TN)).astype(low)
    sent_both = jnp.concatenate(
        [sent_rows.reshape(num_ffn, CAP, D), grad_made.reshape(num_ffn, CAP, D)], axis=2
    )

    arrived = token_gather(sent_both, dims).reshape(-1, 2 * D)
    rows_in = arrived[:, :D]
    grads_in = arrived[:, D:]
    pre_act = dot(rows_in, gu_own)
    gate_part = pre_act[:, :slice_wide]
    up_part = pre_act[:, slice_wide:]
    sigma = jax.nn.sigmoid(gate_part)
    silu = gate_part * sigma
    hidden = (silu * up_part).astype(low)
    made_rows = dot(hidden, down_own).astype(low)
    grad_hidden = dot(grads_in, down_own, NT)
    grad_pre = jnp.concatenate(
        [
            grad_hidden * up_part * sigma * (1.0 + gate_part * (1.0 - sigma)),
            grad_hidden * silu,
        ],
        axis=1,
    ).astype(low)
    grad_rows = dot(grad_pre, gu_own, NT).astype(low)
    parts_back = jnp.concatenate([made_rows, grad_rows], axis=1)
    parts_back = parts_back.reshape(n_col, n_dp, n_row, CAP, 2 * D)
    came_back = token_reduce(parts_back, dims).reshape(num_ffn * CAP, 2 * D)
    expert_out = came_back[:, :D]
    grad_sent = came_back[:, D:]

    grad_gu_own = dot(rows_in, grad_pre, TN).astype(low)
    grad_down_own = dot(hidden, grads_in, TN).astype(low)
    grads_own = jnp.concatenate(
        [grad_gu_own[:, :slice_wide], grad_gu_own[:, slice_wide:], grad_down_own.T], axis=0
    )
    gathered = plane_gather(grads_own.reshape(4, -1, slice_wide), dims)
    gathered = gathered.reshape(n_col * n_row, 3, D, slice_wide)
    whole_all = gathered.transpose(1, 2, 0, 3).reshape(3, D, -1)
    whole_gu = whole_all[:2]
    whole_down_t = whole_all[2]

    is_ffn_first = dot(place_first.astype(low), expert_out)
    is_ffn_second = dot(place_second.astype(low), expert_out)
    picked = jnp.stack([is_ffn_first, is_ffn_second], axis=1)
    copy_sel = (routes == num_ffn + 1).astype(jnp.float32)
    const_sel = (
        routes[:, :, None] == num_ffn + 2 + jnp.arange(2, dtype=jnp.int32)[None, None, :]
    ).astype(jnp.float32)
    const_out = (
        const_mix[:, :, 0:1] * h_two[:, None, :] + const_mix[:, :, 1:2] * const_rows[None, :, :]
    )
    outputs = (
        picked
        + copy_sel[:, :, None] * h_two[:, None, :]
        + const_sel[:, :, 0:1] * const_out[:, None, 0, :]
        + const_sel[:, :, 1:2] * const_out[:, None, 1, :]
    )
    moe_out = valid_rows * jnp.sum(gate_weights[:, :, None] * outputs, axis=1)
    result = (first_sum + moe_out).astype(low)
    grad_gate = jnp.sum(grad_y[:, None, :] * outputs, axis=-1)
    grad_chosen = gate_weights * (
        grad_gate - jnp.sum(gate_weights * grad_gate, axis=-1, keepdims=True)
    )
    grad_logits = jnp.sum(grad_chosen[:, :, None] * pick_table, axis=1)
    const_weight = jnp.sum(const_sel * gate_weights[:, :, None], axis=1)
    mix_first = const_weight * jnp.sum(grad_y * h_two, axis=-1, keepdims=True)
    mix_second = const_weight * jnp.stack(
        [jnp.sum(grad_y * const_rows[0], axis=-1), jnp.sum(grad_y * const_rows[1], axis=-1)], axis=1
    )
    grad_mix = jnp.stack([mix_first, mix_second], axis=-1)
    grad_mix_logits = const_mix * (grad_mix - jnp.sum(const_mix * grad_mix, axis=-1, keepdims=True))
    grad_logits_all = jnp.concatenate(
        [grad_logits, grad_mix_logits.reshape(row_total, 4)], axis=1
    ).astype(low)
    grad_route_full = dot(h_two_low, grad_logits_all, TN)
    const_scale = const_weight * const_mix[:, :, 1]
    grad_const_full = jnp.stack(
        [
            jnp.sum(const_scale[:, 0:1] * grad_y, axis=0),
            jnp.sum(const_scale[:, 1:2] * grad_y, axis=0),
        ]
    )
    back_rows = dot(place_both, grad_sent)
    own_weight = jnp.sum(gate_weights * copy_sel, axis=1, keepdims=True) + jnp.sum(
        const_weight * const_mix[:, :, 0], axis=1, keepdims=True
    )
    grad_h_two = dot(grad_logits_all, full_route, NT) + back_rows + own_weight * grad_y
    grad_first, grad_gain_two = norm_backward(grad_h_two, normed_two, scale_two, gain_two)
    grad_first = grad_first + cotangent.astype(jnp.float32)
    grad_attn = (valid_rows * grad_first).astype(low)
    grad_mixed = functools.reduce(
        jnp.add,
        [
            dot(grad_attn[:, i * wide_out : (i + 1) * wide_out], part, NT)
            for i, part in enumerate(full_out)
        ],
    ).astype(low)
    grad_mixed = grad_mixed.reshape(row_total, HEADS, HEAD)
    grad_values = jnp.einsum(
        "hqk,qhd->khd", probs_low, grad_mixed, preferred_element_type=jnp.float32
    )
    grad_probs = jnp.einsum("qhd,khd->hqk", grad_mixed, values, preferred_element_type=jnp.float32)
    grad_scores = softmax_probs * (
        grad_probs - jnp.sum(softmax_probs * grad_probs, axis=-1, keepdims=True)
    )
    grad_scores = grad_scores.astype(low)
    grad_queries = jnp.einsum(
        "hqk,khd->qhd", grad_scores, key_heads, preferred_element_type=jnp.float32
    ) * HEAD ** (-0.5)
    grad_keys = jnp.einsum(
        "hqk,qhd->khd", grad_scores, queries, preferred_element_type=jnp.float32
    ) * HEAD ** (-0.5)
    grad_qkv_rows = (
        jnp.stack([grad_queries, grad_keys, grad_values], axis=1)
        .reshape(row_total, 3 * D)
        .astype(low)
    )
    grad_h_one = functools.reduce(
        jnp.add,
        [
            dot(grad_qkv_rows[:, i * wide_qkv : (i + 1) * wide_qkv], part, NT)
            for i, part in enumerate(full_qkv)
        ],
    )
    grad_input, grad_gain_one = norm_backward(grad_h_one, normed_one, scale_one, gain_one)
    grad_input = grad_input + grad_first
    grad_gains_full = jnp.stack([grad_gain_one, grad_gain_two])

    grad_small = small_block(grad_route_full, grad_gains_full, grad_const_full).astype(low)
    param_parts = jnp.stack(
        [
            jnp.concatenate(
                [
                    dot(h_one_low, grad_qkv_rows[:, i * wide_qkv : (i + 1) * wide_qkv], TN).astype(
                        low
                    ),
                    dot(mixed_heads, grad_attn[:, i * wide_out : (i + 1) * wide_out], TN).astype(
                        low
                    ),
                    grad_small,
                ],
                axis=1,
            )
            for i in range(n_col)
        ]
    )
    summed = param_reduce(
        param_parts.reshape(n_col, n_dp, n_row, n_col * shard_rows, wide), dims
    )

    def from_col(parts):
        return parts.transpose(1, 0, 2).reshape(parts.shape[1], -1)

    grad_qkv = from_col(summed[:, :, :wide_qkv])
    grad_attn_out = from_col(summed[:, :, wide_qkv : wide_qkv + wide_out])
    sum_small = summed[0, :, wide_qkv + wide_out :]
    grad_route = sum_small[:, :route_cols]
    grad_gains = sum_small[:, route_cols : route_cols + 2].T
    grad_const = sum_small[:, route_cols + 2 : route_cols + 4].T
    moment_qkv, new_qkv = diag_update(w_qkv, grad_qkv, stat_qkv, D ** (-0.5))
    moment_attn_out, new_attn_out = diag_update(w_out, grad_attn_out, stat_out, HEAD ** (-0.5))
    moment_route, new_route = diag_update(route_w, grad_route, stat_route, (4 * D) ** (-0.5))
    moment_gains, new_gains = diag_update(gains, grad_gains, stat_gains, 0.3)
    moment_const, new_const = diag_update(const_vec, grad_const, stat_const, 0.5)

    r = lax.axis_index("row")
    c = lax.axis_index("col")
    owner_place = r * n_col + c
    grad_gu_block = lax.dynamic_slice(
        whole_gu, (0, r * row_depth, c * col_width), (2, row_depth, col_width)
    ).astype(jnp.float32)
    grad_down_block = lax.dynamic_slice(
        whole_down_t, (r * row_depth, c * col_width), (row_depth, col_width)
    ).T.astype(jnp.float32)
    left_rows = left_gu.shape[2]
    right_rows = right_gu.shape[2]
    mine_left = lax.dynamic_slice_in_dim(whole_all, owner_place * left_rows, left_rows, 1)
    mine_right = lax.dynamic_slice_in_dim(whole_all, owner_place * right_rows, right_rows, 2)
    left_sum = jnp.einsum("mif,mjf->mij", mine_left, whole_all, preferred_element_type=jnp.float32)
    right_sum = jnp.einsum(
        "mdi,mdj->mij", mine_right, whole_all, preferred_element_type=jnp.float32
    )
    new_left_gu = 0.5 * left_gu + 0.5 * left_sum[None, :2]
    new_right_gu = 0.5 * right_gu + 0.5 * right_sum[None, :2]
    new_left_down = 0.5 * left_down + 0.5 * right_sum[None, 2]
    new_right_down = 0.5 * right_down + 0.5 * left_sum[None, 2]
    gu_step = jnp.einsum(
        "mid,mdf->mif", left_root_gu[0].astype(low), whole_gu, preferred_element_type=jnp.float32
    )
    gu_step = jnp.einsum(
        "mif,mjf->mij",
        gu_step.astype(low),
        right_root_gu[0].astype(low),
        preferred_element_type=jnp.float32,
    )
    new_gate_up = w_gate_up - SHAMPOO_RATE * gu_step.transpose(1, 0, 2)[None]
    down_step = dot(right_root_down[0].astype(low), whole_down_t)
    down_step = dot(left_root_down[0].astype(low), down_step.astype(low), NT)
    new_down = w_down - SHAMPOO_RATE * down_step[None]
    return (
        result,
        grad_input,
        grad_qkv,
        moment_qkv,
        new_qkv,
        grad_attn_out,
        moment_attn_out,
        new_attn_out,
        grad_route,
        moment_route,
        new_route,
        grad_gains,
        moment_gains,
        new_gains,
        grad_const,
        moment_const,
        new_const,
        grad_gu_block.transpose(1, 0, 2)[None],
        grad_down_block[None],
        new_left_gu,
        new_right_gu,
        new_left_down,
        new_right_down,
        new_gate_up,
        new_down,
    )


def solution(mesh):
    placed = (
        P(("dp", "row", "col"), None),
        P(("dp", "row", "col"), None),
        P(("dp", "row", "col"), None),
        P(("dp", "row", "col"), None),
        P(("dp", "row", "col"), None),
        P(("dp", "row", "col"), None),
        P(("dp", "row", "col"), None),
        P(("dp", "row", "col"), None),
        P(None, ("dp", "row", "col")),
        P(None, ("dp", "row", "col")),
        P(("dp", "row", "col"), None),
        P(("dp", "row", "col"), None),
        P(("dp", "row", "col"), None),
        P(None, ("dp", "row", "col")),
        P(None, ("dp", "row", "col")),
        P("dp", "row", None, "col"),
        P("dp", "col", "row"),
        P("dp", None, ("row", "col"), None),
        P("dp", None, ("row", "col"), None),
        P("dp", ("row", "col"), None),
        P("dp", ("row", "col"), None),
        P("dp", None, "row", None),
        P("dp", None, "col", None),
        P("dp", "col", None),
        P("dp", "row", None),
    )
    return jax.shard_map(
        body,
        mesh=mesh,
        in_specs=placed,
        out_specs=(
            P(("dp", "row", "col"), None),
            P(("dp", "row", "col"), None),
            P(("dp", "row", "col"), None),
            P(("dp", "row", "col"), None),
            P(("dp", "row", "col"), None),
            P(("dp", "row", "col"), None),
            P(("dp", "row", "col"), None),
            P(("dp", "row", "col"), None),
            P(("dp", "row", "col"), None),
            P(("dp", "row", "col"), None),
            P(("dp", "row", "col"), None),
            P(None, ("dp", "row", "col")),
            P(None, ("dp", "row", "col")),
            P(None, ("dp", "row", "col")),
            P(None, ("dp", "row", "col")),
            P(None, ("dp", "row", "col")),
            P(None, ("dp", "row", "col")),
            P("dp", "row", None, "col"),
            P("dp", "col", "row"),
            P("dp", None, ("row", "col"), None),
            P("dp", None, ("row", "col"), None),
            P("dp", ("row", "col"), None),
            P("dp", ("row", "col"), None),
            P("dp", "row", None, "col"),
            P("dp", "col", "row"),
        ),
        check_vma=False,
    )
```

```python
import functools

import jax
import jax.numpy as jnp
from jax import lax
from jax.experimental import pallas as pl
from jax.experimental.pallas import tpu as pltpu
from jax.sharding import PartitionSpec as P

D = 768
HEADS = 12
HEAD = 64
CAP = 32
LANES = 128


NORM_EPS = 1e-06
SHAMPOO_RATE = 0.5
MESH = pl.DeviceIdType.MESH
VMEM_BYTES = 56 * 2**20


def flip(index, bit):
    return index + bit * (1 - 2 * ((index // bit) % 2))


def flip_all(index, mask, bits):
    for dim in range(bits):
        if mask & (1 << dim):
            index = flip(index, 1 << dim)
    return index


def mesh_sizes():
    return tuple(lax.axis_size(name) for name in ("dp", "row", "col"))


def bits_of(count):
    bits = count.bit_length() - 1
    assert 1 << bits == count
    return bits


def greet(over_dp, dims, place):
    n_dp, n_row, n_col = dims
    d, r, c = place
    peers = []
    if over_dp:
        peers += [((d + j) % n_dp, r, c) for j in range(1, n_dp)]
    peers += [(d, flip(r, 1 << dim), c) for dim in range(bits_of(n_row))]
    peers += [(d, r, (c + i) % n_col) for i in range(1, n_col)]
    barrier = pltpu.get_barrier_semaphore()
    for peer in peers:
        pl.semaphore_signal(barrier, inc=1, device_id=peer, device_id_type=MESH)
    pl.semaphore_wait(barrier, len(peers))


def remote(src, dst, send_sem, recv_sem, device):
    return pltpu.make_async_remote_copy(
        src_ref=src,
        dst_ref=dst,
        send_sem=send_sem,
        recv_sem=recv_sem,
        device_id=device,
        device_id_type=MESH,
    )


def spread_blocks(dims, place, chunks, over_dp, own, dp_source, slot, sems):
    n_dp, n_row, n_col = dims
    d, r, c = place
    bits = bits_of(n_row)
    dp_send, dp_recv, row_send, row_recv, col_send, col_recv, own_sem = sems
    sent = []

    def block(j, x):
        return slot(c, j, flip_all(r, x, bits))

    def to_row(j, src, x, bit):
        copy = remote(
            src,
            block(j, x),
            row_send.at[j, x ^ bit],
            row_recv.at[j, x ^ bit],
            (d, flip(r, bit), c),
        )
        copy.start()
        sent.append(copy)

    def to_cols(j, src, x):
        for i in range(1, n_col):
            copy = remote(
                src,
                block(j, x),
                col_send.at[j, x, i],
                col_recv.at[j, x, i],
                (d, r, (c + i) % n_col),
            )
            copy.start()
            sent.append(copy)

    def order(j):
        return [1 << ((j + s) % bits) for s in range(bits)]

    locals_ = []

    def start(j):
        if over_dp and j > 0:
            src = block(j, 0)
            remote(src, src, dp_send.at[j], dp_recv.at[j], (d, r, c)).wait_recv()
        else:
            src = own(j)
            keep = pltpu.make_async_copy(src, block(j, 0), own_sem.at[j])
            keep.start()
            locals_.append(keep)
        for bit in order(j):
            to_row(j, src, 0, bit)
        to_cols(j, src, 0)

    def arrived(j, x, later_dims):
        ref = block(j, x)
        remote(ref, ref, row_send.at[j, x], row_recv.at[j, x], (d, r, c)).wait_recv()
        for later in later_dims:
            to_row(j, ref, x, later)
        to_cols(j, ref, x)

    def pass_on(j):
        have = [0]
        dim_order = order(j)
        for s, bit in enumerate(dim_order[:-1]):
            new = [x ^ bit for x in have]
            for x in new:
                arrived(j, x, dim_order[s + 1 :])
            have += new

    def last_arrivals(j):
        bit = order(j)[-1]
        for x in range(n_row):
            if x & bit:
                arrived(j, x, [])

    start(0)
    if over_dp:
        for j in range(1, n_dp):
            peer = (d + j) % n_dp
            copy = remote(
                dp_source(peer),
                slot(c, ("from", d), r),
                dp_send.at[j],
                dp_recv.at[j],
                (peer, r, c),
            )
            copy.start()
            sent.append(copy)
        for j in range(1, chunks):
            start(j)
            pass_on(j - 1)
        pass_on(chunks - 1)
    else:
        for j in range(1, chunks):
            start(j)
        for j in range(chunks):
            pass_on(j)
    for j in range(chunks):
        last_arrivals(j)
    for j in range(chunks):
        for x in range(n_row):
            for i in range(1, n_col):
                ref = slot((c + n_col - i) % n_col, j, flip_all(r, x, bits))
                remote(ref, ref, col_send.at[j, x, i], col_recv.at[j, x, i], (d, r, c)).wait_recv()
    for copy in sent:
        copy.wait_send()
    for copy in locals_:
        copy.wait()


def spread_sems(dims, chunks):
    n_dp, n_row, n_col = dims
    dma = pltpu.SemaphoreType.DMA
    return [
        dma((n_dp,)),
        dma((n_dp,)),
        dma((chunks, n_row)),
        dma((chunks, n_row)),
        dma((chunks, n_row, n_col)),
        dma((chunks, n_row, n_col)),
        dma((chunks,)),
    ]


def axis_place():
    return tuple(lax.axis_index(name) for name in ("dp", "row", "col"))


def param_gather_kernel(dims, shard_ref, out_ref, swap_ref, block_ref, swap_send, swap_recv, *sems):
    n_dp, n_row, n_col = dims
    place = axis_place()
    d, r, c = place
    rows = shard_ref.shape[1]
    greet(True, dims, place)
    copies = []
    for i in range(1, n_col):
        other = (c + i) % n_col
        copy = remote(
            shard_ref.at[other], swap_ref.at[c], swap_send.at[i], swap_recv.at[i], (d, r, other)
        )
        copy.start()
        copies.append(copy)
    swap_ref[pl.ds(c, 1)] = shard_ref[pl.ds(c, 1)]
    for copy in copies:
        copy.wait()
    for i in range(n_col):
        block_ref[i * rows : (i + 1) * rows, :] = swap_ref[i]
    low_ref = sems[-1]
    low_ref[...] = block_ref[...].astype(jnp.bfloat16)

    def slot(col, j, b):
        k = j[1] if isinstance(j, tuple) else (d + n_dp - j) % n_dp
        return out_ref.at[col, k, b]

    spread_blocks(
        dims, place, n_dp, True, lambda j: low_ref, lambda k: low_ref, slot, sems[:-1]
    )


def param_gather(shard, dims):
    n_dp, n_row, n_col = dims
    _, rows, width = shard.shape
    dma = pltpu.SemaphoreType.DMA
    return pl.pallas_call(
        functools.partial(param_gather_kernel, dims),
        out_shape=jax.ShapeDtypeStruct((n_col, n_dp, n_row, n_col * rows, width), jnp.bfloat16),
        in_specs=[pl.BlockSpec(memory_space=pltpu.VMEM)],
        out_specs=pl.BlockSpec(memory_space=pl.ANY),
        scratch_shapes=[
            pltpu.VMEM((n_col, rows, width), jnp.float32),
            pltpu.VMEM((n_col * rows, width), jnp.float32),
            dma((n_col,)),
            dma((n_col,)),
            *spread_sems(dims, n_dp),
            pltpu.VMEM((n_col * rows, width), jnp.bfloat16),
        ],
        compiler_params=pltpu.CompilerParams(
            collective_id=0, has_side_effects=True, vmem_limit_bytes=VMEM_BYTES
        ),
        name="param_gather",
    )(shard)


def token_gather_kernel(dims, src_ref, out_ref, *sems):
    n_dp, n_row, n_col = dims
    place = axis_place()
    d = place[0]
    greet(True, dims, place)

    def slot(col, j, b):
        k = j[1] if isinstance(j, tuple) else (d + n_dp - j) % n_dp
        return out_ref.at[col, k, b]

    spread_blocks(
        dims,
        place,
        n_dp,
        True,
        lambda j: src_ref.at[d],
        lambda k: src_ref.at[k],
        slot,
        sems,
    )


def token_gather(rows, dims):
    n_dp, n_row, n_col = dims
    _, slots, width = rows.shape
    return pl.pallas_call(
        functools.partial(token_gather_kernel, dims),
        out_shape=jax.ShapeDtypeStruct((n_col, n_dp, n_row, slots, width), rows.dtype),
        in_specs=[pl.BlockSpec(memory_space=pl.ANY)],
        out_specs=pl.BlockSpec(memory_space=pl.ANY),
        scratch_shapes=spread_sems(dims, n_dp),
        compiler_params=pltpu.CompilerParams(
            collective_id=1, has_side_effects=True, vmem_limit_bytes=VMEM_BYTES
        ),
        name="token_gather",
    )(rows)


def plane_gather_kernel(dims, src_ref, out_ref, *sems):
    place = axis_place()
    greet(False, dims, place)
    spread_blocks(
        dims,
        place,
        src_ref.shape[0],
        False,
        lambda j: src_ref.at[j],
        None,
        lambda col, j, b: out_ref.at[col, b, j],
        sems,
    )


def plane_gather(parts, dims):
    n_dp, n_row, n_col = dims
    chunks, rows, width = parts.shape
    return pl.pallas_call(
        functools.partial(plane_gather_kernel, dims),
        out_shape=jax.ShapeDtypeStruct((n_col, n_row, chunks, rows, width), parts.dtype),
        in_specs=[pl.BlockSpec(memory_space=pl.ANY)],
        out_specs=pl.BlockSpec(memory_space=pl.ANY),
        scratch_shapes=spread_sems(dims, chunks),
        compiler_params=pltpu.CompilerParams(
            collective_id=2, has_side_effects=True, vmem_limit_bytes=VMEM_BYTES
        ),
        name="plane_gather",
    )(parts)


def add_low(left, right):
    return (left.astype(jnp.float32) + right.astype(jnp.float32)).astype(jnp.bfloat16)


def reduce_blocks(dims, place, part_ref, bufs, sems, deliver):
    n_dp, n_row, n_col = dims
    d, r, c = place
    bits = bits_of(n_row)
    mine_ref, col_ref, row_ref = bufs
    mine_sem, col_send, col_recv, row_send, row_recv = sems
    steps = list(range(1, n_dp)) + [0]
    sent = []
    held = []
    for t, j in enumerate(steps):
        k = (d + j) % n_dp
        for i in range(1, n_col):
            other = (c + i) % n_col
            copy = remote(
                part_ref.at[other, k],
                col_ref.at[t, i - 1],
                col_send.at[t, i],
                col_recv.at[t, i],
                (d, r, other),
            )
            copy.start()
            sent.append(copy)
        keep = pltpu.make_async_copy(part_ref.at[c, k], mine_ref.at[t], mine_sem.at[t])
        keep.start()
        held.append(keep)

    def order(t):
        return [1 << ((t + s) % bits) for s in range(bits)]

    def send_half(t, s):
        dim_order = order(t)
        bit = dim_order[s]
        before = sum(dim_order[:s])
        for x in range(n_row):
            if not x & before and x & bit:
                copy = remote(
                    mine_ref.at[t, flip_all(r, x, bits)],
                    row_ref.at[t, x ^ bit, s],
                    row_send.at[t, x ^ bit, s],
                    row_recv.at[t, x ^ bit, s],
                    (d, flip(r, bit), c),
                )
                copy.start()
                sent.append(copy)

    def stage_col(t):
        held[t].wait()
        for i in range(1, n_col):
            ref = col_ref.at[t, i - 1]
            remote(ref, ref, col_send.at[t, i], col_recv.at[t, i], (d, r, c)).wait_recv()

        @pl.loop(0, n_row)
        def _(b):
            total = mine_ref[t, b].astype(jnp.float32)
            for i in range(1, n_col):
                total = total + col_ref[t, i - 1, b].astype(jnp.float32)
            mine_ref[t, b] = total.astype(jnp.bfloat16)

        send_half(t, 0)

    def stage_row(t, s):
        dim_order = order(t)
        before = sum(dim_order[: s + 1])
        for y in range(n_row):
            if not y & before:
                ref = row_ref.at[t, y, s]
                remote(
                    ref, ref, row_send.at[t, y, s], row_recv.at[t, y, s], (d, r, c)
                ).wait_recv()
                b = flip_all(r, y, bits)
                mine_ref[t, b] = add_low(mine_ref[t, b], row_ref[t, y, s])
        if s + 1 < bits:
            send_half(t, s + 1)
        else:
            deliver(t, steps[t], mine_ref.at[t, r])

    for t in range(n_dp):
        stage_col(t)
    for s in range(bits):
        for t in range(n_dp):
            stage_row(t, s)
    return sent


def reduce_scratch(dims, rows, width):
    n_dp, n_row, n_col = dims
    bits = bits_of(n_row)
    dma = pltpu.SemaphoreType.DMA
    low = jnp.bfloat16
    return [
        pltpu.VMEM((n_dp, n_row, rows, width), low),
        pltpu.VMEM((n_dp, max(1, n_col - 1), n_row, rows, width), low),
        pltpu.VMEM((n_dp, n_row // 2, bits, rows, width), low)
        if n_row == 2
        else pltpu.VMEM((n_dp, n_row, bits, rows, width), low),
        dma((n_dp,)),
        dma((n_dp, n_col)),
        dma((n_dp, n_col)),
        dma((n_dp, n_row, bits)),
        dma((n_dp, n_row, bits)),
    ]


def token_reduce_kernel(dims, part_ref, out_ref, *scratch):
    n_dp, n_row, n_col = dims
    place = axis_place()
    d, r, c = place
    dp_send, dp_recv, own_sem = scratch[8:]
    greet(True, dims, place)
    late = []

    def deliver(t, j, block):
        if j == 0:
            keep = pltpu.make_async_copy(block, out_ref.at[d], own_sem)
            keep.start()
            late.append(keep.wait)
        else:
            copy = remote(
                block, out_ref.at[d], dp_send.at[j], dp_recv.at[j], ((d + j) % n_dp, r, c)
            )
            copy.start()
            late.append(copy.wait_send)

    sent = reduce_blocks(dims, place, part_ref, scratch[:3], scratch[3:8], deliver)
    for j in range(1, n_dp):
        ref = out_ref.at[(d + n_dp - j) % n_dp]
        remote(ref, ref, dp_send.at[j], dp_recv.at[j], (d, r, c)).wait_recv()
    for copy in sent:
        copy.wait_send()
    for wait in late:
        wait()


def token_reduce(parts, dims):
    n_dp = dims[0]
    slots, width = parts.shape[3:]
    dma = pltpu.SemaphoreType.DMA
    return pl.pallas_call(
        functools.partial(token_reduce_kernel, dims),
        out_shape=jax.ShapeDtypeStruct((n_dp, slots, width), jnp.bfloat16),
        in_specs=[pl.BlockSpec(memory_space=pl.ANY)],
        out_specs=pl.BlockSpec(memory_space=pl.ANY),
        scratch_shapes=[*reduce_scratch(dims, slots, width), dma((n_dp,)), dma((n_dp,)), dma],
        compiler_params=pltpu.CompilerParams(
            collective_id=3, has_side_effects=True, vmem_limit_bytes=VMEM_BYTES
        ),
        name="token_reduce",
    )(parts)


def param_reduce_kernel(dims, part_ref, out_ref, *scratch):
    n_dp, n_row, n_col = dims
    place = axis_place()
    d, r, c = place
    dp_send, dp_recv, dp_ref, swap_send, swap_recv, swap_ref, sum_ref = scratch[8:]
    rows = out_ref.shape[1]
    greet(True, dims, place)
    late = []
    kept = []

    def deliver(t, j, block):
        if j == 0:
            kept.append(block)
        else:
            copy = remote(
                block, dp_ref.at[j], dp_send.at[j], dp_recv.at[j], ((d + j) % n_dp, r, c)
            )
            copy.start()
            late.append(copy)

    sent = reduce_blocks(dims, place, part_ref, scratch[:3], scratch[3:8], deliver)
    total = kept[0][...].astype(jnp.float32)
    for j in range(1, n_dp):
        ref = dp_ref.at[j]
        remote(ref, ref, dp_send.at[j], dp_recv.at[j], (d, r, c)).wait_recv()
        total = total + dp_ref[j].astype(jnp.float32)
    sum_ref[...] = total
    for i in range(n_col):
        swap_ref[i] = sum_ref[i * rows : (i + 1) * rows, :]
    for i in range(1, n_col):
        other = (c + i) % n_col
        copy = remote(
            swap_ref.at[other], out_ref.at[c], swap_send.at[i], swap_recv.at[i], (d, r, other)
        )
        copy.start()
        late.append(copy)
    out_ref[pl.ds(c, 1)] = swap_ref[pl.ds(c, 1)]
    for i in range(1, n_col):
        ref = out_ref.at[(c + n_col - i) % n_col]
        remote(ref, ref, swap_send.at[i], swap_recv.at[i], (d, r, c)).wait_recv()
    for copy in sent:
        copy.wait_send()
    for copy in late:
        copy.wait_send()


def param_reduce(parts, dims):
    n_dp, n_row, n_col = dims
    block_rows, width = parts.shape[3:]
    rows = block_rows // n_col
    dma = pltpu.SemaphoreType.DMA
    return pl.pallas_call(
        functools.partial(param_reduce_kernel, dims),
        out_shape=jax.ShapeDtypeStruct((n_col, rows, width), jnp.float32),
        in_specs=[pl.BlockSpec(memory_space=pl.ANY)],
        out_specs=pl.BlockSpec(memory_space=pltpu.VMEM),
        scratch_shapes=[
            *reduce_scratch(dims, block_rows, width),
            dma((n_dp,)),
            dma((n_dp,)),
            pltpu.VMEM((n_dp, block_rows, width), jnp.bfloat16),
            dma((n_col,)),
            dma((n_col,)),
            pltpu.VMEM((n_col, rows, width), jnp.float32),
            pltpu.VMEM((block_rows, width), jnp.float32),
        ],
        compiler_params=pltpu.CompilerParams(
            collective_id=4, has_side_effects=True, vmem_limit_bytes=VMEM_BYTES
        ),
        name="param_reduce",
    )(parts)


def norm_forward(values, gain_vec):
    norm_scale = lax.rsqrt(jnp.mean(values * values, axis=-1, keepdims=True) + NORM_EPS)
    normed = values * norm_scale
    return (normed * gain_vec, normed, norm_scale)


def norm_backward(grad_out, normed, norm_scale, gain_vec):
    grad_normed = grad_out * gain_vec
    inner_mean = jnp.mean(grad_normed * normed, axis=-1, keepdims=True)
    return (norm_scale * (grad_normed - normed * inner_mean), jnp.sum(grad_out * normed, axis=0))


def attention_probs(queries, key_heads, allowed):
    scores = jnp.einsum(
        "qhd,khd->hqk", queries, key_heads, preferred_element_type=jnp.float32
    ) * HEAD ** (-0.5)
    scores = jnp.where(allowed[None], scores, -1e30)
    top_score = jnp.max(scores, axis=-1, keepdims=True)
    exp_scores = jnp.exp(scores - top_score)
    return exp_scores / jnp.sum(exp_scores, axis=-1, keepdims=True)


def diag_update(weight, grad, state, rate):
    new_state = 0.5 * state + 0.5 * grad * grad
    return (new_state, weight - rate * grad / (jnp.sqrt(new_state) + 1e-08))


def dot(left, right, dims=(((1,), (0,)), ((), ()))):
    return lax.dot_general(left, right, dims, preferred_element_type=jnp.float32)


NT = (((1,), (1,)), ((), ()))
TN = (((0,), (0,)), ((), ()))


def shampoo_kernel(sizes, *refs):
    n_row, n_col, model, slice_wide, tile = sizes
    low = jnp.bfloat16
    (
        grads,
        left_root_gu,
        right_root_down,
        right_root_gu,
        left_root_down,
        left_gu,
        right_down,
        right_gu,
        left_down,
        weight_gu,
        weight_down,
        out_grad_gu,
        out_grad_down,
        out_left_gu,
        out_right_down,
        out_right_gu,
        out_left_down,
        out_weight_gu,
        out_weight_down,
        grad_buf,
        root_buf,
        wide_buf,
        left_buf,
        right_buf,
        weight_buf,
        step_buf,
        lhs_buf,
        in_sem,
        wide_sem,
        out_sem,
    ) = refs
    r = lax.axis_index("row")
    c = lax.axis_index("col")
    owner = r * n_col + c
    blocks = n_row * n_col
    left_rows = left_buf.shape[1]
    right_rows = right_buf.shape[1]
    depth = root_buf.shape[1]
    wide_rows = wide_buf.shape[1]
    tiles = wide_rows // tile
    mats = range(3)
    roots = [left_root_gu.at[0], left_root_gu.at[1], right_root_down]
    wides = [right_root_gu.at[0], right_root_gu.at[1], left_root_down]
    lefts = [left_gu.at[0], left_gu.at[1], right_down]
    rights = [right_gu.at[0], right_gu.at[1], left_down]
    weights = [weight_gu.at[:, 0], weight_gu.at[:, 1], weight_down]
    out_lefts = [out_left_gu.at[0], out_left_gu.at[1], out_right_down]
    out_rights = [out_right_gu.at[0], out_right_gu.at[1], out_left_down]
    out_weights = [out_weight_gu.at[:, 0], out_weight_gu.at[:, 1], out_weight_down]
    out_grads = [out_grad_gu.at[:, 0], out_grad_gu.at[:, 1], out_grad_down]

    def load(m, kind, src, dst):
        copy = pltpu.make_async_copy(src, dst, in_sem.at[m, kind])
        copy.start()
        return copy

    loads = []
    for m in mats:
        span = pl.ds(m * model, model)
        loads.append(
            [
                load(m, 0, grads.at[:, span], grad_buf.at[:, span]),
                load(m, 1, roots[m], root_buf.at[m]),
                load(m, 2, rights[m], right_buf.at[m]),
                load(m, 3, lefts[m], left_buf.at[m]),
                load(m, 4, weights[m], weight_buf.at[m]),
            ]
        )
        for t in range(tiles):
            rows = pl.ds(t * tile, tile)
            copy = pltpu.make_async_copy(
                wides[m].at[rows], wide_buf.at[m, rows], wide_sem.at[m, t]
            )
            copy.start()
            loads[m].append(copy)
    stores = []

    def store(m, kind, src, dst):
        copy = pltpu.make_async_copy(src, dst, out_sem.at[m, kind])
        copy.start()
        stores.append(copy)

    for m in mats:
        span = pl.ds(m * model, model)
        loads[m][0].wait()
        loads[m][1].wait()
        lhs_buf[:right_rows] = grad_buf[owner, span].T
        lhs_buf[right_rows:] = root_buf[m].astype(low)
        loads[m][2].wait()
        loads[m][3].wait()
        left_buf[m] = 0.5 * left_buf[m]

        @pl.loop(0, blocks)
        def _(q):
            cols = pl.ds(pl.multiple_of(q * slice_wide, slice_wide), slice_wide)
            block = grad_buf[q, span]
            made = dot(lhs_buf[...], block)
            right_buf[m, :, cols] = 0.5 * right_buf[m, :, cols] + 0.5 * made[:right_rows]
            step_buf[:, cols] = made[right_rows:].astype(low)
            rows = pl.ds(pl.multiple_of(m * model + owner * left_rows, 16), left_rows)
            left_buf[m] += 0.5 * dot(grad_buf[q, rows], block, NT)

        store(m, 0, right_buf.at[m], out_rights[m])
        store(m, 1, left_buf.at[m], out_lefts[m])
        loads[m][4].wait()
        for t in range(tiles):
            loads[m][5 + t].wait()
            cols = pl.ds(t * tile, tile)
            step = dot(step_buf[...], wide_buf[m, cols].astype(low), NT)
            weight_buf[m, :, cols] = weight_buf[m, :, cols] - SHAMPOO_RATE * step
        store(m, 2, weight_buf.at[m], out_weights[m])
        for b in range(n_row):
            rows = pl.ds(pl.multiple_of(m * model + r * depth, 16), depth)
            wide_buf[m, :depth, b * slice_wide : (b + 1) * slice_wide] = grad_buf[
                c * n_row + b, rows
            ].astype(jnp.float32)
        store(m, 3, wide_buf.at[m, :depth, : n_row * slice_wide], out_grads[m])
    for copy in stores:
        copy.wait()


def shampoo(
    grads,
    left_root_gu,
    right_root_down,
    right_root_gu,
    left_root_down,
    left_gu,
    right_down,
    right_gu,
    left_down,
    weight_gu,
    weight_down,
    n_row,
    n_col,
):
    blocks, _, slice_wide = grads.shape
    model = left_root_gu.shape[2]
    depth = left_root_gu.shape[1]
    wide_rows, wide_cols = left_root_down.shape
    right_rows = left_down.shape[0]
    left_rows = right_down.shape[0]
    tile = min(256, wide_rows)
    f32 = jnp.float32
    dma = pltpu.SemaphoreType.DMA
    any_spec = pl.BlockSpec(memory_space=pl.ANY)
    args = (
        grads,
        left_root_gu,
        right_root_down,
        right_root_gu,
        left_root_down,
        left_gu,
        right_down,
        right_gu,
        left_down,
        weight_gu,
        weight_down,
    )
    return pl.pallas_call(
        functools.partial(shampoo_kernel, (n_row, n_col, model, slice_wide, tile)),
        out_shape=[
            jax.ShapeDtypeStruct(weight_gu.shape, f32),
            jax.ShapeDtypeStruct(weight_down.shape, f32),
            jax.ShapeDtypeStruct(left_gu.shape, f32),
            jax.ShapeDtypeStruct(right_down.shape, f32),
            jax.ShapeDtypeStruct(right_gu.shape, f32),
            jax.ShapeDtypeStruct(left_down.shape, f32),
            jax.ShapeDtypeStruct(weight_gu.shape, f32),
            jax.ShapeDtypeStruct(weight_down.shape, f32),
        ],
        in_specs=[any_spec] * len(args),
        out_specs=[any_spec] * 8,
        scratch_shapes=[
            pltpu.VMEM(grads.shape, jnp.bfloat16),
            pltpu.VMEM((3, depth, model), f32),
            pltpu.VMEM((3, wide_rows, wide_cols), f32),
            pltpu.VMEM((3, left_rows, model), f32),
            pltpu.VMEM((3, right_rows, wide_cols), f32),
            pltpu.VMEM((3, depth, wide_rows), f32),
            pltpu.VMEM((depth, wide_cols), jnp.bfloat16),
            pltpu.VMEM((right_rows + depth, model), jnp.bfloat16),
            dma((3, 5)),
            dma((3, wide_rows // tile)),
            dma((3, 4)),
        ],
        compiler_params=pltpu.CompilerParams(vmem_limit_bytes=60 * 2**20),
        name="shampoo",
    )(*args)


def shampoo_plain(
    grads,
    left_root_gu,
    right_root_down,
    right_root_gu,
    left_root_down,
    left_gu,
    right_down,
    right_gu,
    left_down,
    weight_gu,
    weight_down,
    n_row,
    n_col,
):
    low = jnp.bfloat16
    blocks, _, slice_wide = grads.shape
    model = left_root_gu.shape[2]
    r = lax.axis_index("row")
    c = lax.axis_index("col")
    owner = r * n_col + c
    left_rows = right_down.shape[0]
    right_rows = left_down.shape[0]
    product = functools.partial(jnp.einsum, preferred_element_type=jnp.float32)
    whole = grads.reshape(blocks, 3, model, slice_wide).transpose(1, 2, 0, 3).reshape(3, model, -1)
    mine_left = lax.dynamic_slice_in_dim(whole, owner * left_rows, left_rows, 1)
    mine_right = lax.dynamic_slice_in_dim(whole, owner * right_rows, right_rows, 2)
    left_sum = 0.5 * product("mif,mjf->mij", mine_left, whole)
    right_sum = 0.5 * product("mdi,mdj->mij", mine_right, whole)
    roots = jnp.concatenate([left_root_gu, right_root_down[None]]).astype(low)
    wides = jnp.concatenate([right_root_gu, left_root_down[None]]).astype(low)
    step = product("mid,mdf->mif", roots, whole).astype(low)
    step = SHAMPOO_RATE * product("mif,mjf->mij", step, wides)
    depth, wide_rows = weight_down.shape
    block = lax.dynamic_slice(whole, (0, r * depth, c * wide_rows), (3, depth, wide_rows))
    block = block.astype(jnp.float32)
    return (
        block[:2].transpose(1, 0, 2),
        block[2],
        0.5 * left_gu + left_sum[:2],
        0.5 * right_down + left_sum[2],
        0.5 * right_gu + right_sum[:2],
        0.5 * left_down + right_sum[2],
        weight_gu - step[:2].transpose(1, 0, 2),
        weight_down - step[2],
    )


def body(
    tokens,
    lengths,
    routes,
    prev_logits,
    cotangent,
    w_qkv,
    w_out,
    route_w,
    gains,
    const_vec,
    stat_qkv,
    stat_out,
    stat_route,
    stat_gains,
    stat_const,
    w_gate_up,
    w_down,
    left_gu,
    right_gu,
    left_down,
    right_down,
    left_root_gu,
    right_root_gu,
    left_root_down,
    right_root_down,
):
    dims = mesh_sizes()
    n_dp, n_row, n_col = dims
    low = jnp.bfloat16
    row_total = tokens.shape[0]
    total_experts = prev_logits.shape[1]
    num_ffn = total_experts - 4
    seq_count = lengths.shape[1]
    shard_rows = w_qkv.shape[0]
    wide_qkv = w_qkv.shape[1] // n_col
    wide_out = w_out.shape[1] // n_col
    route_cols = route_w.shape[1]
    wide = wide_qkv + wide_out + LANES

    def by_col(matrix):
        return matrix.reshape(matrix.shape[0], n_col, -1).transpose(1, 0, 2)

    def small_block(route_part, gain_part, const_part):
        together = jnp.concatenate([route_part, gain_part.T, const_part.T], axis=1)
        return jnp.pad(together, ((0, 0), (0, LANES - together.shape[1])))

    small = small_block(route_w, gains, const_vec)
    shard = jnp.concatenate(
        [by_col(w_qkv), by_col(w_out), jnp.broadcast_to(small[None], (n_col, shard_rows, LANES))],
        axis=2,
    )
    whole = param_gather(shard, dims).reshape(n_col, D, wide)
    full_qkv = [whole[i, :, :wide_qkv] for i in range(n_col)]
    full_out = [whole[i, :, wide_qkv : wide_qkv + wide_out] for i in range(n_col)]
    full_small = whole[0, :, wide_qkv + wide_out :]
    full_route = full_small[:, :route_cols]
    row_vectors = full_small[:, route_cols : route_cols + 4].T.astype(jnp.float32)
    gain_one, gain_two, const_rows = row_vectors[0], row_vectors[1], row_vectors[2:4]

    row_depth = w_gate_up.shape[1]
    col_width = w_gate_up.shape[3]
    slice_wide = col_width // n_row
    gu_slices = w_gate_up[0].astype(low).reshape(row_depth, 2, n_row, slice_wide)
    gu_slices = gu_slices.transpose(2, 0, 1, 3)
    gu_own = lax.all_to_all(gu_slices, "row", split_axis=0, concat_axis=0, tiled=True)
    gu_own = gu_own.reshape(n_row * row_depth, 2 * slice_wide)
    down_slices = w_down[0].astype(low).reshape(n_row, slice_wide, row_depth)
    down_own = lax.all_to_all(down_slices, "row", split_axis=0, concat_axis=0, tiled=True)
    down_own = down_own.transpose(1, 0, 2).reshape(slice_wide, n_row * row_depth)

    positions = jnp.arange(row_total, dtype=jnp.int32)
    seq_ends = jnp.cumsum(lengths[0])
    doc_index = jnp.sum((positions[:, None] >= seq_ends[None, :]).astype(jnp.int32), axis=1)
    valid_rows = (doc_index < seq_count).astype(jnp.float32)[:, None]
    allowed = (doc_index[:, None] == doc_index[None, :]) & (
        positions[:, None] >= positions[None, :]
    )
    inputs = tokens.astype(jnp.float32)
    h_one, normed_one, scale_one = norm_forward(inputs, gain_one)
    h_one_low = h_one.astype(low)
    qkv_rows = jnp.concatenate([dot(h_one_low, part) for part in full_qkv], axis=1).astype(low)
    qkv_rows = qkv_rows.reshape(row_total, 3, HEADS, HEAD)
    queries, key_heads, values = (qkv_rows[:, 0], qkv_rows[:, 1], qkv_rows[:, 2])
    softmax_probs = attention_probs(queries, key_heads, allowed)
    probs_low = softmax_probs.astype(low)
    mixed_heads = jnp.einsum("hqk,khd->qhd", probs_low, values, preferred_element_type=jnp.float32)
    mixed_heads = mixed_heads.reshape(row_total, D).astype(low)
    attn_out = jnp.concatenate([dot(mixed_heads, part) for part in full_out], axis=1)
    first_sum = inputs + valid_rows * attn_out
    h_two, normed_two, scale_two = norm_forward(first_sum, gain_two)
    h_two_low = h_two.astype(low)
    logits_all = dot(h_two_low, full_route)
    logits = logits_all[:, :total_experts] + prev_logits
    pick_table = (
        routes[:, :, None] == jnp.arange(total_experts, dtype=jnp.int32)[None, None, :]
    ).astype(jnp.float32)
    chosen = jnp.sum(pick_table * logits[:, None, :], axis=-1)
    gate_weights = jax.nn.softmax(chosen, axis=-1)
    const_mix = jax.nn.softmax(logits_all[:, total_experts:].reshape(row_total, 2, 2), axis=-1)

    earlier = dot(
        (positions[:, None] > positions[None, :]).astype(low),
        jnp.sum(pick_table, axis=1).astype(low),
    )
    slot_index = jnp.sum(earlier[:, None, :] * pick_table, axis=-1).astype(jnp.int32)
    where_in = jnp.where(routes < num_ffn, routes * CAP + slot_index, -1)
    slot_ids = jnp.arange(num_ffn * CAP, dtype=jnp.int32)
    place_first = where_in[:, 0:1] == slot_ids[None, :]
    place_second = where_in[:, 1:2] == slot_ids[None, :]
    place_both = (place_first | place_second).astype(low)
    slot_gate = jnp.sum(
        place_first.astype(jnp.float32) * gate_weights[:, 0:1]
        + place_second.astype(jnp.float32) * gate_weights[:, 1:2],
        axis=0,
    )
    grad_y = cotangent.astype(jnp.float32) * valid_rows
    sent_rows = dot(place_both, h_two_low, TN).astype(low)
    grad_made = (slot_gate[:, None] * dot(place_both, grad_y.astype(low), TN)).astype(low)
    sent_both = jnp.concatenate(
        [sent_rows.reshape(num_ffn, CAP, D), grad_made.reshape(num_ffn, CAP, D)], axis=2
    )

    arrived = token_gather(sent_both, dims).reshape(-1, 2 * D)
    rows_in = arrived[:, :D]
    grads_in = arrived[:, D:]
    pre_act = dot(rows_in, gu_own)
    gate_part = pre_act[:, :slice_wide]
    up_part = pre_act[:, slice_wide:]
    sigma = jax.nn.sigmoid(gate_part)
    silu = gate_part * sigma
    hidden = (silu * up_part).astype(low)
    made_rows = dot(hidden, down_own).astype(low)
    grad_hidden = dot(grads_in, down_own, NT)
    grad_pre = jnp.concatenate(
        [
            grad_hidden * up_part * sigma * (1.0 + gate_part * (1.0 - sigma)),
            grad_hidden * silu,
        ],
        axis=1,
    ).astype(low)
    grad_rows = dot(grad_pre, gu_own, NT).astype(low)
    parts_back = jnp.concatenate([made_rows, grad_rows], axis=1)
    parts_back = parts_back.reshape(n_col, n_dp, n_row, CAP, 2 * D)
    came_back = token_reduce(parts_back, dims).reshape(num_ffn * CAP, 2 * D)
    expert_out = came_back[:, :D]
    grad_sent = came_back[:, D:]

    grad_gu_own = dot(rows_in, grad_pre, TN).astype(low)
    grad_down_own = dot(hidden, grads_in, TN).astype(low)
    grads_own = jnp.concatenate(
        [grad_gu_own[:, :slice_wide], grad_gu_own[:, slice_wide:], grad_down_own.T], axis=0
    )
    gathered = plane_gather(grads_own.reshape(4, -1, slice_wide), dims)
    gathered = gathered.reshape(n_col * n_row, 3 * D, slice_wide)

    is_ffn_first = dot(place_first.astype(low), expert_out)
    is_ffn_second = dot(place_second.astype(low), expert_out)
    picked = jnp.stack([is_ffn_first, is_ffn_second], axis=1)
    copy_sel = (routes == num_ffn + 1).astype(jnp.float32)
    const_sel = (
        routes[:, :, None] == num_ffn + 2 + jnp.arange(2, dtype=jnp.int32)[None, None, :]
    ).astype(jnp.float32)
    const_out = (
        const_mix[:, :, 0:1] * h_two[:, None, :] + const_mix[:, :, 1:2] * const_rows[None, :, :]
    )
    outputs = (
        picked
        + copy_sel[:, :, None] * h_two[:, None, :]
        + const_sel[:, :, 0:1] * const_out[:, None, 0, :]
        + const_sel[:, :, 1:2] * const_out[:, None, 1, :]
    )
    moe_out = valid_rows * jnp.sum(gate_weights[:, :, None] * outputs, axis=1)
    result = (first_sum + moe_out).astype(low)
    grad_gate = jnp.sum(grad_y[:, None, :] * outputs, axis=-1)
    grad_chosen = gate_weights * (
        grad_gate - jnp.sum(gate_weights * grad_gate, axis=-1, keepdims=True)
    )
    grad_logits = jnp.sum(grad_chosen[:, :, None] * pick_table, axis=1)
    const_weight = jnp.sum(const_sel * gate_weights[:, :, None], axis=1)
    mix_first = const_weight * jnp.sum(grad_y * h_two, axis=-1, keepdims=True)
    mix_second = const_weight * jnp.stack(
        [jnp.sum(grad_y * const_rows[0], axis=-1), jnp.sum(grad_y * const_rows[1], axis=-1)], axis=1
    )
    grad_mix = jnp.stack([mix_first, mix_second], axis=-1)
    grad_mix_logits = const_mix * (grad_mix - jnp.sum(const_mix * grad_mix, axis=-1, keepdims=True))
    grad_logits_all = jnp.concatenate(
        [grad_logits, grad_mix_logits.reshape(row_total, 4)], axis=1
    ).astype(low)
    grad_route_full = dot(h_two_low, grad_logits_all, TN)
    const_scale = const_weight * const_mix[:, :, 1]
    grad_const_full = jnp.stack(
        [
            jnp.sum(const_scale[:, 0:1] * grad_y, axis=0),
            jnp.sum(const_scale[:, 1:2] * grad_y, axis=0),
        ]
    )
    back_rows = dot(place_both, grad_sent)
    own_weight = jnp.sum(gate_weights * copy_sel, axis=1, keepdims=True) + jnp.sum(
        const_weight * const_mix[:, :, 0], axis=1, keepdims=True
    )
    grad_h_two = dot(grad_logits_all, full_route, NT) + back_rows + own_weight * grad_y
    grad_first, grad_gain_two = norm_backward(grad_h_two, normed_two, scale_two, gain_two)
    grad_first = grad_first + cotangent.astype(jnp.float32)
    grad_attn = (valid_rows * grad_first).astype(low)
    grad_mixed = functools.reduce(
        jnp.add,
        [
            dot(grad_attn[:, i * wide_out : (i + 1) * wide_out], part, NT)
            for i, part in enumerate(full_out)
        ],
    ).astype(low)
    grad_mixed = grad_mixed.reshape(row_total, HEADS, HEAD)
    grad_values = jnp.einsum(
        "hqk,qhd->khd", probs_low, grad_mixed, preferred_element_type=jnp.float32
    )
    grad_probs = jnp.einsum("qhd,khd->hqk", grad_mixed, values, preferred_element_type=jnp.float32)
    grad_scores = softmax_probs * (
        grad_probs - jnp.sum(softmax_probs * grad_probs, axis=-1, keepdims=True)
    )
    grad_scores = grad_scores.astype(low)
    grad_queries = jnp.einsum(
        "hqk,khd->qhd", grad_scores, key_heads, preferred_element_type=jnp.float32
    ) * HEAD ** (-0.5)
    grad_keys = jnp.einsum(
        "hqk,qhd->khd", grad_scores, queries, preferred_element_type=jnp.float32
    ) * HEAD ** (-0.5)
    grad_qkv_rows = (
        jnp.stack([grad_queries, grad_keys, grad_values], axis=1)
        .reshape(row_total, 3 * D)
        .astype(low)
    )
    grad_h_one = functools.reduce(
        jnp.add,
        [
            dot(grad_qkv_rows[:, i * wide_qkv : (i + 1) * wide_qkv], part, NT)
            for i, part in enumerate(full_qkv)
        ],
    )
    grad_input, grad_gain_one = norm_backward(grad_h_one, normed_one, scale_one, gain_one)
    grad_input = grad_input + grad_first
    grad_gains_full = jnp.stack([grad_gain_one, grad_gain_two])

    grad_small = small_block(grad_route_full, grad_gains_full, grad_const_full).astype(low)
    param_parts = jnp.stack(
        [
            jnp.concatenate(
                [
                    dot(h_one_low, grad_qkv_rows[:, i * wide_qkv : (i + 1) * wide_qkv], TN).astype(
                        low
                    ),
                    dot(mixed_heads, grad_attn[:, i * wide_out : (i + 1) * wide_out], TN).astype(
                        low
                    ),
                    grad_small,
                ],
                axis=1,
            )
            for i in range(n_col)
        ]
    )
    summed = param_reduce(
        param_parts.reshape(n_col, n_dp, n_row, n_col * shard_rows, wide), dims
    )

    def from_col(parts):
        return parts.transpose(1, 0, 2).reshape(parts.shape[1], -1)

    grad_qkv = from_col(summed[:, :, :wide_qkv])
    grad_attn_out = from_col(summed[:, :, wide_qkv : wide_qkv + wide_out])
    sum_small = summed[0, :, wide_qkv + wide_out :]
    grad_route = sum_small[:, :route_cols]
    grad_gains = sum_small[:, route_cols : route_cols + 2].T
    grad_const = sum_small[:, route_cols + 2 : route_cols + 4].T
    moment_qkv, new_qkv = diag_update(w_qkv, grad_qkv, stat_qkv, D ** (-0.5))
    moment_attn_out, new_attn_out = diag_update(w_out, grad_attn_out, stat_out, HEAD ** (-0.5))
    moment_route, new_route = diag_update(route_w, grad_route, stat_route, (4 * D) ** (-0.5))
    moment_gains, new_gains = diag_update(gains, grad_gains, stat_gains, 0.3)
    moment_const, new_const = diag_update(const_vec, grad_const, stat_const, 0.5)

    if slice_wide % LANES == 0:
        update = shampoo
    else:
        update = shampoo_plain
    (
        grad_gate_up,
        grad_down,
        new_left_gu,
        new_right_down,
        new_right_gu,
        new_left_down,
        new_gate_up,
        new_down,
    ) = update(
        gathered,
        left_root_gu[0],
        right_root_down[0],
        right_root_gu[0],
        left_root_down[0],
        left_gu[0],
        right_down[0],
        right_gu[0],
        left_down[0],
        w_gate_up[0],
        w_down[0].T,
        n_row,
        n_col,
    )
    return (
        result,
        grad_input,
        grad_qkv,
        moment_qkv,
        new_qkv,
        grad_attn_out,
        moment_attn_out,
        new_attn_out,
        grad_route,
        moment_route,
        new_route,
        grad_gains,
        moment_gains,
        new_gains,
        grad_const,
        moment_const,
        new_const,
        grad_gate_up[None],
        grad_down.T[None],
        new_left_gu[None],
        new_right_gu[None],
        new_left_down[None],
        new_right_down[None],
        new_gate_up[None],
        new_down.T[None],
    )


def solution(mesh):
    placed = (
        P(("dp", "row", "col"), None),
        P(("dp", "row", "col"), None),
        P(("dp", "row", "col"), None),
        P(("dp", "row", "col"), None),
        P(("dp", "row", "col"), None),
        P(("dp", "row", "col"), None),
        P(("dp", "row", "col"), None),
        P(("dp", "row", "col"), None),
        P(None, ("dp", "row", "col")),
        P(None, ("dp", "row", "col")),
        P(("dp", "row", "col"), None),
        P(("dp", "row", "col"), None),
        P(("dp", "row", "col"), None),
        P(None, ("dp", "row", "col")),
        P(None, ("dp", "row", "col")),
        P("dp", "row", None, "col"),
        P("dp", "col", "row"),
        P("dp", None, ("row", "col"), None),
        P("dp", None, ("row", "col"), None),
        P("dp", ("row", "col"), None),
        P("dp", ("row", "col"), None),
        P("dp", None, "row", None),
        P("dp", None, "col", None),
        P("dp", "col", None),
        P("dp", "row", None),
    )
    return jax.shard_map(
        body,
        mesh=mesh,
        in_specs=placed,
        out_specs=(
            P(("dp", "row", "col"), None),
            P(("dp", "row", "col"), None),
            P(("dp", "row", "col"), None),
            P(("dp", "row", "col"), None),
            P(("dp", "row", "col"), None),
            P(("dp", "row", "col"), None),
            P(("dp", "row", "col"), None),
            P(("dp", "row", "col"), None),
            P(("dp", "row", "col"), None),
            P(("dp", "row", "col"), None),
            P(("dp", "row", "col"), None),
            P(None, ("dp", "row", "col")),
            P(None, ("dp", "row", "col")),
            P(None, ("dp", "row", "col")),
            P(None, ("dp", "row", "col")),
            P(None, ("dp", "row", "col")),
            P(None, ("dp", "row", "col")),
            P("dp", "row", None, "col"),
            P("dp", "col", "row"),
            P("dp", None, ("row", "col"), None),
            P("dp", None, ("row", "col"), None),
            P("dp", ("row", "col"), None),
            P("dp", ("row", "col"), None),
            P("dp", "row", None, "col"),
            P("dp", "col", "row"),
        ),
        check_vma=False,
    )
```

```python
import functools

import jax
import jax.numpy as jnp
from jax import lax
from jax.experimental import pallas as pl
from jax.experimental.pallas import tpu as pltpu
from jax.sharding import PartitionSpec as P

D = 768
HEADS = 12
HEAD = 64
CAP = 32
LANES = 128


NORM_EPS = 1e-06
SHAMPOO_RATE = 0.5
MESH = pl.DeviceIdType.MESH
VMEM_BYTES = 56 * 2**20


def dot(left, right, dims=(((1,), (0,)), ((), ()))):
    return lax.dot_general(left, right, dims, preferred_element_type=jnp.float32)


NT = (((1,), (1,)), ((), ()))
TN = (((0,), (0,)), ((), ()))


def flip(index, bit):
    return index + bit * (1 - 2 * ((index // bit) % 2))


def flip_all(index, mask, bits):
    for dim in range(bits):
        if mask & (1 << dim):
            index = flip(index, 1 << dim)
    return index


def mesh_sizes():
    return tuple(lax.axis_size(name) for name in ("dp", "row", "col"))


def bits_of(count):
    bits = count.bit_length() - 1
    assert 1 << bits == count
    return bits


def greet(over_dp, dims, place, all_rows=False):
    n_dp, n_row, n_col = dims
    d, r, c = place
    peers = []
    if over_dp:
        peers += [((d + j) % n_dp, r, c) for j in range(1, n_dp)]
    if all_rows:
        peers += [(d, (r + i) % n_row, c) for i in range(1, n_row)]
    else:
        peers += [(d, flip(r, 1 << dim), c) for dim in range(bits_of(n_row))]
    peers += [(d, r, (c + i) % n_col) for i in range(1, n_col)]
    barrier = pltpu.get_barrier_semaphore()
    for peer in peers:
        pl.semaphore_signal(barrier, inc=1, device_id=peer, device_id_type=MESH)
    pl.semaphore_wait(barrier, len(peers))


def remote(src, dst, send_sem, recv_sem, device):
    return pltpu.make_async_remote_copy(
        src_ref=src,
        dst_ref=dst,
        send_sem=send_sem,
        recv_sem=recv_sem,
        device_id=device,
        device_id_type=MESH,
    )


def spread_blocks(dims, place, chunks, over_dp, own, dp_source, slot, sems, between=None):
    n_dp, n_row, n_col = dims
    d, r, c = place
    bits = bits_of(n_row)
    dp_send, dp_recv, row_send, row_recv, col_send, col_recv, own_sem = sems
    sent = []

    def block(j, x):
        return slot(c, j, flip_all(r, x, bits))

    def to_row(j, src, x, bit):
        copy = remote(
            src,
            block(j, x),
            row_send.at[j, x ^ bit],
            row_recv.at[j, x ^ bit],
            (d, flip(r, bit), c),
        )
        copy.start()
        sent.append(copy)

    def to_cols(j, src, x):
        for i in range(1, n_col):
            copy = remote(
                src,
                block(j, x),
                col_send.at[j, x, i],
                col_recv.at[j, x, i],
                (d, r, (c + i) % n_col),
            )
            copy.start()
            sent.append(copy)

    def order(j):
        return [1 << ((j + s) % bits) for s in range(bits)]

    locals_ = []

    def start(j):
        if over_dp and j > 0:
            src = block(j, 0)
            remote(src, src, dp_send.at[j], dp_recv.at[j], (d, r, c)).wait_recv()
        elif own is None:
            src = block(j, 0)
        else:
            src = own(j)
            keep = pltpu.make_async_copy(src, block(j, 0), own_sem.at[j])
            keep.start()
            locals_.append(keep)
        for bit in order(j):
            to_row(j, src, 0, bit)
        to_cols(j, src, 0)

    def arrived(j, x, later_dims):
        ref = block(j, x)
        remote(ref, ref, row_send.at[j, x], row_recv.at[j, x], (d, r, c)).wait_recv()
        for later in later_dims:
            to_row(j, ref, x, later)
        to_cols(j, ref, x)

    def pass_on(j):
        have = [0]
        dim_order = order(j)
        for s, bit in enumerate(dim_order[:-1]):
            new = [x ^ bit for x in have]
            for x in new:
                arrived(j, x, dim_order[s + 1 :])
            have += new

    def last_arrivals(j):
        bit = order(j)[-1]
        for x in range(n_row):
            if x & bit:
                arrived(j, x, [])

    start(0)
    if over_dp:
        for j in range(1, n_dp):
            peer = (d + j) % n_dp
            copy = remote(
                dp_source(peer),
                slot(c, ("from", d), r),
                dp_send.at[j],
                dp_recv.at[j],
                (peer, r, c),
            )
            copy.start()
            sent.append(copy)
        for j in range(1, chunks):
            start(j)
            pass_on(j - 1)
        pass_on(chunks - 1)
    else:
        for j in range(1, chunks):
            start(j)
        for j in range(chunks):
            pass_on(j)
    if between is not None:
        between()
    for j in range(chunks):
        last_arrivals(j)
    for j in range(chunks):
        for x in range(n_row):
            for i in range(1, n_col):
                ref = slot((c + n_col - i) % n_col, j, flip_all(r, x, bits))
                remote(ref, ref, col_send.at[j, x, i], col_recv.at[j, x, i], (d, r, c)).wait_recv()
    for copy in locals_:
        copy.wait()
    return [copy.wait_send for copy in sent]


def finish(waits):
    for wait in waits:
        wait()


def spread_sems(dims, chunks):
    n_dp, n_row, n_col = dims
    dma = pltpu.SemaphoreType.DMA
    return [
        dma((n_dp,)),
        dma((n_dp,)),
        dma((chunks, n_row)),
        dma((chunks, n_row)),
        dma((chunks, n_row, n_col)),
        dma((chunks, n_row, n_col)),
        dma((chunks,)),
    ]


def axis_place():
    return tuple(lax.axis_index(name) for name in ("dp", "row", "col"))


def param_gather_kernel(dims, shard_ref, out_ref, swap_ref, block_ref, swap_send, swap_recv, *sems):
    n_dp, n_row, n_col = dims
    place = axis_place()
    d, r, c = place
    rows = shard_ref.shape[1]
    greet(True, dims, place)
    copies = []
    for i in range(1, n_col):
        other = (c + i) % n_col
        copy = remote(
            shard_ref.at[other], swap_ref.at[c], swap_send.at[i], swap_recv.at[i], (d, r, other)
        )
        copy.start()
        copies.append(copy)
    swap_ref[pl.ds(c, 1)] = shard_ref[pl.ds(c, 1)]
    for copy in copies:
        copy.wait()
    for i in range(n_col):
        block_ref[i * rows : (i + 1) * rows, :] = swap_ref[i]
    low_ref = sems[-1]
    low_ref[...] = block_ref[...].astype(jnp.bfloat16)

    def slot(col, j, b):
        k = j[1] if isinstance(j, tuple) else (d + n_dp - j) % n_dp
        return out_ref.at[col, k, b]

    finish(
        spread_blocks(
            dims, place, n_dp, True, lambda j: low_ref, lambda k: low_ref, slot, sems[:-1]
        )
    )


def param_gather(shard, dims):
    n_dp, n_row, n_col = dims
    _, rows, width = shard.shape
    dma = pltpu.SemaphoreType.DMA
    return pl.pallas_call(
        functools.partial(param_gather_kernel, dims),
        out_shape=jax.ShapeDtypeStruct((n_col, n_dp, n_row, n_col * rows, width), jnp.bfloat16),
        in_specs=[pl.BlockSpec(memory_space=pltpu.VMEM)],
        out_specs=pl.BlockSpec(memory_space=pl.ANY),
        scratch_shapes=[
            pltpu.VMEM((n_col, rows, width), jnp.float32),
            pltpu.VMEM((n_col * rows, width), jnp.float32),
            dma((n_col,)),
            dma((n_col,)),
            *spread_sems(dims, n_dp),
            pltpu.VMEM((n_col * rows, width), jnp.bfloat16),
        ],
        compiler_params=pltpu.CompilerParams(
            collective_id=0, has_side_effects=True, vmem_limit_bytes=VMEM_BYTES
        ),
        name="param_gather",
    )(shard)


def token_gather_kernel(dims, src_ref, out_ref, *sems):
    n_dp, n_row, n_col = dims
    place = axis_place()
    d = place[0]
    greet(True, dims, place)

    def slot(col, j, b):
        k = j[1] if isinstance(j, tuple) else (d + n_dp - j) % n_dp
        return out_ref.at[col, k, b]

    finish(
        spread_blocks(
            dims,
            place,
            n_dp,
            True,
            lambda j: src_ref.at[d],
            lambda k: src_ref.at[k],
            slot,
            sems,
        )
    )


def token_gather(rows, dims):
    n_dp, n_row, n_col = dims
    _, slots, width = rows.shape
    return pl.pallas_call(
        functools.partial(token_gather_kernel, dims),
        out_shape=jax.ShapeDtypeStruct((n_col, n_dp, n_row, slots, width), rows.dtype),
        in_specs=[pl.BlockSpec(memory_space=pl.ANY)],
        out_specs=pl.BlockSpec(memory_space=pl.ANY),
        scratch_shapes=spread_sems(dims, n_dp),
        compiler_params=pltpu.CompilerParams(
            collective_id=1, has_side_effects=True, vmem_limit_bytes=VMEM_BYTES
        ),
        name="token_gather",
    )(rows)


def plane_gather_kernel(dims, src_ref, out_ref, *sems):
    place = axis_place()
    greet(False, dims, place)
    finish(
        spread_blocks(
            dims,
            place,
            src_ref.shape[0],
            False,
            lambda j: src_ref.at[j],
            None,
            lambda col, j, b: out_ref.at[col, b, j],
            sems,
        )
    )


def plane_gather(parts, dims):
    n_dp, n_row, n_col = dims
    chunks, rows, width = parts.shape
    return pl.pallas_call(
        functools.partial(plane_gather_kernel, dims),
        out_shape=jax.ShapeDtypeStruct((n_col, n_row, chunks, rows, width), parts.dtype),
        in_specs=[pl.BlockSpec(memory_space=pl.ANY)],
        out_specs=pl.BlockSpec(memory_space=pl.ANY),
        scratch_shapes=spread_sems(dims, chunks),
        compiler_params=pltpu.CompilerParams(
            collective_id=2, has_side_effects=True, vmem_limit_bytes=VMEM_BYTES
        ),
        name="plane_gather",
    )(parts)


def add_low(left, right):
    return (left.astype(jnp.float32) + right.astype(jnp.float32)).astype(jnp.bfloat16)


def reduce_blocks(dims, place, part_ref, bufs, sems, deliver):
    n_dp, n_row, n_col = dims
    d, r, c = place
    bits = bits_of(n_row)
    mine_ref, col_ref, row_ref = bufs
    mine_sem, col_send, col_recv, row_send, row_recv = sems
    steps = list(range(1, n_dp)) + [0]
    sent = []
    held = []
    for t, j in enumerate(steps):
        k = (d + j) % n_dp
        for i in range(1, n_col):
            other = (c + i) % n_col
            copy = remote(
                part_ref.at[other, k],
                col_ref.at[t, i - 1],
                col_send.at[t, i],
                col_recv.at[t, i],
                (d, r, other),
            )
            copy.start()
            sent.append(copy)
        keep = pltpu.make_async_copy(part_ref.at[c, k], mine_ref.at[t], mine_sem.at[t])
        keep.start()
        held.append(keep)

    def order(t):
        return [1 << ((t + s) % bits) for s in range(bits)]

    def send_half(t, s):
        dim_order = order(t)
        bit = dim_order[s]
        before = sum(dim_order[:s])
        for x in range(n_row):
            if not x & before and x & bit:
                copy = remote(
                    mine_ref.at[t, flip_all(r, x, bits)],
                    row_ref.at[t, x ^ bit, s],
                    row_send.at[t, x ^ bit, s],
                    row_recv.at[t, x ^ bit, s],
                    (d, flip(r, bit), c),
                )
                copy.start()
                sent.append(copy)

    def stage_col(t):
        held[t].wait()
        for i in range(1, n_col):
            ref = col_ref.at[t, i - 1]
            remote(ref, ref, col_send.at[t, i], col_recv.at[t, i], (d, r, c)).wait_recv()

        @pl.loop(0, n_row)
        def _(b):
            total = mine_ref[t, b].astype(jnp.float32)
            for i in range(1, n_col):
                total = total + col_ref[t, i - 1, b].astype(jnp.float32)
            mine_ref[t, b] = total.astype(jnp.bfloat16)

        send_half(t, 0)

    def stage_row(t, s):
        dim_order = order(t)
        before = sum(dim_order[: s + 1])
        for y in range(n_row):
            if not y & before:
                ref = row_ref.at[t, y, s]
                remote(
                    ref, ref, row_send.at[t, y, s], row_recv.at[t, y, s], (d, r, c)
                ).wait_recv()
                b = flip_all(r, y, bits)
                mine_ref[t, b] = add_low(mine_ref[t, b], row_ref[t, y, s])
        if s + 1 < bits:
            send_half(t, s + 1)
        else:
            deliver(t, steps[t], mine_ref.at[t, r])

    for t in range(n_dp):
        stage_col(t)
    for s in range(bits):
        for t in range(n_dp):
            stage_row(t, s)
    return sent


def reduce_scratch(dims, rows, width):
    n_dp, n_row, n_col = dims
    bits = bits_of(n_row)
    dma = pltpu.SemaphoreType.DMA
    low = jnp.bfloat16
    return [
        pltpu.VMEM((n_dp, n_row, rows, width), low),
        pltpu.VMEM((n_dp, max(1, n_col - 1), n_row, rows, width), low),
        pltpu.VMEM((n_dp, n_row // 2, bits, rows, width), low)
        if n_row == 2
        else pltpu.VMEM((n_dp, n_row, bits, rows, width), low),
        dma((n_dp,)),
        dma((n_dp, n_col)),
        dma((n_dp, n_col)),
        dma((n_dp, n_row, bits)),
        dma((n_dp, n_row, bits)),
    ]


def token_reduce_kernel(dims, part_ref, out_ref, *scratch):
    n_dp, n_row, n_col = dims
    place = axis_place()
    d, r, c = place
    dp_send, dp_recv, own_sem = scratch[8:]
    greet(True, dims, place)
    late = []

    def deliver(t, j, block):
        if j == 0:
            keep = pltpu.make_async_copy(block, out_ref.at[d], own_sem)
            keep.start()
            late.append(keep.wait)
        else:
            copy = remote(
                block, out_ref.at[d], dp_send.at[j], dp_recv.at[j], ((d + j) % n_dp, r, c)
            )
            copy.start()
            late.append(copy.wait_send)

    sent = reduce_blocks(dims, place, part_ref, scratch[:3], scratch[3:8], deliver)
    for j in range(1, n_dp):
        ref = out_ref.at[(d + n_dp - j) % n_dp]
        remote(ref, ref, dp_send.at[j], dp_recv.at[j], (d, r, c)).wait_recv()
    for copy in sent:
        copy.wait_send()
    for wait in late:
        wait()


def token_reduce(parts, dims):
    n_dp = dims[0]
    slots, width = parts.shape[3:]
    dma = pltpu.SemaphoreType.DMA
    return pl.pallas_call(
        functools.partial(token_reduce_kernel, dims),
        out_shape=jax.ShapeDtypeStruct((n_dp, slots, width), jnp.bfloat16),
        in_specs=[pl.BlockSpec(memory_space=pl.ANY)],
        out_specs=pl.BlockSpec(memory_space=pl.ANY),
        scratch_shapes=[*reduce_scratch(dims, slots, width), dma((n_dp,)), dma((n_dp,)), dma],
        compiler_params=pltpu.CompilerParams(
            collective_id=3, has_side_effects=True, vmem_limit_bytes=VMEM_BYTES
        ),
        name="token_reduce",
    )(parts)


def param_reduce_kernel(dims, part_ref, out_ref, *scratch):
    n_dp, n_row, n_col = dims
    place = axis_place()
    d, r, c = place
    dp_send, dp_recv, dp_ref, swap_send, swap_recv, swap_ref, sum_ref = scratch[8:]
    rows = out_ref.shape[1]
    greet(True, dims, place)
    late = []
    kept = []

    def deliver(t, j, block):
        if j == 0:
            kept.append(block)
        else:
            copy = remote(
                block, dp_ref.at[j], dp_send.at[j], dp_recv.at[j], ((d + j) % n_dp, r, c)
            )
            copy.start()
            late.append(copy)

    sent = reduce_blocks(dims, place, part_ref, scratch[:3], scratch[3:8], deliver)
    total = kept[0][...].astype(jnp.float32)
    for j in range(1, n_dp):
        ref = dp_ref.at[j]
        remote(ref, ref, dp_send.at[j], dp_recv.at[j], (d, r, c)).wait_recv()
        total = total + dp_ref[j].astype(jnp.float32)
    sum_ref[...] = total
    for i in range(n_col):
        swap_ref[i] = sum_ref[i * rows : (i + 1) * rows, :]
    for i in range(1, n_col):
        other = (c + i) % n_col
        copy = remote(
            swap_ref.at[other], out_ref.at[c], swap_send.at[i], swap_recv.at[i], (d, r, other)
        )
        copy.start()
        late.append(copy)
    out_ref[pl.ds(c, 1)] = swap_ref[pl.ds(c, 1)]
    for i in range(1, n_col):
        ref = out_ref.at[(c + n_col - i) % n_col]
        remote(ref, ref, swap_send.at[i], swap_recv.at[i], (d, r, c)).wait_recv()
    for copy in sent:
        copy.wait_send()
    for copy in late:
        copy.wait_send()


def param_reduce(parts, dims):
    n_dp, n_row, n_col = dims
    block_rows, width = parts.shape[3:]
    rows = block_rows // n_col
    dma = pltpu.SemaphoreType.DMA
    return pl.pallas_call(
        functools.partial(param_reduce_kernel, dims),
        out_shape=jax.ShapeDtypeStruct((n_col, rows, width), jnp.float32),
        in_specs=[pl.BlockSpec(memory_space=pl.ANY)],
        out_specs=pl.BlockSpec(memory_space=pltpu.VMEM),
        scratch_shapes=[
            *reduce_scratch(dims, block_rows, width),
            dma((n_dp,)),
            dma((n_dp,)),
            pltpu.VMEM((n_dp, block_rows, width), jnp.bfloat16),
            dma((n_col,)),
            dma((n_col,)),
            pltpu.VMEM((n_col, rows, width), jnp.float32),
            pltpu.VMEM((block_rows, width), jnp.float32),
        ],
        compiler_params=pltpu.CompilerParams(
            collective_id=4, has_side_effects=True, vmem_limit_bytes=VMEM_BYTES
        ),
        name="param_reduce",
    )(parts)


def column(matrix, index):
    return matrix[:, index : index + 1]


def token_masks(lengths_ref, rows, seqs):
    down = lax.broadcasted_iota(jnp.int32, (rows, 1), 0)
    across = lax.broadcasted_iota(jnp.int32, (1, rows), 1)
    end = 0
    doc_down = jnp.zeros((rows, 1), jnp.int32)
    doc_across = jnp.zeros((1, rows), jnp.int32)
    for i in range(seqs):
        end = end + lengths_ref[0, i]
        doc_down = doc_down + (down >= end).astype(jnp.int32)
        doc_across = doc_across + (across >= end).astype(jnp.int32)
    valid = (doc_down < seqs).astype(jnp.float32)
    allowed = (doc_down == doc_across) & (down >= across)
    return valid, allowed


def row_vectors_of(small, first):
    shape = (8, small.shape[1])
    pick = lax.broadcasted_iota(jnp.int32, shape, 1) == first + lax.broadcasted_iota(
        jnp.int32, shape, 0
    )
    return dot(pick.astype(jnp.bfloat16), small, NT)


def half_mask(rows, half):
    return lax.broadcasted_iota(jnp.int32, (rows, LANES), 1) // HEAD == half


def attention_forward(qkv_ref, probs_ref, mixed_ref, allowed):
    rows = qkv_ref.shape[0]
    low = jnp.bfloat16

    @pl.loop(0, HEADS * HEAD // LANES, unroll=2)
    def _(pair):
        def cols(base):
            return pl.ds(pl.multiple_of(base + pair * LANES, LANES), LANES)

        queries = qkv_ref[:, cols(0)]
        key_heads = qkv_ref[:, cols(D)]
        values = qkv_ref[:, cols(2 * D)]
        mixed = jnp.zeros((rows, LANES), jnp.float32)
        for half in range(LANES // HEAD):
            mask = half_mask(rows, half)
            scores = dot(jnp.where(mask, queries, 0), key_heads, NT) * HEAD ** (-0.5)
            scores = jnp.where(allowed, scores, -1e30)
            top_score = jnp.max(scores, axis=-1, keepdims=True)
            exp_scores = jnp.exp(scores - top_score)
            probs = exp_scores / jnp.sum(exp_scores, axis=-1, keepdims=True)
            probs_ref[pair * (LANES // HEAD) + half] = probs
            mixed = mixed + dot(probs.astype(low), jnp.where(mask, values, 0))
        mixed_ref[:, cols(0)] = mixed.astype(low)


def two_way(first, second):
    top = jnp.maximum(first, second)
    exp_first = jnp.exp(first - top)
    exp_second = jnp.exp(second - top)
    total = exp_first + exp_second
    return exp_first / total, exp_second / total


def front_kernel(sizes, *refs):
    dims, num_ffn, wide_qkv, wide_out, route_cols = sizes
    n_dp, n_row, n_col = dims
    low = jnp.bfloat16
    (
        lengths_ref,
        routes_ref,
        prev_ref,
        tokens_ref,
        cotangent_ref,
        shard_ref,
        weight_gu,
        weight_down,
        whole_out,
        parts_ref,
        grads_ref,
        qkv_ref,
        probs_ref,
        mixed_ref,
        first_ref,
        small_ref,
        swap_ref,
        block_ref,
        whole_ref,
        load_ref,
        pack_ref,
        expert_ref,
        stage_ref,
        arrived_ref,
        logits_ref,
        hidden_ref,
        pre_ref,
        swap_send,
        swap_recv,
        load_sem,
        expert_send,
        expert_recv,
        whole_sem,
        *sems,
    ) = refs
    param_sems, token_sems = sems[:7], sems[7:]
    place = axis_place()
    d, r, c = place
    rows = shard_ref.shape[1]
    depth, slice_wide = pack_ref.shape[2:]
    loads = []
    for m, src in enumerate([weight_gu.at[:, 0], weight_gu.at[:, 1], weight_down]):
        copy = pltpu.make_async_copy(src, load_ref.at[m], load_sem.at[m])
        copy.start()
        loads.append(copy)
    greet(True, dims, place, all_rows=True)

    copies = []
    for i in range(1, n_col):
        other = (c + i) % n_col
        copy = remote(
            shard_ref.at[other], swap_ref.at[c], swap_send.at[i], swap_recv.at[i], (d, r, other)
        )
        copy.start()
        copies.append(copy)
    swap_ref[pl.ds(c, 1)] = shard_ref[pl.ds(c, 1)]
    for copy in copies:
        copy.wait()
    for i in range(n_col):
        block_ref[i * rows : (i + 1) * rows, :] = swap_ref[i]
    whole_ref[c, d, r] = block_ref[...].astype(low)

    def param_slot(col, j, b):
        k = j[1] if isinstance(j, tuple) else (d + n_dp - j) % n_dp
        return whole_ref.at[col, k, b]

    waits = []

    def send_experts():
        for m in range(3):
            loads[m].wait()
            for b in range(n_row):
                pack_ref[b, m] = load_ref[m, :, b * slice_wide : (b + 1) * slice_wide].astype(low)
        home = pl.ds(pl.multiple_of(r * depth, 16), depth)
        for i in range(1, n_row):
            other = (r + i) % n_row
            copy = remote(
                pack_ref.at[other],
                expert_ref.at[:, home],
                expert_send.at[i],
                expert_recv.at[i],
                (d, other, c),
            )
            copy.start()
            waits.append(copy.wait_send)
        expert_ref[:, home] = pack_ref[r]

    waits += spread_blocks(
        dims,
        place,
        n_dp,
        True,
        None,
        lambda k: whole_ref.at[c, d, r],
        param_slot,
        param_sems,
        send_experts,
    )
    keep_whole = pltpu.make_async_copy(whole_ref, whole_out, whole_sem)
    keep_whole.start()

    def whole_cols(col, begin, wide):
        return whole_ref[col, :, :, :, begin : begin + wide].reshape(D, wide)

    total = tokens_ref.shape[0]
    valid, allowed = token_masks(lengths_ref, total, lengths_ref.shape[1])
    small = whole_cols(0, wide_qkv + wide_out, LANES)
    vectors = row_vectors_of(small, route_cols)
    inputs = tokens_ref[...].astype(jnp.float32)
    scale_one = lax.rsqrt(jnp.mean(inputs * inputs, axis=-1, keepdims=True) + NORM_EPS)
    h_one = (inputs * scale_one * vectors[0:1]).astype(low)
    for i in range(n_col):
        qkv_ref[:, i * wide_qkv : (i + 1) * wide_qkv] = dot(h_one, whole_cols(i, 0, wide_qkv)).astype(
            low
        )
    attention_forward(qkv_ref, probs_ref, mixed_ref, allowed)
    for i in range(n_col):
        cols = slice(i * wide_out, (i + 1) * wide_out)
        attn_out = dot(mixed_ref[...], whole_cols(i, wide_qkv, wide_out))
        first_ref[:, cols] = tokens_ref[:, cols].astype(jnp.float32) + valid * attn_out
    first_sum = first_ref[...]
    scale_two = lax.rsqrt(jnp.mean(first_sum * first_sum, axis=-1, keepdims=True) + NORM_EPS)
    h_two = (first_sum * scale_two * vectors[1:2]).astype(low)
    logits_ref[...] = jnp.zeros_like(logits_ref)
    logits_ref[:, : prev_ref.shape[1]] = prev_ref[...]
    logits_all = dot(h_two, small)
    logits = logits_all + logits_ref[...]
    lane = lax.broadcasted_iota(jnp.int32, (total, LANES), 1)
    route_first = routes_ref[:, 0:1]
    route_second = routes_ref[:, 1:2]
    pick_first = (lane == route_first).astype(jnp.float32)
    pick_second = (lane == route_second).astype(jnp.float32)
    gates = two_way(
        jnp.sum(pick_first * logits, axis=-1, keepdims=True),
        jnp.sum(pick_second * logits, axis=-1, keepdims=True),
    )
    mix_base = num_ffn + 4
    mixes = []
    for i in range(2):
        mixes += two_way(
            column(logits_all, mix_base + 2 * i), column(logits_all, mix_base + 2 * i + 1)
        )
    before = lax.broadcasted_iota(jnp.int32, (total, total), 0) > lax.broadcasted_iota(
        jnp.int32, (total, total), 1
    )
    earlier = dot(before.astype(low), (pick_first + pick_second).astype(low))
    in_slots = []
    for route, pick in ((route_first, pick_first), (route_second, pick_second)):
        slot_index = jnp.sum(earlier * pick, axis=-1, keepdims=True)
        where_in = (route * CAP).astype(jnp.float32) + slot_index
        in_slots.append(jnp.where(route < num_ffn, where_in, -1.0))
    kept = [*gates, *mixes, *in_slots]
    state = jnp.zeros((total, LANES), jnp.float32)
    for i, value in enumerate(kept):
        state = jnp.where(lane == i, value, state)
    small_ref[...] = state
    slots = num_ffn * CAP
    slot_lane = lax.broadcasted_iota(jnp.int32, (total, slots), 1).astype(jnp.float32)
    places = [(slot_lane == where_in).astype(low) for where_in in in_slots]
    grad_y = cotangent_ref[...].astype(jnp.float32) * valid
    sent = dot(places[0] + places[1], h_two, TN).astype(low)
    made = dot(places[0], (gates[0] * grad_y).astype(low), TN) + dot(
        places[1], (gates[1] * grad_y).astype(low), TN
    )
    stage_ref[:, :, :D] = sent.reshape(num_ffn, CAP, D)
    stage_ref[:, :, D:] = made.astype(low).reshape(num_ffn, CAP, D)

    def token_slot(col, j, b):
        k = j[1] if isinstance(j, tuple) else (d + n_dp - j) % n_dp
        return arrived_ref.at[(col * n_dp + k) * n_row + b]

    arrived_ref[(c * n_dp + d) * n_row + r] = stage_ref[d]
    waits += spread_blocks(
        dims, place, n_dp, True, None, lambda k: stage_ref.at[k], token_slot, token_sems
    )
    for i in range(1, n_row):
        home = pl.ds(pl.multiple_of(((r + n_row - i) % n_row) * depth, 16), depth)
        ref = expert_ref.at[:, home]
        remote(ref, ref, expert_send.at[i], expert_recv.at[i], (d, r, c)).wait_recv()

    blocks = arrived_ref.shape[0]
    group = 8
    tall = group * CAP

    @pl.loop(0, blocks // group)
    def _(t):
        some = arrived_ref[pl.ds(t * group, group)].reshape(tall, 2 * D)
        rows_in = some[:, :D]
        grads_in = some[:, D:]
        span = pl.ds(pl.multiple_of(t * tall, tall), tall)
        gate_part = dot(rows_in, expert_ref[0])
        up_part = dot(rows_in, expert_ref[1])
        grad_hidden = dot(grads_in, expert_ref[2])
        sigma = jax.nn.sigmoid(gate_part)
        silu = gate_part * sigma
        hidden = (silu * up_part).astype(low)
        grad_gate = (
            grad_hidden * up_part * sigma * (1.0 + gate_part * (1.0 - sigma))
        ).astype(low)
        grad_up = (grad_hidden * silu).astype(low)
        hidden_ref[span] = hidden
        pre_ref[span, :slice_wide] = grad_gate
        pre_ref[span, slice_wide:] = grad_up
        made_rows = dot(hidden, expert_ref[2], NT).astype(low)
        grad_rows = dot(grad_gate, expert_ref[0], NT) + dot(grad_up, expert_ref[1], NT)
        out_span = pl.ds(t * group, group)
        parts_ref[out_span, :, :D] = made_rows.reshape(group, CAP, D)
        parts_ref[out_span, :, D:] = grad_rows.astype(low).reshape(group, CAP, D)

    all_rows = arrived_ref[:, :, :D].reshape(blocks * CAP, D)
    all_grads = arrived_ref[:, :, D:].reshape(blocks * CAP, D)
    for m in range(2):
        grads_ref[m * D : (m + 1) * D] = dot(
            all_rows, pre_ref[:, m * slice_wide : (m + 1) * slice_wide], TN
        ).astype(low)
    grads_ref[2 * D :] = dot(all_grads, hidden_ref[...], TN).astype(low)
    keep_whole.wait()
    finish(waits)


def front(lengths, routes, prev_logits, tokens, cotangent, shard, weight_gu, weight_down, dims, widths):
    n_dp, n_row, n_col = dims
    low = jnp.bfloat16
    f32 = jnp.float32
    total = tokens.shape[0]
    _, rows, wide = shard.shape
    num_ffn = prev_logits.shape[1] - 4
    depth, wide_col = weight_down.shape
    slice_wide = wide_col // n_row
    blocks = n_col * n_dp * n_row
    dma = pltpu.SemaphoreType.DMA
    vmem = pl.BlockSpec(memory_space=pltpu.VMEM)
    hbm = pl.BlockSpec(memory_space=pl.ANY)
    whole = (n_col, n_dp, n_row, n_col * rows, wide)
    return pl.pallas_call(
        functools.partial(front_kernel, (dims, num_ffn, *widths)),
        out_shape=[
            jax.ShapeDtypeStruct(whole, low),
            jax.ShapeDtypeStruct((blocks, CAP, 2 * D), low),
            jax.ShapeDtypeStruct((3 * D, slice_wide), low),
            jax.ShapeDtypeStruct((total, 3 * D), low),
            jax.ShapeDtypeStruct((HEADS, total, total), f32),
            jax.ShapeDtypeStruct((total, D), low),
            jax.ShapeDtypeStruct((total, D), f32),
            jax.ShapeDtypeStruct((total, LANES), f32),
        ],
        in_specs=[pl.BlockSpec(memory_space=pltpu.SMEM)] + [vmem] * 5 + [hbm] * 2,
        out_specs=[hbm] + [vmem] * 7,
        scratch_shapes=[
            pltpu.VMEM((n_col, rows, wide), f32),
            pltpu.VMEM((n_col * rows, wide), f32),
            pltpu.VMEM(whole, low),
            pltpu.VMEM((3, depth, wide_col), f32),
            pltpu.VMEM((n_row, 3, depth, slice_wide), low),
            pltpu.VMEM((3, n_row * depth, slice_wide), low),
            pltpu.VMEM((num_ffn, CAP, 2 * D), low),
            pltpu.VMEM((blocks, CAP, 2 * D), low),
            pltpu.VMEM((total, LANES), f32),
            pltpu.VMEM((blocks * CAP, slice_wide), low),
            pltpu.VMEM((blocks * CAP, 2 * slice_wide), low),
            dma((n_col,)),
            dma((n_col,)),
            dma((3,)),
            dma((n_row,)),
            dma((n_row,)),
            dma,
            *spread_sems(dims, n_dp),
            *spread_sems(dims, n_dp),
        ],
        compiler_params=pltpu.CompilerParams(
            collective_id=5, has_side_effects=True, vmem_limit_bytes=VMEM_BYTES
        ),
        name="front",
    )(lengths, routes, prev_logits, tokens, cotangent, shard, weight_gu, weight_down)


def norm_forward(values, gain_vec):
    norm_scale = lax.rsqrt(jnp.mean(values * values, axis=-1, keepdims=True) + NORM_EPS)
    normed = values * norm_scale
    return (normed * gain_vec, normed, norm_scale)


def norm_backward(grad_out, normed, norm_scale, gain_vec):
    grad_normed = grad_out * gain_vec
    inner_mean = jnp.mean(grad_normed * normed, axis=-1, keepdims=True)
    return (norm_scale * (grad_normed - normed * inner_mean), jnp.sum(grad_out * normed, axis=0))


def attention_probs(queries, key_heads, allowed):
    scores = jnp.einsum(
        "qhd,khd->hqk", queries, key_heads, preferred_element_type=jnp.float32
    ) * HEAD ** (-0.5)
    scores = jnp.where(allowed[None], scores, -1e30)
    top_score = jnp.max(scores, axis=-1, keepdims=True)
    exp_scores = jnp.exp(scores - top_score)
    return exp_scores / jnp.sum(exp_scores, axis=-1, keepdims=True)


def diag_update(weight, grad, state, rate):
    new_state = 0.5 * state + 0.5 * grad * grad
    return (new_state, weight - rate * grad / (jnp.sqrt(new_state) + 1e-08))


def shampoo_kernel(sizes, *refs):
    n_row, n_col, model, slice_wide, tile = sizes
    low = jnp.bfloat16
    (
        grads,
        left_root_gu,
        right_root_down,
        right_root_gu,
        left_root_down,
        left_gu,
        right_down,
        right_gu,
        left_down,
        weight_gu,
        weight_down,
        out_grad_gu,
        out_grad_down,
        out_left_gu,
        out_right_down,
        out_right_gu,
        out_left_down,
        out_weight_gu,
        out_weight_down,
        grad_buf,
        root_buf,
        wide_buf,
        left_buf,
        right_buf,
        weight_buf,
        step_buf,
        lhs_buf,
        in_sem,
        wide_sem,
        out_sem,
    ) = refs
    r = lax.axis_index("row")
    c = lax.axis_index("col")
    owner = r * n_col + c
    blocks = n_row * n_col
    left_rows = left_buf.shape[1]
    right_rows = right_buf.shape[1]
    depth = root_buf.shape[1]
    wide_rows = wide_buf.shape[1]
    tiles = wide_rows // tile
    mats = range(3)
    roots = [left_root_gu.at[0], left_root_gu.at[1], right_root_down]
    wides = [right_root_gu.at[0], right_root_gu.at[1], left_root_down]
    lefts = [left_gu.at[0], left_gu.at[1], right_down]
    rights = [right_gu.at[0], right_gu.at[1], left_down]
    weights = [weight_gu.at[:, 0], weight_gu.at[:, 1], weight_down]
    out_lefts = [out_left_gu.at[0], out_left_gu.at[1], out_right_down]
    out_rights = [out_right_gu.at[0], out_right_gu.at[1], out_left_down]
    out_weights = [out_weight_gu.at[:, 0], out_weight_gu.at[:, 1], out_weight_down]
    out_grads = [out_grad_gu.at[:, 0], out_grad_gu.at[:, 1], out_grad_down]

    def load(m, kind, src, dst):
        copy = pltpu.make_async_copy(src, dst, in_sem.at[m, kind])
        copy.start()
        return copy

    loads = []
    for m in mats:
        span = pl.ds(m * model, model)
        loads.append(
            [
                load(m, 0, grads.at[:, span], grad_buf.at[:, span]),
                load(m, 1, roots[m], root_buf.at[m]),
                load(m, 2, rights[m], right_buf.at[m]),
                load(m, 3, lefts[m], left_buf.at[m]),
                load(m, 4, weights[m], weight_buf.at[m]),
            ]
        )
        for t in range(tiles):
            rows = pl.ds(t * tile, tile)
            copy = pltpu.make_async_copy(
                wides[m].at[rows], wide_buf.at[m, rows], wide_sem.at[m, t]
            )
            copy.start()
            loads[m].append(copy)
    stores = []

    def store(m, kind, src, dst):
        copy = pltpu.make_async_copy(src, dst, out_sem.at[m, kind])
        copy.start()
        stores.append(copy)

    for m in mats:
        span = pl.ds(m * model, model)
        loads[m][0].wait()
        loads[m][1].wait()
        lhs_buf[:right_rows] = grad_buf[owner, span].T
        lhs_buf[right_rows:] = root_buf[m].astype(low)
        loads[m][2].wait()
        loads[m][3].wait()
        left_buf[m] = 0.5 * left_buf[m]

        @pl.loop(0, blocks)
        def _(q):
            cols = pl.ds(pl.multiple_of(q * slice_wide, slice_wide), slice_wide)
            block = grad_buf[q, span]
            made = dot(lhs_buf[...], block)
            right_buf[m, :, cols] = 0.5 * right_buf[m, :, cols] + 0.5 * made[:right_rows]
            step_buf[:, cols] = made[right_rows:].astype(low)
            rows = pl.ds(pl.multiple_of(m * model + owner * left_rows, 16), left_rows)
            left_buf[m] += 0.5 * dot(grad_buf[q, rows], block, NT)

        store(m, 0, right_buf.at[m], out_rights[m])
        store(m, 1, left_buf.at[m], out_lefts[m])
        loads[m][4].wait()
        for t in range(tiles):
            loads[m][5 + t].wait()
            cols = pl.ds(t * tile, tile)
            step = dot(step_buf[...], wide_buf[m, cols].astype(low), NT)
            weight_buf[m, :, cols] = weight_buf[m, :, cols] - SHAMPOO_RATE * step
        store(m, 2, weight_buf.at[m], out_weights[m])
        for b in range(n_row):
            rows = pl.ds(pl.multiple_of(m * model + r * depth, 16), depth)
            wide_buf[m, :depth, b * slice_wide : (b + 1) * slice_wide] = grad_buf[
                c * n_row + b, rows
            ].astype(jnp.float32)
        store(m, 3, wide_buf.at[m, :depth, : n_row * slice_wide], out_grads[m])
    for copy in stores:
        copy.wait()


def shampoo(
    grads,
    left_root_gu,
    right_root_down,
    right_root_gu,
    left_root_down,
    left_gu,
    right_down,
    right_gu,
    left_down,
    weight_gu,
    weight_down,
    n_row,
    n_col,
):
    blocks, _, slice_wide = grads.shape
    model = left_root_gu.shape[2]
    depth = left_root_gu.shape[1]
    wide_rows, wide_cols = left_root_down.shape
    right_rows = left_down.shape[0]
    left_rows = right_down.shape[0]
    tile = min(256, wide_rows)
    f32 = jnp.float32
    dma = pltpu.SemaphoreType.DMA
    any_spec = pl.BlockSpec(memory_space=pl.ANY)
    args = (
        grads,
        left_root_gu,
        right_root_down,
        right_root_gu,
        left_root_down,
        left_gu,
        right_down,
        right_gu,
        left_down,
        weight_gu,
        weight_down,
    )
    return pl.pallas_call(
        functools.partial(shampoo_kernel, (n_row, n_col, model, slice_wide, tile)),
        out_shape=[
            jax.ShapeDtypeStruct(weight_gu.shape, f32),
            jax.ShapeDtypeStruct(weight_down.shape, f32),
            jax.ShapeDtypeStruct(left_gu.shape, f32),
            jax.ShapeDtypeStruct(right_down.shape, f32),
            jax.ShapeDtypeStruct(right_gu.shape, f32),
            jax.ShapeDtypeStruct(left_down.shape, f32),
            jax.ShapeDtypeStruct(weight_gu.shape, f32),
            jax.ShapeDtypeStruct(weight_down.shape, f32),
        ],
        in_specs=[any_spec] * len(args),
        out_specs=[any_spec] * 8,
        scratch_shapes=[
            pltpu.VMEM(grads.shape, jnp.bfloat16),
            pltpu.VMEM((3, depth, model), f32),
            pltpu.VMEM((3, wide_rows, wide_cols), f32),
            pltpu.VMEM((3, left_rows, model), f32),
            pltpu.VMEM((3, right_rows, wide_cols), f32),
            pltpu.VMEM((3, depth, wide_rows), f32),
            pltpu.VMEM((depth, wide_cols), jnp.bfloat16),
            pltpu.VMEM((right_rows + depth, model), jnp.bfloat16),
            dma((3, 5)),
            dma((3, wide_rows // tile)),
            dma((3, 4)),
        ],
        compiler_params=pltpu.CompilerParams(vmem_limit_bytes=60 * 2**20),
        name="shampoo",
    )(*args)


def shampoo_plain(
    grads,
    left_root_gu,
    right_root_down,
    right_root_gu,
    left_root_down,
    left_gu,
    right_down,
    right_gu,
    left_down,
    weight_gu,
    weight_down,
    n_row,
    n_col,
):
    low = jnp.bfloat16
    blocks, _, slice_wide = grads.shape
    model = left_root_gu.shape[2]
    r = lax.axis_index("row")
    c = lax.axis_index("col")
    owner = r * n_col + c
    left_rows = right_down.shape[0]
    right_rows = left_down.shape[0]
    product = functools.partial(jnp.einsum, preferred_element_type=jnp.float32)
    whole = grads.reshape(blocks, 3, model, slice_wide).transpose(1, 2, 0, 3).reshape(3, model, -1)
    mine_left = lax.dynamic_slice_in_dim(whole, owner * left_rows, left_rows, 1)
    mine_right = lax.dynamic_slice_in_dim(whole, owner * right_rows, right_rows, 2)
    left_sum = 0.5 * product("mif,mjf->mij", mine_left, whole)
    right_sum = 0.5 * product("mdi,mdj->mij", mine_right, whole)
    roots = jnp.concatenate([left_root_gu, right_root_down[None]]).astype(low)
    wides = jnp.concatenate([right_root_gu, left_root_down[None]]).astype(low)
    step = product("mid,mdf->mif", roots, whole).astype(low)
    step = SHAMPOO_RATE * product("mif,mjf->mij", step, wides)
    depth, wide_rows = weight_down.shape
    block = lax.dynamic_slice(whole, (0, r * depth, c * wide_rows), (3, depth, wide_rows))
    block = block.astype(jnp.float32)
    return (
        block[:2].transpose(1, 0, 2),
        block[2],
        0.5 * left_gu + left_sum[:2],
        0.5 * right_down + left_sum[2],
        0.5 * right_gu + right_sum[:2],
        0.5 * left_down + right_sum[2],
        weight_gu - step[:2].transpose(1, 0, 2),
        weight_down - step[2],
    )


def body_tiled(
    tokens,
    lengths,
    routes,
    prev_logits,
    cotangent,
    w_qkv,
    w_out,
    route_w,
    gains,
    const_vec,
    stat_qkv,
    stat_out,
    stat_route,
    stat_gains,
    stat_const,
    w_gate_up,
    w_down,
    left_gu,
    right_gu,
    left_down,
    right_down,
    left_root_gu,
    right_root_gu,
    left_root_down,
    right_root_down,
):
    dims = mesh_sizes()
    n_dp, n_row, n_col = dims
    low = jnp.bfloat16
    row_total = tokens.shape[0]
    total_experts = prev_logits.shape[1]
    num_ffn = total_experts - 4
    seq_count = lengths.shape[1]
    shard_rows = w_qkv.shape[0]
    wide_qkv = w_qkv.shape[1] // n_col
    wide_out = w_out.shape[1] // n_col
    route_cols = route_w.shape[1]
    wide = wide_qkv + wide_out + LANES

    def by_col(matrix):
        return matrix.reshape(matrix.shape[0], n_col, -1).transpose(1, 0, 2)

    def small_block(route_part, gain_part, const_part):
        together = jnp.concatenate([route_part, gain_part.T, const_part.T], axis=1)
        return jnp.pad(together, ((0, 0), (0, LANES - together.shape[1])))

    small = small_block(route_w, gains, const_vec)
    shard = jnp.concatenate(
        [by_col(w_qkv), by_col(w_out), jnp.broadcast_to(small[None], (n_col, shard_rows, LANES))],
        axis=2,
    )
    whole, parts_back, grads_own, qkv_rows, softmax_probs, mixed_heads, first_sum, state = front(
        lengths,
        routes,
        prev_logits,
        tokens,
        cotangent,
        shard,
        w_gate_up[0],
        w_down[0].T,
        dims,
        (wide_qkv, wide_out, route_cols),
    )
    whole = whole.reshape(n_col, D, wide)
    full_qkv = [whole[i, :, :wide_qkv] for i in range(n_col)]
    full_out = [whole[i, :, wide_qkv : wide_qkv + wide_out] for i in range(n_col)]
    full_small = whole[0, :, wide_qkv + wide_out :]
    full_route = full_small[:, :route_cols]
    row_vectors = full_small[:, route_cols : route_cols + 4].T.astype(jnp.float32)
    gain_one, gain_two, const_rows = row_vectors[0], row_vectors[1], row_vectors[2:4]
    slice_wide = grads_own.shape[1]
    positions = jnp.arange(row_total, dtype=jnp.int32)
    seq_ends = jnp.cumsum(lengths[0])
    doc_index = jnp.sum((positions[:, None] >= seq_ends[None, :]).astype(jnp.int32), axis=1)
    valid_rows = (doc_index < seq_count).astype(jnp.float32)[:, None]
    inputs = tokens.astype(jnp.float32)
    h_one, normed_one, scale_one = norm_forward(inputs, gain_one)
    h_one_low = h_one.astype(low)
    qkv_rows = qkv_rows.reshape(row_total, 3, HEADS, HEAD)
    queries, key_heads, values = (qkv_rows[:, 0], qkv_rows[:, 1], qkv_rows[:, 2])
    probs_low = softmax_probs.astype(low)
    h_two, normed_two, scale_two = norm_forward(first_sum, gain_two)
    h_two_low = h_two.astype(low)
    pick_table = (
        routes[:, :, None] == jnp.arange(total_experts, dtype=jnp.int32)[None, None, :]
    ).astype(jnp.float32)
    gate_weights = state[:, :2]
    const_mix = state[:, 2:6].reshape(row_total, 2, 2)
    where_in = state[:, 6:8].astype(jnp.int32)
    slot_ids = jnp.arange(num_ffn * CAP, dtype=jnp.int32)
    place_first = where_in[:, 0:1] == slot_ids[None, :]
    place_second = where_in[:, 1:2] == slot_ids[None, :]
    place_both = (place_first | place_second).astype(low)
    grad_y = cotangent.astype(jnp.float32) * valid_rows
    parts_back = parts_back.reshape(n_col, n_dp, n_row, CAP, 2 * D)
    came_back = token_reduce(parts_back, dims).reshape(num_ffn * CAP, 2 * D)
    expert_out = came_back[:, :D]
    grad_sent = came_back[:, D:]
    gathered = plane_gather(grads_own.reshape(4, -1, slice_wide), dims)
    gathered = gathered.reshape(n_col * n_row, 3 * D, slice_wide)

    is_ffn_first = dot(place_first.astype(low), expert_out)
    is_ffn_second = dot(place_second.astype(low), expert_out)
    picked = jnp.stack([is_ffn_first, is_ffn_second], axis=1)
    copy_sel = (routes == num_ffn + 1).astype(jnp.float32)
    const_sel = (
        routes[:, :, None] == num_ffn + 2 + jnp.arange(2, dtype=jnp.int32)[None, None, :]
    ).astype(jnp.float32)
    const_out = (
        const_mix[:, :, 0:1] * h_two[:, None, :] + const_mix[:, :, 1:2] * const_rows[None, :, :]
    )
    outputs = (
        picked
        + copy_sel[:, :, None] * h_two[:, None, :]
        + const_sel[:, :, 0:1] * const_out[:, None, 0, :]
        + const_sel[:, :, 1:2] * const_out[:, None, 1, :]
    )
    moe_out = valid_rows * jnp.sum(gate_weights[:, :, None] * outputs, axis=1)
    result = (first_sum + moe_out).astype(low)
    grad_gate = jnp.sum(grad_y[:, None, :] * outputs, axis=-1)
    grad_chosen = gate_weights * (
        grad_gate - jnp.sum(gate_weights * grad_gate, axis=-1, keepdims=True)
    )
    grad_logits = jnp.sum(grad_chosen[:, :, None] * pick_table, axis=1)
    const_weight = jnp.sum(const_sel * gate_weights[:, :, None], axis=1)
    mix_first = const_weight * jnp.sum(grad_y * h_two, axis=-1, keepdims=True)
    mix_second = const_weight * jnp.stack(
        [jnp.sum(grad_y * const_rows[0], axis=-1), jnp.sum(grad_y * const_rows[1], axis=-1)], axis=1
    )
    grad_mix = jnp.stack([mix_first, mix_second], axis=-1)
    grad_mix_logits = const_mix * (grad_mix - jnp.sum(const_mix * grad_mix, axis=-1, keepdims=True))
    grad_logits_all = jnp.concatenate(
        [grad_logits, grad_mix_logits.reshape(row_total, 4)], axis=1
    ).astype(low)
    grad_route_full = dot(h_two_low, grad_logits_all, TN)
    const_scale = const_weight * const_mix[:, :, 1]
    grad_const_full = jnp.stack(
        [
            jnp.sum(const_scale[:, 0:1] * grad_y, axis=0),
            jnp.sum(const_scale[:, 1:2] * grad_y, axis=0),
        ]
    )
    back_rows = dot(place_both, grad_sent)
    own_weight = jnp.sum(gate_weights * copy_sel, axis=1, keepdims=True) + jnp.sum(
        const_weight * const_mix[:, :, 0], axis=1, keepdims=True
    )
    grad_h_two = dot(grad_logits_all, full_route, NT) + back_rows + own_weight * grad_y
    grad_first, grad_gain_two = norm_backward(grad_h_two, normed_two, scale_two, gain_two)
    grad_first = grad_first + cotangent.astype(jnp.float32)
    grad_attn = (valid_rows * grad_first).astype(low)
    grad_mixed = functools.reduce(
        jnp.add,
        [
            dot(grad_attn[:, i * wide_out : (i + 1) * wide_out], part, NT)
            for i, part in enumerate(full_out)
        ],
    ).astype(low)
    grad_mixed = grad_mixed.reshape(row_total, HEADS, HEAD)
    grad_values = jnp.einsum(
        "hqk,qhd->khd", probs_low, grad_mixed, preferred_element_type=jnp.float32
    )
    grad_probs = jnp.einsum("qhd,khd->hqk", grad_mixed, values, preferred_element_type=jnp.float32)
    grad_scores = softmax_probs * (
        grad_probs - jnp.sum(softmax_probs * grad_probs, axis=-1, keepdims=True)
    )
    grad_scores = grad_scores.astype(low)
    grad_queries = jnp.einsum(
        "hqk,khd->qhd", grad_scores, key_heads, preferred_element_type=jnp.float32
    ) * HEAD ** (-0.5)
    grad_keys = jnp.einsum(
        "hqk,qhd->khd", grad_scores, queries, preferred_element_type=jnp.float32
    ) * HEAD ** (-0.5)
    grad_qkv_rows = (
        jnp.stack([grad_queries, grad_keys, grad_values], axis=1)
        .reshape(row_total, 3 * D)
        .astype(low)
    )
    grad_h_one = functools.reduce(
        jnp.add,
        [
            dot(grad_qkv_rows[:, i * wide_qkv : (i + 1) * wide_qkv], part, NT)
            for i, part in enumerate(full_qkv)
        ],
    )
    grad_input, grad_gain_one = norm_backward(grad_h_one, normed_one, scale_one, gain_one)
    grad_input = grad_input + grad_first
    grad_gains_full = jnp.stack([grad_gain_one, grad_gain_two])

    grad_small = small_block(grad_route_full, grad_gains_full, grad_const_full).astype(low)
    param_parts = jnp.stack(
        [
            jnp.concatenate(
                [
                    dot(h_one_low, grad_qkv_rows[:, i * wide_qkv : (i + 1) * wide_qkv], TN).astype(
                        low
                    ),
                    dot(mixed_heads, grad_attn[:, i * wide_out : (i + 1) * wide_out], TN).astype(
                        low
                    ),
                    grad_small,
                ],
                axis=1,
            )
            for i in range(n_col)
        ]
    )
    summed = param_reduce(
        param_parts.reshape(n_col, n_dp, n_row, n_col * shard_rows, wide), dims
    )

    def from_col(parts):
        return parts.transpose(1, 0, 2).reshape(parts.shape[1], -1)

    grad_qkv = from_col(summed[:, :, :wide_qkv])
    grad_attn_out = from_col(summed[:, :, wide_qkv : wide_qkv + wide_out])
    sum_small = summed[0, :, wide_qkv + wide_out :]
    grad_route = sum_small[:, :route_cols]
    grad_gains = sum_small[:, route_cols : route_cols + 2].T
    grad_const = sum_small[:, route_cols + 2 : route_cols + 4].T
    moment_qkv, new_qkv = diag_update(w_qkv, grad_qkv, stat_qkv, D ** (-0.5))
    moment_attn_out, new_attn_out = diag_update(w_out, grad_attn_out, stat_out, HEAD ** (-0.5))
    moment_route, new_route = diag_update(route_w, grad_route, stat_route, (4 * D) ** (-0.5))
    moment_gains, new_gains = diag_update(gains, grad_gains, stat_gains, 0.3)
    moment_const, new_const = diag_update(const_vec, grad_const, stat_const, 0.5)

    (
        grad_gate_up,
        grad_down,
        new_left_gu,
        new_right_down,
        new_right_gu,
        new_left_down,
        new_gate_up,
        new_down,
    ) = shampoo(
        gathered,
        left_root_gu[0],
        right_root_down[0],
        right_root_gu[0],
        left_root_down[0],
        left_gu[0],
        right_down[0],
        right_gu[0],
        left_down[0],
        w_gate_up[0],
        w_down[0].T,
        n_row,
        n_col,
    )
    return (
        result,
        grad_input,
        grad_qkv,
        moment_qkv,
        new_qkv,
        grad_attn_out,
        moment_attn_out,
        new_attn_out,
        grad_route,
        moment_route,
        new_route,
        grad_gains,
        moment_gains,
        new_gains,
        grad_const,
        moment_const,
        new_const,
        grad_gate_up[None],
        grad_down.T[None],
        new_left_gu[None],
        new_right_gu[None],
        new_left_down[None],
        new_right_down[None],
        new_gate_up[None],
        new_down.T[None],
    )


def body(
    tokens,
    lengths,
    routes,
    prev_logits,
    cotangent,
    w_qkv,
    w_out,
    route_w,
    gains,
    const_vec,
    stat_qkv,
    stat_out,
    stat_route,
    stat_gains,
    stat_const,
    w_gate_up,
    w_down,
    left_gu,
    right_gu,
    left_down,
    right_down,
    left_root_gu,
    right_root_gu,
    left_root_down,
    right_root_down,
):
    dims = mesh_sizes()
    n_dp, n_row, n_col = dims
    low = jnp.bfloat16
    row_total = tokens.shape[0]
    total_experts = prev_logits.shape[1]
    num_ffn = total_experts - 4
    seq_count = lengths.shape[1]
    shard_rows = w_qkv.shape[0]
    wide_qkv = w_qkv.shape[1] // n_col
    wide_out = w_out.shape[1] // n_col
    route_cols = route_w.shape[1]
    wide = wide_qkv + wide_out + LANES

    def by_col(matrix):
        return matrix.reshape(matrix.shape[0], n_col, -1).transpose(1, 0, 2)

    def small_block(route_part, gain_part, const_part):
        together = jnp.concatenate([route_part, gain_part.T, const_part.T], axis=1)
        return jnp.pad(together, ((0, 0), (0, LANES - together.shape[1])))

    small = small_block(route_w, gains, const_vec)
    shard = jnp.concatenate(
        [by_col(w_qkv), by_col(w_out), jnp.broadcast_to(small[None], (n_col, shard_rows, LANES))],
        axis=2,
    )
    whole = param_gather(shard, dims).reshape(n_col, D, wide)
    full_qkv = [whole[i, :, :wide_qkv] for i in range(n_col)]
    full_out = [whole[i, :, wide_qkv : wide_qkv + wide_out] for i in range(n_col)]
    full_small = whole[0, :, wide_qkv + wide_out :]
    full_route = full_small[:, :route_cols]
    row_vectors = full_small[:, route_cols : route_cols + 4].T.astype(jnp.float32)
    gain_one, gain_two, const_rows = row_vectors[0], row_vectors[1], row_vectors[2:4]

    row_depth = w_gate_up.shape[1]
    col_width = w_gate_up.shape[3]
    slice_wide = col_width // n_row
    gu_slices = w_gate_up[0].astype(low).reshape(row_depth, 2, n_row, slice_wide)
    gu_slices = gu_slices.transpose(2, 0, 1, 3)
    gu_own = lax.all_to_all(gu_slices, "row", split_axis=0, concat_axis=0, tiled=True)
    gu_own = gu_own.reshape(n_row * row_depth, 2 * slice_wide)
    down_slices = w_down[0].astype(low).reshape(n_row, slice_wide, row_depth)
    down_own = lax.all_to_all(down_slices, "row", split_axis=0, concat_axis=0, tiled=True)
    down_own = down_own.transpose(1, 0, 2).reshape(slice_wide, n_row * row_depth)

    positions = jnp.arange(row_total, dtype=jnp.int32)
    seq_ends = jnp.cumsum(lengths[0])
    doc_index = jnp.sum((positions[:, None] >= seq_ends[None, :]).astype(jnp.int32), axis=1)
    valid_rows = (doc_index < seq_count).astype(jnp.float32)[:, None]
    allowed = (doc_index[:, None] == doc_index[None, :]) & (
        positions[:, None] >= positions[None, :]
    )
    inputs = tokens.astype(jnp.float32)
    h_one, normed_one, scale_one = norm_forward(inputs, gain_one)
    h_one_low = h_one.astype(low)
    qkv_rows = jnp.concatenate([dot(h_one_low, part) for part in full_qkv], axis=1).astype(low)
    qkv_rows = qkv_rows.reshape(row_total, 3, HEADS, HEAD)
    queries, key_heads, values = (qkv_rows[:, 0], qkv_rows[:, 1], qkv_rows[:, 2])
    softmax_probs = attention_probs(queries, key_heads, allowed)
    probs_low = softmax_probs.astype(low)
    mixed_heads = jnp.einsum("hqk,khd->qhd", probs_low, values, preferred_element_type=jnp.float32)
    mixed_heads = mixed_heads.reshape(row_total, D).astype(low)
    attn_out = jnp.concatenate([dot(mixed_heads, part) for part in full_out], axis=1)
    first_sum = inputs + valid_rows * attn_out
    h_two, normed_two, scale_two = norm_forward(first_sum, gain_two)
    h_two_low = h_two.astype(low)
    logits_all = dot(h_two_low, full_route)
    logits = logits_all[:, :total_experts] + prev_logits
    pick_table = (
        routes[:, :, None] == jnp.arange(total_experts, dtype=jnp.int32)[None, None, :]
    ).astype(jnp.float32)
    chosen = jnp.sum(pick_table * logits[:, None, :], axis=-1)
    gate_weights = jax.nn.softmax(chosen, axis=-1)
    const_mix = jax.nn.softmax(logits_all[:, total_experts:].reshape(row_total, 2, 2), axis=-1)

    earlier = dot(
        (positions[:, None] > positions[None, :]).astype(low),
        jnp.sum(pick_table, axis=1).astype(low),
    )
    slot_index = jnp.sum(earlier[:, None, :] * pick_table, axis=-1).astype(jnp.int32)
    where_in = jnp.where(routes < num_ffn, routes * CAP + slot_index, -1)
    slot_ids = jnp.arange(num_ffn * CAP, dtype=jnp.int32)
    place_first = where_in[:, 0:1] == slot_ids[None, :]
    place_second = where_in[:, 1:2] == slot_ids[None, :]
    place_both = (place_first | place_second).astype(low)
    slot_gate = jnp.sum(
        place_first.astype(jnp.float32) * gate_weights[:, 0:1]
        + place_second.astype(jnp.float32) * gate_weights[:, 1:2],
        axis=0,
    )
    grad_y = cotangent.astype(jnp.float32) * valid_rows
    sent_rows = dot(place_both, h_two_low, TN).astype(low)
    grad_made = (slot_gate[:, None] * dot(place_both, grad_y.astype(low), TN)).astype(low)
    sent_both = jnp.concatenate(
        [sent_rows.reshape(num_ffn, CAP, D), grad_made.reshape(num_ffn, CAP, D)], axis=2
    )

    arrived = token_gather(sent_both, dims).reshape(-1, 2 * D)
    rows_in = arrived[:, :D]
    grads_in = arrived[:, D:]
    pre_act = dot(rows_in, gu_own)
    gate_part = pre_act[:, :slice_wide]
    up_part = pre_act[:, slice_wide:]
    sigma = jax.nn.sigmoid(gate_part)
    silu = gate_part * sigma
    hidden = (silu * up_part).astype(low)
    made_rows = dot(hidden, down_own).astype(low)
    grad_hidden = dot(grads_in, down_own, NT)
    grad_pre = jnp.concatenate(
        [
            grad_hidden * up_part * sigma * (1.0 + gate_part * (1.0 - sigma)),
            grad_hidden * silu,
        ],
        axis=1,
    ).astype(low)
    grad_rows = dot(grad_pre, gu_own, NT).astype(low)
    parts_back = jnp.concatenate([made_rows, grad_rows], axis=1)
    parts_back = parts_back.reshape(n_col, n_dp, n_row, CAP, 2 * D)
    came_back = token_reduce(parts_back, dims).reshape(num_ffn * CAP, 2 * D)
    expert_out = came_back[:, :D]
    grad_sent = came_back[:, D:]

    grad_gu_own = dot(rows_in, grad_pre, TN).astype(low)
    grad_down_own = dot(hidden, grads_in, TN).astype(low)
    grads_own = jnp.concatenate(
        [grad_gu_own[:, :slice_wide], grad_gu_own[:, slice_wide:], grad_down_own.T], axis=0
    )
    gathered = plane_gather(grads_own.reshape(4, -1, slice_wide), dims)
    gathered = gathered.reshape(n_col * n_row, 3 * D, slice_wide)

    is_ffn_first = dot(place_first.astype(low), expert_out)
    is_ffn_second = dot(place_second.astype(low), expert_out)
    picked = jnp.stack([is_ffn_first, is_ffn_second], axis=1)
    copy_sel = (routes == num_ffn + 1).astype(jnp.float32)
    const_sel = (
        routes[:, :, None] == num_ffn + 2 + jnp.arange(2, dtype=jnp.int32)[None, None, :]
    ).astype(jnp.float32)
    const_out = (
        const_mix[:, :, 0:1] * h_two[:, None, :] + const_mix[:, :, 1:2] * const_rows[None, :, :]
    )
    outputs = (
        picked
        + copy_sel[:, :, None] * h_two[:, None, :]
        + const_sel[:, :, 0:1] * const_out[:, None, 0, :]
        + const_sel[:, :, 1:2] * const_out[:, None, 1, :]
    )
    moe_out = valid_rows * jnp.sum(gate_weights[:, :, None] * outputs, axis=1)
    result = (first_sum + moe_out).astype(low)
    grad_gate = jnp.sum(grad_y[:, None, :] * outputs, axis=-1)
    grad_chosen = gate_weights * (
        grad_gate - jnp.sum(gate_weights * grad_gate, axis=-1, keepdims=True)
    )
    grad_logits = jnp.sum(grad_chosen[:, :, None] * pick_table, axis=1)
    const_weight = jnp.sum(const_sel * gate_weights[:, :, None], axis=1)
    mix_first = const_weight * jnp.sum(grad_y * h_two, axis=-1, keepdims=True)
    mix_second = const_weight * jnp.stack(
        [jnp.sum(grad_y * const_rows[0], axis=-1), jnp.sum(grad_y * const_rows[1], axis=-1)], axis=1
    )
    grad_mix = jnp.stack([mix_first, mix_second], axis=-1)
    grad_mix_logits = const_mix * (grad_mix - jnp.sum(const_mix * grad_mix, axis=-1, keepdims=True))
    grad_logits_all = jnp.concatenate(
        [grad_logits, grad_mix_logits.reshape(row_total, 4)], axis=1
    ).astype(low)
    grad_route_full = dot(h_two_low, grad_logits_all, TN)
    const_scale = const_weight * const_mix[:, :, 1]
    grad_const_full = jnp.stack(
        [
            jnp.sum(const_scale[:, 0:1] * grad_y, axis=0),
            jnp.sum(const_scale[:, 1:2] * grad_y, axis=0),
        ]
    )
    back_rows = dot(place_both, grad_sent)
    own_weight = jnp.sum(gate_weights * copy_sel, axis=1, keepdims=True) + jnp.sum(
        const_weight * const_mix[:, :, 0], axis=1, keepdims=True
    )
    grad_h_two = dot(grad_logits_all, full_route, NT) + back_rows + own_weight * grad_y
    grad_first, grad_gain_two = norm_backward(grad_h_two, normed_two, scale_two, gain_two)
    grad_first = grad_first + cotangent.astype(jnp.float32)
    grad_attn = (valid_rows * grad_first).astype(low)
    grad_mixed = functools.reduce(
        jnp.add,
        [
            dot(grad_attn[:, i * wide_out : (i + 1) * wide_out], part, NT)
            for i, part in enumerate(full_out)
        ],
    ).astype(low)
    grad_mixed = grad_mixed.reshape(row_total, HEADS, HEAD)
    grad_values = jnp.einsum(
        "hqk,qhd->khd", probs_low, grad_mixed, preferred_element_type=jnp.float32
    )
    grad_probs = jnp.einsum("qhd,khd->hqk", grad_mixed, values, preferred_element_type=jnp.float32)
    grad_scores = softmax_probs * (
        grad_probs - jnp.sum(softmax_probs * grad_probs, axis=-1, keepdims=True)
    )
    grad_scores = grad_scores.astype(low)
    grad_queries = jnp.einsum(
        "hqk,khd->qhd", grad_scores, key_heads, preferred_element_type=jnp.float32
    ) * HEAD ** (-0.5)
    grad_keys = jnp.einsum(
        "hqk,qhd->khd", grad_scores, queries, preferred_element_type=jnp.float32
    ) * HEAD ** (-0.5)
    grad_qkv_rows = (
        jnp.stack([grad_queries, grad_keys, grad_values], axis=1)
        .reshape(row_total, 3 * D)
        .astype(low)
    )
    grad_h_one = functools.reduce(
        jnp.add,
        [
            dot(grad_qkv_rows[:, i * wide_qkv : (i + 1) * wide_qkv], part, NT)
            for i, part in enumerate(full_qkv)
        ],
    )
    grad_input, grad_gain_one = norm_backward(grad_h_one, normed_one, scale_one, gain_one)
    grad_input = grad_input + grad_first
    grad_gains_full = jnp.stack([grad_gain_one, grad_gain_two])

    grad_small = small_block(grad_route_full, grad_gains_full, grad_const_full).astype(low)
    param_parts = jnp.stack(
        [
            jnp.concatenate(
                [
                    dot(h_one_low, grad_qkv_rows[:, i * wide_qkv : (i + 1) * wide_qkv], TN).astype(
                        low
                    ),
                    dot(mixed_heads, grad_attn[:, i * wide_out : (i + 1) * wide_out], TN).astype(
                        low
                    ),
                    grad_small,
                ],
                axis=1,
            )
            for i in range(n_col)
        ]
    )
    summed = param_reduce(
        param_parts.reshape(n_col, n_dp, n_row, n_col * shard_rows, wide), dims
    )

    def from_col(parts):
        return parts.transpose(1, 0, 2).reshape(parts.shape[1], -1)

    grad_qkv = from_col(summed[:, :, :wide_qkv])
    grad_attn_out = from_col(summed[:, :, wide_qkv : wide_qkv + wide_out])
    sum_small = summed[0, :, wide_qkv + wide_out :]
    grad_route = sum_small[:, :route_cols]
    grad_gains = sum_small[:, route_cols : route_cols + 2].T
    grad_const = sum_small[:, route_cols + 2 : route_cols + 4].T
    moment_qkv, new_qkv = diag_update(w_qkv, grad_qkv, stat_qkv, D ** (-0.5))
    moment_attn_out, new_attn_out = diag_update(w_out, grad_attn_out, stat_out, HEAD ** (-0.5))
    moment_route, new_route = diag_update(route_w, grad_route, stat_route, (4 * D) ** (-0.5))
    moment_gains, new_gains = diag_update(gains, grad_gains, stat_gains, 0.3)
    moment_const, new_const = diag_update(const_vec, grad_const, stat_const, 0.5)

    (
        grad_gate_up,
        grad_down,
        new_left_gu,
        new_right_down,
        new_right_gu,
        new_left_down,
        new_gate_up,
        new_down,
    ) = shampoo_plain(
        gathered,
        left_root_gu[0],
        right_root_down[0],
        right_root_gu[0],
        left_root_down[0],
        left_gu[0],
        right_down[0],
        right_gu[0],
        left_down[0],
        w_gate_up[0],
        w_down[0].T,
        n_row,
        n_col,
    )
    return (
        result,
        grad_input,
        grad_qkv,
        moment_qkv,
        new_qkv,
        grad_attn_out,
        moment_attn_out,
        new_attn_out,
        grad_route,
        moment_route,
        new_route,
        grad_gains,
        moment_gains,
        new_gains,
        grad_const,
        moment_const,
        new_const,
        grad_gate_up[None],
        grad_down.T[None],
        new_left_gu[None],
        new_right_gu[None],
        new_left_down[None],
        new_right_down[None],
        new_gate_up[None],
        new_down.T[None],
    )


def solution(mesh):
    placed = (
        P(("dp", "row", "col"), None),
        P(("dp", "row", "col"), None),
        P(("dp", "row", "col"), None),
        P(("dp", "row", "col"), None),
        P(("dp", "row", "col"), None),
        P(("dp", "row", "col"), None),
        P(("dp", "row", "col"), None),
        P(("dp", "row", "col"), None),
        P(None, ("dp", "row", "col")),
        P(None, ("dp", "row", "col")),
        P(("dp", "row", "col"), None),
        P(("dp", "row", "col"), None),
        P(("dp", "row", "col"), None),
        P(None, ("dp", "row", "col")),
        P(None, ("dp", "row", "col")),
        P("dp", "row", None, "col"),
        P("dp", "col", "row"),
        P("dp", None, ("row", "col"), None),
        P("dp", None, ("row", "col"), None),
        P("dp", ("row", "col"), None),
        P("dp", ("row", "col"), None),
        P("dp", None, "row", None),
        P("dp", None, "col", None),
        P("dp", "col", None),
        P("dp", "row", None),
    )
    tiled = 3 * D % (mesh.shape["col"] * LANES) == 0 and D % (mesh.shape["col"] * LANES) == 0
    tiled = tiled and D // mesh.shape["dp"] // mesh.shape["row"] % 16 == 0
    return jax.shard_map(
        body_tiled if tiled else body,
        mesh=mesh,
        in_specs=placed,
        out_specs=(
            P(("dp", "row", "col"), None),
            P(("dp", "row", "col"), None),
            P(("dp", "row", "col"), None),
            P(("dp", "row", "col"), None),
            P(("dp", "row", "col"), None),
            P(("dp", "row", "col"), None),
            P(("dp", "row", "col"), None),
            P(("dp", "row", "col"), None),
            P(("dp", "row", "col"), None),
            P(("dp", "row", "col"), None),
            P(("dp", "row", "col"), None),
            P(None, ("dp", "row", "col")),
            P(None, ("dp", "row", "col")),
            P(None, ("dp", "row", "col")),
            P(None, ("dp", "row", "col")),
            P(None, ("dp", "row", "col")),
            P(None, ("dp", "row", "col")),
            P("dp", "row", None, "col"),
            P("dp", "col", "row"),
            P("dp", None, ("row", "col"), None),
            P("dp", None, ("row", "col"), None),
            P("dp", ("row", "col"), None),
            P("dp", ("row", "col"), None),
            P("dp", "row", None, "col"),
            P("dp", "col", "row"),
        ),
        check_vma=False,
    )
```

```python
import functools
import types

import jax
import jax.numpy as jnp
from jax import lax
from jax.experimental import pallas as pl
from jax.experimental.pallas import tpu as pltpu
from jax.sharding import PartitionSpec as P

D = 768
HEADS = 12
HEAD = 64
CAP = 32
LANES = 128


NORM_EPS = 1e-06
SHAMPOO_RATE = 0.5
MESH = pl.DeviceIdType.MESH
VMEM_BYTES = 56 * 2**20


def dot(left, right, dims=(((1,), (0,)), ((), ()))):
    return lax.dot_general(left, right, dims, preferred_element_type=jnp.float32)


NT = (((1,), (1,)), ((), ()))
TN = (((0,), (0,)), ((), ()))


def flip(index, bit):
    return index + bit * (1 - 2 * ((index // bit) % 2))


def flip_all(index, mask, bits):
    for dim in range(bits):
        if mask & (1 << dim):
            index = flip(index, 1 << dim)
    return index


def mesh_sizes():
    return tuple(lax.axis_size(name) for name in ("dp", "row", "col"))


def bits_of(count):
    bits = count.bit_length() - 1
    assert 1 << bits == count
    return bits


def greet(over_dp, dims, place, all_rows=False):
    n_dp, n_row, n_col = dims
    d, r, c = place
    peers = []
    if over_dp:
        peers += [((d + j) % n_dp, r, c) for j in range(1, n_dp)]
    if all_rows:
        peers += [(d, (r + i) % n_row, c) for i in range(1, n_row)]
    else:
        peers += [(d, flip(r, 1 << dim), c) for dim in range(bits_of(n_row))]
    peers += [(d, r, (c + i) % n_col) for i in range(1, n_col)]
    barrier = pltpu.get_barrier_semaphore()
    for peer in peers:
        pl.semaphore_signal(barrier, inc=1, device_id=peer, device_id_type=MESH)
    pl.semaphore_wait(barrier, len(peers))


def remote(src, dst, send_sem, recv_sem, device):
    return pltpu.make_async_remote_copy(
        src_ref=src,
        dst_ref=dst,
        send_sem=send_sem,
        recv_sem=recv_sem,
        device_id=device,
        device_id_type=MESH,
    )


def plan_spread(dims, place, chunks, over_dp, own, dp_source, slot, sems):
    n_dp, n_row, n_col = dims
    d, r, c = place
    bits = bits_of(n_row)
    dp_send, dp_recv, row_send, row_recv, col_send, col_recv, own_sem = sems
    sent = []

    def block(j, x):
        return slot(c, j, flip_all(r, x, bits))

    def to_row(j, src, x, bit):
        copy = remote(
            src,
            block(j, x),
            row_send.at[j, x ^ bit],
            row_recv.at[j, x ^ bit],
            (d, flip(r, bit), c),
        )
        copy.start()
        sent.append(copy)

    def to_cols(j, src, x):
        for i in range(1, n_col):
            copy = remote(
                src,
                block(j, x),
                col_send.at[j, x, i],
                col_recv.at[j, x, i],
                (d, r, (c + i) % n_col),
            )
            copy.start()
            sent.append(copy)

    def order(j):
        return [1 << ((j + s) % bits) for s in range(bits)]

    locals_ = []

    def start(j):
        if over_dp and j > 0:
            src = block(j, 0)
            remote(src, src, dp_send.at[j], dp_recv.at[j], (d, r, c)).wait_recv()
        elif own is None:
            src = block(j, 0)
        else:
            src = own(j)
            keep = pltpu.make_async_copy(src, block(j, 0), own_sem.at[j])
            keep.start()
            locals_.append(keep)
        for bit in order(j):
            to_row(j, src, 0, bit)
        to_cols(j, src, 0)

    def arrived(j, x, later_dims):
        ref = block(j, x)
        remote(ref, ref, row_send.at[j, x], row_recv.at[j, x], (d, r, c)).wait_recv()
        for later in later_dims:
            to_row(j, ref, x, later)
        to_cols(j, ref, x)

    def pass_on(j):
        have = [0]
        dim_order = order(j)
        for s, bit in enumerate(dim_order[:-1]):
            new = [x ^ bit for x in have]
            for x in new:
                arrived(j, x, dim_order[s + 1 :])
            have += new

    def last_arrivals(j):
        bit = order(j)[-1]
        for x in range(n_row):
            if x & bit:
                arrived(j, x, [])

    def send_dp():
        for j in range(1, n_dp):
            peer = (d + j) % n_dp
            copy = remote(
                dp_source(peer),
                slot(c, ("from", d), r),
                dp_send.at[j],
                dp_recv.at[j],
                (peer, r, c),
            )
            copy.start()
            sent.append(copy)

    def wait_cols():
        for j in range(chunks):
            for x in range(n_row):
                for i in range(1, n_col):
                    ref = slot((c + n_col - i) % n_col, j, flip_all(r, x, bits))
                    remote(
                        ref, ref, col_send.at[j, x, i], col_recv.at[j, x, i], (d, r, c)
                    ).wait_recv()
        for copy in locals_:
            copy.wait()
        return [copy.wait_send for copy in sent]

    return types.SimpleNamespace(
        start=start,
        send_dp=send_dp,
        pass_on=pass_on,
        last_arrivals=last_arrivals,
        wait_cols=wait_cols,
    )


def spread_blocks(dims, place, chunks, over_dp, own, dp_source, slot, sems, between=None):
    plan = plan_spread(dims, place, chunks, over_dp, own, dp_source, slot, sems)
    plan.start(0)
    if over_dp:
        plan.send_dp()
        for j in range(1, chunks):
            plan.start(j)
            plan.pass_on(j - 1)
        plan.pass_on(chunks - 1)
    else:
        for j in range(1, chunks):
            plan.start(j)
        for j in range(chunks):
            plan.pass_on(j)
    if between is not None:
        between()
    for j in range(chunks):
        plan.last_arrivals(j)
    return plan.wait_cols()


def finish(waits):
    for wait in waits:
        wait()


def spread_sems(dims, chunks):
    n_dp, n_row, n_col = dims
    dma = pltpu.SemaphoreType.DMA
    return [
        dma((n_dp,)),
        dma((n_dp,)),
        dma((chunks, n_row)),
        dma((chunks, n_row)),
        dma((chunks, n_row, n_col)),
        dma((chunks, n_row, n_col)),
        dma((chunks,)),
    ]


def axis_place():
    return tuple(lax.axis_index(name) for name in ("dp", "row", "col"))


def param_gather_kernel(dims, shard_ref, out_ref, swap_ref, block_ref, swap_send, swap_recv, *sems):
    n_dp, n_row, n_col = dims
    place = axis_place()
    d, r, c = place
    rows = shard_ref.shape[1]
    greet(True, dims, place)
    copies = []
    for i in range(1, n_col):
        other = (c + i) % n_col
        copy = remote(
            shard_ref.at[other], swap_ref.at[c], swap_send.at[i], swap_recv.at[i], (d, r, other)
        )
        copy.start()
        copies.append(copy)
    swap_ref[pl.ds(c, 1)] = shard_ref[pl.ds(c, 1)]
    for copy in copies:
        copy.wait()
    for i in range(n_col):
        block_ref[i * rows : (i + 1) * rows, :] = swap_ref[i]
    low_ref = sems[-1]
    low_ref[...] = block_ref[...].astype(jnp.bfloat16)

    def slot(col, j, b):
        k = j[1] if isinstance(j, tuple) else (d + n_dp - j) % n_dp
        return out_ref.at[col, k, b]

    finish(
        spread_blocks(
            dims, place, n_dp, True, lambda j: low_ref, lambda k: low_ref, slot, sems[:-1]
        )
    )


def param_gather(shard, dims):
    n_dp, n_row, n_col = dims
    _, rows, width = shard.shape
    dma = pltpu.SemaphoreType.DMA
    return pl.pallas_call(
        functools.partial(param_gather_kernel, dims),
        out_shape=jax.ShapeDtypeStruct((n_col, n_dp, n_row, n_col * rows, width), jnp.bfloat16),
        in_specs=[pl.BlockSpec(memory_space=pltpu.VMEM)],
        out_specs=pl.BlockSpec(memory_space=pl.ANY),
        scratch_shapes=[
            pltpu.VMEM((n_col, rows, width), jnp.float32),
            pltpu.VMEM((n_col * rows, width), jnp.float32),
            dma((n_col,)),
            dma((n_col,)),
            *spread_sems(dims, n_dp),
            pltpu.VMEM((n_col * rows, width), jnp.bfloat16),
        ],
        compiler_params=pltpu.CompilerParams(
            collective_id=0, has_side_effects=True, vmem_limit_bytes=VMEM_BYTES
        ),
        name="param_gather",
    )(shard)


def token_gather_kernel(dims, src_ref, out_ref, *sems):
    n_dp, n_row, n_col = dims
    place = axis_place()
    d = place[0]
    greet(True, dims, place)

    def slot(col, j, b):
        k = j[1] if isinstance(j, tuple) else (d + n_dp - j) % n_dp
        return out_ref.at[col, k, b]

    finish(
        spread_blocks(
            dims,
            place,
            n_dp,
            True,
            lambda j: src_ref.at[d],
            lambda k: src_ref.at[k],
            slot,
            sems,
        )
    )


def token_gather(rows, dims):
    n_dp, n_row, n_col = dims
    _, slots, width = rows.shape
    return pl.pallas_call(
        functools.partial(token_gather_kernel, dims),
        out_shape=jax.ShapeDtypeStruct((n_col, n_dp, n_row, slots, width), rows.dtype),
        in_specs=[pl.BlockSpec(memory_space=pl.ANY)],
        out_specs=pl.BlockSpec(memory_space=pl.ANY),
        scratch_shapes=spread_sems(dims, n_dp),
        compiler_params=pltpu.CompilerParams(
            collective_id=1, has_side_effects=True, vmem_limit_bytes=VMEM_BYTES
        ),
        name="token_gather",
    )(rows)


def plane_gather_kernel(dims, src_ref, out_ref, *sems):
    place = axis_place()
    greet(False, dims, place)
    finish(
        spread_blocks(
            dims,
            place,
            src_ref.shape[0],
            False,
            lambda j: src_ref.at[j],
            None,
            lambda col, j, b: out_ref.at[col, b, j],
            sems,
        )
    )


def plane_gather(parts, dims):
    n_dp, n_row, n_col = dims
    chunks, rows, width = parts.shape
    return pl.pallas_call(
        functools.partial(plane_gather_kernel, dims),
        out_shape=jax.ShapeDtypeStruct((n_col, n_row, chunks, rows, width), parts.dtype),
        in_specs=[pl.BlockSpec(memory_space=pl.ANY)],
        out_specs=pl.BlockSpec(memory_space=pl.ANY),
        scratch_shapes=spread_sems(dims, chunks),
        compiler_params=pltpu.CompilerParams(
            collective_id=2, has_side_effects=True, vmem_limit_bytes=VMEM_BYTES
        ),
        name="plane_gather",
    )(parts)


def add_low(left, right):
    return (left.astype(jnp.float32) + right.astype(jnp.float32)).astype(jnp.bfloat16)


def plan_reduce(dims, place, part_ref, bufs, sems, deliver, direct=False):
    n_dp, n_row, n_col = dims
    d, r, c = place
    bits = bits_of(n_row)
    mine_ref, col_ref, row_ref = bufs
    mine_sem, col_send, col_recv, row_send, row_recv = sems
    steps = list(range(1, n_dp)) + [0]
    sent = []
    held = []

    def send_cols(i):
        other = (c + i) % n_col
        for t, j in enumerate(steps):
            copy = remote(
                part_ref.at[other, (d + j) % n_dp],
                col_ref.at[t, i - 1],
                col_send.at[t, i],
                col_recv.at[t, i],
                (d, r, other),
            )
            copy.start()
            sent.append(copy)

    def load_mine():
        for t, j in enumerate(steps):
            keep = pltpu.make_async_copy(
                part_ref.at[c, (d + j) % n_dp], mine_ref.at[t], mine_sem.at[t]
            )
            keep.start()
            held.append(keep)

    def order(t):
        return [1 << ((t + s) % bits) for s in range(bits)]

    def send_half(t, s):
        dim_order = order(t)
        bit = dim_order[s]
        before = sum(dim_order[:s])
        for x in range(n_row):
            if not x & before and x & bit:
                copy = remote(
                    mine_ref.at[t, flip_all(r, x, bits)],
                    row_ref.at[t, x ^ bit, s],
                    row_send.at[t, x ^ bit, s],
                    row_recv.at[t, x ^ bit, s],
                    (d, flip(r, bit), c),
                )
                copy.start()
                sent.append(copy)

    def sum_cols(t):
        if not direct:
            held[t].wait()
        for i in range(1, n_col):
            ref = col_ref.at[t, i - 1]
            remote(ref, ref, col_send.at[t, i], col_recv.at[t, i], (d, r, c)).wait_recv()
        k = (d + steps[t]) % n_dp

        @pl.loop(0, n_row)
        def _(b):
            total = part_ref[c, k, b] if direct else mine_ref[t, b]
            total = total.astype(jnp.float32)
            for i in range(1, n_col):
                total = total + col_ref[t, i - 1, b].astype(jnp.float32)
            mine_ref[t, b] = total.astype(jnp.bfloat16)

        send_half(t, 0)

    def sum_rows(t, s):
        dim_order = order(t)
        before = sum(dim_order[: s + 1])
        for y in range(n_row):
            if not y & before:
                ref = row_ref.at[t, y, s]
                remote(
                    ref, ref, row_send.at[t, y, s], row_recv.at[t, y, s], (d, r, c)
                ).wait_recv()
                b = flip_all(r, y, bits)
                mine_ref[t, b] = add_low(mine_ref[t, b], row_ref[t, y, s])
        if s + 1 < bits:
            send_half(t, s + 1)
        else:
            deliver(t, steps[t], mine_ref.at[t, r])

    return types.SimpleNamespace(
        send_cols=send_cols, load_mine=load_mine, sum_cols=sum_cols, sum_rows=sum_rows, sent=sent
    )


def reduce_blocks(dims, place, part_ref, bufs, sems, deliver):
    plan = plan_reduce(dims, place, part_ref, bufs, sems, deliver)
    for i in range(1, dims[2]):
        plan.send_cols(i)
    plan.load_mine()
    for t in range(dims[0]):
        plan.sum_cols(t)
    for s in range(bits_of(dims[1])):
        for t in range(dims[0]):
            plan.sum_rows(t, s)
    return plan.sent


def reduce_scratch(dims, rows, width):
    n_dp, n_row, n_col = dims
    bits = bits_of(n_row)
    dma = pltpu.SemaphoreType.DMA
    low = jnp.bfloat16
    return [
        pltpu.VMEM((n_dp, n_row, rows, width), low),
        pltpu.VMEM((n_dp, max(1, n_col - 1), n_row, rows, width), low),
        pltpu.VMEM((n_dp, n_row // 2, bits, rows, width), low)
        if n_row == 2
        else pltpu.VMEM((n_dp, n_row, bits, rows, width), low),
        dma((n_dp,)),
        dma((n_dp, n_col)),
        dma((n_dp, n_col)),
        dma((n_dp, n_row, bits)),
        dma((n_dp, n_row, bits)),
    ]


def token_reduce_kernel(dims, part_ref, out_ref, *scratch):
    n_dp, n_row, n_col = dims
    place = axis_place()
    d, r, c = place
    dp_send, dp_recv, own_sem = scratch[8:]
    greet(True, dims, place)
    late = []

    def deliver(t, j, block):
        if j == 0:
            keep = pltpu.make_async_copy(block, out_ref.at[d], own_sem)
            keep.start()
            late.append(keep.wait)
        else:
            copy = remote(
                block, out_ref.at[d], dp_send.at[j], dp_recv.at[j], ((d + j) % n_dp, r, c)
            )
            copy.start()
            late.append(copy.wait_send)

    sent = reduce_blocks(dims, place, part_ref, scratch[:3], scratch[3:8], deliver)
    for j in range(1, n_dp):
        ref = out_ref.at[(d + n_dp - j) % n_dp]
        remote(ref, ref, dp_send.at[j], dp_recv.at[j], (d, r, c)).wait_recv()
    for copy in sent:
        copy.wait_send()
    for wait in late:
        wait()


def token_reduce(parts, dims):
    n_dp = dims[0]
    slots, width = parts.shape[3:]
    dma = pltpu.SemaphoreType.DMA
    return pl.pallas_call(
        functools.partial(token_reduce_kernel, dims),
        out_shape=jax.ShapeDtypeStruct((n_dp, slots, width), jnp.bfloat16),
        in_specs=[pl.BlockSpec(memory_space=pl.ANY)],
        out_specs=pl.BlockSpec(memory_space=pl.ANY),
        scratch_shapes=[*reduce_scratch(dims, slots, width), dma((n_dp,)), dma((n_dp,)), dma],
        compiler_params=pltpu.CompilerParams(
            collective_id=3, has_side_effects=True, vmem_limit_bytes=VMEM_BYTES
        ),
        name="token_reduce",
    )(parts)


def param_reduce_kernel(dims, part_ref, out_ref, *scratch):
    n_dp, n_row, n_col = dims
    place = axis_place()
    d, r, c = place
    dp_send, dp_recv, dp_ref, swap_send, swap_recv, swap_ref, sum_ref = scratch[8:]
    rows = out_ref.shape[1]
    greet(True, dims, place)
    late = []
    kept = []

    def deliver(t, j, block):
        if j == 0:
            kept.append(block)
        else:
            copy = remote(
                block, dp_ref.at[j], dp_send.at[j], dp_recv.at[j], ((d + j) % n_dp, r, c)
            )
            copy.start()
            late.append(copy)

    sent = reduce_blocks(dims, place, part_ref, scratch[:3], scratch[3:8], deliver)
    total = kept[0][...].astype(jnp.float32)
    for j in range(1, n_dp):
        ref = dp_ref.at[j]
        remote(ref, ref, dp_send.at[j], dp_recv.at[j], (d, r, c)).wait_recv()
        total = total + dp_ref[j].astype(jnp.float32)
    sum_ref[...] = total
    for i in range(n_col):
        swap_ref[i] = sum_ref[i * rows : (i + 1) * rows, :]
    for i in range(1, n_col):
        other = (c + i) % n_col
        copy = remote(
            swap_ref.at[other], out_ref.at[c], swap_send.at[i], swap_recv.at[i], (d, r, other)
        )
        copy.start()
        late.append(copy)
    out_ref[pl.ds(c, 1)] = swap_ref[pl.ds(c, 1)]
    for i in range(1, n_col):
        ref = out_ref.at[(c + n_col - i) % n_col]
        remote(ref, ref, swap_send.at[i], swap_recv.at[i], (d, r, c)).wait_recv()
    for copy in sent:
        copy.wait_send()
    for copy in late:
        copy.wait_send()


def param_reduce(parts, dims):
    n_dp, n_row, n_col = dims
    block_rows, width = parts.shape[3:]
    rows = block_rows // n_col
    dma = pltpu.SemaphoreType.DMA
    return pl.pallas_call(
        functools.partial(param_reduce_kernel, dims),
        out_shape=jax.ShapeDtypeStruct((n_col, rows, width), jnp.float32),
        in_specs=[pl.BlockSpec(memory_space=pl.ANY)],
        out_specs=pl.BlockSpec(memory_space=pltpu.VMEM),
        scratch_shapes=[
            *reduce_scratch(dims, block_rows, width),
            dma((n_dp,)),
            dma((n_dp,)),
            pltpu.VMEM((n_dp, block_rows, width), jnp.bfloat16),
            dma((n_col,)),
            dma((n_col,)),
            pltpu.VMEM((n_col, rows, width), jnp.float32),
            pltpu.VMEM((block_rows, width), jnp.float32),
        ],
        compiler_params=pltpu.CompilerParams(
            collective_id=4, has_side_effects=True, vmem_limit_bytes=VMEM_BYTES
        ),
        name="param_reduce",
    )(parts)


def column(matrix, index):
    return matrix[:, index : index + 1]


def token_masks(lengths_ref, rows, seqs):
    down = lax.broadcasted_iota(jnp.int32, (rows, 1), 0)
    across = lax.broadcasted_iota(jnp.int32, (1, rows), 1)
    end = 0
    doc_down = jnp.zeros((rows, 1), jnp.int32)
    doc_across = jnp.zeros((1, rows), jnp.int32)
    for i in range(seqs):
        end = end + lengths_ref[0, i]
        doc_down = doc_down + (down >= end).astype(jnp.int32)
        doc_across = doc_across + (across >= end).astype(jnp.int32)
    valid = (doc_down < seqs).astype(jnp.float32)
    allowed = (doc_down == doc_across) & (down >= across)
    return valid, allowed


def row_vectors_of(small, first):
    shape = (8, small.shape[1])
    pick = lax.broadcasted_iota(jnp.int32, shape, 1) == first + lax.broadcasted_iota(
        jnp.int32, shape, 0
    )
    return dot(pick.astype(jnp.bfloat16), small, NT)


def half_mask(rows, half):
    return lax.broadcasted_iota(jnp.int32, (rows, LANES), 1) // HEAD == half


def attention_forward(qkv_ref, probs_ref, mixed_ref, allowed):
    rows = qkv_ref.shape[0]
    low = jnp.bfloat16

    @pl.loop(0, HEADS * HEAD // LANES, unroll=2)
    def _(pair):
        def cols(base):
            return pl.ds(pl.multiple_of(base + pair * LANES, LANES), LANES)

        queries = qkv_ref[:, cols(0)]
        key_heads = qkv_ref[:, cols(D)]
        values = qkv_ref[:, cols(2 * D)]
        mixed = jnp.zeros((rows, LANES), jnp.float32)
        for half in range(LANES // HEAD):
            mask = half_mask(rows, half)
            scores = dot(jnp.where(mask, queries, 0), key_heads, NT) * HEAD ** (-0.5)
            scores = jnp.where(allowed, scores, -1e30)
            top_score = jnp.max(scores, axis=-1, keepdims=True)
            exp_scores = jnp.exp(scores - top_score)
            probs = exp_scores / jnp.sum(exp_scores, axis=-1, keepdims=True)
            probs_ref[pair * (LANES // HEAD) + half] = probs
            mixed = mixed + dot(probs.astype(low), jnp.where(mask, values, 0))
        mixed_ref[:, cols(0)] = mixed.astype(low)


def two_way(first, second):
    top = jnp.maximum(first, second)
    exp_first = jnp.exp(first - top)
    exp_second = jnp.exp(second - top)
    total = exp_first + exp_second
    return exp_first / total, exp_second / total


def front_kernel(sizes, *refs):
    dims, num_ffn, wide_qkv, wide_out, route_cols = sizes
    n_dp, n_row, n_col = dims
    low = jnp.bfloat16
    (
        lengths_ref,
        routes_ref,
        prev_ref,
        tokens_ref,
        cotangent_ref,
        shard_ref,
        weight_gu,
        weight_down,
        whole_out,
        parts_ref,
        grads_ref,
        qkv_ref,
        probs_ref,
        mixed_ref,
        first_ref,
        small_ref,
        swap_ref,
        block_ref,
        whole_ref,
        load_ref,
        pack_ref,
        expert_ref,
        stage_ref,
        arrived_ref,
        logits_ref,
        hidden_ref,
        pre_ref,
        swap_send,
        swap_recv,
        load_sem,
        expert_send,
        expert_recv,
        whole_sem,
        *sems,
    ) = refs
    param_sems, token_sems = sems[:7], sems[7:]
    place = axis_place()
    d, r, c = place
    rows = shard_ref.shape[1]
    depth, slice_wide = pack_ref.shape[2:]
    loads = []
    for m, src in enumerate([weight_gu.at[:, 0], weight_gu.at[:, 1], weight_down]):
        copy = pltpu.make_async_copy(src, load_ref.at[m], load_sem.at[m])
        copy.start()
        loads.append(copy)
    greet(True, dims, place, all_rows=True)

    copies = []
    for i in range(1, n_col):
        other = (c + i) % n_col
        copy = remote(
            shard_ref.at[other], swap_ref.at[c], swap_send.at[i], swap_recv.at[i], (d, r, other)
        )
        copy.start()
        copies.append(copy)
    swap_ref[pl.ds(c, 1)] = shard_ref[pl.ds(c, 1)]
    for copy in copies:
        copy.wait()
    for i in range(n_col):
        block_ref[i * rows : (i + 1) * rows, :] = swap_ref[i]
    whole_ref[c, d, r] = block_ref[...].astype(low)

    def param_slot(col, j, b):
        k = j[1] if isinstance(j, tuple) else (d + n_dp - j) % n_dp
        return whole_ref.at[col, k, b]

    waits = []

    def send_experts():
        for m in range(3):
            loads[m].wait()
            for b in range(n_row):
                pack_ref[b, m] = load_ref[m, :, b * slice_wide : (b + 1) * slice_wide].astype(low)
        home = pl.ds(pl.multiple_of(r * depth, 16), depth)
        for i in range(1, n_row):
            other = (r + i) % n_row
            copy = remote(
                pack_ref.at[other],
                expert_ref.at[:, home],
                expert_send.at[i],
                expert_recv.at[i],
                (d, other, c),
            )
            copy.start()
            waits.append(copy.wait_send)
        expert_ref[:, home] = pack_ref[r]

    waits += spread_blocks(
        dims,
        place,
        n_dp,
        True,
        None,
        lambda k: whole_ref.at[c, d, r],
        param_slot,
        param_sems,
        send_experts,
    )
    keep_whole = pltpu.make_async_copy(whole_ref, whole_out, whole_sem)
    keep_whole.start()

    def whole_cols(col, begin, wide):
        return whole_ref[col, :, :, :, begin : begin + wide].reshape(D, wide)

    total = tokens_ref.shape[0]
    valid, allowed = token_masks(lengths_ref, total, lengths_ref.shape[1])
    small = whole_cols(0, wide_qkv + wide_out, LANES)
    vectors = row_vectors_of(small, route_cols)
    inputs = tokens_ref[...].astype(jnp.float32)
    scale_one = lax.rsqrt(jnp.mean(inputs * inputs, axis=-1, keepdims=True) + NORM_EPS)
    h_one = (inputs * scale_one * vectors[0:1]).astype(low)
    for i in range(n_col):
        qkv_ref[:, i * wide_qkv : (i + 1) * wide_qkv] = dot(h_one, whole_cols(i, 0, wide_qkv)).astype(
            low
        )
    attention_forward(qkv_ref, probs_ref, mixed_ref, allowed)
    for i in range(n_col):
        cols = slice(i * wide_out, (i + 1) * wide_out)
        attn_out = dot(mixed_ref[...], whole_cols(i, wide_qkv, wide_out))
        first_ref[:, cols] = tokens_ref[:, cols].astype(jnp.float32) + valid * attn_out
    first_sum = first_ref[...]
    scale_two = lax.rsqrt(jnp.mean(first_sum * first_sum, axis=-1, keepdims=True) + NORM_EPS)
    h_two = (first_sum * scale_two * vectors[1:2]).astype(low)
    logits_ref[...] = jnp.zeros_like(logits_ref)
    logits_ref[:, : prev_ref.shape[1]] = prev_ref[...]
    logits_all = dot(h_two, small)
    logits = logits_all + logits_ref[...]
    lane = lax.broadcasted_iota(jnp.int32, (total, LANES), 1)
    route_first = routes_ref[:, 0:1]
    route_second = routes_ref[:, 1:2]
    pick_first = (lane == route_first).astype(jnp.float32)
    pick_second = (lane == route_second).astype(jnp.float32)
    gates = two_way(
        jnp.sum(pick_first * logits, axis=-1, keepdims=True),
        jnp.sum(pick_second * logits, axis=-1, keepdims=True),
    )
    mix_base = num_ffn + 4
    mixes = []
    for i in range(2):
        mixes += two_way(
            column(logits_all, mix_base + 2 * i), column(logits_all, mix_base + 2 * i + 1)
        )
    before = lax.broadcasted_iota(jnp.int32, (total, total), 0) > lax.broadcasted_iota(
        jnp.int32, (total, total), 1
    )
    earlier = dot(before.astype(low), (pick_first + pick_second).astype(low))
    in_slots = []
    for route, pick in ((route_first, pick_first), (route_second, pick_second)):
        slot_index = jnp.sum(earlier * pick, axis=-1, keepdims=True)
        where_in = (route * CAP).astype(jnp.float32) + slot_index
        in_slots.append(jnp.where(route < num_ffn, where_in, -1.0))
    kept = [*gates, *mixes, *in_slots]
    state = jnp.zeros((total, LANES), jnp.float32)
    for i, value in enumerate(kept):
        state = jnp.where(lane == i, value, state)
    small_ref[...] = state
    slots = num_ffn * CAP
    slot_lane = lax.broadcasted_iota(jnp.int32, (total, slots), 1).astype(jnp.float32)
    places = [(slot_lane == where_in).astype(low) for where_in in in_slots]
    grad_y = cotangent_ref[...].astype(jnp.float32) * valid
    sent = dot(places[0] + places[1], h_two, TN).astype(low)
    made = dot(places[0], (gates[0] * grad_y).astype(low), TN) + dot(
        places[1], (gates[1] * grad_y).astype(low), TN
    )
    stage_ref[:, :, :D] = sent.reshape(num_ffn, CAP, D)
    stage_ref[:, :, D:] = made.astype(low).reshape(num_ffn, CAP, D)

    def token_slot(col, j, b):
        k = j[1] if isinstance(j, tuple) else (d + n_dp - j) % n_dp
        return arrived_ref.at[(col * n_dp + k) * n_row + b]

    arrived_ref[(c * n_dp + d) * n_row + r] = stage_ref[d]
    waits += spread_blocks(
        dims, place, n_dp, True, None, lambda k: stage_ref.at[k], token_slot, token_sems
    )
    for i in range(1, n_row):
        home = pl.ds(pl.multiple_of(((r + n_row - i) % n_row) * depth, 16), depth)
        ref = expert_ref.at[:, home]
        remote(ref, ref, expert_send.at[i], expert_recv.at[i], (d, r, c)).wait_recv()

    blocks = arrived_ref.shape[0]
    group = 8
    tall = group * CAP

    @pl.loop(0, blocks // group)
    def _(t):
        some = arrived_ref[pl.ds(t * group, group)].reshape(tall, 2 * D)
        rows_in = some[:, :D]
        grads_in = some[:, D:]
        span = pl.ds(pl.multiple_of(t * tall, tall), tall)
        gate_part = dot(rows_in, expert_ref[0])
        up_part = dot(rows_in, expert_ref[1])
        grad_hidden = dot(grads_in, expert_ref[2])
        sigma = jax.nn.sigmoid(gate_part)
        silu = gate_part * sigma
        hidden = (silu * up_part).astype(low)
        grad_gate = (
            grad_hidden * up_part * sigma * (1.0 + gate_part * (1.0 - sigma))
        ).astype(low)
        grad_up = (grad_hidden * silu).astype(low)
        hidden_ref[span] = hidden
        pre_ref[span, :slice_wide] = grad_gate
        pre_ref[span, slice_wide:] = grad_up
        made_rows = dot(hidden, expert_ref[2], NT).astype(low)
        grad_rows = dot(grad_gate, expert_ref[0], NT) + dot(grad_up, expert_ref[1], NT)
        out_span = pl.ds(t * group, group)
        parts_ref[out_span, :, :D] = made_rows.reshape(group, CAP, D)
        parts_ref[out_span, :, D:] = grad_rows.astype(low).reshape(group, CAP, D)

    all_rows = arrived_ref[:, :, :D].reshape(blocks * CAP, D)
    all_grads = arrived_ref[:, :, D:].reshape(blocks * CAP, D)
    for m in range(2):
        grads_ref[m * D : (m + 1) * D] = dot(
            all_rows, pre_ref[:, m * slice_wide : (m + 1) * slice_wide], TN
        ).astype(low)
    grads_ref[2 * D :] = dot(all_grads, hidden_ref[...], TN).astype(low)
    keep_whole.wait()
    finish(waits)


def front(lengths, routes, prev_logits, tokens, cotangent, shard, weight_gu, weight_down, dims, widths):
    n_dp, n_row, n_col = dims
    low = jnp.bfloat16
    f32 = jnp.float32
    total = tokens.shape[0]
    _, rows, wide = shard.shape
    num_ffn = prev_logits.shape[1] - 4
    depth, wide_col = weight_down.shape
    slice_wide = wide_col // n_row
    blocks = n_col * n_dp * n_row
    dma = pltpu.SemaphoreType.DMA
    vmem = pl.BlockSpec(memory_space=pltpu.VMEM)
    hbm = pl.BlockSpec(memory_space=pl.ANY)
    whole = (n_col, n_dp, n_row, n_col * rows, wide)
    return pl.pallas_call(
        functools.partial(front_kernel, (dims, num_ffn, *widths)),
        out_shape=[
            jax.ShapeDtypeStruct(whole, low),
            jax.ShapeDtypeStruct((blocks, CAP, 2 * D), low),
            jax.ShapeDtypeStruct((3 * D, slice_wide), low),
            jax.ShapeDtypeStruct((total, 3 * D), low),
            jax.ShapeDtypeStruct((HEADS, total, total), f32),
            jax.ShapeDtypeStruct((total, D), low),
            jax.ShapeDtypeStruct((total, D), f32),
            jax.ShapeDtypeStruct((total, LANES), f32),
        ],
        in_specs=[pl.BlockSpec(memory_space=pltpu.SMEM)] + [vmem] * 5 + [hbm] * 2,
        out_specs=[hbm] + [vmem] * 7,
        scratch_shapes=[
            pltpu.VMEM((n_col, rows, wide), f32),
            pltpu.VMEM((n_col * rows, wide), f32),
            pltpu.VMEM(whole, low),
            pltpu.VMEM((3, depth, wide_col), f32),
            pltpu.VMEM((n_row, 3, depth, slice_wide), low),
            pltpu.VMEM((3, n_row * depth, slice_wide), low),
            pltpu.VMEM((num_ffn, CAP, 2 * D), low),
            pltpu.VMEM((blocks, CAP, 2 * D), low),
            pltpu.VMEM((total, LANES), f32),
            pltpu.VMEM((blocks * CAP, slice_wide), low),
            pltpu.VMEM((blocks * CAP, 2 * slice_wide), low),
            dma((n_col,)),
            dma((n_col,)),
            dma((3,)),
            dma((n_row,)),
            dma((n_row,)),
            dma,
            *spread_sems(dims, n_dp),
            *spread_sems(dims, n_dp),
        ],
        compiler_params=pltpu.CompilerParams(
            collective_id=5, has_side_effects=True, vmem_limit_bytes=VMEM_BYTES
        ),
        name="front",
    )(lengths, routes, prev_logits, tokens, cotangent, shard, weight_gu, weight_down)


def attention_backward(qkv_ref, probs_ref, grad_mixed_ref, grad_qkv_ref):
    rows = qkv_ref.shape[0]
    low = jnp.bfloat16

    @pl.loop(0, HEADS * HEAD // LANES, unroll=2)
    def _(pair):
        def cols(base):
            return pl.ds(pl.multiple_of(base + pair * LANES, LANES), LANES)

        queries = qkv_ref[:, cols(0)]
        key_heads = qkv_ref[:, cols(D)]
        values = qkv_ref[:, cols(2 * D)]
        grad_mixed = grad_mixed_ref[:, cols(0)]
        grad_queries = jnp.zeros((rows, LANES), jnp.float32)
        grad_keys = jnp.zeros((rows, LANES), jnp.float32)
        grad_values = jnp.zeros((rows, LANES), jnp.float32)
        for half in range(LANES // HEAD):
            mask = half_mask(rows, half)
            probs = probs_ref[pair * (LANES // HEAD) + half]
            grad_part = jnp.where(mask, grad_mixed, 0)
            grad_values = grad_values + dot(probs.astype(low), grad_part, TN)
            grad_probs = dot(grad_part, values, NT)
            grad_scores = probs * (
                grad_probs - jnp.sum(probs * grad_probs, axis=-1, keepdims=True)
            )
            grad_scores = grad_scores.astype(low)
            grad_queries = grad_queries + dot(grad_scores, jnp.where(mask, key_heads, 0))
            grad_keys = grad_keys + dot(grad_scores, jnp.where(mask, queries, 0), TN)
        grad_qkv_ref[:, cols(0)] = (grad_queries * HEAD ** (-0.5)).astype(low)
        grad_qkv_ref[:, cols(D)] = (grad_keys * HEAD ** (-0.5)).astype(low)
        grad_qkv_ref[:, cols(2 * D)] = grad_values.astype(low)


def back_kernel(sizes, *refs):
    dims, num_ffn, wide_qkv, wide_out, route_cols, chunks = sizes
    n_dp, n_row, n_col = dims
    low = jnp.bfloat16
    (
        lengths_ref,
        routes_ref,
        state_ref,
        tokens_ref,
        cotangent_ref,
        parts_hbm,
        grads_hbm,
        whole_hbm,
        qkv_hbm,
        probs_hbm,
        mixed_hbm,
        first_hbm,
        result_ref,
        grad_tokens_ref,
        gathered_ref,
        summed_ref,
        whole_ref,
        qkv_ref,
        probs_ref,
        mixed_ref,
        first_ref,
        came_ref,
        grad_attn_ref,
        grad_mixed_ref,
        grad_qkv_ref,
        part_ref,
        dp_ref,
        swap_ref,
        sum_ref,
        load_sem,
        came_send,
        came_recv,
        dp_send,
        dp_recv,
        swap_send,
        swap_recv,
        *more,
    ) = refs
    token_scratch, param_scratch, gather_sems = more[:8], more[8:16], more[16:]
    place = axis_place()
    d, r, c = place
    rows = summed_ref.shape[1]
    loads = []
    for n, (src, dst) in enumerate(
        (
            (first_hbm, first_ref),
            (whole_hbm, whole_ref),
            (qkv_hbm, qkv_ref),
            (probs_hbm, probs_ref),
            (mixed_hbm, mixed_ref),
        )
    ):
        copy = pltpu.make_async_copy(src, dst, load_sem.at[n])
        copy.start()
        loads.append(copy)
    greet(True, dims, place)
    waits = []

    def token_back(t, j, block):
        if j == 0:
            came_ref[d] = block[...]
        else:
            copy = remote(
                block, came_ref.at[d], came_send.at[j], came_recv.at[j], ((d + j) % n_dp, r, c)
            )
            copy.start()
            waits.append(copy.wait_send)

    tokens_plan = plan_reduce(
        dims, place, parts_hbm, token_scratch[:3], token_scratch[3:], token_back
    )
    for i in range(1, n_col):
        tokens_plan.send_cols(i)
    tokens_plan.load_mine()
    for t in range(n_dp):
        tokens_plan.sum_cols(t)
    for s in range(bits_of(n_row)):
        for t in range(n_dp):
            tokens_plan.sum_rows(t, s)

    tall = grads_hbm.shape[0] // chunks
    gather = plan_spread(
        dims,
        place,
        chunks,
        False,
        lambda j: grads_hbm.at[pl.ds(j * tall, tall)],
        None,
        lambda col, j, b: gathered_ref.at[col, b, pl.ds(j * tall, tall)],
        gather_sems,
    )
    for j in range(chunks):
        gather.start(j)

    total = tokens_ref.shape[0]
    valid, _ = token_masks(lengths_ref, total, lengths_ref.shape[1])
    for copy in loads:
        copy.wait()
    small = whole_ref[0, :, wide_qkv + wide_out :]
    vectors = row_vectors_of(small, route_cols)
    gain_one, gain_two = vectors[0:1], vectors[1:2]
    const_rows = [vectors[2:3], vectors[3:4]]
    state = state_ref[...]
    gates = [column(state, 0), column(state, 1)]
    mixes = [[column(state, 2), column(state, 3)], [column(state, 4), column(state, 5)]]
    routes = [routes_ref[:, 0:1], routes_ref[:, 1:2]]
    lane = lax.broadcasted_iota(jnp.int32, (total, LANES), 1)
    picks = [(lane == route).astype(jnp.float32) for route in routes]
    slots = num_ffn * CAP
    slot_lane = lax.broadcasted_iota(jnp.int32, (total, slots), 1).astype(jnp.float32)
    places = [(slot_lane == column(state, 6 + n)).astype(low) for n in range(2)]
    cotangent = cotangent_ref[...].astype(jnp.float32)
    grad_y = cotangent * valid
    grad_y_low = grad_y.astype(low)
    first_sum = first_ref[...]
    scale_two = lax.rsqrt(jnp.mean(first_sum * first_sum, axis=-1, keepdims=True) + NORM_EPS)
    normed_two = first_sum * scale_two
    h_two = normed_two * gain_two
    h_two_low = h_two.astype(low)
    const_sel = [
        [(route == num_ffn + 2 + n).astype(jnp.float32) for n in range(2)] for route in routes
    ]
    for j in range(1, n_dp):
        ref = came_ref.at[(d + n_dp - j) % n_dp]
        remote(ref, ref, came_send.at[j], came_recv.at[j], (d, r, c)).wait_recv()
    expert_out = came_ref[:, :, :D].reshape(slots, D)
    grad_sent = came_ref[:, :, D:].reshape(slots, D)
    moe_out = jnp.zeros_like(first_sum)
    grad_gates = []
    own_weight = jnp.zeros((total, 1), jnp.float32)
    for n in range(2):
        own = (routes[n] == num_ffn + 1).astype(jnp.float32)
        for i in range(2):
            own = own + const_sel[n][i] * mixes[i][0]
        output = dot(places[n], expert_out) + own * h_two
        for i in range(2):
            output = output + const_sel[n][i] * mixes[i][1] * const_rows[i]
        moe_out = moe_out + gates[n] * output
        grad_gates.append(jnp.sum(grad_y * output, axis=-1, keepdims=True))
        own_weight = own_weight + gates[n] * own
    result_ref[...] = (first_sum + valid * moe_out).astype(low)
    mean_gate = gates[0] * grad_gates[0] + gates[1] * grad_gates[1]
    grad_logits = sum(gates[n] * (grad_gates[n] - mean_gate) * picks[n] for n in range(2))
    grad_own = jnp.sum(grad_y * h_two, axis=-1, keepdims=True)
    const_lanes = jnp.zeros((total, LANES), jnp.float32)
    for i in range(2):
        weight = const_sel[0][i] * gates[0] + const_sel[1][i] * gates[1]
        mix_grads = [
            weight * grad_own,
            weight * jnp.sum(grad_y * const_rows[i], axis=-1, keepdims=True),
        ]
        mean_mix = mixes[i][0] * mix_grads[0] + mixes[i][1] * mix_grads[1]
        for n in range(2):
            grad_mix = mixes[i][n] * (mix_grads[n] - mean_mix)
            grad_logits = jnp.where(lane == num_ffn + 4 + 2 * i + n, grad_mix, grad_logits)
        const_lanes = jnp.where(lane == route_cols + 2 + i, weight * mixes[i][1], const_lanes)
    grad_logits = grad_logits.astype(low)

    grad_h_two = (
        dot(grad_logits, small, NT) + dot(places[0] + places[1], grad_sent) + own_weight * grad_y
    )
    grad_normed = grad_h_two * gain_two
    inner_mean = jnp.mean(grad_normed * normed_two, axis=-1, keepdims=True)
    grad_first = scale_two * (grad_normed - normed_two * inner_mean) + cotangent
    grad_tokens_ref[...] = grad_first
    grad_attn_ref[...] = (valid * grad_first).astype(low)
    grad_small = (
        dot(h_two_low, grad_logits, TN)
        + dot(grad_y_low, const_lanes.astype(low), TN)
        + dot((grad_h_two * normed_two).astype(low), (lane == route_cols + 1).astype(low), TN)
    )
    grad_mixed = jnp.zeros((total, D), jnp.float32)
    for i in range(n_col):
        grad_mixed = grad_mixed + dot(
            grad_attn_ref[:, i * wide_out : (i + 1) * wide_out],
            whole_ref[i, :, wide_qkv : wide_qkv + wide_out],
            NT,
        )
    grad_mixed_ref[...] = grad_mixed.astype(low)
    for j in range(chunks // 2):
        gather.pass_on(j)
    attention_backward(qkv_ref, probs_ref, grad_mixed_ref, grad_qkv_ref)
    for j in range(chunks // 2, chunks):
        gather.pass_on(j)
    grad_h_one = jnp.zeros((total, D), jnp.float32)
    for i in range(n_col):
        grad_h_one = grad_h_one + dot(
            grad_qkv_ref[:, i * wide_qkv : (i + 1) * wide_qkv], whole_ref[i, :, :wide_qkv], NT
        )
    inputs = tokens_ref[...].astype(jnp.float32)
    scale_one = lax.rsqrt(jnp.mean(inputs * inputs, axis=-1, keepdims=True) + NORM_EPS)
    normed_one = inputs * scale_one
    h_one = (normed_one * gain_one).astype(low)
    grad_normed = grad_h_one * gain_one
    inner_mean = jnp.mean(grad_normed * normed_one, axis=-1, keepdims=True)
    grad_tokens_ref[...] += scale_one * (grad_normed - normed_one * inner_mean)
    grad_small = grad_small + dot(
        (grad_h_one * normed_one).astype(low), (lane == route_cols).astype(low), TN
    )

    kept = []

    def param_back(t, j, block):
        if j == 0:
            kept.append(block)
        else:
            copy = remote(
                block, dp_ref.at[j], dp_send.at[j], dp_recv.at[j], ((d + j) % n_dp, r, c)
            )
            copy.start()
            waits.append(copy.wait_send)

    params_plan = plan_reduce(
        dims, place, part_ref, param_scratch[:3], param_scratch[3:], param_back, direct=True
    )
    blocked = part_ref.shape[1:4]
    for i in [*range(1, n_col), 0]:
        col = (c + i) % n_col
        qkv_cols = pl.ds(pl.multiple_of(col * wide_qkv, LANES), wide_qkv)
        out_cols = pl.ds(pl.multiple_of(col * wide_out, LANES), wide_out)
        part_ref[col, :, :, :, :wide_qkv] = (
            dot(h_one, grad_qkv_ref[:, qkv_cols], TN).astype(low).reshape(*blocked, wide_qkv)
        )
        part_ref[col, :, :, :, wide_qkv : wide_qkv + wide_out] = (
            dot(mixed_ref[...], grad_attn_ref[:, out_cols], TN)
            .astype(low)
            .reshape(*blocked, wide_out)
        )
        part_ref[col, :, :, :, wide_qkv + wide_out :] = grad_small.astype(low).reshape(
            *blocked, LANES
        )
        if i:
            params_plan.send_cols(i)
    for t in range(n_dp):
        params_plan.sum_cols(t)
    for j in range(chunks):
        gather.last_arrivals(j)
    for s in range(bits_of(n_row)):
        for t in range(n_dp):
            params_plan.sum_rows(t, s)
    waits += gather.wait_cols()
    sums = kept[0][...].astype(jnp.float32)
    for j in range(1, n_dp):
        ref = dp_ref.at[j]
        remote(ref, ref, dp_send.at[j], dp_recv.at[j], (d, r, c)).wait_recv()
        sums = sums + dp_ref[j].astype(jnp.float32)
    sum_ref[...] = sums
    for i in range(n_col):
        swap_ref[i] = sum_ref[i * rows : (i + 1) * rows, :]
    for i in range(1, n_col):
        other = (c + i) % n_col
        copy = remote(
            swap_ref.at[other], summed_ref.at[c], swap_send.at[i], swap_recv.at[i], (d, r, other)
        )
        copy.start()
        waits.append(copy.wait_send)
    summed_ref[pl.ds(c, 1)] = swap_ref[pl.ds(c, 1)]
    for i in range(1, n_col):
        ref = summed_ref.at[(c + n_col - i) % n_col]
        remote(ref, ref, swap_send.at[i], swap_recv.at[i], (d, r, c)).wait_recv()
    finish([copy.wait_send for copy in tokens_plan.sent + params_plan.sent])
    finish(waits)


def back(
    lengths,
    routes,
    state,
    tokens,
    cotangent,
    parts,
    grads,
    whole,
    qkv_rows,
    probs,
    mixed,
    first_sum,
    dims,
    num_ffn,
    widths,
):
    n_dp, n_row, n_col = dims
    low = jnp.bfloat16
    f32 = jnp.float32
    total = tokens.shape[0]
    wide = whole.shape[2]
    block_rows = D // n_dp // n_row
    rows = block_rows // n_col
    chunks = 4
    dma = pltpu.SemaphoreType.DMA
    vmem = pl.BlockSpec(memory_space=pltpu.VMEM)
    hbm = pl.BlockSpec(memory_space=pl.ANY)
    return pl.pallas_call(
        functools.partial(back_kernel, (dims, num_ffn, *widths, chunks)),
        out_shape=[
            jax.ShapeDtypeStruct((total, D), low),
            jax.ShapeDtypeStruct((total, D), f32),
            jax.ShapeDtypeStruct((n_col, n_row, *grads.shape), low),
            jax.ShapeDtypeStruct((n_col, rows, wide), f32),
        ],
        in_specs=[pl.BlockSpec(memory_space=pltpu.SMEM)] + [vmem] * 4 + [hbm] * 7,
        out_specs=[vmem, vmem, hbm, vmem],
        scratch_shapes=[
            pltpu.VMEM(whole.shape, low),
            pltpu.VMEM(qkv_rows.shape, low),
            pltpu.VMEM(probs.shape, f32),
            pltpu.VMEM(mixed.shape, low),
            pltpu.VMEM(first_sum.shape, f32),
            pltpu.VMEM((n_dp, CAP, 2 * D), low),
            pltpu.VMEM((total, D), low),
            pltpu.VMEM((total, D), low),
            pltpu.VMEM((total, 3 * D), low),
            pltpu.VMEM((n_col, n_dp, n_row, block_rows, wide), low),
            pltpu.VMEM((n_dp, block_rows, wide), low),
            pltpu.VMEM((n_col, rows, wide), f32),
            pltpu.VMEM((block_rows, wide), f32),
            dma((5,)),
            dma((n_dp,)),
            dma((n_dp,)),
            dma((n_dp,)),
            dma((n_dp,)),
            dma((n_col,)),
            dma((n_col,)),
            *reduce_scratch(dims, CAP, 2 * D),
            *reduce_scratch(dims, block_rows, wide),
            *spread_sems(dims, chunks),
        ],
        compiler_params=pltpu.CompilerParams(
            collective_id=6, has_side_effects=True, vmem_limit_bytes=VMEM_BYTES
        ),
        name="back",
    )(
        lengths,
        routes,
        state,
        tokens,
        cotangent,
        parts,
        grads,
        whole,
        qkv_rows,
        probs,
        mixed,
        first_sum,
    )


def norm_forward(values, gain_vec):
    norm_scale = lax.rsqrt(jnp.mean(values * values, axis=-1, keepdims=True) + NORM_EPS)
    normed = values * norm_scale
    return (normed * gain_vec, normed, norm_scale)


def norm_backward(grad_out, normed, norm_scale, gain_vec):
    grad_normed = grad_out * gain_vec
    inner_mean = jnp.mean(grad_normed * normed, axis=-1, keepdims=True)
    return (norm_scale * (grad_normed - normed * inner_mean), jnp.sum(grad_out * normed, axis=0))


def attention_probs(queries, key_heads, allowed):
    scores = jnp.einsum(
        "qhd,khd->hqk", queries, key_heads, preferred_element_type=jnp.float32
    ) * HEAD ** (-0.5)
    scores = jnp.where(allowed[None], scores, -1e30)
    top_score = jnp.max(scores, axis=-1, keepdims=True)
    exp_scores = jnp.exp(scores - top_score)
    return exp_scores / jnp.sum(exp_scores, axis=-1, keepdims=True)


def diag_update(weight, grad, state, rate):
    new_state = 0.5 * state + 0.5 * grad * grad
    return (new_state, weight - rate * grad / (jnp.sqrt(new_state) + 1e-08))


def shampoo_kernel(sizes, *refs):
    n_row, n_col, model, slice_wide, tile = sizes
    low = jnp.bfloat16
    (
        grads,
        left_root_gu,
        right_root_down,
        right_root_gu,
        left_root_down,
        left_gu,
        right_down,
        right_gu,
        left_down,
        weight_gu,
        weight_down,
        out_grad_gu,
        out_grad_down,
        out_left_gu,
        out_right_down,
        out_right_gu,
        out_left_down,
        out_weight_gu,
        out_weight_down,
        grad_buf,
        root_buf,
        wide_buf,
        left_buf,
        right_buf,
        weight_buf,
        step_buf,
        lhs_buf,
        in_sem,
        wide_sem,
        out_sem,
    ) = refs
    r = lax.axis_index("row")
    c = lax.axis_index("col")
    owner = r * n_col + c
    blocks = n_row * n_col
    left_rows = left_buf.shape[1]
    right_rows = right_buf.shape[1]
    depth = root_buf.shape[1]
    wide_rows = wide_buf.shape[1]
    tiles = wide_rows // tile
    mats = range(3)
    roots = [left_root_gu.at[0], left_root_gu.at[1], right_root_down]
    wides = [right_root_gu.at[0], right_root_gu.at[1], left_root_down]
    lefts = [left_gu.at[0], left_gu.at[1], right_down]
    rights = [right_gu.at[0], right_gu.at[1], left_down]
    weights = [weight_gu.at[:, 0], weight_gu.at[:, 1], weight_down]
    out_lefts = [out_left_gu.at[0], out_left_gu.at[1], out_right_down]
    out_rights = [out_right_gu.at[0], out_right_gu.at[1], out_left_down]
    out_weights = [out_weight_gu.at[:, 0], out_weight_gu.at[:, 1], out_weight_down]
    out_grads = [out_grad_gu.at[:, 0], out_grad_gu.at[:, 1], out_grad_down]

    def load(m, kind, src, dst):
        copy = pltpu.make_async_copy(src, dst, in_sem.at[m, kind])
        copy.start()
        return copy

    loads = []
    for m in mats:
        span = pl.ds(m * model, model)
        loads.append(
            [
                load(m, 0, grads.at[:, span], grad_buf.at[:, span]),
                load(m, 1, roots[m], root_buf.at[m]),
                load(m, 2, rights[m], right_buf.at[m]),
                load(m, 3, lefts[m], left_buf.at[m]),
                load(m, 4, weights[m], weight_buf.at[m]),
            ]
        )
        for t in range(tiles):
            rows = pl.ds(t * tile, tile)
            copy = pltpu.make_async_copy(
                wides[m].at[rows], wide_buf.at[m, rows], wide_sem.at[m, t]
            )
            copy.start()
            loads[m].append(copy)
    stores = []

    def store(m, kind, src, dst):
        copy = pltpu.make_async_copy(src, dst, out_sem.at[m, kind])
        copy.start()
        stores.append(copy)

    for m in mats:
        span = pl.ds(m * model, model)
        loads[m][0].wait()
        loads[m][1].wait()
        lhs_buf[:right_rows] = grad_buf[owner, span].T
        lhs_buf[right_rows:] = root_buf[m].astype(low)
        loads[m][2].wait()
        loads[m][3].wait()
        left_buf[m] = 0.5 * left_buf[m]

        @pl.loop(0, blocks)
        def _(q):
            cols = pl.ds(pl.multiple_of(q * slice_wide, slice_wide), slice_wide)
            block = grad_buf[q, span]
            made = dot(lhs_buf[...], block)
            right_buf[m, :, cols] = 0.5 * right_buf[m, :, cols] + 0.5 * made[:right_rows]
            step_buf[:, cols] = made[right_rows:].astype(low)
            rows = pl.ds(pl.multiple_of(m * model + owner * left_rows, 16), left_rows)
            left_buf[m] += 0.5 * dot(grad_buf[q, rows], block, NT)

        store(m, 0, right_buf.at[m], out_rights[m])
        store(m, 1, left_buf.at[m], out_lefts[m])
        loads[m][4].wait()
        for t in range(tiles):
            loads[m][5 + t].wait()
            cols = pl.ds(t * tile, tile)
            step = dot(step_buf[...], wide_buf[m, cols].astype(low), NT)
            weight_buf[m, :, cols] = weight_buf[m, :, cols] - SHAMPOO_RATE * step
        store(m, 2, weight_buf.at[m], out_weights[m])
        for b in range(n_row):
            rows = pl.ds(pl.multiple_of(m * model + r * depth, 16), depth)
            wide_buf[m, :depth, b * slice_wide : (b + 1) * slice_wide] = grad_buf[
                c * n_row + b, rows
            ].astype(jnp.float32)
        store(m, 3, wide_buf.at[m, :depth, : n_row * slice_wide], out_grads[m])
    for copy in stores:
        copy.wait()


def shampoo(
    grads,
    left_root_gu,
    right_root_down,
    right_root_gu,
    left_root_down,
    left_gu,
    right_down,
    right_gu,
    left_down,
    weight_gu,
    weight_down,
    n_row,
    n_col,
):
    blocks, _, slice_wide = grads.shape
    model = left_root_gu.shape[2]
    depth = left_root_gu.shape[1]
    wide_rows, wide_cols = left_root_down.shape
    right_rows = left_down.shape[0]
    left_rows = right_down.shape[0]
    tile = min(256, wide_rows)
    f32 = jnp.float32
    dma = pltpu.SemaphoreType.DMA
    any_spec = pl.BlockSpec(memory_space=pl.ANY)
    args = (
        grads,
        left_root_gu,
        right_root_down,
        right_root_gu,
        left_root_down,
        left_gu,
        right_down,
        right_gu,
        left_down,
        weight_gu,
        weight_down,
    )
    return pl.pallas_call(
        functools.partial(shampoo_kernel, (n_row, n_col, model, slice_wide, tile)),
        out_shape=[
            jax.ShapeDtypeStruct(weight_gu.shape, f32),
            jax.ShapeDtypeStruct(weight_down.shape, f32),
            jax.ShapeDtypeStruct(left_gu.shape, f32),
            jax.ShapeDtypeStruct(right_down.shape, f32),
            jax.ShapeDtypeStruct(right_gu.shape, f32),
            jax.ShapeDtypeStruct(left_down.shape, f32),
            jax.ShapeDtypeStruct(weight_gu.shape, f32),
            jax.ShapeDtypeStruct(weight_down.shape, f32),
        ],
        in_specs=[any_spec] * len(args),
        out_specs=[any_spec] * 8,
        scratch_shapes=[
            pltpu.VMEM(grads.shape, jnp.bfloat16),
            pltpu.VMEM((3, depth, model), f32),
            pltpu.VMEM((3, wide_rows, wide_cols), f32),
            pltpu.VMEM((3, left_rows, model), f32),
            pltpu.VMEM((3, right_rows, wide_cols), f32),
            pltpu.VMEM((3, depth, wide_rows), f32),
            pltpu.VMEM((depth, wide_cols), jnp.bfloat16),
            pltpu.VMEM((right_rows + depth, model), jnp.bfloat16),
            dma((3, 5)),
            dma((3, wide_rows // tile)),
            dma((3, 4)),
        ],
        compiler_params=pltpu.CompilerParams(vmem_limit_bytes=60 * 2**20),
        name="shampoo",
    )(*args)


def shampoo_plain(
    grads,
    left_root_gu,
    right_root_down,
    right_root_gu,
    left_root_down,
    left_gu,
    right_down,
    right_gu,
    left_down,
    weight_gu,
    weight_down,
    n_row,
    n_col,
):
    low = jnp.bfloat16
    blocks, _, slice_wide = grads.shape
    model = left_root_gu.shape[2]
    r = lax.axis_index("row")
    c = lax.axis_index("col")
    owner = r * n_col + c
    left_rows = right_down.shape[0]
    right_rows = left_down.shape[0]
    product = functools.partial(jnp.einsum, preferred_element_type=jnp.float32)
    whole = grads.reshape(blocks, 3, model, slice_wide).transpose(1, 2, 0, 3).reshape(3, model, -1)
    mine_left = lax.dynamic_slice_in_dim(whole, owner * left_rows, left_rows, 1)
    mine_right = lax.dynamic_slice_in_dim(whole, owner * right_rows, right_rows, 2)
    left_sum = 0.5 * product("mif,mjf->mij", mine_left, whole)
    right_sum = 0.5 * product("mdi,mdj->mij", mine_right, whole)
    roots = jnp.concatenate([left_root_gu, right_root_down[None]]).astype(low)
    wides = jnp.concatenate([right_root_gu, left_root_down[None]]).astype(low)
    step = product("mid,mdf->mif", roots, whole).astype(low)
    step = SHAMPOO_RATE * product("mif,mjf->mij", step, wides)
    depth, wide_rows = weight_down.shape
    block = lax.dynamic_slice(whole, (0, r * depth, c * wide_rows), (3, depth, wide_rows))
    block = block.astype(jnp.float32)
    return (
        block[:2].transpose(1, 0, 2),
        block[2],
        0.5 * left_gu + left_sum[:2],
        0.5 * right_down + left_sum[2],
        0.5 * right_gu + right_sum[:2],
        0.5 * left_down + right_sum[2],
        weight_gu - step[:2].transpose(1, 0, 2),
        weight_down - step[2],
    )


def body_tiled(
    tokens,
    lengths,
    routes,
    prev_logits,
    cotangent,
    w_qkv,
    w_out,
    route_w,
    gains,
    const_vec,
    stat_qkv,
    stat_out,
    stat_route,
    stat_gains,
    stat_const,
    w_gate_up,
    w_down,
    left_gu,
    right_gu,
    left_down,
    right_down,
    left_root_gu,
    right_root_gu,
    left_root_down,
    right_root_down,
):
    dims = mesh_sizes()
    n_dp, n_row, n_col = dims
    shard_rows = w_qkv.shape[0]
    wide_qkv = w_qkv.shape[1] // n_col
    wide_out = w_out.shape[1] // n_col
    route_cols = route_w.shape[1]
    wide = wide_qkv + wide_out + LANES

    def by_col(matrix):
        return matrix.reshape(matrix.shape[0], n_col, -1).transpose(1, 0, 2)

    def small_block(route_part, gain_part, const_part):
        together = jnp.concatenate([route_part, gain_part.T, const_part.T], axis=1)
        return jnp.pad(together, ((0, 0), (0, LANES - together.shape[1])))

    small = small_block(route_w, gains, const_vec)
    shard = jnp.concatenate(
        [by_col(w_qkv), by_col(w_out), jnp.broadcast_to(small[None], (n_col, shard_rows, LANES))],
        axis=2,
    )
    whole, parts_back, grads_own, qkv_rows, softmax_probs, mixed_heads, first_sum, state = front(
        lengths,
        routes,
        prev_logits,
        tokens,
        cotangent,
        shard,
        w_gate_up[0],
        w_down[0].T,
        dims,
        (wide_qkv, wide_out, route_cols),
    )
    result, grad_input, gathered, summed = back(
        lengths,
        routes,
        state,
        tokens,
        cotangent,
        parts_back.reshape(n_col, n_dp, n_row, CAP, 2 * D),
        grads_own,
        whole.reshape(n_col, D, wide),
        qkv_rows,
        softmax_probs,
        mixed_heads,
        first_sum,
        dims,
        prev_logits.shape[1] - 4,
        (wide_qkv, wide_out, route_cols),
    )
    gathered = gathered.reshape(n_col * n_row, *grads_own.shape)

    def from_col(parts):
        return parts.transpose(1, 0, 2).reshape(parts.shape[1], -1)

    grad_qkv = from_col(summed[:, :, :wide_qkv])
    grad_attn_out = from_col(summed[:, :, wide_qkv : wide_qkv + wide_out])
    sum_small = summed[0, :, wide_qkv + wide_out :]
    grad_route = sum_small[:, :route_cols]
    grad_gains = sum_small[:, route_cols : route_cols + 2].T
    grad_const = sum_small[:, route_cols + 2 : route_cols + 4].T
    moment_qkv, new_qkv = diag_update(w_qkv, grad_qkv, stat_qkv, D ** (-0.5))
    moment_attn_out, new_attn_out = diag_update(w_out, grad_attn_out, stat_out, HEAD ** (-0.5))
    moment_route, new_route = diag_update(route_w, grad_route, stat_route, (4 * D) ** (-0.5))
    moment_gains, new_gains = diag_update(gains, grad_gains, stat_gains, 0.3)
    moment_const, new_const = diag_update(const_vec, grad_const, stat_const, 0.5)

    (
        grad_gate_up,
        grad_down,
        new_left_gu,
        new_right_down,
        new_right_gu,
        new_left_down,
        new_gate_up,
        new_down,
    ) = shampoo(
        gathered,
        left_root_gu[0],
        right_root_down[0],
        right_root_gu[0],
        left_root_down[0],
        left_gu[0],
        right_down[0],
        right_gu[0],
        left_down[0],
        w_gate_up[0],
        w_down[0].T,
        n_row,
        n_col,
    )
    return (
        result,
        grad_input,
        grad_qkv,
        moment_qkv,
        new_qkv,
        grad_attn_out,
        moment_attn_out,
        new_attn_out,
        grad_route,
        moment_route,
        new_route,
        grad_gains,
        moment_gains,
        new_gains,
        grad_const,
        moment_const,
        new_const,
        grad_gate_up[None],
        grad_down.T[None],
        new_left_gu[None],
        new_right_gu[None],
        new_left_down[None],
        new_right_down[None],
        new_gate_up[None],
        new_down.T[None],
    )


def body(
    tokens,
    lengths,
    routes,
    prev_logits,
    cotangent,
    w_qkv,
    w_out,
    route_w,
    gains,
    const_vec,
    stat_qkv,
    stat_out,
    stat_route,
    stat_gains,
    stat_const,
    w_gate_up,
    w_down,
    left_gu,
    right_gu,
    left_down,
    right_down,
    left_root_gu,
    right_root_gu,
    left_root_down,
    right_root_down,
):
    dims = mesh_sizes()
    n_dp, n_row, n_col = dims
    low = jnp.bfloat16
    row_total = tokens.shape[0]
    total_experts = prev_logits.shape[1]
    num_ffn = total_experts - 4
    seq_count = lengths.shape[1]
    shard_rows = w_qkv.shape[0]
    wide_qkv = w_qkv.shape[1] // n_col
    wide_out = w_out.shape[1] // n_col
    route_cols = route_w.shape[1]
    wide = wide_qkv + wide_out + LANES

    def by_col(matrix):
        return matrix.reshape(matrix.shape[0], n_col, -1).transpose(1, 0, 2)

    def small_block(route_part, gain_part, const_part):
        together = jnp.concatenate([route_part, gain_part.T, const_part.T], axis=1)
        return jnp.pad(together, ((0, 0), (0, LANES - together.shape[1])))

    small = small_block(route_w, gains, const_vec)
    shard = jnp.concatenate(
        [by_col(w_qkv), by_col(w_out), jnp.broadcast_to(small[None], (n_col, shard_rows, LANES))],
        axis=2,
    )
    whole = param_gather(shard, dims).reshape(n_col, D, wide)
    full_qkv = [whole[i, :, :wide_qkv] for i in range(n_col)]
    full_out = [whole[i, :, wide_qkv : wide_qkv + wide_out] for i in range(n_col)]
    full_small = whole[0, :, wide_qkv + wide_out :]
    full_route = full_small[:, :route_cols]
    row_vectors = full_small[:, route_cols : route_cols + 4].T.astype(jnp.float32)
    gain_one, gain_two, const_rows = row_vectors[0], row_vectors[1], row_vectors[2:4]

    row_depth = w_gate_up.shape[1]
    col_width = w_gate_up.shape[3]
    slice_wide = col_width // n_row
    gu_slices = w_gate_up[0].astype(low).reshape(row_depth, 2, n_row, slice_wide)
    gu_slices = gu_slices.transpose(2, 0, 1, 3)
    gu_own = lax.all_to_all(gu_slices, "row", split_axis=0, concat_axis=0, tiled=True)
    gu_own = gu_own.reshape(n_row * row_depth, 2 * slice_wide)
    down_slices = w_down[0].astype(low).reshape(n_row, slice_wide, row_depth)
    down_own = lax.all_to_all(down_slices, "row", split_axis=0, concat_axis=0, tiled=True)
    down_own = down_own.transpose(1, 0, 2).reshape(slice_wide, n_row * row_depth)

    positions = jnp.arange(row_total, dtype=jnp.int32)
    seq_ends = jnp.cumsum(lengths[0])
    doc_index = jnp.sum((positions[:, None] >= seq_ends[None, :]).astype(jnp.int32), axis=1)
    valid_rows = (doc_index < seq_count).astype(jnp.float32)[:, None]
    allowed = (doc_index[:, None] == doc_index[None, :]) & (
        positions[:, None] >= positions[None, :]
    )
    inputs = tokens.astype(jnp.float32)
    h_one, normed_one, scale_one = norm_forward(inputs, gain_one)
    h_one_low = h_one.astype(low)
    qkv_rows = jnp.concatenate([dot(h_one_low, part) for part in full_qkv], axis=1).astype(low)
    qkv_rows = qkv_rows.reshape(row_total, 3, HEADS, HEAD)
    queries, key_heads, values = (qkv_rows[:, 0], qkv_rows[:, 1], qkv_rows[:, 2])
    softmax_probs = attention_probs(queries, key_heads, allowed)
    probs_low = softmax_probs.astype(low)
    mixed_heads = jnp.einsum("hqk,khd->qhd", probs_low, values, preferred_element_type=jnp.float32)
    mixed_heads = mixed_heads.reshape(row_total, D).astype(low)
    attn_out = jnp.concatenate([dot(mixed_heads, part) for part in full_out], axis=1)
    first_sum = inputs + valid_rows * attn_out
    h_two, normed_two, scale_two = norm_forward(first_sum, gain_two)
    h_two_low = h_two.astype(low)
    logits_all = dot(h_two_low, full_route)
    logits = logits_all[:, :total_experts] + prev_logits
    pick_table = (
        routes[:, :, None] == jnp.arange(total_experts, dtype=jnp.int32)[None, None, :]
    ).astype(jnp.float32)
    chosen = jnp.sum(pick_table * logits[:, None, :], axis=-1)
    gate_weights = jax.nn.softmax(chosen, axis=-1)
    const_mix = jax.nn.softmax(logits_all[:, total_experts:].reshape(row_total, 2, 2), axis=-1)

    earlier = dot(
        (positions[:, None] > positions[None, :]).astype(low),
        jnp.sum(pick_table, axis=1).astype(low),
    )
    slot_index = jnp.sum(earlier[:, None, :] * pick_table, axis=-1).astype(jnp.int32)
    where_in = jnp.where(routes < num_ffn, routes * CAP + slot_index, -1)
    slot_ids = jnp.arange(num_ffn * CAP, dtype=jnp.int32)
    place_first = where_in[:, 0:1] == slot_ids[None, :]
    place_second = where_in[:, 1:2] == slot_ids[None, :]
    place_both = (place_first | place_second).astype(low)
    slot_gate = jnp.sum(
        place_first.astype(jnp.float32) * gate_weights[:, 0:1]
        + place_second.astype(jnp.float32) * gate_weights[:, 1:2],
        axis=0,
    )
    grad_y = cotangent.astype(jnp.float32) * valid_rows
    sent_rows = dot(place_both, h_two_low, TN).astype(low)
    grad_made = (slot_gate[:, None] * dot(place_both, grad_y.astype(low), TN)).astype(low)
    sent_both = jnp.concatenate(
        [sent_rows.reshape(num_ffn, CAP, D), grad_made.reshape(num_ffn, CAP, D)], axis=2
    )

    arrived = token_gather(sent_both, dims).reshape(-1, 2 * D)
    rows_in = arrived[:, :D]
    grads_in = arrived[:, D:]
    pre_act = dot(rows_in, gu_own)
    gate_part = pre_act[:, :slice_wide]
    up_part = pre_act[:, slice_wide:]
    sigma = jax.nn.sigmoid(gate_part)
    silu = gate_part * sigma
    hidden = (silu * up_part).astype(low)
    made_rows = dot(hidden, down_own).astype(low)
    grad_hidden = dot(grads_in, down_own, NT)
    grad_pre = jnp.concatenate(
        [
            grad_hidden * up_part * sigma * (1.0 + gate_part * (1.0 - sigma)),
            grad_hidden * silu,
        ],
        axis=1,
    ).astype(low)
    grad_rows = dot(grad_pre, gu_own, NT).astype(low)
    parts_back = jnp.concatenate([made_rows, grad_rows], axis=1)
    parts_back = parts_back.reshape(n_col, n_dp, n_row, CAP, 2 * D)
    came_back = token_reduce(parts_back, dims).reshape(num_ffn * CAP, 2 * D)
    expert_out = came_back[:, :D]
    grad_sent = came_back[:, D:]

    grad_gu_own = dot(rows_in, grad_pre, TN).astype(low)
    grad_down_own = dot(hidden, grads_in, TN).astype(low)
    grads_own = jnp.concatenate(
        [grad_gu_own[:, :slice_wide], grad_gu_own[:, slice_wide:], grad_down_own.T], axis=0
    )
    gathered = plane_gather(grads_own.reshape(4, -1, slice_wide), dims)
    gathered = gathered.reshape(n_col * n_row, 3 * D, slice_wide)

    is_ffn_first = dot(place_first.astype(low), expert_out)
    is_ffn_second = dot(place_second.astype(low), expert_out)
    picked = jnp.stack([is_ffn_first, is_ffn_second], axis=1)
    copy_sel = (routes == num_ffn + 1).astype(jnp.float32)
    const_sel = (
        routes[:, :, None] == num_ffn + 2 + jnp.arange(2, dtype=jnp.int32)[None, None, :]
    ).astype(jnp.float32)
    const_out = (
        const_mix[:, :, 0:1] * h_two[:, None, :] + const_mix[:, :, 1:2] * const_rows[None, :, :]
    )
    outputs = (
        picked
        + copy_sel[:, :, None] * h_two[:, None, :]
        + const_sel[:, :, 0:1] * const_out[:, None, 0, :]
        + const_sel[:, :, 1:2] * const_out[:, None, 1, :]
    )
    moe_out = valid_rows * jnp.sum(gate_weights[:, :, None] * outputs, axis=1)
    result = (first_sum + moe_out).astype(low)
    grad_gate = jnp.sum(grad_y[:, None, :] * outputs, axis=-1)
    grad_chosen = gate_weights * (
        grad_gate - jnp.sum(gate_weights * grad_gate, axis=-1, keepdims=True)
    )
    grad_logits = jnp.sum(grad_chosen[:, :, None] * pick_table, axis=1)
    const_weight = jnp.sum(const_sel * gate_weights[:, :, None], axis=1)
    mix_first = const_weight * jnp.sum(grad_y * h_two, axis=-1, keepdims=True)
    mix_second = const_weight * jnp.stack(
        [jnp.sum(grad_y * const_rows[0], axis=-1), jnp.sum(grad_y * const_rows[1], axis=-1)], axis=1
    )
    grad_mix = jnp.stack([mix_first, mix_second], axis=-1)
    grad_mix_logits = const_mix * (grad_mix - jnp.sum(const_mix * grad_mix, axis=-1, keepdims=True))
    grad_logits_all = jnp.concatenate(
        [grad_logits, grad_mix_logits.reshape(row_total, 4)], axis=1
    ).astype(low)
    grad_route_full = dot(h_two_low, grad_logits_all, TN)
    const_scale = const_weight * const_mix[:, :, 1]
    grad_const_full = jnp.stack(
        [
            jnp.sum(const_scale[:, 0:1] * grad_y, axis=0),
            jnp.sum(const_scale[:, 1:2] * grad_y, axis=0),
        ]
    )
    back_rows = dot(place_both, grad_sent)
    own_weight = jnp.sum(gate_weights * copy_sel, axis=1, keepdims=True) + jnp.sum(
        const_weight * const_mix[:, :, 0], axis=1, keepdims=True
    )
    grad_h_two = dot(grad_logits_all, full_route, NT) + back_rows + own_weight * grad_y
    grad_first, grad_gain_two = norm_backward(grad_h_two, normed_two, scale_two, gain_two)
    grad_first = grad_first + cotangent.astype(jnp.float32)
    grad_attn = (valid_rows * grad_first).astype(low)
    grad_mixed = functools.reduce(
        jnp.add,
        [
            dot(grad_attn[:, i * wide_out : (i + 1) * wide_out], part, NT)
            for i, part in enumerate(full_out)
        ],
    ).astype(low)
    grad_mixed = grad_mixed.reshape(row_total, HEADS, HEAD)
    grad_values = jnp.einsum(
        "hqk,qhd->khd", probs_low, grad_mixed, preferred_element_type=jnp.float32
    )
    grad_probs = jnp.einsum("qhd,khd->hqk", grad_mixed, values, preferred_element_type=jnp.float32)
    grad_scores = softmax_probs * (
        grad_probs - jnp.sum(softmax_probs * grad_probs, axis=-1, keepdims=True)
    )
    grad_scores = grad_scores.astype(low)
    grad_queries = jnp.einsum(
        "hqk,khd->qhd", grad_scores, key_heads, preferred_element_type=jnp.float32
    ) * HEAD ** (-0.5)
    grad_keys = jnp.einsum(
        "hqk,qhd->khd", grad_scores, queries, preferred_element_type=jnp.float32
    ) * HEAD ** (-0.5)
    grad_qkv_rows = (
        jnp.stack([grad_queries, grad_keys, grad_values], axis=1)
        .reshape(row_total, 3 * D)
        .astype(low)
    )
    grad_h_one = functools.reduce(
        jnp.add,
        [
            dot(grad_qkv_rows[:, i * wide_qkv : (i + 1) * wide_qkv], part, NT)
            for i, part in enumerate(full_qkv)
        ],
    )
    grad_input, grad_gain_one = norm_backward(grad_h_one, normed_one, scale_one, gain_one)
    grad_input = grad_input + grad_first
    grad_gains_full = jnp.stack([grad_gain_one, grad_gain_two])

    grad_small = small_block(grad_route_full, grad_gains_full, grad_const_full).astype(low)
    param_parts = jnp.stack(
        [
            jnp.concatenate(
                [
                    dot(h_one_low, grad_qkv_rows[:, i * wide_qkv : (i + 1) * wide_qkv], TN).astype(
                        low
                    ),
                    dot(mixed_heads, grad_attn[:, i * wide_out : (i + 1) * wide_out], TN).astype(
                        low
                    ),
                    grad_small,
                ],
                axis=1,
            )
            for i in range(n_col)
        ]
    )
    summed = param_reduce(
        param_parts.reshape(n_col, n_dp, n_row, n_col * shard_rows, wide), dims
    )

    def from_col(parts):
        return parts.transpose(1, 0, 2).reshape(parts.shape[1], -1)

    grad_qkv = from_col(summed[:, :, :wide_qkv])
    grad_attn_out = from_col(summed[:, :, wide_qkv : wide_qkv + wide_out])
    sum_small = summed[0, :, wide_qkv + wide_out :]
    grad_route = sum_small[:, :route_cols]
    grad_gains = sum_small[:, route_cols : route_cols + 2].T
    grad_const = sum_small[:, route_cols + 2 : route_cols + 4].T
    moment_qkv, new_qkv = diag_update(w_qkv, grad_qkv, stat_qkv, D ** (-0.5))
    moment_attn_out, new_attn_out = diag_update(w_out, grad_attn_out, stat_out, HEAD ** (-0.5))
    moment_route, new_route = diag_update(route_w, grad_route, stat_route, (4 * D) ** (-0.5))
    moment_gains, new_gains = diag_update(gains, grad_gains, stat_gains, 0.3)
    moment_const, new_const = diag_update(const_vec, grad_const, stat_const, 0.5)

    (
        grad_gate_up,
        grad_down,
        new_left_gu,
        new_right_down,
        new_right_gu,
        new_left_down,
        new_gate_up,
        new_down,
    ) = shampoo_plain(
        gathered,
        left_root_gu[0],
        right_root_down[0],
        right_root_gu[0],
        left_root_down[0],
        left_gu[0],
        right_down[0],
        right_gu[0],
        left_down[0],
        w_gate_up[0],
        w_down[0].T,
        n_row,
        n_col,
    )
    return (
        result,
        grad_input,
        grad_qkv,
        moment_qkv,
        new_qkv,
        grad_attn_out,
        moment_attn_out,
        new_attn_out,
        grad_route,
        moment_route,
        new_route,
        grad_gains,
        moment_gains,
        new_gains,
        grad_const,
        moment_const,
        new_const,
        grad_gate_up[None],
        grad_down.T[None],
        new_left_gu[None],
        new_right_gu[None],
        new_left_down[None],
        new_right_down[None],
        new_gate_up[None],
        new_down.T[None],
    )


def solution(mesh):
    placed = (
        P(("dp", "row", "col"), None),
        P(("dp", "row", "col"), None),
        P(("dp", "row", "col"), None),
        P(("dp", "row", "col"), None),
        P(("dp", "row", "col"), None),
        P(("dp", "row", "col"), None),
        P(("dp", "row", "col"), None),
        P(("dp", "row", "col"), None),
        P(None, ("dp", "row", "col")),
        P(None, ("dp", "row", "col")),
        P(("dp", "row", "col"), None),
        P(("dp", "row", "col"), None),
        P(("dp", "row", "col"), None),
        P(None, ("dp", "row", "col")),
        P(None, ("dp", "row", "col")),
        P("dp", "row", None, "col"),
        P("dp", "col", "row"),
        P("dp", None, ("row", "col"), None),
        P("dp", None, ("row", "col"), None),
        P("dp", ("row", "col"), None),
        P("dp", ("row", "col"), None),
        P("dp", None, "row", None),
        P("dp", None, "col", None),
        P("dp", "col", None),
        P("dp", "row", None),
    )
    tiled = 3 * D % (mesh.shape["col"] * LANES) == 0 and D % (mesh.shape["col"] * LANES) == 0
    tiled = tiled and D // mesh.shape["dp"] // mesh.shape["row"] % 16 == 0
    return jax.shard_map(
        body_tiled if tiled else body,
        mesh=mesh,
        in_specs=placed,
        out_specs=(
            P(("dp", "row", "col"), None),
            P(("dp", "row", "col"), None),
            P(("dp", "row", "col"), None),
            P(("dp", "row", "col"), None),
            P(("dp", "row", "col"), None),
            P(("dp", "row", "col"), None),
            P(("dp", "row", "col"), None),
            P(("dp", "row", "col"), None),
            P(("dp", "row", "col"), None),
            P(("dp", "row", "col"), None),
            P(("dp", "row", "col"), None),
            P(None, ("dp", "row", "col")),
            P(None, ("dp", "row", "col")),
            P(None, ("dp", "row", "col")),
            P(None, ("dp", "row", "col")),
            P(None, ("dp", "row", "col")),
            P(None, ("dp", "row", "col")),
            P("dp", "row", None, "col"),
            P("dp", "col", "row"),
            P("dp", None, ("row", "col"), None),
            P("dp", None, ("row", "col"), None),
            P("dp", ("row", "col"), None),
            P("dp", ("row", "col"), None),
            P("dp", "row", None, "col"),
            P("dp", "col", "row"),
        ),
        check_vma=False,
    )
```

```python
import functools
import types

import jax
import jax.numpy as jnp
from jax import lax
from jax.experimental import pallas as pl
from jax.experimental.pallas import tpu as pltpu
from jax.sharding import PartitionSpec as P

D = 768
HEADS = 12
HEAD = 64
CAP = 32
LANES = 128


NORM_EPS = 1e-06
SHAMPOO_RATE = 0.5
MESH = pl.DeviceIdType.MESH
VMEM_BYTES = 62 * 2**20


def dot(left, right, dims=(((1,), (0,)), ((), ()))):
    return lax.dot_general(left, right, dims, preferred_element_type=jnp.float32)


NT = (((1,), (1,)), ((), ()))
TN = (((0,), (0,)), ((), ()))


def flip(index, bit):
    return index + bit * (1 - 2 * ((index // bit) % 2))


def flip_all(index, mask, bits):
    for dim in range(bits):
        if mask & (1 << dim):
            index = flip(index, 1 << dim)
    return index


def mesh_sizes():
    return tuple(lax.axis_size(name) for name in ("dp", "row", "col"))


def bits_of(count):
    bits = count.bit_length() - 1
    assert 1 << bits == count
    return bits


def greet(over_dp, dims, place, all_rows=False):
    n_dp, n_row, n_col = dims
    d, r, c = place
    peers = []
    if over_dp:
        peers += [((d + j) % n_dp, r, c) for j in range(1, n_dp)]
    if all_rows:
        peers += [(d, (r + i) % n_row, c) for i in range(1, n_row)]
    else:
        peers += [(d, flip(r, 1 << dim), c) for dim in range(bits_of(n_row))]
    peers += [(d, r, (c + i) % n_col) for i in range(1, n_col)]
    barrier = pltpu.get_barrier_semaphore()
    for peer in peers:
        pl.semaphore_signal(barrier, inc=1, device_id=peer, device_id_type=MESH)
    pl.semaphore_wait(barrier, len(peers))


def remote(src, dst, send_sem, recv_sem, device):
    return pltpu.make_async_remote_copy(
        src_ref=src,
        dst_ref=dst,
        send_sem=send_sem,
        recv_sem=recv_sem,
        device_id=device,
        device_id_type=MESH,
    )


def plan_spread(dims, place, chunks, over_dp, own, dp_source, slot, sems):
    n_dp, n_row, n_col = dims
    d, r, c = place
    bits = bits_of(n_row)
    dp_send, dp_recv, row_send, row_recv, col_send, col_recv, own_sem = sems
    sent = []

    def block(j, x):
        return slot(c, j, flip_all(r, x, bits))

    def to_row(j, src, x, bit):
        copy = remote(
            src,
            block(j, x),
            row_send.at[j, x ^ bit],
            row_recv.at[j, x ^ bit],
            (d, flip(r, bit), c),
        )
        copy.start()
        sent.append(copy)

    def to_cols(j, src, x):
        for i in range(1, n_col):
            copy = remote(
                src,
                block(j, x),
                col_send.at[j, x, i],
                col_recv.at[j, x, i],
                (d, r, (c + i) % n_col),
            )
            copy.start()
            sent.append(copy)

    def order(j):
        return [1 << ((j + s) % bits) for s in range(bits)]

    locals_ = {}

    def start(j):
        if over_dp and j > 0:
            src = block(j, 0)
            remote(src, src, dp_send.at[j], dp_recv.at[j], (d, r, c)).wait_recv()
        elif own is None:
            src = block(j, 0)
        else:
            src = own(j)
            keep = pltpu.make_async_copy(src, block(j, 0), own_sem.at[j])
            keep.start()
            locals_[j] = keep
        for bit in order(j):
            to_row(j, src, 0, bit)
        to_cols(j, src, 0)

    def arrived(j, x, later_dims):
        ref = block(j, x)
        remote(ref, ref, row_send.at[j, x], row_recv.at[j, x], (d, r, c)).wait_recv()
        for later in later_dims:
            to_row(j, ref, x, later)
        to_cols(j, ref, x)

    def pass_on(j):
        have = [0]
        dim_order = order(j)
        for s, bit in enumerate(dim_order[:-1]):
            new = [x ^ bit for x in have]
            for x in new:
                arrived(j, x, dim_order[s + 1 :])
            have += new

    def last_arrivals(j):
        bit = order(j)[-1]
        for x in range(n_row):
            if x & bit:
                arrived(j, x, [])

    def send_dp():
        for j in range(1, n_dp):
            peer = (d + j) % n_dp
            copy = remote(
                dp_source(peer),
                slot(c, ("from", d), r),
                dp_send.at[j],
                dp_recv.at[j],
                (peer, r, c),
            )
            copy.start()
            sent.append(copy)

    def wait_cols(j):
        for x in range(n_row):
            for i in range(1, n_col):
                ref = slot((c + n_col - i) % n_col, j, flip_all(r, x, bits))
                remote(ref, ref, col_send.at[j, x, i], col_recv.at[j, x, i], (d, r, c)).wait_recv()
        if j in locals_:
            locals_[j].wait()

    def sends():
        return [copy.wait_send for copy in sent]

    return types.SimpleNamespace(
        start=start,
        send_dp=send_dp,
        pass_on=pass_on,
        last_arrivals=last_arrivals,
        wait_cols=wait_cols,
        sends=sends,
    )


def spread_blocks(dims, place, chunks, over_dp, own, dp_source, slot, sems, between=None):
    plan = plan_spread(dims, place, chunks, over_dp, own, dp_source, slot, sems)
    plan.start(0)
    if over_dp:
        plan.send_dp()
        for j in range(1, chunks):
            plan.start(j)
            plan.pass_on(j - 1)
        plan.pass_on(chunks - 1)
    else:
        for j in range(1, chunks):
            plan.start(j)
        for j in range(chunks):
            plan.pass_on(j)
    if between is not None:
        between()
    for j in range(chunks):
        plan.last_arrivals(j)
    for j in range(chunks):
        plan.wait_cols(j)
    return plan.sends()


def finish(waits):
    for wait in waits:
        wait()


def spread_sems(dims, chunks):
    n_dp, n_row, n_col = dims
    dma = pltpu.SemaphoreType.DMA
    return [
        dma((n_dp,)),
        dma((n_dp,)),
        dma((chunks, n_row)),
        dma((chunks, n_row)),
        dma((chunks, n_row, n_col)),
        dma((chunks, n_row, n_col)),
        dma((chunks,)),
    ]


def axis_place():
    return tuple(lax.axis_index(name) for name in ("dp", "row", "col"))


def param_gather_kernel(dims, shard_ref, out_ref, swap_ref, block_ref, swap_send, swap_recv, *sems):
    n_dp, n_row, n_col = dims
    place = axis_place()
    d, r, c = place
    rows = shard_ref.shape[1]
    greet(True, dims, place)
    copies = []
    for i in range(1, n_col):
        other = (c + i) % n_col
        copy = remote(
            shard_ref.at[other], swap_ref.at[c], swap_send.at[i], swap_recv.at[i], (d, r, other)
        )
        copy.start()
        copies.append(copy)
    swap_ref[pl.ds(c, 1)] = shard_ref[pl.ds(c, 1)]
    for copy in copies:
        copy.wait()
    for i in range(n_col):
        block_ref[i * rows : (i + 1) * rows, :] = swap_ref[i]
    low_ref = sems[-1]
    low_ref[...] = block_ref[...].astype(jnp.bfloat16)

    def slot(col, j, b):
        k = j[1] if isinstance(j, tuple) else (d + n_dp - j) % n_dp
        return out_ref.at[col, k, b]

    finish(
        spread_blocks(
            dims, place, n_dp, True, lambda j: low_ref, lambda k: low_ref, slot, sems[:-1]
        )
    )


def param_gather(shard, dims):
    n_dp, n_row, n_col = dims
    _, rows, width = shard.shape
    dma = pltpu.SemaphoreType.DMA
    return pl.pallas_call(
        functools.partial(param_gather_kernel, dims),
        out_shape=jax.ShapeDtypeStruct((n_col, n_dp, n_row, n_col * rows, width), jnp.bfloat16),
        in_specs=[pl.BlockSpec(memory_space=pltpu.VMEM)],
        out_specs=pl.BlockSpec(memory_space=pl.ANY),
        scratch_shapes=[
            pltpu.VMEM((n_col, rows, width), jnp.float32),
            pltpu.VMEM((n_col * rows, width), jnp.float32),
            dma((n_col,)),
            dma((n_col,)),
            *spread_sems(dims, n_dp),
            pltpu.VMEM((n_col * rows, width), jnp.bfloat16),
        ],
        compiler_params=pltpu.CompilerParams(
            collective_id=0, has_side_effects=True, vmem_limit_bytes=VMEM_BYTES
        ),
        name="param_gather",
    )(shard)


def token_gather_kernel(dims, src_ref, out_ref, *sems):
    n_dp, n_row, n_col = dims
    place = axis_place()
    d = place[0]
    greet(True, dims, place)

    def slot(col, j, b):
        k = j[1] if isinstance(j, tuple) else (d + n_dp - j) % n_dp
        return out_ref.at[col, k, b]

    finish(
        spread_blocks(
            dims,
            place,
            n_dp,
            True,
            lambda j: src_ref.at[d],
            lambda k: src_ref.at[k],
            slot,
            sems,
        )
    )


def token_gather(rows, dims):
    n_dp, n_row, n_col = dims
    _, slots, width = rows.shape
    return pl.pallas_call(
        functools.partial(token_gather_kernel, dims),
        out_shape=jax.ShapeDtypeStruct((n_col, n_dp, n_row, slots, width), rows.dtype),
        in_specs=[pl.BlockSpec(memory_space=pl.ANY)],
        out_specs=pl.BlockSpec(memory_space=pl.ANY),
        scratch_shapes=spread_sems(dims, n_dp),
        compiler_params=pltpu.CompilerParams(
            collective_id=1, has_side_effects=True, vmem_limit_bytes=VMEM_BYTES
        ),
        name="token_gather",
    )(rows)


def plane_gather_kernel(dims, src_ref, out_ref, *sems):
    place = axis_place()
    greet(False, dims, place)
    finish(
        spread_blocks(
            dims,
            place,
            src_ref.shape[0],
            False,
            lambda j: src_ref.at[j],
            None,
            lambda col, j, b: out_ref.at[col, b, j],
            sems,
        )
    )


def plane_gather(parts, dims):
    n_dp, n_row, n_col = dims
    chunks, rows, width = parts.shape
    return pl.pallas_call(
        functools.partial(plane_gather_kernel, dims),
        out_shape=jax.ShapeDtypeStruct((n_col, n_row, chunks, rows, width), parts.dtype),
        in_specs=[pl.BlockSpec(memory_space=pl.ANY)],
        out_specs=pl.BlockSpec(memory_space=pl.ANY),
        scratch_shapes=spread_sems(dims, chunks),
        compiler_params=pltpu.CompilerParams(
            collective_id=2, has_side_effects=True, vmem_limit_bytes=VMEM_BYTES
        ),
        name="plane_gather",
    )(parts)


def add_low(left, right):
    return (left.astype(jnp.float32) + right.astype(jnp.float32)).astype(jnp.bfloat16)


def plan_reduce(dims, place, part_at, bufs, sems, deliver, direct=False):
    n_dp, n_row, n_col = dims
    d, r, c = place
    bits = bits_of(n_row)
    mine_ref, col_ref, row_ref = bufs
    mine_sem, col_send, col_recv, row_send, row_recv = sems
    steps = list(range(1, n_dp)) + [0]
    sent = []
    held = []

    def send_cols(i):
        other = (c + i) % n_col
        for t, j in enumerate(steps):
            copy = remote(
                part_at(other, (d + j) % n_dp),
                col_ref.at[t, i - 1],
                col_send.at[t, i],
                col_recv.at[t, i],
                (d, r, other),
            )
            copy.start()
            sent.append(copy)

    def load_mine():
        for t, j in enumerate(steps):
            keep = pltpu.make_async_copy(
                part_at(c, (d + j) % n_dp), mine_ref.at[t], mine_sem.at[t]
            )
            keep.start()
            held.append(keep)

    width = mine_ref.shape[-1]
    cut = (width // LANES + 1) // 2 * LANES
    spans = [pl.ds(0, cut), pl.ds(cut, width - cut)]

    def order(half):
        return [1 << ((half + s) % bits) for s in range(bits)]

    def send_half(t, half, s):
        dim_order = order(half)
        bit = dim_order[s]
        before = sum(dim_order[:s])
        span = spans[half]
        for x in range(n_row):
            if not x & before and x & bit:
                at = x ^ bit
                copy = remote(
                    mine_ref.at[t, flip_all(r, x, bits), :, span],
                    row_ref.at[t, slot_of(half, s, at), :, span],
                    row_send.at[t, half, s, at],
                    row_recv.at[t, half, s, at],
                    (d, flip(r, bit), c),
                )
                copy.start()
                sent.append(copy)

    def slot_of(half, s, at):
        places = []
        before = 0
        for step, bit in enumerate(order(half)):
            before += bit
            places += [(step, y) for y in range(n_row) if not y & before]
        return places.index((s, at))

    def sum_cols(t):
        if not direct:
            held[t].wait()
        for i in range(1, n_col):
            ref = col_ref.at[t, i - 1]
            remote(ref, ref, col_send.at[t, i], col_recv.at[t, i], (d, r, c)).wait_recv()
        k = (d + steps[t]) % n_dp

        @pl.loop(0, n_row)
        def _(b):
            total = part_at(c, k)[b] if direct else mine_ref[t, b]
            total = total.astype(jnp.float32)
            for i in range(1, n_col):
                total = total + col_ref[t, i - 1, b].astype(jnp.float32)
            mine_ref[t, b] = total.astype(jnp.bfloat16)

        for half in range(2):
            send_half(t, half, 0)

    def sum_rows(t, s):
        for half in range(2):
            before = sum(order(half)[: s + 1])
            span = spans[half]
            for y in range(n_row):
                if not y & before:
                    slot = slot_of(half, s, y)
                    ref = row_ref.at[t, slot, :, span]
                    remote(
                        ref,
                        ref,
                        row_send.at[t, half, s, y],
                        row_recv.at[t, half, s, y],
                        (d, r, c),
                    ).wait_recv()
                    b = flip_all(r, y, bits)
                    mine_ref[t, b, :, span] = add_low(mine_ref[t, b, :, span], row_ref[t, slot, :, span])
            if s + 1 < bits:
                send_half(t, half, s + 1)
        if s + 1 == bits:
            deliver(t, steps[t], mine_ref.at[t, r])

    def sum_all(between=None):
        ticks = n_dp + bits + 1
        for tick in range(ticks):
            if tick + 1 == ticks and between is not None:
                between()
            if tick < n_dp:
                sum_cols(tick)
            for s in reversed(range(bits)):
                t = tick - 2 - s
                if 0 <= t < n_dp:
                    sum_rows(t, s)

    return types.SimpleNamespace(
        send_cols=send_cols,
        load_mine=load_mine,
        sum_cols=sum_cols,
        sum_rows=sum_rows,
        sum_all=sum_all,
        sent=sent,
    )


def reduce_blocks(dims, place, part_ref, bufs, sems, deliver):
    plan = plan_reduce(dims, place, lambda col, k: part_ref.at[col, k], bufs, sems, deliver)
    for i in range(1, dims[2]):
        plan.send_cols(i)
    plan.load_mine()
    plan.sum_all()
    return plan.sent


def reduce_scratch(dims, rows, width):
    n_dp, n_row, n_col = dims
    bits = bits_of(n_row)
    dma = pltpu.SemaphoreType.DMA
    low = jnp.bfloat16
    return [
        pltpu.VMEM((n_dp, n_row, rows, width), low),
        pltpu.VMEM((n_dp, max(1, n_col - 1), n_row, rows, width), low),
        pltpu.VMEM((n_dp, n_row - 1, rows, width), low),
        dma((n_dp,)),
        dma((n_dp, n_col)),
        dma((n_dp, n_col)),
        dma((n_dp, 2, bits, n_row)),
        dma((n_dp, 2, bits, n_row)),
    ]


def token_reduce_kernel(dims, part_ref, out_ref, *scratch):
    n_dp, n_row, n_col = dims
    place = axis_place()
    d, r, c = place
    dp_send, dp_recv, own_sem = scratch[8:]
    greet(True, dims, place)
    late = []

    def deliver(t, j, block):
        if j == 0:
            keep = pltpu.make_async_copy(block, out_ref.at[d], own_sem)
            keep.start()
            late.append(keep.wait)
        else:
            copy = remote(
                block, out_ref.at[d], dp_send.at[j], dp_recv.at[j], ((d + j) % n_dp, r, c)
            )
            copy.start()
            late.append(copy.wait_send)

    sent = reduce_blocks(dims, place, part_ref, scratch[:3], scratch[3:8], deliver)
    for j in range(1, n_dp):
        ref = out_ref.at[(d + n_dp - j) % n_dp]
        remote(ref, ref, dp_send.at[j], dp_recv.at[j], (d, r, c)).wait_recv()
    for copy in sent:
        copy.wait_send()
    for wait in late:
        wait()


def token_reduce(parts, dims):
    n_dp = dims[0]
    slots, width = parts.shape[3:]
    dma = pltpu.SemaphoreType.DMA
    return pl.pallas_call(
        functools.partial(token_reduce_kernel, dims),
        out_shape=jax.ShapeDtypeStruct((n_dp, slots, width), jnp.bfloat16),
        in_specs=[pl.BlockSpec(memory_space=pl.ANY)],
        out_specs=pl.BlockSpec(memory_space=pl.ANY),
        scratch_shapes=[*reduce_scratch(dims, slots, width), dma((n_dp,)), dma((n_dp,)), dma],
        compiler_params=pltpu.CompilerParams(
            collective_id=3, has_side_effects=True, vmem_limit_bytes=VMEM_BYTES
        ),
        name="token_reduce",
    )(parts)


def param_reduce_kernel(dims, part_ref, out_ref, *scratch):
    n_dp, n_row, n_col = dims
    place = axis_place()
    d, r, c = place
    dp_send, dp_recv, dp_ref, swap_send, swap_recv, swap_ref, sum_ref = scratch[8:]
    rows = out_ref.shape[1]
    greet(True, dims, place)
    late = []
    kept = []

    def deliver(t, j, block):
        if j == 0:
            kept.append(block)
        else:
            copy = remote(
                block, dp_ref.at[j], dp_send.at[j], dp_recv.at[j], ((d + j) % n_dp, r, c)
            )
            copy.start()
            late.append(copy)

    sent = reduce_blocks(dims, place, part_ref, scratch[:3], scratch[3:8], deliver)
    total = kept[0][...].astype(jnp.float32)
    for j in range(1, n_dp):
        ref = dp_ref.at[j]
        remote(ref, ref, dp_send.at[j], dp_recv.at[j], (d, r, c)).wait_recv()
        total = total + dp_ref[j].astype(jnp.float32)
    sum_ref[...] = total
    for i in range(n_col):
        swap_ref[i] = sum_ref[i * rows : (i + 1) * rows, :]
    for i in range(1, n_col):
        other = (c + i) % n_col
        copy = remote(
            swap_ref.at[other], out_ref.at[c], swap_send.at[i], swap_recv.at[i], (d, r, other)
        )
        copy.start()
        late.append(copy)
    out_ref[pl.ds(c, 1)] = swap_ref[pl.ds(c, 1)]
    for i in range(1, n_col):
        ref = out_ref.at[(c + n_col - i) % n_col]
        remote(ref, ref, swap_send.at[i], swap_recv.at[i], (d, r, c)).wait_recv()
    for copy in sent:
        copy.wait_send()
    for copy in late:
        copy.wait_send()


def param_reduce(parts, dims):
    n_dp, n_row, n_col = dims
    block_rows, width = parts.shape[3:]
    rows = block_rows // n_col
    dma = pltpu.SemaphoreType.DMA
    return pl.pallas_call(
        functools.partial(param_reduce_kernel, dims),
        out_shape=jax.ShapeDtypeStruct((n_col, rows, width), jnp.float32),
        in_specs=[pl.BlockSpec(memory_space=pl.ANY)],
        out_specs=pl.BlockSpec(memory_space=pltpu.VMEM),
        scratch_shapes=[
            *reduce_scratch(dims, block_rows, width),
            dma((n_dp,)),
            dma((n_dp,)),
            pltpu.VMEM((n_dp, block_rows, width), jnp.bfloat16),
            dma((n_col,)),
            dma((n_col,)),
            pltpu.VMEM((n_col, rows, width), jnp.float32),
            pltpu.VMEM((block_rows, width), jnp.float32),
        ],
        compiler_params=pltpu.CompilerParams(
            collective_id=4, has_side_effects=True, vmem_limit_bytes=VMEM_BYTES
        ),
        name="param_reduce",
    )(parts)


def column(matrix, index):
    return matrix[:, index : index + 1]


def token_masks(lengths_ref, rows, seqs):
    down = lax.broadcasted_iota(jnp.int32, (rows, 1), 0)
    across = lax.broadcasted_iota(jnp.int32, (1, rows), 1)
    end = 0
    doc_down = jnp.zeros((rows, 1), jnp.int32)
    doc_across = jnp.zeros((1, rows), jnp.int32)
    for i in range(seqs):
        end = end + lengths_ref[0, i]
        doc_down = doc_down + (down >= end).astype(jnp.int32)
        doc_across = doc_across + (across >= end).astype(jnp.int32)
    valid = (doc_down < seqs).astype(jnp.float32)
    allowed = (doc_down == doc_across) & (down >= across)
    return valid, allowed


def row_vectors_of(small, first):
    shape = (8, small.shape[1])
    pick = lax.broadcasted_iota(jnp.int32, shape, 1) == first + lax.broadcasted_iota(
        jnp.int32, shape, 0
    )
    return dot(pick.astype(jnp.bfloat16), small, NT)


def half_mask(rows, half):
    return lax.broadcasted_iota(jnp.int32, (rows, LANES), 1) // HEAD == half


def attention_forward(qkv_ref, probs_ref, mixed_ref, allowed):
    rows = qkv_ref.shape[0]
    low = jnp.bfloat16

    @pl.loop(0, HEADS * HEAD // LANES, unroll=2)
    def _(pair):
        def cols(base):
            return pl.ds(pl.multiple_of(base + pair * LANES, LANES), LANES)

        queries = qkv_ref[:, cols(0)]
        key_heads = qkv_ref[:, cols(D)]
        values = qkv_ref[:, cols(2 * D)]
        mixed = jnp.zeros((rows, LANES), jnp.float32)
        for half in range(LANES // HEAD):
            mask = half_mask(rows, half)
            scores = dot(jnp.where(mask, queries, 0), key_heads, NT) * HEAD ** (-0.5)
            scores = jnp.where(allowed, scores, -1e30)
            top_score = jnp.max(scores, axis=-1, keepdims=True)
            exp_scores = jnp.exp(scores - top_score)
            probs = exp_scores / jnp.sum(exp_scores, axis=-1, keepdims=True)
            probs_ref[pair * (LANES // HEAD) + half] = probs
            mixed = mixed + dot(probs.astype(low), jnp.where(mask, values, 0))
        mixed_ref[:, cols(0)] = mixed.astype(low)


def two_way(first, second):
    top = jnp.maximum(first, second)
    exp_first = jnp.exp(first - top)
    exp_second = jnp.exp(second - top)
    total = exp_first + exp_second
    return exp_first / total, exp_second / total


def attention_backward(qkv_ref, probs_ref, grad_mixed_ref, grad_qkv_ref):
    rows = qkv_ref.shape[0]
    low = jnp.bfloat16

    @pl.loop(0, HEADS * HEAD // LANES, unroll=2)
    def _(pair):
        def cols(base):
            return pl.ds(pl.multiple_of(base + pair * LANES, LANES), LANES)

        queries = qkv_ref[:, cols(0)]
        key_heads = qkv_ref[:, cols(D)]
        values = qkv_ref[:, cols(2 * D)]
        grad_mixed = grad_mixed_ref[:, cols(0)]
        grad_queries = jnp.zeros((rows, LANES), jnp.float32)
        grad_keys = jnp.zeros((rows, LANES), jnp.float32)
        grad_values = jnp.zeros((rows, LANES), jnp.float32)
        for half in range(LANES // HEAD):
            mask = half_mask(rows, half)
            probs = probs_ref[pair * (LANES // HEAD) + half]
            grad_part = jnp.where(mask, grad_mixed, 0)
            grad_values = grad_values + dot(probs.astype(low), grad_part, TN)
            grad_probs = dot(grad_part, values, NT)
            grad_scores = probs * (
                grad_probs - jnp.sum(probs * grad_probs, axis=-1, keepdims=True)
            )
            grad_scores = grad_scores.astype(low)
            grad_queries = grad_queries + dot(grad_scores, jnp.where(mask, key_heads, 0))
            grad_keys = grad_keys + dot(grad_scores, jnp.where(mask, queries, 0), TN)
        grad_qkv_ref[:, cols(0)] = (grad_queries * HEAD ** (-0.5)).astype(low)
        grad_qkv_ref[:, cols(D)] = (grad_keys * HEAD ** (-0.5)).astype(low)
        grad_qkv_ref[:, cols(2 * D)] = grad_values.astype(low)


def layer_kernel(sizes, *refs):
    dims, num_ffn, wide_qkv, wide_out, route_cols, chunks = sizes
    n_dp, n_row, n_col = dims
    low = jnp.bfloat16
    (
        lengths_ref,
        routes_ref,
        prev_ref,
        tokens_ref,
        cotangent_ref,
        w_qkv_ref,
        w_out_ref,
        route_w_ref,
        gains_ref,
        const_ref,
        weight_gu,
        weight_down,
        left_root_gu,
        right_root_down,
        right_root_gu,
        left_root_down,
        result_ref,
        grad_tokens_ref,
        summed_ref,
        right_sum_out,
        left_sum_out,
        step_out,
        block_out,
        shard_ref,
        turn_ref,
        swap_ref,
        block_ref,
        whole_ref,
        pack_ref,
        expert_ref,
        stage_ref,
        arrived_ref,
        hidden_ref,
        pre_ref,
        grads_ref,
        qkv_ref,
        probs_ref,
        mixed_ref,
        first_ref,
        came_ref,
        grad_attn_ref,
        grad_mixed_ref,
        grad_qkv_ref,
        part_ref,
        dp_ref,
        end_ref,
        sum_ref,
        gathered_ref,
        root_ref,
        tile_ref,
        half_step_ref,
        lhs_ref,
        right_sum_ref,
        left_sum_ref,
        left_low_ref,
        step_ref,
        swap_send,
        swap_recv,
        load_sem,
        expert_send,
        expert_recv,
        root_sem,
        tile_sem,
        store_sem,
        came_send,
        came_recv,
        dp_send,
        dp_recv,
        end_send,
        end_recv,
        *more,
    ) = refs
    param_sems, token_sems, gather_sems = more[:7], more[7:14], more[14:21]
    token_scratch, param_scratch = more[21:29], more[29:37]
    place = axis_place()
    d, r, c = place
    rows = shard_ref.shape[1]
    depth, slice_wide = pack_ref.shape[2:]
    held, tile = tile_ref.shape[:2]
    wide_col = n_row * slice_wide
    pieces = [(0, min(tile, depth), 0)]
    if depth > tile:
        pieces.append((tile, depth - tile, wide_col))
    loads = []
    for m, src in enumerate([weight_gu.at[:, 0], weight_gu.at[:, 1], weight_down]):
        for n, (begin, tall, shift) in enumerate(pieces):
            copy = pltpu.make_async_copy(
                src.at[pl.ds(begin, tall)],
                tile_ref.at[m, pl.ds(0, tall), pl.ds(shift, wide_col)],
                load_sem.at[m, n],
            )
            copy.start()
            loads.append(copy)
    roots = [left_root_gu.at[0], left_root_gu.at[1], right_root_down]
    root_loads = []
    for m in range(3):
        copy = pltpu.make_async_copy(roots[m], root_ref.at[m], root_sem.at[m])
        copy.start()
        root_loads.append(copy)
    turn_ref[...] = jnp.zeros_like(turn_ref)
    at = 0
    for ref in (route_w_ref, gains_ref, const_ref):
        turn_ref[at : at + ref.shape[0], : ref.shape[1]] = ref[...]
        at += ref.shape[0]
    small_shard = turn_ref[...].T[:rows]
    for i in range(n_col):
        shard_ref[i, :, :wide_qkv] = w_qkv_ref[:, i * wide_qkv : (i + 1) * wide_qkv]
        shard_ref[i, :, wide_qkv : wide_qkv + wide_out] = w_out_ref[
            :, i * wide_out : (i + 1) * wide_out
        ]
        shard_ref[i, :, wide_qkv + wide_out :] = small_shard
    greet(True, dims, place, all_rows=True)

    copies = []
    for i in range(1, n_col):
        other = (c + i) % n_col
        copy = remote(
            shard_ref.at[other], swap_ref.at[c], swap_send.at[i], swap_recv.at[i], (d, r, other)
        )
        copy.start()
        copies.append(copy)
    swap_ref[pl.ds(c, 1)] = shard_ref[pl.ds(c, 1)]
    for copy in copies:
        copy.wait()
    for i in range(n_col):
        block_ref[i * rows : (i + 1) * rows, :] = swap_ref[i]
    whole_ref[c, d, r] = block_ref[...].astype(low)

    def param_slot(col, j, b):
        k = j[1] if isinstance(j, tuple) else (d + n_dp - j) % n_dp
        return whole_ref.at[col, k, b]

    waits = []

    def send_experts():
        for copy in loads:
            copy.wait()
        for m in range(3):
            for b in range(n_row):
                for begin, tall, shift in pieces:
                    at = shift + b * slice_wide
                    pack_ref[b, m, begin : begin + tall] = tile_ref[
                        m, :tall, at : at + slice_wide
                    ].astype(low)
        home = pl.ds(pl.multiple_of(r * depth, 16), depth)
        for i in range(1, n_row):
            other = (r + i) % n_row
            copy = remote(
                pack_ref.at[other],
                expert_ref.at[:, home],
                expert_send.at[i],
                expert_recv.at[i],
                (d, other, c),
            )
            copy.start()
            waits.append(copy.wait_send)
        expert_ref[:, home] = pack_ref[r]

    waits += spread_blocks(
        dims,
        place,
        n_dp,
        True,
        None,
        lambda k: whole_ref.at[c, d, r],
        param_slot,
        param_sems,
        send_experts,
    )
    def whole_cols(col, begin, wide):
        return whole_ref[col, :, :, :, begin : begin + wide].reshape(D, wide)

    total = tokens_ref.shape[0]
    valid, allowed = token_masks(lengths_ref, total, lengths_ref.shape[1])
    small = whole_cols(0, wide_qkv + wide_out, LANES)
    vectors = row_vectors_of(small, route_cols)
    inputs = tokens_ref[...].astype(jnp.float32)
    scale_one = lax.rsqrt(jnp.mean(inputs * inputs, axis=-1, keepdims=True) + NORM_EPS)
    h_one = (inputs * scale_one * vectors[0:1]).astype(low)
    for i in range(n_col):
        qkv_ref[:, i * wide_qkv : (i + 1) * wide_qkv] = dot(h_one, whole_cols(i, 0, wide_qkv)).astype(
            low
        )
    attention_forward(qkv_ref, probs_ref, mixed_ref, allowed)
    for i in range(n_col):
        cols = slice(i * wide_out, (i + 1) * wide_out)
        attn_out = dot(mixed_ref[...], whole_cols(i, wide_qkv, wide_out))
        first_ref[:, cols] = tokens_ref[:, cols].astype(jnp.float32) + valid * attn_out
    first_sum = first_ref[...]
    scale_two = lax.rsqrt(jnp.mean(first_sum * first_sum, axis=-1, keepdims=True) + NORM_EPS)
    h_two = (first_sum * scale_two * vectors[1:2]).astype(low)
    experts = prev_ref.shape[0]
    turn_ref[...] = jnp.zeros_like(turn_ref)
    turn_ref[:experts] = prev_ref[...]
    turn_ref[experts : experts + 2] = routes_ref[...].astype(jnp.float32)
    turned = turn_ref[...].T
    logits_all = dot(h_two, small)
    lane = lax.broadcasted_iota(jnp.int32, (total, LANES), 1)
    logits = logits_all + jnp.where(lane < experts, turned, 0.0)
    route_first = column(turned, experts).astype(jnp.int32)
    route_second = column(turned, experts + 1).astype(jnp.int32)
    pick_first = (lane == route_first).astype(jnp.float32)
    pick_second = (lane == route_second).astype(jnp.float32)
    gates = two_way(
        jnp.sum(pick_first * logits, axis=-1, keepdims=True),
        jnp.sum(pick_second * logits, axis=-1, keepdims=True),
    )
    mix_base = num_ffn + 4
    mixes = []
    for i in range(2):
        mixes += two_way(
            column(logits_all, mix_base + 2 * i), column(logits_all, mix_base + 2 * i + 1)
        )
    before = lax.broadcasted_iota(jnp.int32, (total, total), 0) > lax.broadcasted_iota(
        jnp.int32, (total, total), 1
    )
    earlier = dot(before.astype(low), (pick_first + pick_second).astype(low))
    in_slots = []
    for route, pick in ((route_first, pick_first), (route_second, pick_second)):
        slot_index = jnp.sum(earlier * pick, axis=-1, keepdims=True)
        where_in = (route * CAP).astype(jnp.float32) + slot_index
        in_slots.append(jnp.where(route < num_ffn, where_in, -1.0))
    slots = num_ffn * CAP
    slot_lane = lax.broadcasted_iota(jnp.int32, (total, slots), 1).astype(jnp.float32)
    places = [(slot_lane == where_in).astype(low) for where_in in in_slots]
    grad_y = cotangent_ref[...].astype(jnp.float32) * valid
    sent = dot(places[0] + places[1], h_two, TN).astype(low)
    made = dot(places[0], (gates[0] * grad_y).astype(low), TN) + dot(
        places[1], (gates[1] * grad_y).astype(low), TN
    )
    stage_ref[:, :, :D] = sent.reshape(num_ffn, CAP, D)
    stage_ref[:, :, D:] = made.astype(low).reshape(num_ffn, CAP, D)

    def token_slot(col, j, b):
        k = j[1] if isinstance(j, tuple) else (d + n_dp - j) % n_dp
        return arrived_ref.at[(col * n_dp + k) * n_row + b]

    arrived_ref[(c * n_dp + d) * n_row + r] = stage_ref[d]
    waits += spread_blocks(
        dims, place, n_dp, True, None, lambda k: stage_ref.at[k], token_slot, token_sems
    )
    for i in range(1, n_row):
        home = pl.ds(pl.multiple_of(((r + n_row - i) % n_row) * depth, 16), depth)
        ref = expert_ref.at[:, home]
        remote(ref, ref, expert_send.at[i], expert_recv.at[i], (d, r, c)).wait_recv()

    wides = [right_root_gu.at[0], right_root_gu.at[1], left_root_down]
    tiles = left_root_down.shape[0] // tile
    tile_loads = []

    def load_tile(n):
        if n < 3 * tiles:
            copy = pltpu.make_async_copy(
                wides[n // tiles].at[pl.ds(n % tiles * tile, tile)],
                tile_ref.at[n % held],
                tile_sem.at[n],
            )
            copy.start()
            tile_loads.append(copy)

    for n in range(held):
        load_tile(n)

    def token_back(t, j, block):
        if j == 0:
            came_ref[d] = block[...]
        else:
            copy = remote(
                block, came_ref.at[d], came_send.at[j], came_recv.at[j], ((d + j) % n_dp, r, c)
            )
            copy.start()
            waits.append(copy.wait_send)

    tokens_plan = plan_reduce(
        dims,
        place,
        lambda col, k: part_ref.at[col, k, :, pl.ds(0, CAP), pl.ds(0, 2 * D)],
        token_scratch[:3],
        token_scratch[3:],
        token_back,
        direct=True,
    )

    blocks = arrived_ref.shape[0]
    group = 2
    tall = group * n_row * CAP
    for i in [*range(1, n_col), 0]:
        col = (c + i) % n_col

        @pl.loop(0, n_dp // group)
        def _(t):
            first = (col * n_dp + t * group) * n_row
            some = arrived_ref[pl.ds(first, group * n_row)].reshape(tall, 2 * D)
            rows_in = some[:, :D]
            grads_in = some[:, D:]
            span = pl.ds(pl.multiple_of(first * CAP, tall), tall)
            gate_part = dot(rows_in, expert_ref[0])
            up_part = dot(rows_in, expert_ref[1])
            grad_hidden = dot(grads_in, expert_ref[2])
            sigma = jax.nn.sigmoid(gate_part)
            silu = gate_part * sigma
            hidden = (silu * up_part).astype(low)
            grad_gate = (
                grad_hidden * up_part * sigma * (1.0 + gate_part * (1.0 - sigma))
            ).astype(low)
            grad_up = (grad_hidden * silu).astype(low)
            hidden_ref[span] = hidden
            pre_ref[span, :slice_wide] = grad_gate
            pre_ref[span, slice_wide:] = grad_up
            made_rows = dot(hidden, expert_ref[2], NT).astype(low)
            grad_rows = dot(grad_gate, expert_ref[0], NT) + dot(grad_up, expert_ref[1], NT)
            ks = pl.ds(t * group, group)
            shape = (group, n_row, CAP, D)
            part_ref[col, ks, :, :CAP, :D] = made_rows.reshape(shape)
            part_ref[col, ks, :, :CAP, D : 2 * D] = grad_rows.astype(low).reshape(shape)

        if i:
            tokens_plan.send_cols(i)

    for t in range(n_dp):
        tokens_plan.sum_cols(t)
    all_rows = arrived_ref[:, :, :D].reshape(blocks * CAP, D)
    all_grads = arrived_ref[:, :, D:].reshape(blocks * CAP, D)
    for m in range(2):
        grads_ref[m * D : (m + 1) * D] = dot(
            all_rows, pre_ref[:, m * slice_wide : (m + 1) * slice_wide], TN
        ).astype(low)
    grads_ref[2 * D :] = dot(all_grads, hidden_ref[...], TN).astype(low)
    for s in range(bits_of(n_row) - 1):
        for t in range(n_dp):
            tokens_plan.sum_rows(t, s)

    tall = grads_ref.shape[0] // chunks
    gather = plan_spread(
        dims,
        place,
        chunks,
        False,
        lambda j: grads_ref.at[pl.ds(j * tall, tall)],
        None,
        lambda col, j, b: gathered_ref.at[col * n_row + b, pl.ds(j * tall, tall)],
        gather_sems,
    )
    for j in range(chunks):
        gather.start(j)
    for t in range(n_dp):
        tokens_plan.sum_rows(t, bits_of(n_row) - 1)

    gain_one, gain_two = vectors[0:1], vectors[1:2]
    const_rows = [vectors[2:3], vectors[3:4]]
    mixes = [mixes[:2], mixes[2:]]
    routes = [route_first, route_second]
    picks = [pick_first, pick_second]
    cotangent = cotangent_ref[...].astype(jnp.float32)
    grad_y = cotangent * valid
    grad_y_low = grad_y.astype(low)
    first_sum = first_ref[...]
    scale_two = lax.rsqrt(jnp.mean(first_sum * first_sum, axis=-1, keepdims=True) + NORM_EPS)
    normed_two = first_sum * scale_two
    h_two = normed_two * gain_two
    h_two_low = h_two.astype(low)
    const_sel = [
        [(route == num_ffn + 2 + n).astype(jnp.float32) for n in range(2)] for route in routes
    ]
    for j in range(1, n_dp):
        ref = came_ref.at[(d + n_dp - j) % n_dp]
        remote(ref, ref, came_send.at[j], came_recv.at[j], (d, r, c)).wait_recv()
    expert_out = came_ref[:, :, :D].reshape(slots, D)
    grad_sent = came_ref[:, :, D:].reshape(slots, D)
    moe_out = jnp.zeros_like(first_sum)
    grad_gates = []
    own_weight = jnp.zeros((total, 1), jnp.float32)
    for n in range(2):
        own = (routes[n] == num_ffn + 1).astype(jnp.float32)
        for i in range(2):
            own = own + const_sel[n][i] * mixes[i][0]
        output = dot(places[n], expert_out) + own * h_two
        for i in range(2):
            output = output + const_sel[n][i] * mixes[i][1] * const_rows[i]
        moe_out = moe_out + gates[n] * output
        grad_gates.append(jnp.sum(grad_y * output, axis=-1, keepdims=True))
        own_weight = own_weight + gates[n] * own
    result_ref[...] = (first_sum + valid * moe_out).astype(low)
    mean_gate = gates[0] * grad_gates[0] + gates[1] * grad_gates[1]
    grad_logits = sum(gates[n] * (grad_gates[n] - mean_gate) * picks[n] for n in range(2))
    grad_own = jnp.sum(grad_y * h_two, axis=-1, keepdims=True)
    const_lanes = jnp.zeros((total, LANES), jnp.float32)
    for i in range(2):
        weight = const_sel[0][i] * gates[0] + const_sel[1][i] * gates[1]
        mix_grads = [
            weight * grad_own,
            weight * jnp.sum(grad_y * const_rows[i], axis=-1, keepdims=True),
        ]
        mean_mix = mixes[i][0] * mix_grads[0] + mixes[i][1] * mix_grads[1]
        for n in range(2):
            grad_mix = mixes[i][n] * (mix_grads[n] - mean_mix)
            grad_logits = jnp.where(lane == num_ffn + 4 + 2 * i + n, grad_mix, grad_logits)
        const_lanes = jnp.where(lane == route_cols + 2 + i, weight * mixes[i][1], const_lanes)
    grad_logits = grad_logits.astype(low)

    grad_h_two = (
        dot(grad_logits, small, NT) + dot(places[0] + places[1], grad_sent) + own_weight * grad_y
    )
    grad_normed = grad_h_two * gain_two
    inner_mean = jnp.mean(grad_normed * normed_two, axis=-1, keepdims=True)
    grad_first = scale_two * (grad_normed - normed_two * inner_mean) + cotangent
    grad_tokens_ref[...] = grad_first
    grad_attn_ref[...] = (valid * grad_first).astype(low)
    grad_small = (
        dot(h_two_low, grad_logits, TN)
        + dot(grad_y_low, const_lanes.astype(low), TN)
        + dot((grad_h_two * normed_two).astype(low), (lane == route_cols + 1).astype(low), TN)
    )
    grad_mixed = jnp.zeros((total, D), jnp.float32)
    for i in range(n_col):
        grad_mixed = grad_mixed + dot(
            grad_attn_ref[:, i * wide_out : (i + 1) * wide_out],
            whole_cols(i, wide_qkv, wide_out),
            NT,
        )
    grad_mixed_ref[...] = grad_mixed.astype(low)
    attention_backward(qkv_ref, probs_ref, grad_mixed_ref, grad_qkv_ref)
    grad_h_one = jnp.zeros((total, D), jnp.float32)
    for i in range(n_col):
        grad_h_one = grad_h_one + dot(
            grad_qkv_ref[:, i * wide_qkv : (i + 1) * wide_qkv], whole_cols(i, 0, wide_qkv), NT
        )
    inputs = tokens_ref[...].astype(jnp.float32)
    scale_one = lax.rsqrt(jnp.mean(inputs * inputs, axis=-1, keepdims=True) + NORM_EPS)
    normed_one = inputs * scale_one
    h_one = (normed_one * gain_one).astype(low)
    grad_normed = grad_h_one * gain_one
    inner_mean = jnp.mean(grad_normed * normed_one, axis=-1, keepdims=True)
    grad_tokens_ref[...] += scale_one * (grad_normed - normed_one * inner_mean)
    grad_small = grad_small + dot(
        (grad_h_one * normed_one).astype(low), (lane == route_cols).astype(low), TN
    )

    kept = []

    def param_back(t, j, block):
        if j == 0:
            kept.append(block)
        else:
            copy = remote(
                block, dp_ref.at[j], dp_send.at[j], dp_recv.at[j], ((d + j) % n_dp, r, c)
            )
            copy.start()
            waits.append(copy.wait_send)

    params_plan = plan_reduce(
        dims,
        place,
        lambda col, k: part_ref.at[col, k],
        param_scratch[:3],
        param_scratch[3:],
        param_back,
        direct=True,
    )
    finish([copy.wait_send for copy in tokens_plan.sent])
    blocked = part_ref.shape[1:4]
    for i in [*range(1, n_col), 0]:
        col = (c + i) % n_col
        qkv_cols = pl.ds(pl.multiple_of(col * wide_qkv, LANES), wide_qkv)
        out_cols = pl.ds(pl.multiple_of(col * wide_out, LANES), wide_out)
        part_ref[col, :, :, :, :wide_qkv] = (
            dot(h_one, grad_qkv_ref[:, qkv_cols], TN).astype(low).reshape(*blocked, wide_qkv)
        )
        part_ref[col, :, :, :, wide_qkv : wide_qkv + wide_out] = (
            dot(mixed_ref[...], grad_attn_ref[:, out_cols], TN)
            .astype(low)
            .reshape(*blocked, wide_out)
        )
        part_ref[col, :, :, :, wide_qkv + wide_out :] = grad_small.astype(low).reshape(
            *blocked, LANES
        )
        if i:
            params_plan.send_cols(i)
    for t in range(n_dp):
        params_plan.sum_cols(t)
    gather.pass_on(0)
    for t in range(n_dp):
        params_plan.sum_rows(t, 0)
    for j in range(1, chunks):
        gather.pass_on(j)
    for s in range(1, bits_of(n_row)):
        for t in range(n_dp):
            params_plan.sum_rows(t, s)

    owner = r * n_col + c
    right_rows = right_sum_ref.shape[1]
    left_rows = left_sum_ref.shape[0]
    stores = []

    def store(m, kind, src, dst):
        copy = pltpu.make_async_copy(src, dst, store_sem.at[m, kind])
        copy.start()
        stores.append(copy)

    def shampoo_products(m):
        for j in range(m * chunks // 3, (m + 1) * chunks // 3):
            gather.last_arrivals(j)
        for j in range(m * chunks // 3, (m + 1) * chunks // 3):
            gather.wait_cols(j)
        span = pl.ds(m * D, D)
        home = pl.ds(pl.multiple_of(m * D + r * depth, 16), depth)
        for b in range(n_row):
            store(m, 3 + b, gathered_ref.at[c * n_row + b, home], block_out.at[m, b])
        root_loads[m].wait()
        lhs_ref[:right_rows] = gathered_ref[owner, span].T
        lhs_ref[right_rows:] = root_ref[m].astype(low)
        left_sum_ref[...] = jnp.zeros_like(left_sum_ref)

        @pl.loop(0, n_row * n_col)
        def _(q):
            cols = pl.ds(pl.multiple_of(q * slice_wide, slice_wide), slice_wide)
            block = gathered_ref[q, span]
            made = dot(lhs_ref[...], block)
            right_sum_ref[m, :, cols] = (0.5 * made[:right_rows]).astype(low)
            half_step_ref[:, cols] = made[right_rows:].astype(low)
            some = pl.ds(pl.multiple_of(m * D + owner * left_rows, 16), left_rows)
            left_sum_ref[...] += dot(gathered_ref[q, some], block, NT)

        left_low_ref[m] = (0.5 * left_sum_ref[...]).astype(low)
        store(m, 0, right_sum_ref.at[m], right_sum_out.at[m])
        store(m, 1, left_low_ref.at[m], left_sum_out.at[m])
        for t in range(tiles):
            n = m * tiles + t
            tile_loads[n].wait()
            step = dot(half_step_ref[...], tile_ref[n % held].astype(low), NT)
            step_ref[m, :, t * tile : (t + 1) * tile] = (SHAMPOO_RATE * step).astype(low)
            load_tile(n + held)
        store(m, 2, step_ref.at[m], step_out.at[m])

    shampoo_products(0)
    shampoo_products(1)
    sums = kept[0][...].astype(jnp.float32)
    for j in range(1, n_dp):
        ref = dp_ref.at[j]
        remote(ref, ref, dp_send.at[j], dp_recv.at[j], (d, r, c)).wait_recv()
        sums = sums + dp_ref[j].astype(jnp.float32)
    sum_ref[...] = sums
    for i in range(n_col):
        end_ref[i] = sum_ref[i * rows : (i + 1) * rows, :]
    for i in range(1, n_col):
        other = (c + i) % n_col
        copy = remote(
            end_ref.at[other], summed_ref.at[c], end_send.at[i], end_recv.at[i], (d, r, other)
        )
        copy.start()
        waits.append(copy.wait_send)
    summed_ref[pl.ds(c, 1)] = end_ref[pl.ds(c, 1)]
    shampoo_products(2)
    for i in range(1, n_col):
        ref = summed_ref.at[(c + n_col - i) % n_col]
        remote(ref, ref, end_send.at[i], end_recv.at[i], (d, r, c)).wait_recv()
    waits += gather.sends()
    waits += [copy.wait for copy in stores]
    finish([copy.wait_send for copy in params_plan.sent])
    finish(waits)


def layer(
    lengths,
    routes,
    prev_logits,
    tokens,
    cotangent,
    w_qkv,
    w_out,
    route_w,
    gains,
    const_vec,
    weight_gu,
    weight_down,
    left_root_gu,
    right_root_down,
    right_root_gu,
    left_root_down,
    dims,
    widths,
):
    n_dp, n_row, n_col = dims
    low = jnp.bfloat16
    f32 = jnp.float32
    total = tokens.shape[0]
    rows = w_qkv.shape[0]
    wide = widths[0] + widths[1] + LANES
    num_ffn = prev_logits.shape[0] - 4
    depth, wide_col = weight_down.shape
    slice_wide = wide_col // n_row
    blocks = n_col * n_dp * n_row
    block_rows = n_col * rows
    wide_rows, wide_cols = left_root_down.shape
    right_rows = wide_cols // n_row // n_col
    left_rows = D // n_row // n_col
    tile = LANES
    chunks = 6
    dma = pltpu.SemaphoreType.DMA
    vmem = pl.BlockSpec(memory_space=pltpu.VMEM)
    hbm = pl.BlockSpec(memory_space=pl.ANY)
    whole = (n_col, n_dp, n_row, block_rows, wide)
    assert depth <= 2 * tile and 2 * wide_col <= wide_cols and wide >= 2 * D
    return pl.pallas_call(
        functools.partial(layer_kernel, (dims, num_ffn, *widths, chunks)),
        out_shape=[
            jax.ShapeDtypeStruct((total, D), low),
            jax.ShapeDtypeStruct((total, D), f32),
            jax.ShapeDtypeStruct((n_col, rows, wide), f32),
            jax.ShapeDtypeStruct((3, right_rows, wide_cols), low),
            jax.ShapeDtypeStruct((3, left_rows, D), low),
            jax.ShapeDtypeStruct((3, depth, wide_rows), low),
            jax.ShapeDtypeStruct((3, n_row, depth, slice_wide), low),
        ],
        in_specs=[pl.BlockSpec(memory_space=pltpu.SMEM)] + [vmem] * 9 + [hbm] * 6,
        out_specs=[vmem] * 3 + [hbm] * 4,
        scratch_shapes=[
            pltpu.VMEM((n_col, rows, wide), f32),
            pltpu.VMEM((LANES, LANES), f32),
            pltpu.VMEM((n_col, rows, wide), f32),
            pltpu.VMEM((block_rows, wide), f32),
            pltpu.VMEM(whole, low),
            pltpu.VMEM((n_row, 3, depth, slice_wide), low),
            pltpu.VMEM((3, n_row * depth, slice_wide), low),
            pltpu.VMEM((num_ffn, CAP, 2 * D), low),
            pltpu.VMEM((blocks, CAP, 2 * D), low),
            pltpu.VMEM((blocks * CAP, slice_wide), low),
            pltpu.VMEM((blocks * CAP, 2 * slice_wide), low),
            pltpu.VMEM((3 * D, slice_wide), low),
            pltpu.VMEM((total, 3 * D), low),
            pltpu.VMEM((HEADS, total, total), f32),
            pltpu.VMEM((total, D), low),
            pltpu.VMEM((total, D), f32),
            pltpu.VMEM((n_dp, CAP, 2 * D), low),
            pltpu.VMEM((total, D), low),
            pltpu.VMEM((total, D), low),
            pltpu.VMEM((total, 3 * D), low),
            pltpu.VMEM(whole, low),
            pltpu.VMEM((n_dp, block_rows, wide), low),
            pltpu.VMEM((n_col, rows, wide), f32),
            pltpu.VMEM((block_rows, wide), f32),
            pltpu.VMEM((n_col * n_row, 3 * D, slice_wide), low),
            pltpu.VMEM((3, depth, D), f32),
            pltpu.VMEM((3, tile, wide_cols), f32),
            pltpu.VMEM((depth, wide_cols), low),
            pltpu.VMEM((right_rows + depth, D), low),
            pltpu.VMEM((3, right_rows, wide_cols), low),
            pltpu.VMEM((left_rows, D), f32),
            pltpu.VMEM((3, left_rows, D), low),
            pltpu.VMEM((3, depth, wide_rows), low),
            dma((n_col,)),
            dma((n_col,)),
            dma((3, 2)),
            dma((n_row,)),
            dma((n_row,)),
            dma((3,)),
            dma((3 * wide_rows // tile,)),
            dma((3, 3 + n_row)),
            dma((n_dp,)),
            dma((n_dp,)),
            dma((n_dp,)),
            dma((n_dp,)),
            dma((n_col,)),
            dma((n_col,)),
            *spread_sems(dims, n_dp),
            *spread_sems(dims, n_dp),
            *spread_sems(dims, chunks),
            *reduce_scratch(dims, CAP, 2 * D),
            *reduce_scratch(dims, block_rows, wide),
        ],
        compiler_params=pltpu.CompilerParams(
            collective_id=5, has_side_effects=True, vmem_limit_bytes=VMEM_BYTES
        ),
        name="layer",
    )(
        lengths,
        routes,
        prev_logits,
        tokens,
        cotangent,
        w_qkv,
        w_out,
        route_w,
        gains,
        const_vec,
        weight_gu,
        weight_down,
        left_root_gu,
        right_root_down,
        right_root_gu,
        left_root_down,
    )


def norm_forward(values, gain_vec):
    norm_scale = lax.rsqrt(jnp.mean(values * values, axis=-1, keepdims=True) + NORM_EPS)
    normed = values * norm_scale
    return (normed * gain_vec, normed, norm_scale)


def norm_backward(grad_out, normed, norm_scale, gain_vec):
    grad_normed = grad_out * gain_vec
    inner_mean = jnp.mean(grad_normed * normed, axis=-1, keepdims=True)
    return (norm_scale * (grad_normed - normed * inner_mean), jnp.sum(grad_out * normed, axis=0))


def attention_probs(queries, key_heads, allowed):
    scores = jnp.einsum(
        "qhd,khd->hqk", queries, key_heads, preferred_element_type=jnp.float32
    ) * HEAD ** (-0.5)
    scores = jnp.where(allowed[None], scores, -1e30)
    top_score = jnp.max(scores, axis=-1, keepdims=True)
    exp_scores = jnp.exp(scores - top_score)
    return exp_scores / jnp.sum(exp_scores, axis=-1, keepdims=True)


def diag_update(weight, grad, state, rate):
    new_state = 0.5 * state + 0.5 * grad * grad
    return (new_state, weight - rate * grad / (jnp.sqrt(new_state) + 1e-08))


def diagonal_updates(widths, n_col, summed_ref, in_refs, out_refs, turn_ref):
    wide_qkv, wide_out, route_cols = widths
    rows = summed_ref.shape[1]
    rates = (D ** (-0.5), HEAD ** (-0.5), (4 * D) ** (-0.5), 0.3, 0.5)

    def update(n, cols, grad):
        weight, state = in_refs[2 * n], in_refs[2 * n + 1]
        grad_ref, moment_ref, new_ref = out_refs[3 * n : 3 * n + 3]
        moment, new = diag_update(weight[:, cols], grad, state[:, cols], rates[n])
        grad_ref[:, cols] = grad
        moment_ref[:, cols] = moment
        new_ref[:, cols] = new

    for i in range(n_col):
        update(0, pl.ds(i * wide_qkv, wide_qkv), summed_ref[i, :, :wide_qkv])
        update(
            1, pl.ds(i * wide_out, wide_out), summed_ref[i, :, wide_qkv : wide_qkv + wide_out]
        )
    turn_ref[...] = jnp.zeros_like(turn_ref)
    turn_ref[:rows] = summed_ref[0, :, wide_qkv + wide_out :]
    turned = turn_ref[...].T
    whole = pl.ds(0, rows)
    update(2, whole, turned[:route_cols, :rows])
    update(3, whole, turned[route_cols : route_cols + 2, :rows])
    update(4, whole, turned[route_cols + 2 : route_cols + 4, :rows])


def finish_kernel(sizes, *refs):
    n_col, widths = sizes
    (
        right_sum,
        left_sum,
        step,
        block,
        left_gu,
        right_down,
        right_gu,
        left_down,
        weight_gu,
        weight_down,
        result,
        grad_tokens,
        summed,
        *diag,
        out_grad_gu,
        out_grad_down,
        out_left_gu,
        out_right_down,
        out_right_gu,
        out_left_down,
        out_weight_gu,
        out_weight_down,
        out_result,
        out_grad_tokens,
        right_sum_buf,
        left_sum_buf,
        step_buf,
        block_buf,
        right_buf,
        left_buf,
        weight_buf,
        grad_buf,
        result_buf,
        tokens_buf,
        turn_buf,
        in_sem,
        out_sem,
    ) = refs
    diag_in, diag_out = diag[:10], diag[10:]
    mats = range(3)
    f32 = jnp.float32
    n_row, _, slice_wide = block_buf.shape[1:]
    lefts = [left_gu.at[0], left_gu.at[1], right_down]
    rights = [right_gu.at[0], right_gu.at[1], left_down]
    weights = [weight_gu.at[:, 0], weight_gu.at[:, 1], weight_down]
    out_lefts = [out_left_gu.at[0], out_left_gu.at[1], out_right_down]
    out_rights = [out_right_gu.at[0], out_right_gu.at[1], out_left_down]
    out_weights = [out_weight_gu.at[:, 0], out_weight_gu.at[:, 1], out_weight_down]
    out_grads = [out_grad_gu.at[:, 0], out_grad_gu.at[:, 1], out_grad_down]
    loads = {}

    def load(m, kind, src, dst):
        copy = pltpu.make_async_copy(src, dst, in_sem.at[m, kind])
        copy.start()
        loads[m, kind] = copy

    stores = []

    def store(m, kind, src, dst):
        copy = pltpu.make_async_copy(src, dst, out_sem.at[m, kind])
        copy.start()
        stores.append(copy)

    for m in mats:
        load(m, 0, right_sum.at[m], right_sum_buf.at[m])
        load(m, 1, rights[m], right_buf.at[m])
        load(m, 2, block.at[m], block_buf.at[m])
        load(m, 3, step.at[m], step_buf.at[m])
        load(m, 4, weights[m], weight_buf.at[m])
        load(m, 5, left_sum.at[m], left_sum_buf.at[m])
        load(m, 6, lefts[m], left_buf.at[m])
    load(0, 7, result, result_buf)
    load(1, 7, grad_tokens, tokens_buf)
    diagonal_updates(widths, n_col, summed, diag_in, diag_out, turn_buf)
    for m in mats:
        loads[m, 0].wait()
        loads[m, 1].wait()
        right_buf[m] = 0.5 * right_buf[m] + right_sum_buf[m].astype(f32)
        store(m, 0, right_buf.at[m], out_rights[m])
        loads[m, 2].wait()
        for b in range(n_row):
            grad_buf[m, :, b * slice_wide : (b + 1) * slice_wide] = block_buf[m, b].astype(f32)
        store(m, 1, grad_buf.at[m], out_grads[m])
        loads[m, 3].wait()
        loads[m, 4].wait()
        weight_buf[m] = weight_buf[m] - step_buf[m].astype(f32)
        store(m, 2, weight_buf.at[m], out_weights[m])
        loads[m, 5].wait()
        loads[m, 6].wait()
        left_buf[m] = 0.5 * left_buf[m] + left_sum_buf[m].astype(f32)
        store(m, 3, left_buf.at[m], out_lefts[m])
    loads[0, 7].wait()
    store(0, 4, result_buf, out_result)
    loads[1, 7].wait()
    store(1, 4, tokens_buf, out_grad_tokens)
    for copy in stores:
        copy.wait()


def finish_update(
    products,
    left_gu,
    right_down,
    right_gu,
    left_down,
    weight_gu,
    weight_down,
    result,
    grad_tokens,
    summed,
    diag_in,
    n_col,
    widths,
):
    f32 = jnp.float32
    dma = pltpu.SemaphoreType.DMA
    hbm = pl.BlockSpec(memory_space=pl.ANY)
    vmem = pl.BlockSpec(memory_space=pltpu.VMEM)
    right_sum, left_sum, step, block = products
    args = (
        *products,
        left_gu,
        right_down,
        right_gu,
        left_down,
        weight_gu,
        weight_down,
        result,
        grad_tokens,
        summed,
        *diag_in,
    )
    outs = [weight for weight in diag_in[::2] for _ in range(3)]
    outs += [weight_gu, weight_down, left_gu, right_down, right_gu, left_down]
    outs += [weight_gu, weight_down, result, grad_tokens]
    return pl.pallas_call(
        functools.partial(finish_kernel, (n_col, widths)),
        out_shape=[jax.ShapeDtypeStruct(like.shape, like.dtype) for like in outs],
        in_specs=[hbm] * 12 + [vmem] * 11,
        out_specs=[vmem] * 15 + [hbm] * 10,
        scratch_shapes=[
            pltpu.VMEM(right_sum.shape, right_sum.dtype),
            pltpu.VMEM(left_sum.shape, left_sum.dtype),
            pltpu.VMEM(step.shape, step.dtype),
            pltpu.VMEM(block.shape, block.dtype),
            pltpu.VMEM(right_sum.shape, f32),
            pltpu.VMEM(left_sum.shape, f32),
            pltpu.VMEM(step.shape, f32),
            pltpu.VMEM(step.shape, f32),
            pltpu.VMEM(result.shape, result.dtype),
            pltpu.VMEM(grad_tokens.shape, f32),
            pltpu.VMEM((LANES, LANES), f32),
            dma((3, 8)),
            dma((3, 5)),
        ],
        compiler_params=pltpu.CompilerParams(vmem_limit_bytes=VMEM_BYTES),
        name="finish",
    )(*args)


def shampoo_plain(
    grads,
    left_root_gu,
    right_root_down,
    right_root_gu,
    left_root_down,
    left_gu,
    right_down,
    right_gu,
    left_down,
    weight_gu,
    weight_down,
    n_row,
    n_col,
):
    low = jnp.bfloat16
    blocks, _, slice_wide = grads.shape
    model = left_root_gu.shape[2]
    r = lax.axis_index("row")
    c = lax.axis_index("col")
    owner = r * n_col + c
    left_rows = right_down.shape[0]
    right_rows = left_down.shape[0]
    product = functools.partial(jnp.einsum, preferred_element_type=jnp.float32)
    whole = grads.reshape(blocks, 3, model, slice_wide).transpose(1, 2, 0, 3).reshape(3, model, -1)
    mine_left = lax.dynamic_slice_in_dim(whole, owner * left_rows, left_rows, 1)
    mine_right = lax.dynamic_slice_in_dim(whole, owner * right_rows, right_rows, 2)
    left_sum = 0.5 * product("mif,mjf->mij", mine_left, whole)
    right_sum = 0.5 * product("mdi,mdj->mij", mine_right, whole)
    roots = jnp.concatenate([left_root_gu, right_root_down[None]]).astype(low)
    wides = jnp.concatenate([right_root_gu, left_root_down[None]]).astype(low)
    step = product("mid,mdf->mif", roots, whole).astype(low)
    step = SHAMPOO_RATE * product("mif,mjf->mij", step, wides)
    depth, wide_rows = weight_down.shape
    block = lax.dynamic_slice(whole, (0, r * depth, c * wide_rows), (3, depth, wide_rows))
    block = block.astype(jnp.float32)
    return (
        block[:2].transpose(1, 0, 2),
        block[2],
        0.5 * left_gu + left_sum[:2],
        0.5 * right_down + left_sum[2],
        0.5 * right_gu + right_sum[:2],
        0.5 * left_down + right_sum[2],
        weight_gu - step[:2].transpose(1, 0, 2),
        weight_down - step[2],
    )


def body_tiled(
    tokens,
    lengths,
    routes,
    prev_logits,
    cotangent,
    w_qkv,
    w_out,
    route_w,
    gains,
    const_vec,
    stat_qkv,
    stat_out,
    stat_route,
    stat_gains,
    stat_const,
    w_gate_up,
    w_down,
    left_gu,
    right_gu,
    left_down,
    right_down,
    left_root_gu,
    right_root_gu,
    left_root_down,
    right_root_down,
):
    dims = mesh_sizes()
    n_col = dims[2]
    wide_qkv = w_qkv.shape[1] // n_col
    wide_out = w_out.shape[1] // n_col
    widths = (wide_qkv, wide_out, route_w.shape[1])
    result, grad_input, summed, *products = layer(
        lengths,
        routes.T,
        prev_logits.T,
        tokens,
        cotangent,
        w_qkv,
        w_out,
        route_w.T,
        gains,
        const_vec,
        w_gate_up[0],
        w_down[0].T,
        left_root_gu[0],
        right_root_down[0],
        right_root_gu[0],
        left_root_down[0],
        dims,
        widths,
    )
    outs = finish_update(
        products,
        left_gu[0],
        right_down[0],
        right_gu[0],
        left_down[0],
        w_gate_up[0],
        w_down[0].T,
        result,
        grad_input,
        summed,
        [
            w_qkv,
            stat_qkv,
            w_out,
            stat_out,
            route_w.T,
            stat_route.T,
            gains,
            stat_gains,
            const_vec,
            stat_const,
        ],
        n_col,
        widths,
    )
    diag = list(outs[:15])
    diag[6:9] = [part.T for part in diag[6:9]]
    (
        grad_gate_up,
        grad_down,
        new_left_gu,
        new_right_down,
        new_right_gu,
        new_left_down,
        new_gate_up,
        new_down,
        result,
        grad_input,
    ) = outs[15:]
    return (
        result,
        grad_input,
        *diag,
        grad_gate_up[None],
        grad_down.T[None],
        new_left_gu[None],
        new_right_gu[None],
        new_left_down[None],
        new_right_down[None],
        new_gate_up[None],
        new_down.T[None],
    )


def body(
    tokens,
    lengths,
    routes,
    prev_logits,
    cotangent,
    w_qkv,
    w_out,
    route_w,
    gains,
    const_vec,
    stat_qkv,
    stat_out,
    stat_route,
    stat_gains,
    stat_const,
    w_gate_up,
    w_down,
    left_gu,
    right_gu,
    left_down,
    right_down,
    left_root_gu,
    right_root_gu,
    left_root_down,
    right_root_down,
):
    dims = mesh_sizes()
    n_dp, n_row, n_col = dims
    low = jnp.bfloat16
    row_total = tokens.shape[0]
    total_experts = prev_logits.shape[1]
    num_ffn = total_experts - 4
    seq_count = lengths.shape[1]
    shard_rows = w_qkv.shape[0]
    wide_qkv = w_qkv.shape[1] // n_col
    wide_out = w_out.shape[1] // n_col
    route_cols = route_w.shape[1]
    wide = wide_qkv + wide_out + LANES

    def by_col(matrix):
        return matrix.reshape(matrix.shape[0], n_col, -1).transpose(1, 0, 2)

    def small_block(route_part, gain_part, const_part):
        together = jnp.concatenate([route_part, gain_part.T, const_part.T], axis=1)
        return jnp.pad(together, ((0, 0), (0, LANES - together.shape[1])))

    small = small_block(route_w, gains, const_vec)
    shard = jnp.concatenate(
        [by_col(w_qkv), by_col(w_out), jnp.broadcast_to(small[None], (n_col, shard_rows, LANES))],
        axis=2,
    )
    whole = param_gather(shard, dims).reshape(n_col, D, wide)
    full_qkv = [whole[i, :, :wide_qkv] for i in range(n_col)]
    full_out = [whole[i, :, wide_qkv : wide_qkv + wide_out] for i in range(n_col)]
    full_small = whole[0, :, wide_qkv + wide_out :]
    full_route = full_small[:, :route_cols]
    row_vectors = full_small[:, route_cols : route_cols + 4].T.astype(jnp.float32)
    gain_one, gain_two, const_rows = row_vectors[0], row_vectors[1], row_vectors[2:4]

    row_depth = w_gate_up.shape[1]
    col_width = w_gate_up.shape[3]
    slice_wide = col_width // n_row
    gu_slices = w_gate_up[0].astype(low).reshape(row_depth, 2, n_row, slice_wide)
    gu_slices = gu_slices.transpose(2, 0, 1, 3)
    gu_own = lax.all_to_all(gu_slices, "row", split_axis=0, concat_axis=0, tiled=True)
    gu_own = gu_own.reshape(n_row * row_depth, 2 * slice_wide)
    down_slices = w_down[0].astype(low).reshape(n_row, slice_wide, row_depth)
    down_own = lax.all_to_all(down_slices, "row", split_axis=0, concat_axis=0, tiled=True)
    down_own = down_own.transpose(1, 0, 2).reshape(slice_wide, n_row * row_depth)

    positions = jnp.arange(row_total, dtype=jnp.int32)
    seq_ends = jnp.cumsum(lengths[0])
    doc_index = jnp.sum((positions[:, None] >= seq_ends[None, :]).astype(jnp.int32), axis=1)
    valid_rows = (doc_index < seq_count).astype(jnp.float32)[:, None]
    allowed = (doc_index[:, None] == doc_index[None, :]) & (
        positions[:, None] >= positions[None, :]
    )
    inputs = tokens.astype(jnp.float32)
    h_one, normed_one, scale_one = norm_forward(inputs, gain_one)
    h_one_low = h_one.astype(low)
    qkv_rows = jnp.concatenate([dot(h_one_low, part) for part in full_qkv], axis=1).astype(low)
    qkv_rows = qkv_rows.reshape(row_total, 3, HEADS, HEAD)
    queries, key_heads, values = (qkv_rows[:, 0], qkv_rows[:, 1], qkv_rows[:, 2])
    softmax_probs = attention_probs(queries, key_heads, allowed)
    probs_low = softmax_probs.astype(low)
    mixed_heads = jnp.einsum("hqk,khd->qhd", probs_low, values, preferred_element_type=jnp.float32)
    mixed_heads = mixed_heads.reshape(row_total, D).astype(low)
    attn_out = jnp.concatenate([dot(mixed_heads, part) for part in full_out], axis=1)
    first_sum = inputs + valid_rows * attn_out
    h_two, normed_two, scale_two = norm_forward(first_sum, gain_two)
    h_two_low = h_two.astype(low)
    logits_all = dot(h_two_low, full_route)
    logits = logits_all[:, :total_experts] + prev_logits
    pick_table = (
        routes[:, :, None] == jnp.arange(total_experts, dtype=jnp.int32)[None, None, :]
    ).astype(jnp.float32)
    chosen = jnp.sum(pick_table * logits[:, None, :], axis=-1)
    gate_weights = jax.nn.softmax(chosen, axis=-1)
    const_mix = jax.nn.softmax(logits_all[:, total_experts:].reshape(row_total, 2, 2), axis=-1)

    earlier = dot(
        (positions[:, None] > positions[None, :]).astype(low),
        jnp.sum(pick_table, axis=1).astype(low),
    )
    slot_index = jnp.sum(earlier[:, None, :] * pick_table, axis=-1).astype(jnp.int32)
    where_in = jnp.where(routes < num_ffn, routes * CAP + slot_index, -1)
    slot_ids = jnp.arange(num_ffn * CAP, dtype=jnp.int32)
    place_first = where_in[:, 0:1] == slot_ids[None, :]
    place_second = where_in[:, 1:2] == slot_ids[None, :]
    place_both = (place_first | place_second).astype(low)
    slot_gate = jnp.sum(
        place_first.astype(jnp.float32) * gate_weights[:, 0:1]
        + place_second.astype(jnp.float32) * gate_weights[:, 1:2],
        axis=0,
    )
    grad_y = cotangent.astype(jnp.float32) * valid_rows
    sent_rows = dot(place_both, h_two_low, TN).astype(low)
    grad_made = (slot_gate[:, None] * dot(place_both, grad_y.astype(low), TN)).astype(low)
    sent_both = jnp.concatenate(
        [sent_rows.reshape(num_ffn, CAP, D), grad_made.reshape(num_ffn, CAP, D)], axis=2
    )

    arrived = token_gather(sent_both, dims).reshape(-1, 2 * D)
    rows_in = arrived[:, :D]
    grads_in = arrived[:, D:]
    pre_act = dot(rows_in, gu_own)
    gate_part = pre_act[:, :slice_wide]
    up_part = pre_act[:, slice_wide:]
    sigma = jax.nn.sigmoid(gate_part)
    silu = gate_part * sigma
    hidden = (silu * up_part).astype(low)
    made_rows = dot(hidden, down_own).astype(low)
    grad_hidden = dot(grads_in, down_own, NT)
    grad_pre = jnp.concatenate(
        [
            grad_hidden * up_part * sigma * (1.0 + gate_part * (1.0 - sigma)),
            grad_hidden * silu,
        ],
        axis=1,
    ).astype(low)
    grad_rows = dot(grad_pre, gu_own, NT).astype(low)
    parts_back = jnp.concatenate([made_rows, grad_rows], axis=1)
    parts_back = parts_back.reshape(n_col, n_dp, n_row, CAP, 2 * D)
    came_back = token_reduce(parts_back, dims).reshape(num_ffn * CAP, 2 * D)
    expert_out = came_back[:, :D]
    grad_sent = came_back[:, D:]

    grad_gu_own = dot(rows_in, grad_pre, TN).astype(low)
    grad_down_own = dot(hidden, grads_in, TN).astype(low)
    grads_own = jnp.concatenate(
        [grad_gu_own[:, :slice_wide], grad_gu_own[:, slice_wide:], grad_down_own.T], axis=0
    )
    gathered = plane_gather(grads_own.reshape(4, -1, slice_wide), dims)
    gathered = gathered.reshape(n_col * n_row, 3 * D, slice_wide)

    is_ffn_first = dot(place_first.astype(low), expert_out)
    is_ffn_second = dot(place_second.astype(low), expert_out)
    picked = jnp.stack([is_ffn_first, is_ffn_second], axis=1)
    copy_sel = (routes == num_ffn + 1).astype(jnp.float32)
    const_sel = (
        routes[:, :, None] == num_ffn + 2 + jnp.arange(2, dtype=jnp.int32)[None, None, :]
    ).astype(jnp.float32)
    const_out = (
        const_mix[:, :, 0:1] * h_two[:, None, :] + const_mix[:, :, 1:2] * const_rows[None, :, :]
    )
    outputs = (
        picked
        + copy_sel[:, :, None] * h_two[:, None, :]
        + const_sel[:, :, 0:1] * const_out[:, None, 0, :]
        + const_sel[:, :, 1:2] * const_out[:, None, 1, :]
    )
    moe_out = valid_rows * jnp.sum(gate_weights[:, :, None] * outputs, axis=1)
    result = (first_sum + moe_out).astype(low)
    grad_gate = jnp.sum(grad_y[:, None, :] * outputs, axis=-1)
    grad_chosen = gate_weights * (
        grad_gate - jnp.sum(gate_weights * grad_gate, axis=-1, keepdims=True)
    )
    grad_logits = jnp.sum(grad_chosen[:, :, None] * pick_table, axis=1)
    const_weight = jnp.sum(const_sel * gate_weights[:, :, None], axis=1)
    mix_first = const_weight * jnp.sum(grad_y * h_two, axis=-1, keepdims=True)
    mix_second = const_weight * jnp.stack(
        [jnp.sum(grad_y * const_rows[0], axis=-1), jnp.sum(grad_y * const_rows[1], axis=-1)], axis=1
    )
    grad_mix = jnp.stack([mix_first, mix_second], axis=-1)
    grad_mix_logits = const_mix * (grad_mix - jnp.sum(const_mix * grad_mix, axis=-1, keepdims=True))
    grad_logits_all = jnp.concatenate(
        [grad_logits, grad_mix_logits.reshape(row_total, 4)], axis=1
    ).astype(low)
    grad_route_full = dot(h_two_low, grad_logits_all, TN)
    const_scale = const_weight * const_mix[:, :, 1]
    grad_const_full = jnp.stack(
        [
            jnp.sum(const_scale[:, 0:1] * grad_y, axis=0),
            jnp.sum(const_scale[:, 1:2] * grad_y, axis=0),
        ]
    )
    back_rows = dot(place_both, grad_sent)
    own_weight = jnp.sum(gate_weights * copy_sel, axis=1, keepdims=True) + jnp.sum(
        const_weight * const_mix[:, :, 0], axis=1, keepdims=True
    )
    grad_h_two = dot(grad_logits_all, full_route, NT) + back_rows + own_weight * grad_y
    grad_first, grad_gain_two = norm_backward(grad_h_two, normed_two, scale_two, gain_two)
    grad_first = grad_first + cotangent.astype(jnp.float32)
    grad_attn = (valid_rows * grad_first).astype(low)
    grad_mixed = functools.reduce(
        jnp.add,
        [
            dot(grad_attn[:, i * wide_out : (i + 1) * wide_out], part, NT)
            for i, part in enumerate(full_out)
        ],
    ).astype(low)
    grad_mixed = grad_mixed.reshape(row_total, HEADS, HEAD)
    grad_values = jnp.einsum(
        "hqk,qhd->khd", probs_low, grad_mixed, preferred_element_type=jnp.float32
    )
    grad_probs = jnp.einsum("qhd,khd->hqk", grad_mixed, values, preferred_element_type=jnp.float32)
    grad_scores = softmax_probs * (
        grad_probs - jnp.sum(softmax_probs * grad_probs, axis=-1, keepdims=True)
    )
    grad_scores = grad_scores.astype(low)
    grad_queries = jnp.einsum(
        "hqk,khd->qhd", grad_scores, key_heads, preferred_element_type=jnp.float32
    ) * HEAD ** (-0.5)
    grad_keys = jnp.einsum(
        "hqk,qhd->khd", grad_scores, queries, preferred_element_type=jnp.float32
    ) * HEAD ** (-0.5)
    grad_qkv_rows = (
        jnp.stack([grad_queries, grad_keys, grad_values], axis=1)
        .reshape(row_total, 3 * D)
        .astype(low)
    )
    grad_h_one = functools.reduce(
        jnp.add,
        [
            dot(grad_qkv_rows[:, i * wide_qkv : (i + 1) * wide_qkv], part, NT)
            for i, part in enumerate(full_qkv)
        ],
    )
    grad_input, grad_gain_one = norm_backward(grad_h_one, normed_one, scale_one, gain_one)
    grad_input = grad_input + grad_first
    grad_gains_full = jnp.stack([grad_gain_one, grad_gain_two])

    grad_small = small_block(grad_route_full, grad_gains_full, grad_const_full).astype(low)
    param_parts = jnp.stack(
        [
            jnp.concatenate(
                [
                    dot(h_one_low, grad_qkv_rows[:, i * wide_qkv : (i + 1) * wide_qkv], TN).astype(
                        low
                    ),
                    dot(mixed_heads, grad_attn[:, i * wide_out : (i + 1) * wide_out], TN).astype(
                        low
                    ),
                    grad_small,
                ],
                axis=1,
            )
            for i in range(n_col)
        ]
    )
    summed = param_reduce(
        param_parts.reshape(n_col, n_dp, n_row, n_col * shard_rows, wide), dims
    )

    def from_col(parts):
        return parts.transpose(1, 0, 2).reshape(parts.shape[1], -1)

    grad_qkv = from_col(summed[:, :, :wide_qkv])
    grad_attn_out = from_col(summed[:, :, wide_qkv : wide_qkv + wide_out])
    sum_small = summed[0, :, wide_qkv + wide_out :]
    grad_route = sum_small[:, :route_cols]
    grad_gains = sum_small[:, route_cols : route_cols + 2].T
    grad_const = sum_small[:, route_cols + 2 : route_cols + 4].T
    moment_qkv, new_qkv = diag_update(w_qkv, grad_qkv, stat_qkv, D ** (-0.5))
    moment_attn_out, new_attn_out = diag_update(w_out, grad_attn_out, stat_out, HEAD ** (-0.5))
    moment_route, new_route = diag_update(route_w, grad_route, stat_route, (4 * D) ** (-0.5))
    moment_gains, new_gains = diag_update(gains, grad_gains, stat_gains, 0.3)
    moment_const, new_const = diag_update(const_vec, grad_const, stat_const, 0.5)

    (
        grad_gate_up,
        grad_down,
        new_left_gu,
        new_right_down,
        new_right_gu,
        new_left_down,
        new_gate_up,
        new_down,
    ) = shampoo_plain(
        gathered,
        left_root_gu[0],
        right_root_down[0],
        right_root_gu[0],
        left_root_down[0],
        left_gu[0],
        right_down[0],
        right_gu[0],
        left_down[0],
        w_gate_up[0],
        w_down[0].T,
        n_row,
        n_col,
    )
    return (
        result,
        grad_input,
        grad_qkv,
        moment_qkv,
        new_qkv,
        grad_attn_out,
        moment_attn_out,
        new_attn_out,
        grad_route,
        moment_route,
        new_route,
        grad_gains,
        moment_gains,
        new_gains,
        grad_const,
        moment_const,
        new_const,
        grad_gate_up[None],
        grad_down.T[None],
        new_left_gu[None],
        new_right_gu[None],
        new_left_down[None],
        new_right_down[None],
        new_gate_up[None],
        new_down.T[None],
    )


def solution(mesh):
    placed = (
        P(("dp", "row", "col"), None),
        P(("dp", "row", "col"), None),
        P(("dp", "row", "col"), None),
        P(("dp", "row", "col"), None),
        P(("dp", "row", "col"), None),
        P(("dp", "row", "col"), None),
        P(("dp", "row", "col"), None),
        P(("dp", "row", "col"), None),
        P(None, ("dp", "row", "col")),
        P(None, ("dp", "row", "col")),
        P(("dp", "row", "col"), None),
        P(("dp", "row", "col"), None),
        P(("dp", "row", "col"), None),
        P(None, ("dp", "row", "col")),
        P(None, ("dp", "row", "col")),
        P("dp", "row", None, "col"),
        P("dp", "col", "row"),
        P("dp", None, ("row", "col"), None),
        P("dp", None, ("row", "col"), None),
        P("dp", ("row", "col"), None),
        P("dp", ("row", "col"), None),
        P("dp", None, "row", None),
        P("dp", None, "col", None),
        P("dp", "col", None),
        P("dp", "row", None),
    )
    tiled = 3 * D % (mesh.shape["col"] * LANES) == 0 and D % (mesh.shape["col"] * LANES) == 0
    tiled = tiled and D // mesh.shape["dp"] // mesh.shape["row"] % 16 == 0
    return jax.shard_map(
        body_tiled if tiled else body,
        mesh=mesh,
        in_specs=placed,
        out_specs=(
            P(("dp", "row", "col"), None),
            P(("dp", "row", "col"), None),
            P(("dp", "row", "col"), None),
            P(("dp", "row", "col"), None),
            P(("dp", "row", "col"), None),
            P(("dp", "row", "col"), None),
            P(("dp", "row", "col"), None),
            P(("dp", "row", "col"), None),
            P(("dp", "row", "col"), None),
            P(("dp", "row", "col"), None),
            P(("dp", "row", "col"), None),
            P(None, ("dp", "row", "col")),
            P(None, ("dp", "row", "col")),
            P(None, ("dp", "row", "col")),
            P(None, ("dp", "row", "col")),
            P(None, ("dp", "row", "col")),
            P(None, ("dp", "row", "col")),
            P("dp", "row", None, "col"),
            P("dp", "col", "row"),
            P("dp", None, ("row", "col"), None),
            P("dp", None, ("row", "col"), None),
            P("dp", ("row", "col"), None),
            P("dp", ("row", "col"), None),
            P("dp", "row", None, "col"),
            P("dp", "col", "row"),
        ),
        check_vma=False,
    )
```

```python
import functools
import types

import jax
import jax.numpy as jnp
from jax import lax
from jax.experimental import pallas as pl
from jax.experimental.pallas import tpu as pltpu
from jax.sharding import PartitionSpec as P

D = 768
HEADS = 12
HEAD = 64
CAP = 32
LANES = 128


NORM_EPS = 1e-06
SHAMPOO_RATE = 0.5
MESH = pl.DeviceIdType.MESH
VMEM_BYTES = 62 * 2**20


def dot(left, right, dims=(((1,), (0,)), ((), ()))):
    return lax.dot_general(left, right, dims, preferred_element_type=jnp.float32)


NT = (((1,), (1,)), ((), ()))
TN = (((0,), (0,)), ((), ()))


def flip(index, bit):
    return index + bit * (1 - 2 * ((index // bit) % 2))


def flip_all(index, mask, bits):
    for dim in range(bits):
        if mask & (1 << dim):
            index = flip(index, 1 << dim)
    return index


def dp_order(d, p, count):
    if p == 0:
        return d
    upper = d // max(1, count // 2)
    low_d = d + upper * (count - 1 - 2 * d)
    at = p - 1 + (p - 1 - low_d + count) // count
    return at + upper * (count - 1 - 2 * at)


def mesh_sizes():
    return tuple(lax.axis_size(name) for name in ("dp", "row", "col"))


def bits_of(count):
    bits = count.bit_length() - 1
    assert 1 << bits == count
    return bits


def greet(over_dp, dims, place, all_rows=False):
    n_dp, n_row, n_col = dims
    d, r, c = place
    peers = []
    if over_dp:
        peers += [((d + j) % n_dp, r, c) for j in range(1, n_dp)]
    if all_rows:
        peers += [(d, (r + i) % n_row, c) for i in range(1, n_row)]
    else:
        peers += [(d, flip(r, 1 << dim), c) for dim in range(bits_of(n_row))]
    peers += [(d, r, (c + i) % n_col) for i in range(1, n_col)]
    barrier = pltpu.get_barrier_semaphore()
    for peer in peers:
        pl.semaphore_signal(barrier, inc=1, device_id=peer, device_id_type=MESH)
    pl.semaphore_wait(barrier, len(peers))


def remote(src, dst, send_sem, recv_sem, device):
    return pltpu.make_async_remote_copy(
        src_ref=src,
        dst_ref=dst,
        send_sem=send_sem,
        recv_sem=recv_sem,
        device_id=device,
        device_id_type=MESH,
    )


def plan_spread(dims, place, chunks, over_dp, own, dp_source, slot, sems):
    n_dp, n_row, n_col = dims
    d, r, c = place
    bits = bits_of(n_row)
    dp_send, dp_recv, row_send, row_recv, col_send, col_recv, own_sem = sems
    sent = []

    def block(j, x):
        return slot(c, j, flip_all(r, x, bits))

    def to_row(j, src, x, bit):
        copy = remote(
            src,
            block(j, x),
            row_send.at[j, (x ^ bit) - 1],
            row_recv.at[j, (x ^ bit) - 1],
            (d, flip(r, bit), c),
        )
        copy.start()
        sent.append(copy)

    def to_cols(j, src, x):
        for i in range(1, n_col):
            copy = remote(
                src,
                block(j, x),
                col_send.at[j, x, i - 1],
                col_recv.at[j, x, i - 1],
                (d, r, (c + i) % n_col),
            )
            copy.start()
            sent.append(copy)

    def order(j):
        return [1 << ((j + s) % bits) for s in range(bits)]

    locals_ = {}

    def start(j):
        if over_dp and j > 0:
            src = block(j, 0)
            origin = dp_order(d, j, n_dp)
            remote(src, src, dp_send.at[j - 1], dp_recv.at[origin], (d, r, c)).wait_recv()
        elif own is None:
            src = block(j, 0)
        else:
            src = own(j)
            keep = pltpu.make_async_copy(src, block(j, 0), own_sem.at[j])
            keep.start()
            locals_[j] = keep
        for bit in order(j):
            to_row(j, src, 0, bit)
        to_cols(j, src, 0)

    def arrived(j, x, later_dims):
        ref = block(j, x)
        remote(ref, ref, row_send.at[j, x - 1], row_recv.at[j, x - 1], (d, r, c)).wait_recv()
        for later in later_dims:
            to_row(j, ref, x, later)
        to_cols(j, ref, x)

    def pass_on(j):
        have = [0]
        dim_order = order(j)
        for s, bit in enumerate(dim_order[:-1]):
            new = [x ^ bit for x in have]
            for x in new:
                arrived(j, x, dim_order[s + 1 :])
            have += new

    def last_arrivals(j):
        bit = order(j)[-1]
        for x in range(n_row):
            if x & bit:
                arrived(j, x, [])

    def send_dp():
        for j in range(1, n_dp):
            peer = dp_order(d, j, n_dp)
            copy = remote(
                dp_source(peer),
                slot(c, ("from", d), r),
                dp_send.at[j - 1],
                dp_recv.at[d],
                (peer, r, c),
            )
            copy.start()
            sent.append(copy)

    def wait_cols(j):
        for x in range(n_row):
            for i in range(1, n_col):
                ref = slot((c + n_col - i) % n_col, j, flip_all(r, x, bits))
                remote(
                    ref, ref, col_send.at[j, x, i - 1], col_recv.at[j, x, i - 1], (d, r, c)
                ).wait_recv()
        if j in locals_:
            locals_[j].wait()

    def sends():
        return [copy.wait_send for copy in sent]

    return types.SimpleNamespace(
        start=start,
        send_dp=send_dp,
        pass_on=pass_on,
        last_arrivals=last_arrivals,
        wait_cols=wait_cols,
        sends=sends,
    )


def spread_blocks(dims, place, chunks, over_dp, own, dp_source, slot, sems, between=None):
    plan = plan_spread(dims, place, chunks, over_dp, own, dp_source, slot, sems)
    plan.start(0)
    if over_dp:
        plan.send_dp()
        for j in range(1, chunks):
            plan.start(j)
            plan.pass_on(j - 1)
        plan.pass_on(chunks - 1)
    else:
        for j in range(1, chunks):
            plan.start(j)
        for j in range(chunks):
            plan.pass_on(j)
    if between is not None:
        between()
    for j in range(chunks):
        plan.last_arrivals(j)
    for j in range(chunks):
        plan.wait_cols(j)
    return plan.sends()


def finish(waits):
    for wait in waits:
        wait()


def spread_sems(dims, chunks, copied=True):
    n_dp, n_row, n_col = dims
    dma = pltpu.SemaphoreType.DMA
    return [
        dma((max(1, n_dp - 1),)),
        dma((n_dp,)),
        dma((chunks, max(1, n_row - 1))),
        dma((chunks, max(1, n_row - 1))),
        dma((chunks, n_row, max(1, n_col - 1))),
        dma((chunks, n_row, max(1, n_col - 1))),
        dma((chunks if copied else 1,)),
    ]


def axis_place():
    return tuple(lax.axis_index(name) for name in ("dp", "row", "col"))


def param_gather_kernel(dims, shard_ref, out_ref, swap_ref, block_ref, swap_send, swap_recv, *sems):
    n_dp, n_row, n_col = dims
    place = axis_place()
    d, r, c = place
    rows = shard_ref.shape[1]
    greet(True, dims, place)
    copies = []
    for i in range(1, n_col):
        other = (c + i) % n_col
        copy = remote(
            shard_ref.at[other], swap_ref.at[c], swap_send.at[i], swap_recv.at[i], (d, r, other)
        )
        copy.start()
        copies.append(copy)
    swap_ref[pl.ds(c, 1)] = shard_ref[pl.ds(c, 1)]
    for copy in copies:
        copy.wait()
    for i in range(n_col):
        block_ref[i * rows : (i + 1) * rows, :] = swap_ref[i]
    low_ref = sems[-1]
    low_ref[...] = block_ref[...].astype(jnp.bfloat16)

    def slot(col, j, b):
        k = j[1] if isinstance(j, tuple) else dp_order(d, j, n_dp)
        return out_ref.at[col, k, b]

    finish(
        spread_blocks(
            dims, place, n_dp, True, lambda j: low_ref, lambda k: low_ref, slot, sems[:-1]
        )
    )


def param_gather(shard, dims):
    n_dp, n_row, n_col = dims
    _, rows, width = shard.shape
    dma = pltpu.SemaphoreType.DMA
    return pl.pallas_call(
        functools.partial(param_gather_kernel, dims),
        out_shape=jax.ShapeDtypeStruct((n_col, n_dp, n_row, n_col * rows, width), jnp.bfloat16),
        in_specs=[pl.BlockSpec(memory_space=pltpu.VMEM)],
        out_specs=pl.BlockSpec(memory_space=pl.ANY),
        scratch_shapes=[
            pltpu.VMEM((n_col, rows, width), jnp.float32),
            pltpu.VMEM((n_col * rows, width), jnp.float32),
            dma((n_col,)),
            dma((n_col,)),
            *spread_sems(dims, n_dp),
            pltpu.VMEM((n_col * rows, width), jnp.bfloat16),
        ],
        compiler_params=pltpu.CompilerParams(
            collective_id=0, has_side_effects=True, vmem_limit_bytes=VMEM_BYTES
        ),
        name="param_gather",
    )(shard)


def token_gather_kernel(dims, src_ref, out_ref, *sems):
    n_dp, n_row, n_col = dims
    place = axis_place()
    d = place[0]
    greet(True, dims, place)

    def slot(col, j, b):
        k = j[1] if isinstance(j, tuple) else dp_order(d, j, n_dp)
        return out_ref.at[col, k, b]

    finish(
        spread_blocks(
            dims,
            place,
            n_dp,
            True,
            lambda j: src_ref.at[d],
            lambda k: src_ref.at[k],
            slot,
            sems,
        )
    )


def token_gather(rows, dims):
    n_dp, n_row, n_col = dims
    _, slots, width = rows.shape
    return pl.pallas_call(
        functools.partial(token_gather_kernel, dims),
        out_shape=jax.ShapeDtypeStruct((n_col, n_dp, n_row, slots, width), rows.dtype),
        in_specs=[pl.BlockSpec(memory_space=pl.ANY)],
        out_specs=pl.BlockSpec(memory_space=pl.ANY),
        scratch_shapes=spread_sems(dims, n_dp),
        compiler_params=pltpu.CompilerParams(
            collective_id=1, has_side_effects=True, vmem_limit_bytes=VMEM_BYTES
        ),
        name="token_gather",
    )(rows)


def plane_gather_kernel(dims, src_ref, out_ref, *sems):
    place = axis_place()
    greet(False, dims, place)
    finish(
        spread_blocks(
            dims,
            place,
            src_ref.shape[0],
            False,
            lambda j: src_ref.at[j],
            None,
            lambda col, j, b: out_ref.at[col, b, j],
            sems,
        )
    )


def plane_gather(parts, dims):
    n_dp, n_row, n_col = dims
    chunks, rows, width = parts.shape
    return pl.pallas_call(
        functools.partial(plane_gather_kernel, dims),
        out_shape=jax.ShapeDtypeStruct((n_col, n_row, chunks, rows, width), parts.dtype),
        in_specs=[pl.BlockSpec(memory_space=pl.ANY)],
        out_specs=pl.BlockSpec(memory_space=pl.ANY),
        scratch_shapes=spread_sems(dims, chunks),
        compiler_params=pltpu.CompilerParams(
            collective_id=2, has_side_effects=True, vmem_limit_bytes=VMEM_BYTES
        ),
        name="plane_gather",
    )(parts)


def add_low(left, right):
    return (left.astype(jnp.float32) + right.astype(jnp.float32)).astype(jnp.bfloat16)


def plan_reduce(
    dims, place, part_at, bufs, sems, deliver, direct=False, far_first=True, lanes=None
):
    n_dp, n_row, n_col = dims
    d, r, c = place
    bits = bits_of(n_row)
    mine_ref, col_ref, row_ref = bufs
    mine_sem, col_send, col_recv, row_send, row_recv = sems
    steps = list(reversed(range(n_dp))) if far_first else list(range(n_dp))
    homes = [dp_order(d, p, n_dp) for p in steps]
    sent = []
    held = []

    def send_cols(t):
        for i in range(1, n_col):
            other = (c + i) % n_col
            copy = remote(
                part_at(other, homes[t]),
                col_ref.at[t, i - 1],
                col_send.at[t, i - 1],
                col_recv.at[t, i - 1],
                (d, r, other),
            )
            copy.start()
            sent.append(copy)

    def load_mine():
        for t in range(n_dp):
            keep = pltpu.make_async_copy(part_at(c, homes[t]), mine_ref.at[t], mine_sem.at[t])
            keep.start()
            held.append(keep)

    begin, width = lanes or (0, mine_ref.shape[-1])
    cut = (width // LANES + 1) // 2 * LANES
    spans = [pl.ds(begin, cut), pl.ds(begin + cut, width - cut)]
    marks = [pl.ds(0, cut), pl.ds(cut, width - cut)]

    def order(half):
        return [1 << ((half + s) % bits) for s in range(bits)]

    def send_half(t, half, s):
        dim_order = order(half)
        bit = dim_order[s]
        before = sum(dim_order[:s])
        span = spans[half]
        for x in range(n_row):
            if not x & before and x & bit:
                at = x ^ bit
                copy = remote(
                    mine_ref.at[t, flip_all(r, x, bits), :, span],
                    row_ref.at[t, slot_of(half, s, at), :, marks[half]],
                    row_send.at[t, half, slot_of(half, s, at)],
                    row_recv.at[t, half, slot_of(half, s, at)],
                    (d, flip(r, bit), c),
                )
                copy.start()
                sent.append(copy)

    def slot_of(half, s, at):
        places = []
        before = 0
        for step, bit in enumerate(order(half)):
            before += bit
            places += [(step, y) for y in range(n_row) if not y & before]
        return places.index((s, at))

    def sum_cols(t, send=True):
        if not direct:
            held[t].wait()
        for i in range(1, n_col):
            ref = col_ref.at[t, i - 1]
            remote(
                ref, ref, col_send.at[t, i - 1], col_recv.at[t, i - 1], (d, r, c)
            ).wait_recv()
        k = homes[t]

        @pl.loop(0, n_row)
        def _(b):
            total = part_at(c, k)[b] if direct else mine_ref[t, b]
            total = total.astype(jnp.float32)
            for i in range(1, n_col):
                total = total + col_ref[t, i - 1, b].astype(jnp.float32)
            mine_ref[t, b] = total.astype(jnp.bfloat16)

        if send:
            send_first(t)

    def send_first(t):
        for half in range(2):
            send_half(t, half, 0)

    def sum_rows(t, s):
        for half in range(2):
            before = sum(order(half)[: s + 1])
            span = spans[half]
            for y in range(n_row):
                if not y & before:
                    slot = slot_of(half, s, y)
                    ref = row_ref.at[t, slot, :, marks[half]]
                    remote(
                        ref,
                        ref,
                        row_send.at[t, half, slot],
                        row_recv.at[t, half, slot],
                        (d, r, c),
                    ).wait_recv()
                    b = flip_all(r, y, bits)
                    mine_ref[t, b, :, span] = add_low(mine_ref[t, b, :, span], ref[...])
            if s + 1 < bits:
                send_half(t, half, s + 1)
        if s + 1 == bits:
            deliver(steps[t], homes[t], mine_ref.at[t, r])

    def sum_all(between=None):
        ticks = n_dp + bits + 1
        for tick in range(ticks):
            if tick + 1 == ticks and between is not None:
                between()
            if tick < n_dp:
                sum_cols(tick)
            for s in reversed(range(bits)):
                t = tick - 2 - s
                if 0 <= t < n_dp:
                    sum_rows(t, s)

    return types.SimpleNamespace(
        send_cols=send_cols,
        load_mine=load_mine,
        sum_cols=sum_cols,
        send_first=send_first,
        homes=homes,
        sum_rows=sum_rows,
        sum_all=sum_all,
        sent=sent,
    )


def plan_dp_first(dims, place, mine_ref, homes, begin, scratch):
    n_dp, n_row, n_col = dims
    d, r, c = place
    bits = bits_of(n_row)
    in_ref, acc_ref, row_ref, dp_send, dp_recv, row_send, row_recv = scratch
    wide = acc_ref.shape[-1]
    cut = (wide // LANES + 1) // 2 * LANES
    spans = [pl.ds(0, cut), pl.ds(cut, wide - cut)]
    lanes = pl.ds(begin, wide)
    sent = []

    def send_dp(t):
        p = n_dp - 1 - t
        if p:
            copy = remote(
                mine_ref.at[t, :, :, lanes],
                in_ref.at[d],
                dp_send.at[p - 1],
                dp_recv.at[d],
                (homes[t], r, c),
            )
            copy.start()
            sent.append(copy)

    def order(half):
        return [1 << ((half + s) % bits) for s in range(bits)]

    def steps(half):
        before = 0
        places = []
        for bit in order(half):
            before += bit
            places.append([y for y in range(n_row) if not y & before])
        return places

    def slot_of(half, s, y):
        return sum(len(step) for step in steps(half)[:s]) + steps(half)[s].index(y)

    def send_half(half, s):
        bit = order(half)[s]
        for y in steps(half)[s]:
            slot = slot_of(half, s, y)
            copy = remote(
                acc_ref.at[flip_all(r, y ^ bit, bits), :, spans[half]],
                row_ref.at[slot, :, spans[half]],
                row_send.at[half, slot],
                row_recv.at[half, slot],
                (d, flip(r, bit), c),
            )
            copy.start()
            sent.append(copy)

    def sum_dp():
        for p in range(1, n_dp):
            k = homes[n_dp - 1 - p]
            ref = in_ref.at[k]
            remote(ref, ref, dp_send.at[p - 1], dp_recv.at[k], (d, r, c)).wait_recv()

        @pl.loop(0, n_row)
        def _(b):
            total = mine_ref[n_dp - 1, b, :, lanes].astype(jnp.float32)
            for p in range(1, n_dp):
                total = total + in_ref[homes[n_dp - 1 - p], b].astype(jnp.float32)
            acc_ref[b] = total.astype(jnp.bfloat16)

        for half in range(2):
            send_half(half, 0)

    def sum_rows(s):
        for half in range(2):
            for y in steps(half)[s]:
                slot = slot_of(half, s, y)
                ref = row_ref.at[slot, :, spans[half]]
                remote(
                    ref, ref, row_send.at[half, slot], row_recv.at[half, slot], (d, r, c)
                ).wait_recv()
                b = flip_all(r, y, bits)
                acc_ref[b, :, spans[half]] = add_low(acc_ref[b, :, spans[half]], ref[...])
            if s + 1 < bits:
                send_half(half, s + 1)

    return types.SimpleNamespace(
        send_dp=send_dp, sum_dp=sum_dp, sum_rows=sum_rows, total=lambda: acc_ref[r], sent=sent
    )


def dp_first_scratch(dims, rows, width):
    n_dp, n_row, n_col = dims
    dma = pltpu.SemaphoreType.DMA
    low = jnp.bfloat16
    return [
        pltpu.VMEM((n_dp, n_row, rows, width), low),
        pltpu.VMEM((n_row, rows, width), low),
        pltpu.VMEM((max(1, n_row - 1), rows, width), low),
        dma((max(1, n_dp - 1),)),
        dma((n_dp,)),
        dma((2, max(1, n_row - 1))),
        dma((2, max(1, n_row - 1))),
    ]


def reduce_blocks(dims, place, part_ref, bufs, sems, deliver):
    plan = plan_reduce(dims, place, lambda col, k: part_ref.at[col, k], bufs, sems, deliver)
    for t in range(dims[0]):
        plan.send_cols(t)
    plan.load_mine()
    plan.sum_all()
    return plan.sent


def reduce_scratch(dims, rows, width, copied=True, lanes=None):
    n_dp, n_row, n_col = dims
    dma = pltpu.SemaphoreType.DMA
    low = jnp.bfloat16
    return [
        pltpu.VMEM((n_dp, n_row, rows, width), low),
        pltpu.VMEM((n_dp, max(1, n_col - 1), n_row, rows, width), low),
        pltpu.VMEM((n_dp, max(1, n_row - 1), rows, lanes or width), low),
        dma((n_dp if copied else 1,)),
        dma((n_dp, max(1, n_col - 1))),
        dma((n_dp, max(1, n_col - 1))),
        dma((n_dp, 2, max(1, n_row - 1))),
        dma((n_dp, 2, max(1, n_row - 1))),
    ]


def token_reduce_kernel(dims, part_ref, out_ref, *scratch):
    n_dp, n_row, n_col = dims
    place = axis_place()
    d, r, c = place
    dp_send, dp_recv, own_sem = scratch[8:]
    greet(True, dims, place)
    late = []

    def deliver(p, k, block):
        if p == 0:
            keep = pltpu.make_async_copy(block, out_ref.at[d], own_sem)
            keep.start()
            late.append(keep.wait)
        else:
            copy = remote(block, out_ref.at[d], dp_send.at[p], dp_recv.at[d], (k, r, c))
            copy.start()
            late.append(copy.wait_send)

    sent = reduce_blocks(dims, place, part_ref, scratch[:3], scratch[3:8], deliver)
    for p in range(1, n_dp):
        k = dp_order(d, p, n_dp)
        ref = out_ref.at[k]
        remote(ref, ref, dp_send.at[p], dp_recv.at[k], (d, r, c)).wait_recv()
    for copy in sent:
        copy.wait_send()
    for wait in late:
        wait()


def token_reduce(parts, dims):
    n_dp = dims[0]
    slots, width = parts.shape[3:]
    dma = pltpu.SemaphoreType.DMA
    return pl.pallas_call(
        functools.partial(token_reduce_kernel, dims),
        out_shape=jax.ShapeDtypeStruct((n_dp, slots, width), jnp.bfloat16),
        in_specs=[pl.BlockSpec(memory_space=pl.ANY)],
        out_specs=pl.BlockSpec(memory_space=pl.ANY),
        scratch_shapes=[*reduce_scratch(dims, slots, width), dma((n_dp,)), dma((n_dp,)), dma],
        compiler_params=pltpu.CompilerParams(
            collective_id=3, has_side_effects=True, vmem_limit_bytes=VMEM_BYTES
        ),
        name="token_reduce",
    )(parts)


def param_reduce_kernel(dims, part_ref, out_ref, *scratch):
    n_dp, n_row, n_col = dims
    place = axis_place()
    d, r, c = place
    dp_send, dp_recv, dp_ref, swap_send, swap_recv, swap_ref, sum_ref = scratch[8:]
    rows = out_ref.shape[1]
    greet(True, dims, place)
    late = []
    kept = []

    def deliver(p, k, block):
        if p == 0:
            kept.append(block)
        else:
            copy = remote(block, dp_ref.at[d], dp_send.at[p], dp_recv.at[d], (k, r, c))
            copy.start()
            late.append(copy)

    sent = reduce_blocks(dims, place, part_ref, scratch[:3], scratch[3:8], deliver)
    total = kept[0][...].astype(jnp.float32)
    for p in range(1, n_dp):
        k = dp_order(d, p, n_dp)
        ref = dp_ref.at[k]
        remote(ref, ref, dp_send.at[p], dp_recv.at[k], (d, r, c)).wait_recv()
        total = total + dp_ref[k].astype(jnp.float32)
    sum_ref[...] = total
    for i in range(n_col):
        swap_ref[i] = sum_ref[i * rows : (i + 1) * rows, :]
    for i in range(1, n_col):
        other = (c + i) % n_col
        copy = remote(
            swap_ref.at[other], out_ref.at[c], swap_send.at[i], swap_recv.at[i], (d, r, other)
        )
        copy.start()
        late.append(copy)
    out_ref[pl.ds(c, 1)] = swap_ref[pl.ds(c, 1)]
    for i in range(1, n_col):
        ref = out_ref.at[(c + n_col - i) % n_col]
        remote(ref, ref, swap_send.at[i], swap_recv.at[i], (d, r, c)).wait_recv()
    for copy in sent:
        copy.wait_send()
    for copy in late:
        copy.wait_send()


def param_reduce(parts, dims):
    n_dp, n_row, n_col = dims
    block_rows, width = parts.shape[3:]
    rows = block_rows // n_col
    dma = pltpu.SemaphoreType.DMA
    return pl.pallas_call(
        functools.partial(param_reduce_kernel, dims),
        out_shape=jax.ShapeDtypeStruct((n_col, rows, width), jnp.float32),
        in_specs=[pl.BlockSpec(memory_space=pl.ANY)],
        out_specs=pl.BlockSpec(memory_space=pltpu.VMEM),
        scratch_shapes=[
            *reduce_scratch(dims, block_rows, width),
            dma((n_dp,)),
            dma((n_dp,)),
            pltpu.VMEM((n_dp, block_rows, width), jnp.bfloat16),
            dma((n_col,)),
            dma((n_col,)),
            pltpu.VMEM((n_col, rows, width), jnp.float32),
            pltpu.VMEM((block_rows, width), jnp.float32),
        ],
        compiler_params=pltpu.CompilerParams(
            collective_id=4, has_side_effects=True, vmem_limit_bytes=VMEM_BYTES
        ),
        name="param_reduce",
    )(parts)


def column(matrix, index):
    return matrix[:, index : index + 1]


def token_masks(lengths_ref, rows, seqs):
    down = lax.broadcasted_iota(jnp.int32, (rows, 1), 0)
    across = lax.broadcasted_iota(jnp.int32, (1, rows), 1)
    end = 0
    doc_down = jnp.zeros((rows, 1), jnp.int32)
    doc_across = jnp.zeros((1, rows), jnp.int32)
    for i in range(seqs):
        end = end + lengths_ref[0, i]
        doc_down = doc_down + (down >= end).astype(jnp.int32)
        doc_across = doc_across + (across >= end).astype(jnp.int32)
    valid = (doc_down < seqs).astype(jnp.float32)
    allowed = (doc_down == doc_across) & (down >= across)
    return valid, allowed


def row_vectors_of(small, first):
    shape = (8, small.shape[1])
    pick = lax.broadcasted_iota(jnp.int32, shape, 1) == first + lax.broadcasted_iota(
        jnp.int32, shape, 0
    )
    return dot(pick.astype(jnp.bfloat16), small, NT)


def half_mask(rows, half):
    return lax.broadcasted_iota(jnp.int32, (rows, LANES), 1) // HEAD == half


def attention_forward(qkv_ref, probs_ref, mixed_ref, allowed, first, last):
    rows = qkv_ref.shape[0]
    low = jnp.bfloat16

    @pl.loop(first, last, unroll=3)
    def _(pair):
        def cols(base):
            return pl.ds(pl.multiple_of(base + pair * LANES, LANES), LANES)

        queries = qkv_ref[:, cols(0)]
        key_heads = qkv_ref[:, cols(D)]
        values = qkv_ref[:, cols(2 * D)]
        mixed = jnp.zeros((rows, LANES), jnp.float32)
        for half in range(LANES // HEAD):
            mask = half_mask(rows, half)
            scores = dot(jnp.where(mask, queries, 0), key_heads, NT) * HEAD ** (-0.5)
            scores = jnp.where(allowed, scores, -1e30)
            top_score = jnp.max(scores, axis=-1, keepdims=True)
            exp_scores = jnp.exp(scores - top_score)
            probs = exp_scores / jnp.sum(exp_scores, axis=-1, keepdims=True)
            probs_ref[pair * (LANES // HEAD) + half] = probs
            mixed = mixed + dot(probs.astype(low), jnp.where(mask, values, 0))
        mixed_ref[:, cols(0)] = mixed.astype(low)


def two_way(first, second):
    top = jnp.maximum(first, second)
    exp_first = jnp.exp(first - top)
    exp_second = jnp.exp(second - top)
    total = exp_first + exp_second
    return exp_first / total, exp_second / total


def attention_backward(qkv_ref, probs_ref, grad_mixed_ref, grad_qkv_ref):
    rows = qkv_ref.shape[0]
    low = jnp.bfloat16

    @pl.loop(0, HEADS * HEAD // LANES, unroll=2)
    def _(pair):
        def cols(base):
            return pl.ds(pl.multiple_of(base + pair * LANES, LANES), LANES)

        queries = qkv_ref[:, cols(0)]
        key_heads = qkv_ref[:, cols(D)]
        values = qkv_ref[:, cols(2 * D)]
        grad_mixed = grad_mixed_ref[:, cols(0)]
        grad_queries = jnp.zeros((rows, LANES), jnp.float32)
        grad_keys = jnp.zeros((rows, LANES), jnp.float32)
        grad_values = jnp.zeros((rows, LANES), jnp.float32)
        for half in range(LANES // HEAD):
            mask = half_mask(rows, half)
            probs = probs_ref[pair * (LANES // HEAD) + half]
            grad_part = jnp.where(mask, grad_mixed, 0)
            grad_values = grad_values + dot(probs.astype(low), grad_part, TN)
            grad_probs = dot(grad_part, values, NT)
            grad_scores = probs * (
                grad_probs - jnp.sum(probs * grad_probs, axis=-1, keepdims=True)
            )
            grad_scores = grad_scores.astype(low)
            grad_queries = grad_queries + dot(grad_scores, jnp.where(mask, key_heads, 0))
            grad_keys = grad_keys + dot(grad_scores, jnp.where(mask, queries, 0), TN)
        grad_qkv_ref[:, cols(0)] = (grad_queries * HEAD ** (-0.5)).astype(low)
        grad_qkv_ref[:, cols(D)] = (grad_keys * HEAD ** (-0.5)).astype(low)
        grad_qkv_ref[:, cols(2 * D)] = grad_values.astype(low)


def layer_kernel(sizes, *refs):
    dims, num_ffn, wide_qkv, wide_out, route_cols, chunks = sizes
    n_dp, n_row, n_col = dims
    low = jnp.bfloat16
    (
        lengths_ref,
        routes_ref,
        prev_ref,
        tokens_ref,
        cotangent_ref,
        w_qkv_ref,
        w_out_ref,
        route_w_ref,
        gains_ref,
        const_ref,
        weight_gu,
        weight_down,
        left_root_gu,
        right_root_down,
        right_root_gu,
        left_root_down,
        result_ref,
        grad_tokens_ref,
        summed_ref,
        right_sum_out,
        left_sum_out,
        step_out,
        block_out,
        shard_ref,
        turn_ref,
        swap_ref,
        block_ref,
        whole_ref,
        pack_ref,
        expert_ref,
        stage_ref,
        arrived_ref,
        hidden_ref,
        pre_ref,
        grads_ref,
        qkv_ref,
        probs_ref,
        mixed_ref,
        first_ref,
        came_ref,
        grad_attn_ref,
        grad_mixed_ref,
        grad_qkv_ref,
        part_ref,
        dp_ref,
        end_ref,
        sum_ref,
        gathered_ref,
        root_ref,
        tile_ref,
        half_step_ref,
        lhs_ref,
        right_sum_ref,
        left_sum_ref,
        left_low_ref,
        step_ref,
        swap_send,
        swap_recv,
        load_sem,
        expert_send,
        expert_recv,
        root_sem,
        tile_sem,
        store_sem,
        came_send,
        came_recv,
        dp_send,
        dp_recv,
        end_send,
        end_recv,
        *more,
    ) = refs
    param_sems, out_sems, token_sems, gather_sems = (more[7 * n : 7 * n + 7] for n in range(4))
    token_scratch, param_scratch, first_scratch = more[28:36], more[36:44], more[44:]
    place = axis_place()
    d, r, c = place
    rows = shard_ref.shape[1]
    depth, slice_wide = pack_ref.shape[2:]
    held, tile = tile_ref.shape[:2]
    wide_col = n_row * slice_wide
    staged = []
    loads = []
    for m, src in enumerate([weight_gu.at[:, 0], weight_gu.at[:, 1], weight_down]):
        begin = m % 2 * wide_col
        staged.append((m // 2, begin))
        dst = tile_ref.at[m // 2, pl.ds(0, depth), pl.ds(begin, wide_col)]
        copy = pltpu.make_async_copy(src, dst, load_sem.at[m])
        copy.start()
        loads.append(copy)
    roots = [left_root_gu.at[0], left_root_gu.at[1], right_root_down]
    root_loads = []
    for m in range(3):
        copy = pltpu.make_async_copy(roots[m], root_ref.at[m], root_sem.at[m])
        copy.start()
        root_loads.append(copy)
    turn_ref[...] = jnp.zeros_like(turn_ref)
    out_at = wide_qkv + LANES
    at = 0
    for ref in (route_w_ref, gains_ref, const_ref):
        turn_ref[at : at + ref.shape[0], : ref.shape[1]] = ref[...]
        at += ref.shape[0]
    small_shard = turn_ref[...].T[:rows]
    for i in range(n_col):
        shard_ref[i, :, :wide_qkv] = w_qkv_ref[:, i * wide_qkv : (i + 1) * wide_qkv]
        shard_ref[i, :, wide_qkv:out_at] = small_shard
        shard_ref[i, :, out_at:] = w_out_ref[:, i * wide_out : (i + 1) * wide_out]
    greet(True, dims, place, all_rows=True)

    copies = []
    for i in range(1, n_col):
        other = (c + i) % n_col
        copy = remote(
            shard_ref.at[other], swap_ref.at[c], swap_send.at[i], swap_recv.at[i], (d, r, other)
        )
        copy.start()
        copies.append(copy)
    swap_ref[pl.ds(c, 1)] = shard_ref[pl.ds(c, 1)]
    for copy in copies:
        copy.wait()
    for i in range(n_col):
        block_ref[i * rows : (i + 1) * rows, :] = swap_ref[i]
    whole_ref[c, d, r] = block_ref[...].astype(low)

    def plan_params(begin, wide, sems):
        span = pl.ds(begin, wide)

        def slot(col, j, b):
            k = j[1] if isinstance(j, tuple) else dp_order(d, j, n_dp)
            return whole_ref.at[col, k, b, :, span]

        own = whole_ref.at[c, d, r, :, span]
        return plan_spread(dims, place, n_dp, True, None, lambda k: own, slot, sems)

    qkv_plan = plan_params(0, out_at, param_sems)
    out_plan = plan_params(out_at, wide_out, out_sems)
    waits = []

    def send_experts():
        for copy in loads:
            copy.wait()
        for m, (slot, begin) in enumerate(staged):
            for b in range(n_row):
                at = begin + b * slice_wide
                pack_ref[b, m] = tile_ref[slot, :depth, at : at + slice_wide].astype(low)
        home = pl.ds(pl.multiple_of(r * depth, 16), depth)
        for i in range(1, n_row):
            other = (r + i) % n_row
            copy = remote(
                pack_ref.at[other],
                expert_ref.at[:, home],
                expert_send.at[i],
                expert_recv.at[i],
                (d, other, c),
            )
            copy.start()
            waits.append(copy.wait_send)
        expert_ref[:, home] = pack_ref[r]

    for plan in (qkv_plan, out_plan):
        plan.start(0)
        plan.send_dp()
    for plan in (qkv_plan, out_plan):
        for j in range(1, n_dp):
            plan.start(j)
            plan.pass_on(j - 1)
        plan.pass_on(n_dp - 1)
    send_experts()
    for j in range(n_dp):
        qkv_plan.last_arrivals(j)
    for j in range(n_dp):
        qkv_plan.wait_cols(j)

    def whole_cols(col, begin, wide):
        return whole_ref[col, :, :, :, begin : begin + wide].reshape(D, wide)

    total = tokens_ref.shape[0]
    valid, allowed = token_masks(lengths_ref, total, lengths_ref.shape[1])
    small = whole_cols(0, wide_qkv, LANES)
    vectors = row_vectors_of(small, route_cols)
    inputs = tokens_ref[...].astype(jnp.float32)
    scale_one = lax.rsqrt(jnp.mean(inputs * inputs, axis=-1, keepdims=True) + NORM_EPS)
    h_one = (inputs * scale_one * vectors[0:1]).astype(low)
    for i in range(n_col):
        qkv_ref[:, i * wide_qkv : (i + 1) * wide_qkv] = dot(h_one, whole_cols(i, 0, wide_qkv)).astype(
            low
        )
    pairs = HEADS * HEAD // LANES
    attention_forward(qkv_ref, probs_ref, mixed_ref, allowed, 0, pairs // 2)
    for j in range(n_dp):
        out_plan.last_arrivals(j)
    attention_forward(qkv_ref, probs_ref, mixed_ref, allowed, pairs // 2, pairs)
    for j in range(n_dp):
        out_plan.wait_cols(j)
    waits += qkv_plan.sends() + out_plan.sends()
    for i in range(n_col):
        cols = slice(i * wide_out, (i + 1) * wide_out)
        attn_out = dot(mixed_ref[...], whole_cols(i, out_at, wide_out))
        first_ref[:, cols] = tokens_ref[:, cols].astype(jnp.float32) + valid * attn_out
    first_sum = first_ref[...]
    scale_two = lax.rsqrt(jnp.mean(first_sum * first_sum, axis=-1, keepdims=True) + NORM_EPS)
    h_two = (first_sum * scale_two * vectors[1:2]).astype(low)
    experts = prev_ref.shape[0]
    turn_ref[...] = jnp.zeros_like(turn_ref)
    turn_ref[:experts] = prev_ref[...]
    turn_ref[experts : experts + 2] = routes_ref[...].astype(jnp.float32)
    turned = turn_ref[...].T
    logits_all = dot(h_two, small)
    lane = lax.broadcasted_iota(jnp.int32, (total, LANES), 1)
    logits = logits_all + jnp.where(lane < experts, turned, 0.0)
    route_first = column(turned, experts).astype(jnp.int32)
    route_second = column(turned, experts + 1).astype(jnp.int32)
    pick_first = (lane == route_first).astype(jnp.float32)
    pick_second = (lane == route_second).astype(jnp.float32)
    gates = two_way(
        jnp.sum(pick_first * logits, axis=-1, keepdims=True),
        jnp.sum(pick_second * logits, axis=-1, keepdims=True),
    )
    mix_base = num_ffn + 4
    mixes = []
    for i in range(2):
        mixes += two_way(
            column(logits_all, mix_base + 2 * i), column(logits_all, mix_base + 2 * i + 1)
        )
    before = lax.broadcasted_iota(jnp.int32, (total, total), 0) > lax.broadcasted_iota(
        jnp.int32, (total, total), 1
    )
    earlier = dot(before.astype(low), (pick_first + pick_second).astype(low))
    in_slots = []
    for route, pick in ((route_first, pick_first), (route_second, pick_second)):
        slot_index = jnp.sum(earlier * pick, axis=-1, keepdims=True)
        where_in = (route * CAP).astype(jnp.float32) + slot_index
        in_slots.append(jnp.where(route < num_ffn, where_in, -1.0))
    slots = num_ffn * CAP
    slot_lane = lax.broadcasted_iota(jnp.int32, (total, slots), 1).astype(jnp.float32)
    places = [(slot_lane == where_in).astype(low) for where_in in in_slots]
    grad_y = cotangent_ref[...].astype(jnp.float32) * valid
    sent = dot(places[0] + places[1], h_two, TN).astype(low)
    made = dot(places[0], (gates[0] * grad_y).astype(low), TN) + dot(
        places[1], (gates[1] * grad_y).astype(low), TN
    )
    stage_ref[:, :, :D] = sent.reshape(num_ffn, CAP, D)
    stage_ref[:, :, D:] = made.astype(low).reshape(num_ffn, CAP, D)

    def token_slot(col, j, b):
        k = j[1] if isinstance(j, tuple) else dp_order(d, j, n_dp)
        return arrived_ref.at[k, col, b]

    arrived_ref[d, c, r] = stage_ref[d]
    rows_plan = plan_spread(
        dims, place, n_dp, True, None, lambda k: stage_ref.at[k], token_slot, token_sems
    )
    rows_plan.start(0)
    rows_plan.send_dp()
    rows_plan.start(1)
    rows_plan.pass_on(0)

    wides = [right_root_gu.at[0], right_root_gu.at[1], left_root_down]
    tiles = left_root_down.shape[0] // tile
    tile_loads = []

    def load_tile(n):
        if n < 3 * tiles:
            copy = pltpu.make_async_copy(
                wides[n // tiles].at[pl.ds(n % tiles * tile, tile)],
                tile_ref.at[n % held],
                tile_sem.at[n],
            )
            copy.start()
            tile_loads.append(copy)

    for n in range(held):
        load_tile(n)

    def token_back(p, k, block):
        if p == 0:
            came_ref[d] = block[...]
        else:
            copy = remote(block, came_ref.at[d], came_send.at[p - 1], came_recv.at[d], (k, r, c))
            copy.start()
            waits.append(copy.wait_send)

    tokens_plan = plan_reduce(
        dims,
        place,
        lambda col, k: part_ref.at[col, k, :, pl.ds(0, CAP), pl.ds(0, 2 * D)],
        token_scratch[:3],
        token_scratch[3:],
        token_back,
        direct=True,
        far_first=False,
    )

    tall = n_col * n_row * CAP

    def expert_rows(p):
        k = dp_order(d, p, n_dp)
        some = arrived_ref[k].reshape(tall, 2 * D)
        rows_in = some[:, :D]
        grads_in = some[:, D:]
        gate_part = dot(rows_in, expert_ref[0])
        up_part = dot(rows_in, expert_ref[1])
        grad_hidden = dot(grads_in, expert_ref[2])
        sigma = jax.nn.sigmoid(gate_part)
        silu = gate_part * sigma
        hidden = (silu * up_part).astype(low)
        grad_gate = (grad_hidden * up_part * sigma * (1.0 + gate_part * (1.0 - sigma))).astype(low)
        grad_up = (grad_hidden * silu).astype(low)
        hidden_ref[k] = hidden
        pre_ref[k, :, :slice_wide] = grad_gate
        pre_ref[k, :, slice_wide:] = grad_up
        made_rows = dot(hidden, expert_ref[2], NT).astype(low)
        grad_rows = (dot(grad_gate, expert_ref[0], NT) + dot(grad_up, expert_ref[1], NT)).astype(low)
        for col in range(n_col):
            span = slice(col * n_row * CAP, (col + 1) * n_row * CAP)
            part_ref[col, k, :, :CAP, :D] = made_rows[span].reshape(n_row, CAP, D)
            part_ref[col, k, :, :CAP, D : 2 * D] = grad_rows[span].reshape(n_row, CAP, D)
        tokens_plan.send_cols(p)

    def chunk_in(p):
        if p + 2 < n_dp:
            rows_plan.start(p + 2)
        if p + 1 < n_dp:
            rows_plan.pass_on(p + 1)
        if p == 0:
            for i in range(1, n_row):
                home = pl.ds(pl.multiple_of(((r + n_row - i) % n_row) * depth, 16), depth)
                ref = expert_ref.at[:, home]
                remote(ref, ref, expert_send.at[i], expert_recv.at[i], (d, r, c)).wait_recv()
        rows_plan.last_arrivals(p)
        rows_plan.wait_cols(p)
        expert_rows(p)

    bits = bits_of(n_row)

    def sums_before(t):
        for s in range(bits):
            if 0 <= t - 1 - s:
                tokens_plan.sum_rows(t - 1 - s, s)

    chunk_in(0)
    for t in range(n_dp - 1):
        if t < n_dp - 2:
            chunk_in(t + 1)
        tokens_plan.sum_cols(t)
        sums_before(t)
    if n_dp > 1:
        chunk_in(n_dp - 1)
    tokens_plan.sum_cols(n_dp - 1)
    sums_before(n_dp - 1)
    waits += rows_plan.sends()
    all_count = n_dp * tall
    all_rows = arrived_ref[:, :, :, :, :D].reshape(all_count, D)
    all_grads = arrived_ref[:, :, :, :, D:].reshape(all_count, D)
    for m in range(2):
        grads_ref[m * D : (m + 1) * D] = dot(
            all_rows,
            pre_ref[:, :, m * slice_wide : (m + 1) * slice_wide].reshape(all_count, slice_wide),
            TN,
        ).astype(low)
    grads_ref[2 * D :] = dot(
        all_grads, hidden_ref[...].reshape(all_count, slice_wide), TN
    ).astype(low)
    tall = grads_ref.shape[0] // chunks
    gather = plan_spread(
        dims,
        place,
        chunks,
        False,
        lambda j: grads_ref.at[pl.ds(j * tall, tall)],
        None,
        lambda col, j, b: gathered_ref.at[col * n_row + b, pl.ds(j * tall, tall)],
        gather_sems,
    )
    for t in range(n_dp, n_dp + bits):
        for s in range(bits):
            if 0 <= t - 1 - s < n_dp:
                tokens_plan.sum_rows(t - 1 - s, s)
        if t == n_dp + bits - 2:
            for j in range(chunks):
                gather.start(j)

    gain_one, gain_two = vectors[0:1], vectors[1:2]
    const_rows = [vectors[2:3], vectors[3:4]]
    mixes = [mixes[:2], mixes[2:]]
    routes = [route_first, route_second]
    picks = [pick_first, pick_second]
    cotangent = cotangent_ref[...].astype(jnp.float32)
    grad_y = cotangent * valid
    grad_y_low = grad_y.astype(low)
    first_sum = first_ref[...]
    scale_two = lax.rsqrt(jnp.mean(first_sum * first_sum, axis=-1, keepdims=True) + NORM_EPS)
    normed_two = first_sum * scale_two
    h_two = normed_two * gain_two
    h_two_low = h_two.astype(low)
    const_sel = [
        [(route == num_ffn + 2 + n).astype(jnp.float32) for n in range(2)] for route in routes
    ]
    for p in range(1, n_dp):
        k = dp_order(d, p, n_dp)
        ref = came_ref.at[k]
        remote(ref, ref, came_send.at[p - 1], came_recv.at[k], (d, r, c)).wait_recv()
    expert_out = came_ref[:, :, :D].reshape(slots, D)
    grad_sent = came_ref[:, :, D:].reshape(slots, D)
    moe_out = jnp.zeros_like(first_sum)
    grad_gates = []
    own_weight = jnp.zeros((total, 1), jnp.float32)
    for n in range(2):
        own = (routes[n] == num_ffn + 1).astype(jnp.float32)
        for i in range(2):
            own = own + const_sel[n][i] * mixes[i][0]
        output = dot(places[n], expert_out) + own * h_two
        for i in range(2):
            output = output + const_sel[n][i] * mixes[i][1] * const_rows[i]
        moe_out = moe_out + gates[n] * output
        grad_gates.append(jnp.sum(grad_y * output, axis=-1, keepdims=True))
        own_weight = own_weight + gates[n] * own
    result_ref[...] = (first_sum + valid * moe_out).astype(low)
    mean_gate = gates[0] * grad_gates[0] + gates[1] * grad_gates[1]
    grad_logits = sum(gates[n] * (grad_gates[n] - mean_gate) * picks[n] for n in range(2))
    grad_own = jnp.sum(grad_y * h_two, axis=-1, keepdims=True)
    const_lanes = jnp.zeros((total, LANES), jnp.float32)
    for i in range(2):
        weight = const_sel[0][i] * gates[0] + const_sel[1][i] * gates[1]
        mix_grads = [
            weight * grad_own,
            weight * jnp.sum(grad_y * const_rows[i], axis=-1, keepdims=True),
        ]
        mean_mix = mixes[i][0] * mix_grads[0] + mixes[i][1] * mix_grads[1]
        for n in range(2):
            grad_mix = mixes[i][n] * (mix_grads[n] - mean_mix)
            grad_logits = jnp.where(lane == num_ffn + 4 + 2 * i + n, grad_mix, grad_logits)
        const_lanes = jnp.where(lane == route_cols + 2 + i, weight * mixes[i][1], const_lanes)
    grad_logits = grad_logits.astype(low)

    grad_h_two = (
        dot(grad_logits, small, NT) + dot(places[0] + places[1], grad_sent) + own_weight * grad_y
    )
    grad_normed = grad_h_two * gain_two
    inner_mean = jnp.mean(grad_normed * normed_two, axis=-1, keepdims=True)
    grad_first = scale_two * (grad_normed - normed_two * inner_mean) + cotangent
    grad_tokens_ref[...] = grad_first
    grad_attn_ref[...] = (valid * grad_first).astype(low)
    grad_small = (
        dot(h_two_low, grad_logits, TN)
        + dot(grad_y_low, const_lanes.astype(low), TN)
        + dot((grad_h_two * normed_two).astype(low), (lane == route_cols + 1).astype(low), TN)
    )
    grad_mixed = jnp.zeros((total, D), jnp.float32)
    for i in range(n_col):
        grad_mixed = grad_mixed + dot(
            grad_attn_ref[:, i * wide_out : (i + 1) * wide_out],
            whole_cols(i, out_at, wide_out),
            NT,
        )
    grad_mixed_ref[...] = grad_mixed.astype(low)
    attention_backward(qkv_ref, probs_ref, grad_mixed_ref, grad_qkv_ref)
    grad_h_one = jnp.zeros((total, D), jnp.float32)
    for i in range(n_col):
        grad_h_one = grad_h_one + dot(
            grad_qkv_ref[:, i * wide_qkv : (i + 1) * wide_qkv], whole_cols(i, 0, wide_qkv), NT
        )
    inputs = tokens_ref[...].astype(jnp.float32)
    scale_one = lax.rsqrt(jnp.mean(inputs * inputs, axis=-1, keepdims=True) + NORM_EPS)
    normed_one = inputs * scale_one
    h_one = (normed_one * gain_one).astype(low)
    grad_normed = grad_h_one * gain_one
    inner_mean = jnp.mean(grad_normed * normed_one, axis=-1, keepdims=True)
    grad_tokens_ref[...] += scale_one * (grad_normed - normed_one * inner_mean)
    grad_small = grad_small + dot(
        (grad_h_one * normed_one).astype(low), (lane == route_cols).astype(low), TN
    )

    kept = []
    split = dp_ref.shape[2]

    def param_back(p, k, block):
        if p == 0:
            kept.append(block)
        else:
            block = block.at[:, pl.ds(0, split)]
            copy = remote(block, dp_ref.at[d], dp_send.at[p - 1], dp_recv.at[d], (k, r, c))
            copy.start()
            waits.append(copy.wait_send)

    params_plan = plan_reduce(
        dims,
        place,
        lambda col, k: part_ref.at[col, k],
        param_scratch[:3],
        param_scratch[3:],
        param_back,
        direct=True,
        lanes=(0, split),
    )
    first_plan = plan_dp_first(dims, place, param_scratch[0], params_plan.homes, split, first_scratch)
    finish([copy.wait_send for copy in tokens_plan.sent])
    blocked = part_ref.shape[1:4]
    for i in [*range(1, n_col), 0]:
        col = (c + i) % n_col
        qkv_cols = pl.ds(pl.multiple_of(col * wide_qkv, LANES), wide_qkv)
        out_cols = pl.ds(pl.multiple_of(col * wide_out, LANES), wide_out)
        part_ref[col, :, :, :, :wide_qkv] = (
            dot(h_one, grad_qkv_ref[:, qkv_cols], TN).astype(low).reshape(*blocked, wide_qkv)
        )
        part_ref[col, :, :, :, out_at:] = (
            dot(mixed_ref[...], grad_attn_ref[:, out_cols], TN)
            .astype(low)
            .reshape(*blocked, wide_out)
        )
        part_ref[col, :, :, :, wide_qkv:out_at] = grad_small.astype(low).reshape(*blocked, LANES)
        if i == n_col - 1:
            for t in range(n_dp):
                params_plan.send_cols(t)
    gather.pass_on(0)
    gather.pass_on(1)
    for t in range(n_dp):
        params_plan.sum_cols(t, False)
        first_plan.send_dp(t)
    for j in range(2, chunks):
        gather.pass_on(j)
    for t in range(n_dp):
        params_plan.send_first(t)

    owner = r * n_col + c
    right_rows = right_sum_ref.shape[1]
    left_rows = left_sum_ref.shape[0]
    stores = []

    def store(m, kind, src, dst):
        copy = pltpu.make_async_copy(src, dst, store_sem.at[m, kind])
        copy.start()
        stores.append(copy)

    def shampoo_products(m):
        for j in range(m * chunks // 3, (m + 1) * chunks // 3):
            gather.last_arrivals(j)
        for j in range(m * chunks // 3, (m + 1) * chunks // 3):
            gather.wait_cols(j)
        span = pl.ds(m * D, D)
        home = pl.ds(pl.multiple_of(m * D + r * depth, 16), depth)
        for b in range(n_row):
            store(m, 3 + b, gathered_ref.at[c * n_row + b, home], block_out.at[m, b])
        root_loads[m].wait()
        lhs_ref[:right_rows] = gathered_ref[owner, span].T
        lhs_ref[right_rows:] = root_ref[m].astype(low)
        left_sum_ref[...] = jnp.zeros_like(left_sum_ref)

        @pl.loop(0, n_row * n_col, unroll=2)
        def _(q):
            cols = pl.ds(pl.multiple_of(q * slice_wide, slice_wide), slice_wide)
            block = gathered_ref[q, span]
            made = dot(lhs_ref[...], block)
            right_sum_ref[m, :, cols] = (0.5 * made[:right_rows]).astype(low)
            half_step_ref[:, cols] = made[right_rows:].astype(low)
            some = pl.ds(pl.multiple_of(m * D + owner * left_rows, 16), left_rows)
            left_sum_ref[...] += dot(gathered_ref[q, some], block, NT)

        left_low_ref[m] = (0.5 * left_sum_ref[...]).astype(low)
        store(m, 0, right_sum_ref.at[m], right_sum_out.at[m])
        store(m, 1, left_low_ref.at[m], left_sum_out.at[m])
        for t in range(tiles):
            n = m * tiles + t
            tile_loads[n].wait()
            step = dot(half_step_ref[...], tile_ref[n % held].astype(low), NT)
            step_ref[m, :, t * tile : (t + 1) * tile] = (SHAMPOO_RATE * step).astype(low)
            load_tile(n + held)
        store(m, 2, step_ref.at[m], step_out.at[m])

    shampoo_products(0)
    shampoo_products(1)
    for t in range(n_dp // 2):
        params_plan.sum_rows(t, 0)
    shampoo_products(2)
    for t in range(n_dp // 2, n_dp):
        params_plan.sum_rows(t, 0)
    first_plan.sum_dp()
    for s in range(1, bits):
        for t in range(n_dp):
            params_plan.sum_rows(t, s)
    for s in range(bits):
        first_plan.sum_rows(s)
    sums = kept[0][:, :split].astype(jnp.float32)
    for p in range(1, n_dp):
        k = dp_order(d, p, n_dp)
        ref = dp_ref.at[k]
        remote(ref, ref, dp_send.at[p - 1], dp_recv.at[k], (d, r, c)).wait_recv()
        sums = sums + dp_ref[k].astype(jnp.float32)
    sum_ref[:, :split] = sums
    sum_ref[:, split:] = first_plan.total().astype(jnp.float32)
    for i in range(n_col):
        end_ref[i] = sum_ref[i * rows : (i + 1) * rows, :]
    for i in range(1, n_col):
        other = (c + i) % n_col
        copy = remote(
            end_ref.at[other], summed_ref.at[c], end_send.at[i], end_recv.at[i], (d, r, other)
        )
        copy.start()
        waits.append(copy.wait_send)
    summed_ref[pl.ds(c, 1)] = end_ref[pl.ds(c, 1)]
    for i in range(1, n_col):
        ref = summed_ref.at[(c + n_col - i) % n_col]
        remote(ref, ref, end_send.at[i], end_recv.at[i], (d, r, c)).wait_recv()
    waits += gather.sends()
    waits += [copy.wait for copy in stores]
    finish([copy.wait_send for copy in params_plan.sent + first_plan.sent])
    finish(waits)


def layer(
    lengths,
    routes,
    prev_logits,
    tokens,
    cotangent,
    w_qkv,
    w_out,
    route_w,
    gains,
    const_vec,
    weight_gu,
    weight_down,
    left_root_gu,
    right_root_down,
    right_root_gu,
    left_root_down,
    dims,
    widths,
):
    n_dp, n_row, n_col = dims
    low = jnp.bfloat16
    f32 = jnp.float32
    total = tokens.shape[0]
    rows = w_qkv.shape[0]
    wide = widths[0] + widths[1] + LANES
    num_ffn = prev_logits.shape[0] - 4
    depth, wide_col = weight_down.shape
    slice_wide = wide_col // n_row
    block_rows = n_col * rows
    wide_rows, wide_cols = left_root_down.shape
    right_rows = wide_cols // n_row // n_col
    left_rows = D // n_row // n_col
    tile = 2 * LANES
    split = wide * 5 // 8 // LANES * LANES
    chunks = 6
    dma = pltpu.SemaphoreType.DMA
    vmem = pl.BlockSpec(memory_space=pltpu.VMEM)
    hbm = pl.BlockSpec(memory_space=pl.ANY)
    whole = (n_col, n_dp, n_row, block_rows, wide)
    assert depth <= tile and 2 * wide_col <= wide_cols and wide >= 2 * D
    return pl.pallas_call(
        functools.partial(layer_kernel, (dims, num_ffn, *widths, chunks)),
        out_shape=[
            jax.ShapeDtypeStruct((total, D), low),
            jax.ShapeDtypeStruct((total, D), f32),
            jax.ShapeDtypeStruct((n_col, rows, wide), f32),
            jax.ShapeDtypeStruct((3, right_rows, wide_cols), low),
            jax.ShapeDtypeStruct((3, left_rows, D), low),
            jax.ShapeDtypeStruct((3, depth, wide_rows), low),
            jax.ShapeDtypeStruct((3, n_row, depth, slice_wide), low),
        ],
        in_specs=[pl.BlockSpec(memory_space=pltpu.SMEM)] + [vmem] * 9 + [hbm] * 6,
        out_specs=[vmem] * 3 + [hbm] * 4,
        scratch_shapes=[
            pltpu.VMEM((n_col, rows, wide), f32),
            pltpu.VMEM((LANES, LANES), f32),
            pltpu.VMEM((n_col, rows, wide), f32),
            pltpu.VMEM((block_rows, wide), f32),
            pltpu.VMEM(whole, low),
            pltpu.VMEM((n_row, 3, depth, slice_wide), low),
            pltpu.VMEM((3, n_row * depth, slice_wide), low),
            pltpu.VMEM((num_ffn, CAP, 2 * D), low),
            pltpu.VMEM((n_dp, n_col, n_row, CAP, 2 * D), low),
            pltpu.VMEM((n_dp, n_col * n_row * CAP, slice_wide), low),
            pltpu.VMEM((n_dp, n_col * n_row * CAP, 2 * slice_wide), low),
            pltpu.VMEM((3 * D, slice_wide), low),
            pltpu.VMEM((total, 3 * D), low),
            pltpu.VMEM((HEADS, total, total), f32),
            pltpu.VMEM((total, D), low),
            pltpu.VMEM((total, D), f32),
            pltpu.VMEM((n_dp, CAP, 2 * D), low),
            pltpu.VMEM((total, D), low),
            pltpu.VMEM((total, D), low),
            pltpu.VMEM((total, 3 * D), low),
            pltpu.VMEM(whole, low),
            pltpu.VMEM((n_dp, block_rows, split), low),
            pltpu.VMEM((n_col, rows, wide), f32),
            pltpu.VMEM((block_rows, wide), f32),
            pltpu.VMEM((n_col * n_row, 3 * D, slice_wide), low),
            pltpu.VMEM((3, depth, D), f32),
            pltpu.VMEM((2, tile, wide_cols), f32),
            pltpu.VMEM((depth, wide_cols), low),
            pltpu.VMEM((right_rows + depth, D), low),
            pltpu.VMEM((3, right_rows, wide_cols), low),
            pltpu.VMEM((left_rows, D), f32),
            pltpu.VMEM((3, left_rows, D), low),
            pltpu.VMEM((3, depth, wide_rows), low),
            dma((n_col,)),
            dma((n_col,)),
            dma((3,)),
            dma((n_row,)),
            dma((n_row,)),
            dma((3,)),
            dma((3 * wide_rows // tile,)),
            dma((3, 3 + n_row)),
            dma((n_dp,)),
            dma((n_dp,)),
            dma((n_dp,)),
            dma((n_dp,)),
            dma((n_col,)),
            dma((n_col,)),
            *spread_sems(dims, n_dp, copied=False),
            *spread_sems(dims, n_dp, copied=False),
            *spread_sems(dims, n_dp, copied=False),
            *spread_sems(dims, chunks),
            *reduce_scratch(dims, CAP, 2 * D, copied=False),
            *reduce_scratch(dims, block_rows, wide, copied=False, lanes=split),
            *dp_first_scratch(dims, block_rows, wide - split),
        ],
        compiler_params=pltpu.CompilerParams(
            collective_id=5, has_side_effects=True, vmem_limit_bytes=VMEM_BYTES
        ),
        name="layer",
    )(
        lengths,
        routes,
        prev_logits,
        tokens,
        cotangent,
        w_qkv,
        w_out,
        route_w,
        gains,
        const_vec,
        weight_gu,
        weight_down,
        left_root_gu,
        right_root_down,
        right_root_gu,
        left_root_down,
    )


def norm_forward(values, gain_vec):
    norm_scale = lax.rsqrt(jnp.mean(values * values, axis=-1, keepdims=True) + NORM_EPS)
    normed = values * norm_scale
    return (normed * gain_vec, normed, norm_scale)


def norm_backward(grad_out, normed, norm_scale, gain_vec):
    grad_normed = grad_out * gain_vec
    inner_mean = jnp.mean(grad_normed * normed, axis=-1, keepdims=True)
    return (norm_scale * (grad_normed - normed * inner_mean), jnp.sum(grad_out * normed, axis=0))


def attention_probs(queries, key_heads, allowed):
    scores = jnp.einsum(
        "qhd,khd->hqk", queries, key_heads, preferred_element_type=jnp.float32
    ) * HEAD ** (-0.5)
    scores = jnp.where(allowed[None], scores, -1e30)
    top_score = jnp.max(scores, axis=-1, keepdims=True)
    exp_scores = jnp.exp(scores - top_score)
    return exp_scores / jnp.sum(exp_scores, axis=-1, keepdims=True)


def diag_update(weight, grad, state, rate):
    new_state = 0.5 * state + 0.5 * grad * grad
    return (new_state, weight - rate * grad / (jnp.sqrt(new_state) + 1e-08))


def diagonal_updates(widths, n_col, summed_ref, in_refs, out_refs, turn_ref):
    wide_qkv, wide_out, route_cols = widths
    rows = summed_ref.shape[1]
    rates = (D ** (-0.5), HEAD ** (-0.5), (4 * D) ** (-0.5), 0.3, 0.5)

    def update(n, cols, grad):
        weight, state = in_refs[2 * n], in_refs[2 * n + 1]
        grad_ref, moment_ref, new_ref = out_refs[3 * n : 3 * n + 3]
        moment, new = diag_update(weight[:, cols], grad, state[:, cols], rates[n])
        grad_ref[:, cols] = grad
        moment_ref[:, cols] = moment
        new_ref[:, cols] = new

    for i in range(n_col):
        update(0, pl.ds(i * wide_qkv, wide_qkv), summed_ref[i, :, :wide_qkv])
        update(1, pl.ds(i * wide_out, wide_out), summed_ref[i, :, wide_qkv + LANES :])
    turn_ref[...] = jnp.zeros_like(turn_ref)
    turn_ref[:rows] = summed_ref[0, :, wide_qkv : wide_qkv + LANES]
    turned = turn_ref[...].T
    whole = pl.ds(0, rows)
    update(2, whole, turned[:route_cols, :rows])
    update(3, whole, turned[route_cols : route_cols + 2, :rows])
    update(4, whole, turned[route_cols + 2 : route_cols + 4, :rows])


def finish_kernel(sizes, *refs):
    n_col, widths = sizes
    (
        right_sum,
        left_sum,
        step,
        block,
        left_gu,
        right_down,
        right_gu,
        left_down,
        weight_gu,
        weight_down,
        result,
        grad_tokens,
        summed,
        *diag,
        out_grad_gu,
        out_grad_down,
        out_left_gu,
        out_right_down,
        out_right_gu,
        out_left_down,
        out_weight_gu,
        out_weight_down,
        out_result,
        out_grad_tokens,
        right_sum_buf,
        left_sum_buf,
        step_buf,
        block_buf,
        right_buf,
        left_buf,
        weight_buf,
        grad_buf,
        result_buf,
        tokens_buf,
        turn_buf,
        in_sem,
        out_sem,
    ) = refs
    diag_in, diag_out = diag[:10], diag[10:]
    mats = range(3)
    f32 = jnp.float32
    n_row, _, slice_wide = block_buf.shape[1:]
    lefts = [left_gu.at[0], left_gu.at[1], right_down]
    rights = [right_gu.at[0], right_gu.at[1], left_down]
    weights = [weight_gu.at[:, 0], weight_gu.at[:, 1], weight_down]
    out_lefts = [out_left_gu.at[0], out_left_gu.at[1], out_right_down]
    out_rights = [out_right_gu.at[0], out_right_gu.at[1], out_left_down]
    out_weights = [out_weight_gu.at[:, 0], out_weight_gu.at[:, 1], out_weight_down]
    out_grads = [out_grad_gu.at[:, 0], out_grad_gu.at[:, 1], out_grad_down]
    loads = {}

    def load(m, kind, src, dst):
        copy = pltpu.make_async_copy(src, dst, in_sem.at[m, kind])
        copy.start()
        loads[m, kind] = copy

    stores = []

    def store(m, kind, src, dst):
        copy = pltpu.make_async_copy(src, dst, out_sem.at[m, kind])
        copy.start()
        stores.append(copy)

    for m in mats:
        load(m, 0, right_sum.at[m], right_sum_buf.at[m])
        load(m, 1, rights[m], right_buf.at[m])
        load(m, 2, block.at[m], block_buf.at[m])
        load(m, 3, step.at[m], step_buf.at[m])
        load(m, 4, weights[m], weight_buf.at[m])
        load(m, 5, left_sum.at[m], left_sum_buf.at[m])
        load(m, 6, lefts[m], left_buf.at[m])
    load(0, 7, result, result_buf)
    load(1, 7, grad_tokens, tokens_buf)
    diagonal_updates(widths, n_col, summed, diag_in, diag_out, turn_buf)
    for m in mats:
        loads[m, 0].wait()
        loads[m, 1].wait()
        right_buf[m] = 0.5 * right_buf[m] + right_sum_buf[m].astype(f32)
        store(m, 0, right_buf.at[m], out_rights[m])
        loads[m, 2].wait()
        for b in range(n_row):
            grad_buf[m, :, b * slice_wide : (b + 1) * slice_wide] = block_buf[m, b].astype(f32)
        store(m, 1, grad_buf.at[m], out_grads[m])
        loads[m, 3].wait()
        loads[m, 4].wait()
        weight_buf[m] = weight_buf[m] - step_buf[m].astype(f32)
        store(m, 2, weight_buf.at[m], out_weights[m])
        loads[m, 5].wait()
        loads[m, 6].wait()
        left_buf[m] = 0.5 * left_buf[m] + left_sum_buf[m].astype(f32)
        store(m, 3, left_buf.at[m], out_lefts[m])
    loads[0, 7].wait()
    store(0, 4, result_buf, out_result)
    loads[1, 7].wait()
    store(1, 4, tokens_buf, out_grad_tokens)
    for copy in stores:
        copy.wait()


def finish_update(
    products,
    left_gu,
    right_down,
    right_gu,
    left_down,
    weight_gu,
    weight_down,
    result,
    grad_tokens,
    summed,
    diag_in,
    n_col,
    widths,
):
    f32 = jnp.float32
    dma = pltpu.SemaphoreType.DMA
    hbm = pl.BlockSpec(memory_space=pl.ANY)
    vmem = pl.BlockSpec(memory_space=pltpu.VMEM)
    right_sum, left_sum, step, block = products
    args = (
        *products,
        left_gu,
        right_down,
        right_gu,
        left_down,
        weight_gu,
        weight_down,
        result,
        grad_tokens,
        summed,
        *diag_in,
    )
    outs = [weight for weight in diag_in[::2] for _ in range(3)]
    outs += [weight_gu, weight_down, left_gu, right_down, right_gu, left_down]
    outs += [weight_gu, weight_down, result, grad_tokens]
    return pl.pallas_call(
        functools.partial(finish_kernel, (n_col, widths)),
        out_shape=[jax.ShapeDtypeStruct(like.shape, like.dtype) for like in outs],
        in_specs=[hbm] * 12 + [vmem] * 11,
        out_specs=[vmem] * 15 + [hbm] * 10,
        scratch_shapes=[
            pltpu.VMEM(right_sum.shape, right_sum.dtype),
            pltpu.VMEM(left_sum.shape, left_sum.dtype),
            pltpu.VMEM(step.shape, step.dtype),
            pltpu.VMEM(block.shape, block.dtype),
            pltpu.VMEM(right_sum.shape, f32),
            pltpu.VMEM(left_sum.shape, f32),
            pltpu.VMEM(step.shape, f32),
            pltpu.VMEM(step.shape, f32),
            pltpu.VMEM(result.shape, result.dtype),
            pltpu.VMEM(grad_tokens.shape, f32),
            pltpu.VMEM((LANES, LANES), f32),
            dma((3, 8)),
            dma((3, 5)),
        ],
        compiler_params=pltpu.CompilerParams(vmem_limit_bytes=VMEM_BYTES),
        name="finish",
    )(*args)


def shampoo_plain(
    grads,
    left_root_gu,
    right_root_down,
    right_root_gu,
    left_root_down,
    left_gu,
    right_down,
    right_gu,
    left_down,
    weight_gu,
    weight_down,
    n_row,
    n_col,
):
    low = jnp.bfloat16
    blocks, _, slice_wide = grads.shape
    model = left_root_gu.shape[2]
    r = lax.axis_index("row")
    c = lax.axis_index("col")
    owner = r * n_col + c
    left_rows = right_down.shape[0]
    right_rows = left_down.shape[0]
    product = functools.partial(jnp.einsum, preferred_element_type=jnp.float32)
    whole = grads.reshape(blocks, 3, model, slice_wide).transpose(1, 2, 0, 3).reshape(3, model, -1)
    mine_left = lax.dynamic_slice_in_dim(whole, owner * left_rows, left_rows, 1)
    mine_right = lax.dynamic_slice_in_dim(whole, owner * right_rows, right_rows, 2)
    left_sum = 0.5 * product("mif,mjf->mij", mine_left, whole)
    right_sum = 0.5 * product("mdi,mdj->mij", mine_right, whole)
    roots = jnp.concatenate([left_root_gu, right_root_down[None]]).astype(low)
    wides = jnp.concatenate([right_root_gu, left_root_down[None]]).astype(low)
    step = product("mid,mdf->mif", roots, whole).astype(low)
    step = SHAMPOO_RATE * product("mif,mjf->mij", step, wides)
    depth, wide_rows = weight_down.shape
    block = lax.dynamic_slice(whole, (0, r * depth, c * wide_rows), (3, depth, wide_rows))
    block = block.astype(jnp.float32)
    return (
        block[:2].transpose(1, 0, 2),
        block[2],
        0.5 * left_gu + left_sum[:2],
        0.5 * right_down + left_sum[2],
        0.5 * right_gu + right_sum[:2],
        0.5 * left_down + right_sum[2],
        weight_gu - step[:2].transpose(1, 0, 2),
        weight_down - step[2],
    )


def body_tiled(
    tokens,
    lengths,
    routes,
    prev_logits,
    cotangent,
    w_qkv,
    w_out,
    route_w,
    gains,
    const_vec,
    stat_qkv,
    stat_out,
    stat_route,
    stat_gains,
    stat_const,
    w_gate_up,
    w_down,
    left_gu,
    right_gu,
    left_down,
    right_down,
    left_root_gu,
    right_root_gu,
    left_root_down,
    right_root_down,
):
    dims = mesh_sizes()
    n_col = dims[2]
    wide_qkv = w_qkv.shape[1] // n_col
    wide_out = w_out.shape[1] // n_col
    widths = (wide_qkv, wide_out, route_w.shape[1])
    result, grad_input, summed, *products = layer(
        lengths,
        routes.T,
        prev_logits.T,
        tokens,
        cotangent,
        w_qkv,
        w_out,
        route_w.T,
        gains,
        const_vec,
        w_gate_up[0],
        w_down[0].T,
        left_root_gu[0],
        right_root_down[0],
        right_root_gu[0],
        left_root_down[0],
        dims,
        widths,
    )
    outs = finish_update(
        products,
        left_gu[0],
        right_down[0],
        right_gu[0],
        left_down[0],
        w_gate_up[0],
        w_down[0].T,
        result,
        grad_input,
        summed,
        [
            w_qkv,
            stat_qkv,
            w_out,
            stat_out,
            route_w.T,
            stat_route.T,
            gains,
            stat_gains,
            const_vec,
            stat_const,
        ],
        n_col,
        widths,
    )
    diag = list(outs[:15])
    diag[6:9] = [part.T for part in diag[6:9]]
    (
        grad_gate_up,
        grad_down,
        new_left_gu,
        new_right_down,
        new_right_gu,
        new_left_down,
        new_gate_up,
        new_down,
        result,
        grad_input,
    ) = outs[15:]
    return (
        result,
        grad_input,
        *diag,
        grad_gate_up[None],
        grad_down.T[None],
        new_left_gu[None],
        new_right_gu[None],
        new_left_down[None],
        new_right_down[None],
        new_gate_up[None],
        new_down.T[None],
    )


def body(
    tokens,
    lengths,
    routes,
    prev_logits,
    cotangent,
    w_qkv,
    w_out,
    route_w,
    gains,
    const_vec,
    stat_qkv,
    stat_out,
    stat_route,
    stat_gains,
    stat_const,
    w_gate_up,
    w_down,
    left_gu,
    right_gu,
    left_down,
    right_down,
    left_root_gu,
    right_root_gu,
    left_root_down,
    right_root_down,
):
    dims = mesh_sizes()
    n_dp, n_row, n_col = dims
    low = jnp.bfloat16
    row_total = tokens.shape[0]
    total_experts = prev_logits.shape[1]
    num_ffn = total_experts - 4
    seq_count = lengths.shape[1]
    shard_rows = w_qkv.shape[0]
    wide_qkv = w_qkv.shape[1] // n_col
    wide_out = w_out.shape[1] // n_col
    route_cols = route_w.shape[1]
    wide = wide_qkv + wide_out + LANES

    def by_col(matrix):
        return matrix.reshape(matrix.shape[0], n_col, -1).transpose(1, 0, 2)

    def small_block(route_part, gain_part, const_part):
        together = jnp.concatenate([route_part, gain_part.T, const_part.T], axis=1)
        return jnp.pad(together, ((0, 0), (0, LANES - together.shape[1])))

    small = small_block(route_w, gains, const_vec)
    shard = jnp.concatenate(
        [by_col(w_qkv), by_col(w_out), jnp.broadcast_to(small[None], (n_col, shard_rows, LANES))],
        axis=2,
    )
    whole = param_gather(shard, dims).reshape(n_col, D, wide)
    full_qkv = [whole[i, :, :wide_qkv] for i in range(n_col)]
    full_out = [whole[i, :, wide_qkv : wide_qkv + wide_out] for i in range(n_col)]
    full_small = whole[0, :, wide_qkv + wide_out :]
    full_route = full_small[:, :route_cols]
    row_vectors = full_small[:, route_cols : route_cols + 4].T.astype(jnp.float32)
    gain_one, gain_two, const_rows = row_vectors[0], row_vectors[1], row_vectors[2:4]

    row_depth = w_gate_up.shape[1]
    col_width = w_gate_up.shape[3]
    slice_wide = col_width // n_row
    gu_slices = w_gate_up[0].astype(low).reshape(row_depth, 2, n_row, slice_wide)
    gu_slices = gu_slices.transpose(2, 0, 1, 3)
    gu_own = lax.all_to_all(gu_slices, "row", split_axis=0, concat_axis=0, tiled=True)
    gu_own = gu_own.reshape(n_row * row_depth, 2 * slice_wide)
    down_slices = w_down[0].astype(low).reshape(n_row, slice_wide, row_depth)
    down_own = lax.all_to_all(down_slices, "row", split_axis=0, concat_axis=0, tiled=True)
    down_own = down_own.transpose(1, 0, 2).reshape(slice_wide, n_row * row_depth)

    positions = jnp.arange(row_total, dtype=jnp.int32)
    seq_ends = jnp.cumsum(lengths[0])
    doc_index = jnp.sum((positions[:, None] >= seq_ends[None, :]).astype(jnp.int32), axis=1)
    valid_rows = (doc_index < seq_count).astype(jnp.float32)[:, None]
    allowed = (doc_index[:, None] == doc_index[None, :]) & (
        positions[:, None] >= positions[None, :]
    )
    inputs = tokens.astype(jnp.float32)
    h_one, normed_one, scale_one = norm_forward(inputs, gain_one)
    h_one_low = h_one.astype(low)
    qkv_rows = jnp.concatenate([dot(h_one_low, part) for part in full_qkv], axis=1).astype(low)
    qkv_rows = qkv_rows.reshape(row_total, 3, HEADS, HEAD)
    queries, key_heads, values = (qkv_rows[:, 0], qkv_rows[:, 1], qkv_rows[:, 2])
    softmax_probs = attention_probs(queries, key_heads, allowed)
    probs_low = softmax_probs.astype(low)
    mixed_heads = jnp.einsum("hqk,khd->qhd", probs_low, values, preferred_element_type=jnp.float32)
    mixed_heads = mixed_heads.reshape(row_total, D).astype(low)
    attn_out = jnp.concatenate([dot(mixed_heads, part) for part in full_out], axis=1)
    first_sum = inputs + valid_rows * attn_out
    h_two, normed_two, scale_two = norm_forward(first_sum, gain_two)
    h_two_low = h_two.astype(low)
    logits_all = dot(h_two_low, full_route)
    logits = logits_all[:, :total_experts] + prev_logits
    pick_table = (
        routes[:, :, None] == jnp.arange(total_experts, dtype=jnp.int32)[None, None, :]
    ).astype(jnp.float32)
    chosen = jnp.sum(pick_table * logits[:, None, :], axis=-1)
    gate_weights = jax.nn.softmax(chosen, axis=-1)
    const_mix = jax.nn.softmax(logits_all[:, total_experts:].reshape(row_total, 2, 2), axis=-1)

    earlier = dot(
        (positions[:, None] > positions[None, :]).astype(low),
        jnp.sum(pick_table, axis=1).astype(low),
    )
    slot_index = jnp.sum(earlier[:, None, :] * pick_table, axis=-1).astype(jnp.int32)
    where_in = jnp.where(routes < num_ffn, routes * CAP + slot_index, -1)
    slot_ids = jnp.arange(num_ffn * CAP, dtype=jnp.int32)
    place_first = where_in[:, 0:1] == slot_ids[None, :]
    place_second = where_in[:, 1:2] == slot_ids[None, :]
    place_both = (place_first | place_second).astype(low)
    slot_gate = jnp.sum(
        place_first.astype(jnp.float32) * gate_weights[:, 0:1]
        + place_second.astype(jnp.float32) * gate_weights[:, 1:2],
        axis=0,
    )
    grad_y = cotangent.astype(jnp.float32) * valid_rows
    sent_rows = dot(place_both, h_two_low, TN).astype(low)
    grad_made = (slot_gate[:, None] * dot(place_both, grad_y.astype(low), TN)).astype(low)
    sent_both = jnp.concatenate(
        [sent_rows.reshape(num_ffn, CAP, D), grad_made.reshape(num_ffn, CAP, D)], axis=2
    )

    arrived = token_gather(sent_both, dims).reshape(-1, 2 * D)
    rows_in = arrived[:, :D]
    grads_in = arrived[:, D:]
    pre_act = dot(rows_in, gu_own)
    gate_part = pre_act[:, :slice_wide]
    up_part = pre_act[:, slice_wide:]
    sigma = jax.nn.sigmoid(gate_part)
    silu = gate_part * sigma
    hidden = (silu * up_part).astype(low)
    made_rows = dot(hidden, down_own).astype(low)
    grad_hidden = dot(grads_in, down_own, NT)
    grad_pre = jnp.concatenate(
        [
            grad_hidden * up_part * sigma * (1.0 + gate_part * (1.0 - sigma)),
            grad_hidden * silu,
        ],
        axis=1,
    ).astype(low)
    grad_rows = dot(grad_pre, gu_own, NT).astype(low)
    parts_back = jnp.concatenate([made_rows, grad_rows], axis=1)
    parts_back = parts_back.reshape(n_col, n_dp, n_row, CAP, 2 * D)
    came_back = token_reduce(parts_back, dims).reshape(num_ffn * CAP, 2 * D)
    expert_out = came_back[:, :D]
    grad_sent = came_back[:, D:]

    grad_gu_own = dot(rows_in, grad_pre, TN).astype(low)
    grad_down_own = dot(hidden, grads_in, TN).astype(low)
    grads_own = jnp.concatenate(
        [grad_gu_own[:, :slice_wide], grad_gu_own[:, slice_wide:], grad_down_own.T], axis=0
    )
    gathered = plane_gather(grads_own.reshape(4, -1, slice_wide), dims)
    gathered = gathered.reshape(n_col * n_row, 3 * D, slice_wide)

    is_ffn_first = dot(place_first.astype(low), expert_out)
    is_ffn_second = dot(place_second.astype(low), expert_out)
    picked = jnp.stack([is_ffn_first, is_ffn_second], axis=1)
    copy_sel = (routes == num_ffn + 1).astype(jnp.float32)
    const_sel = (
        routes[:, :, None] == num_ffn + 2 + jnp.arange(2, dtype=jnp.int32)[None, None, :]
    ).astype(jnp.float32)
    const_out = (
        const_mix[:, :, 0:1] * h_two[:, None, :] + const_mix[:, :, 1:2] * const_rows[None, :, :]
    )
    outputs = (
        picked
        + copy_sel[:, :, None] * h_two[:, None, :]
        + const_sel[:, :, 0:1] * const_out[:, None, 0, :]
        + const_sel[:, :, 1:2] * const_out[:, None, 1, :]
    )
    moe_out = valid_rows * jnp.sum(gate_weights[:, :, None] * outputs, axis=1)
    result = (first_sum + moe_out).astype(low)
    grad_gate = jnp.sum(grad_y[:, None, :] * outputs, axis=-1)
    grad_chosen = gate_weights * (
        grad_gate - jnp.sum(gate_weights * grad_gate, axis=-1, keepdims=True)
    )
    grad_logits = jnp.sum(grad_chosen[:, :, None] * pick_table, axis=1)
    const_weight = jnp.sum(const_sel * gate_weights[:, :, None], axis=1)
    mix_first = const_weight * jnp.sum(grad_y * h_two, axis=-1, keepdims=True)
    mix_second = const_weight * jnp.stack(
        [jnp.sum(grad_y * const_rows[0], axis=-1), jnp.sum(grad_y * const_rows[1], axis=-1)], axis=1
    )
    grad_mix = jnp.stack([mix_first, mix_second], axis=-1)
    grad_mix_logits = const_mix * (grad_mix - jnp.sum(const_mix * grad_mix, axis=-1, keepdims=True))
    grad_logits_all = jnp.concatenate(
        [grad_logits, grad_mix_logits.reshape(row_total, 4)], axis=1
    ).astype(low)
    grad_route_full = dot(h_two_low, grad_logits_all, TN)
    const_scale = const_weight * const_mix[:, :, 1]
    grad_const_full = jnp.stack(
        [
            jnp.sum(const_scale[:, 0:1] * grad_y, axis=0),
            jnp.sum(const_scale[:, 1:2] * grad_y, axis=0),
        ]
    )
    back_rows = dot(place_both, grad_sent)
    own_weight = jnp.sum(gate_weights * copy_sel, axis=1, keepdims=True) + jnp.sum(
        const_weight * const_mix[:, :, 0], axis=1, keepdims=True
    )
    grad_h_two = dot(grad_logits_all, full_route, NT) + back_rows + own_weight * grad_y
    grad_first, grad_gain_two = norm_backward(grad_h_two, normed_two, scale_two, gain_two)
    grad_first = grad_first + cotangent.astype(jnp.float32)
    grad_attn = (valid_rows * grad_first).astype(low)
    grad_mixed = functools.reduce(
        jnp.add,
        [
            dot(grad_attn[:, i * wide_out : (i + 1) * wide_out], part, NT)
            for i, part in enumerate(full_out)
        ],
    ).astype(low)
    grad_mixed = grad_mixed.reshape(row_total, HEADS, HEAD)
    grad_values = jnp.einsum(
        "hqk,qhd->khd", probs_low, grad_mixed, preferred_element_type=jnp.float32
    )
    grad_probs = jnp.einsum("qhd,khd->hqk", grad_mixed, values, preferred_element_type=jnp.float32)
    grad_scores = softmax_probs * (
        grad_probs - jnp.sum(softmax_probs * grad_probs, axis=-1, keepdims=True)
    )
    grad_scores = grad_scores.astype(low)
    grad_queries = jnp.einsum(
        "hqk,khd->qhd", grad_scores, key_heads, preferred_element_type=jnp.float32
    ) * HEAD ** (-0.5)
    grad_keys = jnp.einsum(
        "hqk,qhd->khd", grad_scores, queries, preferred_element_type=jnp.float32
    ) * HEAD ** (-0.5)
    grad_qkv_rows = (
        jnp.stack([grad_queries, grad_keys, grad_values], axis=1)
        .reshape(row_total, 3 * D)
        .astype(low)
    )
    grad_h_one = functools.reduce(
        jnp.add,
        [
            dot(grad_qkv_rows[:, i * wide_qkv : (i + 1) * wide_qkv], part, NT)
            for i, part in enumerate(full_qkv)
        ],
    )
    grad_input, grad_gain_one = norm_backward(grad_h_one, normed_one, scale_one, gain_one)
    grad_input = grad_input + grad_first
    grad_gains_full = jnp.stack([grad_gain_one, grad_gain_two])

    grad_small = small_block(grad_route_full, grad_gains_full, grad_const_full).astype(low)
    param_parts = jnp.stack(
        [
            jnp.concatenate(
                [
                    dot(h_one_low, grad_qkv_rows[:, i * wide_qkv : (i + 1) * wide_qkv], TN).astype(
                        low
                    ),
                    dot(mixed_heads, grad_attn[:, i * wide_out : (i + 1) * wide_out], TN).astype(
                        low
                    ),
                    grad_small,
                ],
                axis=1,
            )
            for i in range(n_col)
        ]
    )
    summed = param_reduce(
        param_parts.reshape(n_col, n_dp, n_row, n_col * shard_rows, wide), dims
    )

    def from_col(parts):
        return parts.transpose(1, 0, 2).reshape(parts.shape[1], -1)

    grad_qkv = from_col(summed[:, :, :wide_qkv])
    grad_attn_out = from_col(summed[:, :, wide_qkv : wide_qkv + wide_out])
    sum_small = summed[0, :, wide_qkv + wide_out :]
    grad_route = sum_small[:, :route_cols]
    grad_gains = sum_small[:, route_cols : route_cols + 2].T
    grad_const = sum_small[:, route_cols + 2 : route_cols + 4].T
    moment_qkv, new_qkv = diag_update(w_qkv, grad_qkv, stat_qkv, D ** (-0.5))
    moment_attn_out, new_attn_out = diag_update(w_out, grad_attn_out, stat_out, HEAD ** (-0.5))
    moment_route, new_route = diag_update(route_w, grad_route, stat_route, (4 * D) ** (-0.5))
    moment_gains, new_gains = diag_update(gains, grad_gains, stat_gains, 0.3)
    moment_const, new_const = diag_update(const_vec, grad_const, stat_const, 0.5)

    (
        grad_gate_up,
        grad_down,
        new_left_gu,
        new_right_down,
        new_right_gu,
        new_left_down,
        new_gate_up,
        new_down,
    ) = shampoo_plain(
        gathered,
        left_root_gu[0],
        right_root_down[0],
        right_root_gu[0],
        left_root_down[0],
        left_gu[0],
        right_down[0],
        right_gu[0],
        left_down[0],
        w_gate_up[0],
        w_down[0].T,
        n_row,
        n_col,
    )
    return (
        result,
        grad_input,
        grad_qkv,
        moment_qkv,
        new_qkv,
        grad_attn_out,
        moment_attn_out,
        new_attn_out,
        grad_route,
        moment_route,
        new_route,
        grad_gains,
        moment_gains,
        new_gains,
        grad_const,
        moment_const,
        new_const,
        grad_gate_up[None],
        grad_down.T[None],
        new_left_gu[None],
        new_right_gu[None],
        new_left_down[None],
        new_right_down[None],
        new_gate_up[None],
        new_down.T[None],
    )


def solution(mesh):
    placed = (
        P(("dp", "row", "col"), None),
        P(("dp", "row", "col"), None),
        P(("dp", "row", "col"), None),
        P(("dp", "row", "col"), None),
        P(("dp", "row", "col"), None),
        P(("dp", "row", "col"), None),
        P(("dp", "row", "col"), None),
        P(("dp", "row", "col"), None),
        P(None, ("dp", "row", "col")),
        P(None, ("dp", "row", "col")),
        P(("dp", "row", "col"), None),
        P(("dp", "row", "col"), None),
        P(("dp", "row", "col"), None),
        P(None, ("dp", "row", "col")),
        P(None, ("dp", "row", "col")),
        P("dp", "row", None, "col"),
        P("dp", "col", "row"),
        P("dp", None, ("row", "col"), None),
        P("dp", None, ("row", "col"), None),
        P("dp", ("row", "col"), None),
        P("dp", ("row", "col"), None),
        P("dp", None, "row", None),
        P("dp", None, "col", None),
        P("dp", "col", None),
        P("dp", "row", None),
    )
    tiled = 3 * D % (mesh.shape["col"] * LANES) == 0 and D % (mesh.shape["col"] * LANES) == 0
    tiled = tiled and D // mesh.shape["dp"] // mesh.shape["row"] % 16 == 0
    return jax.shard_map(
        body_tiled if tiled else body,
        mesh=mesh,
        in_specs=placed,
        out_specs=(
            P(("dp", "row", "col"), None),
            P(("dp", "row", "col"), None),
            P(("dp", "row", "col"), None),
            P(("dp", "row", "col"), None),
            P(("dp", "row", "col"), None),
            P(("dp", "row", "col"), None),
            P(("dp", "row", "col"), None),
            P(("dp", "row", "col"), None),
            P(("dp", "row", "col"), None),
            P(("dp", "row", "col"), None),
            P(("dp", "row", "col"), None),
            P(None, ("dp", "row", "col")),
            P(None, ("dp", "row", "col")),
            P(None, ("dp", "row", "col")),
            P(None, ("dp", "row", "col")),
            P(None, ("dp", "row", "col")),
            P(None, ("dp", "row", "col")),
            P("dp", "row", None, "col"),
            P("dp", "col", "row"),
            P("dp", None, ("row", "col"), None),
            P("dp", None, ("row", "col"), None),
            P("dp", ("row", "col"), None),
            P("dp", ("row", "col"), None),
            P("dp", "row", None, "col"),
            P("dp", "col", "row"),
        ),
        check_vma=False,
    )
```

```python
import functools
import types

import jax
import jax.numpy as jnp
from jax import lax
from jax.experimental import pallas as pl
from jax.experimental.pallas import tpu as pltpu
from jax.sharding import PartitionSpec as P

D = 768
HEADS = 12
HEAD = 64
CAP = 32
LANES = 128


NORM_EPS = 1e-06
SHAMPOO_RATE = 0.5
MESH = pl.DeviceIdType.MESH
VMEM_BYTES = 62 * 2**20


def dot(left, right, dims=(((1,), (0,)), ((), ()))):
    return lax.dot_general(left, right, dims, preferred_element_type=jnp.float32)


NT = (((1,), (1,)), ((), ()))
TN = (((0,), (0,)), ((), ()))


def flip(index, bit):
    return index + bit * (1 - 2 * ((index // bit) % 2))


def flip_all(index, mask, bits):
    for dim in range(bits):
        if mask & (1 << dim):
            index = flip(index, 1 << dim)
    return index


def dp_order(d, p, count):
    if p == 0:
        return d
    upper = d // max(1, count // 2)
    low_d = d + upper * (count - 1 - 2 * d)
    at = p - 1 + (p - 1 - low_d + count) // count
    return at + upper * (count - 1 - 2 * at)


def mesh_sizes():
    return tuple(lax.axis_size(name) for name in ("dp", "row", "col"))


def bits_of(count):
    bits = count.bit_length() - 1
    assert 1 << bits == count
    return bits


def greet(over_dp, dims, place, all_rows=False):
    n_dp, n_row, n_col = dims
    d, r, c = place
    peers = []
    if over_dp:
        peers += [((d + j) % n_dp, r, c) for j in range(1, n_dp)]
    if all_rows:
        peers += [(d, (r + i) % n_row, c) for i in range(1, n_row)]
    else:
        peers += [(d, flip(r, 1 << dim), c) for dim in range(bits_of(n_row))]
    peers += [(d, r, (c + i) % n_col) for i in range(1, n_col)]
    barrier = pltpu.get_barrier_semaphore()
    for peer in peers:
        pl.semaphore_signal(barrier, inc=1, device_id=peer, device_id_type=MESH)
    pl.semaphore_wait(barrier, len(peers))


def remote(src, dst, send_sem, recv_sem, device):
    return pltpu.make_async_remote_copy(
        src_ref=src,
        dst_ref=dst,
        send_sem=send_sem,
        recv_sem=recv_sem,
        device_id=device,
        device_id_type=MESH,
    )


def plan_spread(dims, place, chunks, over_dp, own, dp_source, slot, sems):
    n_dp, n_row, n_col = dims
    d, r, c = place
    bits = bits_of(n_row)
    dp_send, dp_recv, row_send, row_recv, col_send, col_recv, own_sem = sems
    sent = []

    def block(j, x):
        return slot(c, j, flip_all(r, x, bits))

    def to_row(j, src, x, bit):
        copy = remote(
            src,
            block(j, x),
            row_send.at[j, (x ^ bit) - 1],
            row_recv.at[j, (x ^ bit) - 1],
            (d, flip(r, bit), c),
        )
        copy.start()
        sent.append(copy)

    def to_cols(j, src, x):
        for i in range(1, n_col):
            copy = remote(
                src,
                block(j, x),
                col_send.at[j, x, i - 1],
                col_recv.at[j, x, i - 1],
                (d, r, (c + i) % n_col),
            )
            copy.start()
            sent.append(copy)

    def order(j):
        return [1 << ((j + s) % bits) for s in range(bits)]

    locals_ = {}

    def start(j):
        if over_dp and j > 0:
            src = block(j, 0)
            origin = dp_order(d, j, n_dp)
            remote(src, src, dp_send.at[j - 1], dp_recv.at[origin], (d, r, c)).wait_recv()
        elif own is None:
            src = block(j, 0)
        else:
            src = own(j)
            keep = pltpu.make_async_copy(src, block(j, 0), own_sem.at[j])
            keep.start()
            locals_[j] = keep
        for bit in order(j):
            to_row(j, src, 0, bit)
        to_cols(j, src, 0)

    def arrived(j, x, later_dims):
        ref = block(j, x)
        remote(ref, ref, row_send.at[j, x - 1], row_recv.at[j, x - 1], (d, r, c)).wait_recv()
        for later in later_dims:
            to_row(j, ref, x, later)
        to_cols(j, ref, x)

    def pass_on(j):
        have = [0]
        dim_order = order(j)
        for s, bit in enumerate(dim_order[:-1]):
            new = [x ^ bit for x in have]
            for x in new:
                arrived(j, x, dim_order[s + 1 :])
            have += new

    def last_arrivals(j):
        bit = order(j)[-1]
        for x in range(n_row):
            if x & bit:
                arrived(j, x, [])

    def send_dp():
        for j in range(1, n_dp):
            peer = dp_order(d, j, n_dp)
            copy = remote(
                dp_source(peer),
                slot(c, ("from", d), r),
                dp_send.at[j - 1],
                dp_recv.at[d],
                (peer, r, c),
            )
            copy.start()
            sent.append(copy)

    def wait_cols(j):
        for x in range(n_row):
            for i in range(1, n_col):
                ref = slot((c + n_col - i) % n_col, j, flip_all(r, x, bits))
                remote(
                    ref, ref, col_send.at[j, x, i - 1], col_recv.at[j, x, i - 1], (d, r, c)
                ).wait_recv()
        if j in locals_:
            locals_[j].wait()

    def sends():
        return [copy.wait_send for copy in sent]

    return types.SimpleNamespace(
        start=start,
        send_dp=send_dp,
        pass_on=pass_on,
        last_arrivals=last_arrivals,
        wait_cols=wait_cols,
        sends=sends,
    )


def spread_blocks(dims, place, chunks, over_dp, own, dp_source, slot, sems, between=None):
    plan = plan_spread(dims, place, chunks, over_dp, own, dp_source, slot, sems)
    plan.start(0)
    if over_dp:
        plan.send_dp()
        for j in range(1, chunks):
            plan.start(j)
            plan.pass_on(j - 1)
        plan.pass_on(chunks - 1)
    else:
        for j in range(1, chunks):
            plan.start(j)
        for j in range(chunks):
            plan.pass_on(j)
    if between is not None:
        between()
    for j in range(chunks):
        plan.last_arrivals(j)
    for j in range(chunks):
        plan.wait_cols(j)
    return plan.sends()


def finish(waits):
    for wait in waits:
        wait()


def spread_sems(dims, chunks, copied=True):
    n_dp, n_row, n_col = dims
    dma = pltpu.SemaphoreType.DMA
    return [
        dma((max(1, n_dp - 1),)),
        dma((n_dp,)),
        dma((chunks, max(1, n_row - 1))),
        dma((chunks, max(1, n_row - 1))),
        dma((chunks, n_row, max(1, n_col - 1))),
        dma((chunks, n_row, max(1, n_col - 1))),
        dma((chunks if copied else 1,)),
    ]


def axis_place():
    return tuple(lax.axis_index(name) for name in ("dp", "row", "col"))


def param_gather_kernel(dims, shard_ref, out_ref, swap_ref, block_ref, swap_send, swap_recv, *sems):
    n_dp, n_row, n_col = dims
    place = axis_place()
    d, r, c = place
    rows = shard_ref.shape[1]
    greet(True, dims, place)
    copies = []
    for i in range(1, n_col):
        other = (c + i) % n_col
        copy = remote(
            shard_ref.at[other], swap_ref.at[c], swap_send.at[i], swap_recv.at[i], (d, r, other)
        )
        copy.start()
        copies.append(copy)
    swap_ref[pl.ds(c, 1)] = shard_ref[pl.ds(c, 1)]
    for copy in copies:
        copy.wait()
    for i in range(n_col):
        block_ref[i * rows : (i + 1) * rows, :] = swap_ref[i]
    low_ref = sems[-1]
    low_ref[...] = block_ref[...].astype(jnp.bfloat16)

    def slot(col, j, b):
        k = j[1] if isinstance(j, tuple) else dp_order(d, j, n_dp)
        return out_ref.at[col, k, b]

    finish(
        spread_blocks(
            dims, place, n_dp, True, lambda j: low_ref, lambda k: low_ref, slot, sems[:-1]
        )
    )


def param_gather(shard, dims):
    n_dp, n_row, n_col = dims
    _, rows, width = shard.shape
    dma = pltpu.SemaphoreType.DMA
    return pl.pallas_call(
        functools.partial(param_gather_kernel, dims),
        out_shape=jax.ShapeDtypeStruct((n_col, n_dp, n_row, n_col * rows, width), jnp.bfloat16),
        in_specs=[pl.BlockSpec(memory_space=pltpu.VMEM)],
        out_specs=pl.BlockSpec(memory_space=pl.ANY),
        scratch_shapes=[
            pltpu.VMEM((n_col, rows, width), jnp.float32),
            pltpu.VMEM((n_col * rows, width), jnp.float32),
            dma((n_col,)),
            dma((n_col,)),
            *spread_sems(dims, n_dp),
            pltpu.VMEM((n_col * rows, width), jnp.bfloat16),
        ],
        compiler_params=pltpu.CompilerParams(
            collective_id=0, has_side_effects=True, vmem_limit_bytes=VMEM_BYTES
        ),
        name="param_gather",
    )(shard)


def token_gather_kernel(dims, src_ref, out_ref, *sems):
    n_dp, n_row, n_col = dims
    place = axis_place()
    d = place[0]
    greet(True, dims, place)

    def slot(col, j, b):
        k = j[1] if isinstance(j, tuple) else dp_order(d, j, n_dp)
        return out_ref.at[col, k, b]

    finish(
        spread_blocks(
            dims,
            place,
            n_dp,
            True,
            lambda j: src_ref.at[d],
            lambda k: src_ref.at[k],
            slot,
            sems,
        )
    )


def token_gather(rows, dims):
    n_dp, n_row, n_col = dims
    _, slots, width = rows.shape
    return pl.pallas_call(
        functools.partial(token_gather_kernel, dims),
        out_shape=jax.ShapeDtypeStruct((n_col, n_dp, n_row, slots, width), rows.dtype),
        in_specs=[pl.BlockSpec(memory_space=pl.ANY)],
        out_specs=pl.BlockSpec(memory_space=pl.ANY),
        scratch_shapes=spread_sems(dims, n_dp),
        compiler_params=pltpu.CompilerParams(
            collective_id=1, has_side_effects=True, vmem_limit_bytes=VMEM_BYTES
        ),
        name="token_gather",
    )(rows)


def plane_gather_kernel(dims, src_ref, out_ref, *sems):
    place = axis_place()
    greet(False, dims, place)
    finish(
        spread_blocks(
            dims,
            place,
            src_ref.shape[0],
            False,
            lambda j: src_ref.at[j],
            None,
            lambda col, j, b: out_ref.at[col, b, j],
            sems,
        )
    )


def plane_gather(parts, dims):
    n_dp, n_row, n_col = dims
    chunks, rows, width = parts.shape
    return pl.pallas_call(
        functools.partial(plane_gather_kernel, dims),
        out_shape=jax.ShapeDtypeStruct((n_col, n_row, chunks, rows, width), parts.dtype),
        in_specs=[pl.BlockSpec(memory_space=pl.ANY)],
        out_specs=pl.BlockSpec(memory_space=pl.ANY),
        scratch_shapes=spread_sems(dims, chunks),
        compiler_params=pltpu.CompilerParams(
            collective_id=2, has_side_effects=True, vmem_limit_bytes=VMEM_BYTES
        ),
        name="plane_gather",
    )(parts)


def add_low(left, right):
    return (left.astype(jnp.float32) + right.astype(jnp.float32)).astype(jnp.bfloat16)


def plan_reduce(
    dims, place, part_at, bufs, sems, deliver, direct=False, far_first=True, lanes=None
):
    n_dp, n_row, n_col = dims
    d, r, c = place
    bits = bits_of(n_row)
    mine_ref, col_ref, row_ref = bufs
    mine_sem, col_send, col_recv, row_send, row_recv = sems
    steps = list(reversed(range(n_dp))) if far_first else list(range(n_dp))
    homes = [dp_order(d, p, n_dp) for p in steps]
    sent = []
    held = []

    def send_cols(t):
        for i in range(1, n_col):
            other = (c + i) % n_col
            copy = remote(
                part_at(other, homes[t]),
                col_ref.at[t, i - 1],
                col_send.at[t, i - 1],
                col_recv.at[t, i - 1],
                (d, r, other),
            )
            copy.start()
            sent.append(copy)

    def load_mine():
        for t in range(n_dp):
            keep = pltpu.make_async_copy(part_at(c, homes[t]), mine_ref.at[t], mine_sem.at[t])
            keep.start()
            held.append(keep)

    begin, width = lanes or (0, mine_ref.shape[-1])
    cut = (width // LANES + 1) // 2 * LANES
    spans = [pl.ds(begin, cut), pl.ds(begin + cut, width - cut)]
    marks = [pl.ds(0, cut), pl.ds(cut, width - cut)]

    def order(half):
        return [1 << ((half + s) % bits) for s in range(bits)]

    def send_half(t, half, s):
        dim_order = order(half)
        bit = dim_order[s]
        before = sum(dim_order[:s])
        span = spans[half]
        for x in range(n_row):
            if not x & before and x & bit:
                at = x ^ bit
                copy = remote(
                    mine_ref.at[t, flip_all(r, x, bits), :, span],
                    row_ref.at[t, slot_of(half, s, at), :, marks[half]],
                    row_send.at[t, half, slot_of(half, s, at)],
                    row_recv.at[t, half, slot_of(half, s, at)],
                    (d, flip(r, bit), c),
                )
                copy.start()
                sent.append(copy)

    def slot_of(half, s, at):
        places = []
        before = 0
        for step, bit in enumerate(order(half)):
            before += bit
            places += [(step, y) for y in range(n_row) if not y & before]
        return places.index((s, at))

    def sum_cols(t, send=True):
        if not direct:
            held[t].wait()
        for i in range(1, n_col):
            ref = col_ref.at[t, i - 1]
            remote(
                ref, ref, col_send.at[t, i - 1], col_recv.at[t, i - 1], (d, r, c)
            ).wait_recv()
        k = homes[t]

        @pl.loop(0, n_row)
        def _(b):
            total = part_at(c, k)[b] if direct else mine_ref[t, b]
            total = total.astype(jnp.float32)
            for i in range(1, n_col):
                total = total + col_ref[t, i - 1, b].astype(jnp.float32)
            mine_ref[t, b] = total.astype(jnp.bfloat16)

        if send:
            send_first(t)

    def send_first(t):
        for half in range(2):
            send_half(t, half, 0)

    def sum_rows(t, s):
        for half in range(2):
            before = sum(order(half)[: s + 1])
            span = spans[half]
            for y in range(n_row):
                if not y & before:
                    slot = slot_of(half, s, y)
                    ref = row_ref.at[t, slot, :, marks[half]]
                    remote(
                        ref,
                        ref,
                        row_send.at[t, half, slot],
                        row_recv.at[t, half, slot],
                        (d, r, c),
                    ).wait_recv()
                    b = flip_all(r, y, bits)
                    mine_ref[t, b, :, span] = add_low(mine_ref[t, b, :, span], ref[...])
            if s + 1 < bits:
                send_half(t, half, s + 1)
        if s + 1 == bits:
            deliver(steps[t], homes[t], mine_ref.at[t, r])

    def sum_all(between=None):
        ticks = n_dp + bits + 1
        for tick in range(ticks):
            if tick + 1 == ticks and between is not None:
                between()
            if tick < n_dp:
                sum_cols(tick)
            for s in reversed(range(bits)):
                t = tick - 2 - s
                if 0 <= t < n_dp:
                    sum_rows(t, s)

    return types.SimpleNamespace(
        send_cols=send_cols,
        load_mine=load_mine,
        sum_cols=sum_cols,
        send_first=send_first,
        homes=homes,
        sum_rows=sum_rows,
        sum_all=sum_all,
        sent=sent,
    )


def plan_dp_first(dims, place, mine_ref, homes, begin, scratch):
    n_dp, n_row, n_col = dims
    d, r, c = place
    bits = bits_of(n_row)
    in_ref, acc_ref, row_ref, dp_send, dp_recv, row_send, row_recv = scratch
    wide = acc_ref.shape[-1]
    cut = (wide // LANES + 1) // 2 * LANES
    spans = [pl.ds(0, cut), pl.ds(cut, wide - cut)]
    lanes = pl.ds(begin, wide)
    sent = []

    def send_dp(t):
        p = n_dp - 1 - t
        if p:
            copy = remote(
                mine_ref.at[t, :, :, lanes],
                in_ref.at[d],
                dp_send.at[p - 1],
                dp_recv.at[d],
                (homes[t], r, c),
            )
            copy.start()
            sent.append(copy)

    def order(half):
        return [1 << ((half + s) % bits) for s in range(bits)]

    def steps(half):
        before = 0
        places = []
        for bit in order(half):
            before += bit
            places.append([y for y in range(n_row) if not y & before])
        return places

    def slot_of(half, s, y):
        return sum(len(step) for step in steps(half)[:s]) + steps(half)[s].index(y)

    def send_half(half, s):
        bit = order(half)[s]
        for y in steps(half)[s]:
            slot = slot_of(half, s, y)
            copy = remote(
                acc_ref.at[flip_all(r, y ^ bit, bits), :, spans[half]],
                row_ref.at[slot, :, spans[half]],
                row_send.at[half, slot],
                row_recv.at[half, slot],
                (d, flip(r, bit), c),
            )
            copy.start()
            sent.append(copy)

    def sum_dp():
        for p in range(1, n_dp):
            k = homes[n_dp - 1 - p]
            ref = in_ref.at[k]
            remote(ref, ref, dp_send.at[p - 1], dp_recv.at[k], (d, r, c)).wait_recv()

        @pl.loop(0, n_row)
        def _(b):
            total = mine_ref[n_dp - 1, b, :, lanes].astype(jnp.float32)
            for p in range(1, n_dp):
                total = total + in_ref[homes[n_dp - 1 - p], b].astype(jnp.float32)
            acc_ref[b] = total.astype(jnp.bfloat16)

        for half in range(2):
            send_half(half, 0)

    def sum_rows(s):
        for half in range(2):
            for y in steps(half)[s]:
                slot = slot_of(half, s, y)
                ref = row_ref.at[slot, :, spans[half]]
                remote(
                    ref, ref, row_send.at[half, slot], row_recv.at[half, slot], (d, r, c)
                ).wait_recv()
                b = flip_all(r, y, bits)
                acc_ref[b, :, spans[half]] = add_low(acc_ref[b, :, spans[half]], ref[...])
            if s + 1 < bits:
                send_half(half, s + 1)

    return types.SimpleNamespace(
        send_dp=send_dp, sum_dp=sum_dp, sum_rows=sum_rows, total=lambda: acc_ref[r], sent=sent
    )


def dp_first_scratch(dims, rows, width):
    n_dp, n_row, n_col = dims
    dma = pltpu.SemaphoreType.DMA
    low = jnp.bfloat16
    return [
        pltpu.VMEM((n_dp, n_row, rows, width), low),
        pltpu.VMEM((n_row, rows, width), low),
        pltpu.VMEM((max(1, n_row - 1), rows, width), low),
        dma((max(1, n_dp - 1),)),
        dma((n_dp,)),
        dma((2, max(1, n_row - 1))),
        dma((2, max(1, n_row - 1))),
    ]


def reduce_blocks(dims, place, part_ref, bufs, sems, deliver):
    plan = plan_reduce(dims, place, lambda col, k: part_ref.at[col, k], bufs, sems, deliver)
    for t in range(dims[0]):
        plan.send_cols(t)
    plan.load_mine()
    plan.sum_all()
    return plan.sent


def reduce_scratch(dims, rows, width, copied=True, lanes=None):
    n_dp, n_row, n_col = dims
    dma = pltpu.SemaphoreType.DMA
    low = jnp.bfloat16
    return [
        pltpu.VMEM((n_dp, n_row, rows, width), low),
        pltpu.VMEM((n_dp, max(1, n_col - 1), n_row, rows, width), low),
        pltpu.VMEM((n_dp, max(1, n_row - 1), rows, lanes or width), low),
        dma((n_dp if copied else 1,)),
        dma((n_dp, max(1, n_col - 1))),
        dma((n_dp, max(1, n_col - 1))),
        dma((n_dp, 2, max(1, n_row - 1))),
        dma((n_dp, 2, max(1, n_row - 1))),
    ]


def token_reduce_kernel(dims, part_ref, out_ref, *scratch):
    n_dp, n_row, n_col = dims
    place = axis_place()
    d, r, c = place
    dp_send, dp_recv, own_sem = scratch[8:]
    greet(True, dims, place)
    late = []

    def deliver(p, k, block):
        if p == 0:
            keep = pltpu.make_async_copy(block, out_ref.at[d], own_sem)
            keep.start()
            late.append(keep.wait)
        else:
            copy = remote(block, out_ref.at[d], dp_send.at[p], dp_recv.at[d], (k, r, c))
            copy.start()
            late.append(copy.wait_send)

    sent = reduce_blocks(dims, place, part_ref, scratch[:3], scratch[3:8], deliver)
    for p in range(1, n_dp):
        k = dp_order(d, p, n_dp)
        ref = out_ref.at[k]
        remote(ref, ref, dp_send.at[p], dp_recv.at[k], (d, r, c)).wait_recv()
    for copy in sent:
        copy.wait_send()
    for wait in late:
        wait()


def token_reduce(parts, dims):
    n_dp = dims[0]
    slots, width = parts.shape[3:]
    dma = pltpu.SemaphoreType.DMA
    return pl.pallas_call(
        functools.partial(token_reduce_kernel, dims),
        out_shape=jax.ShapeDtypeStruct((n_dp, slots, width), jnp.bfloat16),
        in_specs=[pl.BlockSpec(memory_space=pl.ANY)],
        out_specs=pl.BlockSpec(memory_space=pl.ANY),
        scratch_shapes=[*reduce_scratch(dims, slots, width), dma((n_dp,)), dma((n_dp,)), dma],
        compiler_params=pltpu.CompilerParams(
            collective_id=3, has_side_effects=True, vmem_limit_bytes=VMEM_BYTES
        ),
        name="token_reduce",
    )(parts)


def param_reduce_kernel(dims, part_ref, out_ref, *scratch):
    n_dp, n_row, n_col = dims
    place = axis_place()
    d, r, c = place
    dp_send, dp_recv, dp_ref, swap_send, swap_recv, swap_ref, sum_ref = scratch[8:]
    rows = out_ref.shape[1]
    greet(True, dims, place)
    late = []
    kept = []

    def deliver(p, k, block):
        if p == 0:
            kept.append(block)
        else:
            copy = remote(block, dp_ref.at[d], dp_send.at[p], dp_recv.at[d], (k, r, c))
            copy.start()
            late.append(copy)

    sent = reduce_blocks(dims, place, part_ref, scratch[:3], scratch[3:8], deliver)
    total = kept[0][...].astype(jnp.float32)
    for p in range(1, n_dp):
        k = dp_order(d, p, n_dp)
        ref = dp_ref.at[k]
        remote(ref, ref, dp_send.at[p], dp_recv.at[k], (d, r, c)).wait_recv()
        total = total + dp_ref[k].astype(jnp.float32)
    sum_ref[...] = total
    for i in range(n_col):
        swap_ref[i] = sum_ref[i * rows : (i + 1) * rows, :]
    for i in range(1, n_col):
        other = (c + i) % n_col
        copy = remote(
            swap_ref.at[other], out_ref.at[c], swap_send.at[i], swap_recv.at[i], (d, r, other)
        )
        copy.start()
        late.append(copy)
    out_ref[pl.ds(c, 1)] = swap_ref[pl.ds(c, 1)]
    for i in range(1, n_col):
        ref = out_ref.at[(c + n_col - i) % n_col]
        remote(ref, ref, swap_send.at[i], swap_recv.at[i], (d, r, c)).wait_recv()
    for copy in sent:
        copy.wait_send()
    for copy in late:
        copy.wait_send()


def param_reduce(parts, dims):
    n_dp, n_row, n_col = dims
    block_rows, width = parts.shape[3:]
    rows = block_rows // n_col
    dma = pltpu.SemaphoreType.DMA
    return pl.pallas_call(
        functools.partial(param_reduce_kernel, dims),
        out_shape=jax.ShapeDtypeStruct((n_col, rows, width), jnp.float32),
        in_specs=[pl.BlockSpec(memory_space=pl.ANY)],
        out_specs=pl.BlockSpec(memory_space=pltpu.VMEM),
        scratch_shapes=[
            *reduce_scratch(dims, block_rows, width),
            dma((n_dp,)),
            dma((n_dp,)),
            pltpu.VMEM((n_dp, block_rows, width), jnp.bfloat16),
            dma((n_col,)),
            dma((n_col,)),
            pltpu.VMEM((n_col, rows, width), jnp.float32),
            pltpu.VMEM((block_rows, width), jnp.float32),
        ],
        compiler_params=pltpu.CompilerParams(
            collective_id=4, has_side_effects=True, vmem_limit_bytes=VMEM_BYTES
        ),
        name="param_reduce",
    )(parts)


def column(matrix, index):
    return matrix[:, index : index + 1]


def token_masks(lengths_ref, rows, seqs):
    down = lax.broadcasted_iota(jnp.int32, (rows, 1), 0)
    across = lax.broadcasted_iota(jnp.int32, (1, rows), 1)
    end = 0
    doc_down = jnp.zeros((rows, 1), jnp.int32)
    doc_across = jnp.zeros((1, rows), jnp.int32)
    for i in range(seqs):
        end = end + lengths_ref[0, i]
        doc_down = doc_down + (down >= end).astype(jnp.int32)
        doc_across = doc_across + (across >= end).astype(jnp.int32)
    valid = (doc_down < seqs).astype(jnp.float32)
    allowed = (doc_down == doc_across) & (down >= across)
    return valid, allowed


def row_vectors_of(small, first):
    shape = (8, small.shape[1])
    pick = lax.broadcasted_iota(jnp.int32, shape, 1) == first + lax.broadcasted_iota(
        jnp.int32, shape, 0
    )
    return dot(pick.astype(jnp.bfloat16), small, NT)


def half_mask(rows, half):
    return lax.broadcasted_iota(jnp.int32, (rows, LANES), 1) // HEAD == half


def attention_forward(qkv_ref, probs_ref, mixed_ref, allowed, first, last):
    rows = qkv_ref.shape[0]
    low = jnp.bfloat16

    @pl.loop(first, last, unroll=3)
    def _(pair):
        def cols(base):
            return pl.ds(pl.multiple_of(base + pair * LANES, LANES), LANES)

        queries = qkv_ref[:, cols(0)]
        key_heads = qkv_ref[:, cols(D)]
        values = qkv_ref[:, cols(2 * D)]
        mixed = jnp.zeros((rows, LANES), jnp.float32)
        for half in range(LANES // HEAD):
            mask = half_mask(rows, half)
            scores = dot(jnp.where(mask, queries, 0), key_heads, NT) * HEAD ** (-0.5)
            scores = jnp.where(allowed, scores, -1e30)
            top_score = jnp.max(scores, axis=-1, keepdims=True)
            exp_scores = jnp.exp(scores - top_score)
            probs = exp_scores / jnp.sum(exp_scores, axis=-1, keepdims=True)
            probs_ref[pair * (LANES // HEAD) + half] = probs
            mixed = mixed + dot(probs.astype(low), jnp.where(mask, values, 0))
        mixed_ref[:, cols(0)] = mixed.astype(low)


def two_way(first, second):
    top = jnp.maximum(first, second)
    exp_first = jnp.exp(first - top)
    exp_second = jnp.exp(second - top)
    total = exp_first + exp_second
    return exp_first / total, exp_second / total


def attention_backward(qkv_ref, probs_ref, grad_mixed_ref, grad_qkv_ref):
    rows = qkv_ref.shape[0]
    low = jnp.bfloat16

    @pl.loop(0, HEADS * HEAD // LANES, unroll=2)
    def _(pair):
        def cols(base):
            return pl.ds(pl.multiple_of(base + pair * LANES, LANES), LANES)

        queries = qkv_ref[:, cols(0)]
        key_heads = qkv_ref[:, cols(D)]
        values = qkv_ref[:, cols(2 * D)]
        grad_mixed = grad_mixed_ref[:, cols(0)]
        grad_queries = jnp.zeros((rows, LANES), jnp.float32)
        grad_keys = jnp.zeros((rows, LANES), jnp.float32)
        grad_values = jnp.zeros((rows, LANES), jnp.float32)
        for half in range(LANES // HEAD):
            mask = half_mask(rows, half)
            probs = probs_ref[pair * (LANES // HEAD) + half]
            grad_part = jnp.where(mask, grad_mixed, 0)
            grad_values = grad_values + dot(probs.astype(low), grad_part, TN)
            grad_probs = dot(grad_part, values, NT)
            grad_scores = probs * (
                grad_probs - jnp.sum(probs * grad_probs, axis=-1, keepdims=True)
            )
            grad_scores = grad_scores.astype(low)
            grad_queries = grad_queries + dot(grad_scores, jnp.where(mask, key_heads, 0))
            grad_keys = grad_keys + dot(grad_scores, jnp.where(mask, queries, 0), TN)
        grad_qkv_ref[:, cols(0)] = (grad_queries * HEAD ** (-0.5)).astype(low)
        grad_qkv_ref[:, cols(D)] = (grad_keys * HEAD ** (-0.5)).astype(low)
        grad_qkv_ref[:, cols(2 * D)] = grad_values.astype(low)


def layer_kernel(sizes, *refs):
    dims, num_ffn, wide_qkv, wide_out, route_cols, chunks = sizes
    n_dp, n_row, n_col = dims
    low = jnp.bfloat16
    (
        lengths_ref,
        routes_ref,
        prev_ref,
        tokens_ref,
        cotangent_ref,
        w_qkv_ref,
        w_out_ref,
        route_w_ref,
        gains_ref,
        const_ref,
        weight_gu,
        weight_down,
        left_root_gu,
        right_root_down,
        right_root_gu,
        left_root_down,
        result_out,
        grad_tokens_out,
        summed_ref,
        right_sum_out,
        left_sum_out,
        step_out,
        block_out,
        shard_ref,
        turn_ref,
        swap_ref,
        block_ref,
        whole_ref,
        pack_ref,
        expert_ref,
        stage_ref,
        arrived_ref,
        hidden_ref,
        pre_ref,
        grads_ref,
        qkv_ref,
        probs_ref,
        mixed_ref,
        first_ref,
        came_ref,
        grad_attn_ref,
        grad_mixed_ref,
        grad_qkv_ref,
        part_ref,
        dp_ref,
        end_ref,
        sum_ref,
        gathered_ref,
        root_ref,
        tile_ref,
        half_step_ref,
        lhs_ref,
        right_sum_ref,
        left_sum_ref,
        left_low_ref,
        step_ref,
        result_ref,
        grad_tokens_ref,
        swap_send,
        swap_recv,
        load_sem,
        expert_send,
        expert_recv,
        root_sem,
        tile_sem,
        store_sem,
        done_sem,
        came_send,
        came_recv,
        dp_send,
        dp_recv,
        end_send,
        end_recv,
        *more,
    ) = refs
    param_sems, out_sems, token_sems, gather_sems = (more[7 * n : 7 * n + 7] for n in range(4))
    token_scratch, param_scratch, first_scratch = more[28:36], more[36:44], more[44:]
    place = axis_place()
    d, r, c = place
    rows = shard_ref.shape[1]
    depth, slice_wide = pack_ref.shape[2:]
    held, tile = tile_ref.shape[:2]
    wide_col = n_row * slice_wide
    staged = []
    loads = []
    for m, src in enumerate([weight_gu.at[:, 0], weight_gu.at[:, 1], weight_down]):
        begin = m % 2 * wide_col
        staged.append((m // 2, begin))
        dst = tile_ref.at[m // 2, pl.ds(0, depth), pl.ds(begin, wide_col)]
        copy = pltpu.make_async_copy(src, dst, load_sem.at[m])
        copy.start()
        loads.append(copy)
    roots = [left_root_gu.at[0], left_root_gu.at[1], right_root_down]
    root_loads = []
    for m in range(3):
        copy = pltpu.make_async_copy(roots[m], root_ref.at[m], root_sem.at[m])
        copy.start()
        root_loads.append(copy)
    turn_ref[...] = jnp.zeros_like(turn_ref)
    out_at = wide_qkv + LANES
    at = 0
    for ref in (route_w_ref, gains_ref, const_ref):
        turn_ref[at : at + ref.shape[0], : ref.shape[1]] = ref[...]
        at += ref.shape[0]
    small_shard = turn_ref[...].T[:rows]
    for i in range(n_col):
        shard_ref[i, :, :wide_qkv] = w_qkv_ref[:, i * wide_qkv : (i + 1) * wide_qkv]
        shard_ref[i, :, wide_qkv:out_at] = small_shard
        shard_ref[i, :, out_at:] = w_out_ref[:, i * wide_out : (i + 1) * wide_out]
    greet(True, dims, place, all_rows=True)

    copies = []
    for i in range(1, n_col):
        other = (c + i) % n_col
        copy = remote(
            shard_ref.at[other], swap_ref.at[c], swap_send.at[i], swap_recv.at[i], (d, r, other)
        )
        copy.start()
        copies.append(copy)
    swap_ref[pl.ds(c, 1)] = shard_ref[pl.ds(c, 1)]
    for copy in copies:
        copy.wait()
    for i in range(n_col):
        block_ref[i * rows : (i + 1) * rows, :] = swap_ref[i]
    whole_ref[c, d, r] = block_ref[...].astype(low)

    def plan_params(begin, wide, sems):
        span = pl.ds(begin, wide)

        def slot(col, j, b):
            k = j[1] if isinstance(j, tuple) else dp_order(d, j, n_dp)
            return whole_ref.at[col, k, b, :, span]

        own = whole_ref.at[c, d, r, :, span]
        return plan_spread(dims, place, n_dp, True, None, lambda k: own, slot, sems)

    qkv_plan = plan_params(0, out_at, param_sems)
    out_plan = plan_params(out_at, wide_out, out_sems)
    waits = []

    bits = bits_of(n_row)
    near = [1 << dim for dim in range(bits)]

    def pack_experts():
        for copy in loads:
            copy.wait()
        for m, (slot, begin) in enumerate(staged):
            for b in range(n_row):
                at = begin + b * slice_wide
                pack_ref[b, m] = tile_ref[slot, :depth, at : at + slice_wide].astype(low)
        expert_ref[:, pl.ds(pl.multiple_of(r * depth, 16), depth)] = pack_ref[r]

    def send_experts(masks):
        home = pl.ds(pl.multiple_of(r * depth, 16), depth)
        for x in masks:
            other = flip_all(r, x, bits)
            copy = remote(
                pack_ref.at[other],
                expert_ref.at[:, home],
                expert_send.at[x - 1],
                expert_recv.at[x - 1],
                (d, other, c),
            )
            copy.start()
            waits.append(copy.wait_send)

    for plan in (qkv_plan, out_plan):
        plan.start(0)
        plan.send_dp()
    pack_experts()
    send_experts(near)
    for j in range(1, n_dp):
        qkv_plan.start(j)
        qkv_plan.pass_on(j - 1)
    for j in range(1, n_dp):
        out_plan.start(j)
    qkv_plan.pass_on(n_dp - 1)
    for j in range(n_dp):
        out_plan.pass_on(j)
    send_experts([x for x in range(1, n_row) if x not in near])
    for j in range(n_dp):
        qkv_plan.last_arrivals(j)
    for j in range(n_dp):
        qkv_plan.wait_cols(j)

    def whole_cols(col, begin, wide):
        return whole_ref[col, :, :, :, begin : begin + wide].reshape(D, wide)

    total = tokens_ref.shape[0]
    valid, allowed = token_masks(lengths_ref, total, lengths_ref.shape[1])
    small = whole_cols(0, wide_qkv, LANES)
    vectors = row_vectors_of(small, route_cols)
    inputs = tokens_ref[...].astype(jnp.float32)
    scale_one = lax.rsqrt(jnp.mean(inputs * inputs, axis=-1, keepdims=True) + NORM_EPS)
    h_one = (inputs * scale_one * vectors[0:1]).astype(low)
    for i in range(n_col):
        qkv_ref[:, i * wide_qkv : (i + 1) * wide_qkv] = dot(h_one, whole_cols(i, 0, wide_qkv)).astype(
            low
        )
    pairs = HEADS * HEAD // LANES
    attention_forward(qkv_ref, probs_ref, mixed_ref, allowed, 0, pairs // 2)
    for j in range(n_dp):
        out_plan.last_arrivals(j)
    attention_forward(qkv_ref, probs_ref, mixed_ref, allowed, pairs // 2, pairs)
    for j in range(n_dp):
        out_plan.wait_cols(j)
    waits += qkv_plan.sends() + out_plan.sends()
    for i in range(n_col):
        cols = slice(i * wide_out, (i + 1) * wide_out)
        attn_out = dot(mixed_ref[...], whole_cols(i, out_at, wide_out))
        first_ref[:, cols] = tokens_ref[:, cols].astype(jnp.float32) + valid * attn_out
    first_sum = first_ref[...]
    scale_two = lax.rsqrt(jnp.mean(first_sum * first_sum, axis=-1, keepdims=True) + NORM_EPS)
    h_two = (first_sum * scale_two * vectors[1:2]).astype(low)
    experts = prev_ref.shape[0]
    turn_ref[...] = jnp.zeros_like(turn_ref)
    turn_ref[:experts] = prev_ref[...]
    turn_ref[experts : experts + 2] = routes_ref[...].astype(jnp.float32)
    turned = turn_ref[...].T
    logits_all = dot(h_two, small)
    lane = lax.broadcasted_iota(jnp.int32, (total, LANES), 1)
    logits = logits_all + jnp.where(lane < experts, turned, 0.0)
    route_first = column(turned, experts).astype(jnp.int32)
    route_second = column(turned, experts + 1).astype(jnp.int32)
    pick_first = (lane == route_first).astype(jnp.float32)
    pick_second = (lane == route_second).astype(jnp.float32)
    gates = two_way(
        jnp.sum(pick_first * logits, axis=-1, keepdims=True),
        jnp.sum(pick_second * logits, axis=-1, keepdims=True),
    )
    mix_base = num_ffn + 4
    mixes = []
    for i in range(2):
        mixes += two_way(
            column(logits_all, mix_base + 2 * i), column(logits_all, mix_base + 2 * i + 1)
        )
    before = lax.broadcasted_iota(jnp.int32, (total, total), 0) > lax.broadcasted_iota(
        jnp.int32, (total, total), 1
    )
    earlier = dot(before.astype(low), (pick_first + pick_second).astype(low))
    in_slots = []
    for route, pick in ((route_first, pick_first), (route_second, pick_second)):
        slot_index = jnp.sum(earlier * pick, axis=-1, keepdims=True)
        where_in = (route * CAP).astype(jnp.float32) + slot_index
        in_slots.append(jnp.where(route < num_ffn, where_in, -1.0))
    slots = num_ffn * CAP
    slot_lane = lax.broadcasted_iota(jnp.int32, (total, slots), 1).astype(jnp.float32)
    places = [(slot_lane == where_in).astype(low) for where_in in in_slots]
    grad_y = cotangent_ref[...].astype(jnp.float32) * valid
    sent = dot(places[0] + places[1], h_two, TN).astype(low)
    made = dot(places[0], (gates[0] * grad_y).astype(low), TN) + dot(
        places[1], (gates[1] * grad_y).astype(low), TN
    )
    stage_ref[:, :, :D] = sent.reshape(num_ffn, CAP, D)
    stage_ref[:, :, D:] = made.astype(low).reshape(num_ffn, CAP, D)

    def token_slot(col, j, b):
        k = j[1] if isinstance(j, tuple) else dp_order(d, j, n_dp)
        return arrived_ref.at[k, col, b]

    arrived_ref[d, c, r] = stage_ref[d]
    rows_plan = plan_spread(
        dims, place, n_dp, True, None, lambda k: stage_ref.at[k], token_slot, token_sems
    )
    rows_plan.start(0)
    rows_plan.send_dp()
    rows_plan.start(1)
    rows_plan.pass_on(0)

    wides = [right_root_gu.at[0], right_root_gu.at[1], left_root_down]
    tiles = left_root_down.shape[0] // tile
    tile_loads = []

    def load_tile(n):
        if n < 3 * tiles:
            copy = pltpu.make_async_copy(
                wides[n // tiles].at[pl.ds(n % tiles * tile, tile)],
                tile_ref.at[n % held],
                tile_sem.at[n],
            )
            copy.start()
            tile_loads.append(copy)

    for n in range(held):
        load_tile(n)

    def token_back(p, k, block):
        if p == 0:
            came_ref[d] = block[...]
        else:
            copy = remote(block, came_ref.at[d], came_send.at[p - 1], came_recv.at[d], (k, r, c))
            copy.start()
            waits.append(copy.wait_send)

    tokens_plan = plan_reduce(
        dims,
        place,
        lambda col, k: part_ref.at[col, k, :, pl.ds(0, CAP), pl.ds(0, 2 * D)],
        token_scratch[:3],
        token_scratch[3:],
        token_back,
        direct=True,
        far_first=False,
    )

    tall = n_col * n_row * CAP

    def expert_rows(p):
        k = dp_order(d, p, n_dp)
        some = arrived_ref[k].reshape(tall, 2 * D)
        rows_in = some[:, :D]
        grads_in = some[:, D:]
        gate_part = dot(rows_in, expert_ref[0])
        up_part = dot(rows_in, expert_ref[1])
        grad_hidden = dot(grads_in, expert_ref[2])
        sigma = jax.nn.sigmoid(gate_part)
        silu = gate_part * sigma
        hidden = (silu * up_part).astype(low)
        grad_gate = (grad_hidden * up_part * sigma * (1.0 + gate_part * (1.0 - sigma))).astype(low)
        grad_up = (grad_hidden * silu).astype(low)
        hidden_ref[k] = hidden
        pre_ref[k, :, :slice_wide] = grad_gate
        pre_ref[k, :, slice_wide:] = grad_up
        made_rows = dot(hidden, expert_ref[2], NT).astype(low)
        grad_rows = (dot(grad_gate, expert_ref[0], NT) + dot(grad_up, expert_ref[1], NT)).astype(low)
        for col in range(n_col):
            span = slice(col * n_row * CAP, (col + 1) * n_row * CAP)
            part_ref[col, k, :, :CAP, :D] = made_rows[span].reshape(n_row, CAP, D)
            part_ref[col, k, :, :CAP, D : 2 * D] = grad_rows[span].reshape(n_row, CAP, D)
        tokens_plan.send_cols(p)

    def chunk_in(p):
        if p + 2 < n_dp:
            rows_plan.start(p + 2)
        if p + 1 < n_dp:
            rows_plan.pass_on(p + 1)
        if p == 0:
            for x in range(1, n_row):
                home = pl.ds(pl.multiple_of(flip_all(r, x, bits) * depth, 16), depth)
                ref = expert_ref.at[:, home]
                remote(
                    ref, ref, expert_send.at[x - 1], expert_recv.at[x - 1], (d, r, c)
                ).wait_recv()
        rows_plan.last_arrivals(p)
        rows_plan.wait_cols(p)
        expert_rows(p)

    def sums_before(t):
        for s in range(bits):
            if 0 <= t - 1 - s:
                tokens_plan.sum_rows(t - 1 - s, s)

    chunk_in(0)
    for t in range(n_dp - 1):
        if t < n_dp - 2:
            chunk_in(t + 1)
        tokens_plan.sum_cols(t)
        sums_before(t)
    if n_dp > 1:
        chunk_in(n_dp - 1)
    tokens_plan.sum_cols(n_dp - 1)
    sums_before(n_dp - 1)
    waits += rows_plan.sends()
    all_count = n_dp * tall
    all_rows = arrived_ref[:, :, :, :, :D].reshape(all_count, D)
    all_grads = arrived_ref[:, :, :, :, D:].reshape(all_count, D)
    for m in range(2):
        grads_ref[m * D : (m + 1) * D] = dot(
            all_rows,
            pre_ref[:, :, m * slice_wide : (m + 1) * slice_wide].reshape(all_count, slice_wide),
            TN,
        ).astype(low)
    grads_ref[2 * D :] = dot(
        all_grads, hidden_ref[...].reshape(all_count, slice_wide), TN
    ).astype(low)
    tall = grads_ref.shape[0] // chunks
    gather = plan_spread(
        dims,
        place,
        chunks,
        False,
        lambda j: grads_ref.at[pl.ds(j * tall, tall)],
        None,
        lambda col, j, b: gathered_ref.at[col * n_row + b, pl.ds(j * tall, tall)],
        gather_sems,
    )
    gather.start(0)
    for t in range(n_dp, n_dp + bits):
        for s in range(bits):
            if 0 <= t - 1 - s < n_dp:
                tokens_plan.sum_rows(t - 1 - s, s)
        if t == n_dp + bits - 2:
            for j in range(1, chunks):
                gather.start(j)

    gain_one, gain_two = vectors[0:1], vectors[1:2]
    const_rows = [vectors[2:3], vectors[3:4]]
    mixes = [mixes[:2], mixes[2:]]
    routes = [route_first, route_second]
    picks = [pick_first, pick_second]
    cotangent = cotangent_ref[...].astype(jnp.float32)
    grad_y = cotangent * valid
    grad_y_low = grad_y.astype(low)
    first_sum = first_ref[...]
    scale_two = lax.rsqrt(jnp.mean(first_sum * first_sum, axis=-1, keepdims=True) + NORM_EPS)
    normed_two = first_sum * scale_two
    h_two = normed_two * gain_two
    h_two_low = h_two.astype(low)
    const_sel = [
        [(route == num_ffn + 2 + n).astype(jnp.float32) for n in range(2)] for route in routes
    ]
    for p in range(1, n_dp):
        k = dp_order(d, p, n_dp)
        ref = came_ref.at[k]
        remote(ref, ref, came_send.at[p - 1], came_recv.at[k], (d, r, c)).wait_recv()
    expert_out = came_ref[:, :, :D].reshape(slots, D)
    grad_sent = came_ref[:, :, D:].reshape(slots, D)
    moe_out = jnp.zeros_like(first_sum)
    grad_gates = []
    own_weight = jnp.zeros((total, 1), jnp.float32)
    for n in range(2):
        own = (routes[n] == num_ffn + 1).astype(jnp.float32)
        for i in range(2):
            own = own + const_sel[n][i] * mixes[i][0]
        output = dot(places[n], expert_out) + own * h_two
        for i in range(2):
            output = output + const_sel[n][i] * mixes[i][1] * const_rows[i]
        moe_out = moe_out + gates[n] * output
        grad_gates.append(jnp.sum(grad_y * output, axis=-1, keepdims=True))
        own_weight = own_weight + gates[n] * own
    result_ref[...] = (first_sum + valid * moe_out).astype(low)
    copy = pltpu.make_async_copy(result_ref, result_out, done_sem.at[0])
    copy.start()
    waits.append(copy.wait)
    mean_gate = gates[0] * grad_gates[0] + gates[1] * grad_gates[1]
    grad_logits = sum(gates[n] * (grad_gates[n] - mean_gate) * picks[n] for n in range(2))
    grad_own = jnp.sum(grad_y * h_two, axis=-1, keepdims=True)
    const_lanes = jnp.zeros((total, LANES), jnp.float32)
    for i in range(2):
        weight = const_sel[0][i] * gates[0] + const_sel[1][i] * gates[1]
        mix_grads = [
            weight * grad_own,
            weight * jnp.sum(grad_y * const_rows[i], axis=-1, keepdims=True),
        ]
        mean_mix = mixes[i][0] * mix_grads[0] + mixes[i][1] * mix_grads[1]
        for n in range(2):
            grad_mix = mixes[i][n] * (mix_grads[n] - mean_mix)
            grad_logits = jnp.where(lane == num_ffn + 4 + 2 * i + n, grad_mix, grad_logits)
        const_lanes = jnp.where(lane == route_cols + 2 + i, weight * mixes[i][1], const_lanes)
    grad_logits = grad_logits.astype(low)

    grad_h_two = (
        dot(grad_logits, small, NT) + dot(places[0] + places[1], grad_sent) + own_weight * grad_y
    )
    grad_normed = grad_h_two * gain_two
    inner_mean = jnp.mean(grad_normed * normed_two, axis=-1, keepdims=True)
    grad_first = scale_two * (grad_normed - normed_two * inner_mean) + cotangent
    grad_tokens_ref[...] = grad_first
    grad_attn_ref[...] = (valid * grad_first).astype(low)
    grad_small = (
        dot(h_two_low, grad_logits, TN)
        + dot(grad_y_low, const_lanes.astype(low), TN)
        + dot((grad_h_two * normed_two).astype(low), (lane == route_cols + 1).astype(low), TN)
    )
    grad_mixed = jnp.zeros((total, D), jnp.float32)
    for i in range(n_col):
        grad_mixed = grad_mixed + dot(
            grad_attn_ref[:, i * wide_out : (i + 1) * wide_out],
            whole_cols(i, out_at, wide_out),
            NT,
        )
    grad_mixed_ref[...] = grad_mixed.astype(low)
    attention_backward(qkv_ref, probs_ref, grad_mixed_ref, grad_qkv_ref)
    grad_h_one = jnp.zeros((total, D), jnp.float32)
    for i in range(n_col):
        grad_h_one = grad_h_one + dot(
            grad_qkv_ref[:, i * wide_qkv : (i + 1) * wide_qkv], whole_cols(i, 0, wide_qkv), NT
        )
    inputs = tokens_ref[...].astype(jnp.float32)
    scale_one = lax.rsqrt(jnp.mean(inputs * inputs, axis=-1, keepdims=True) + NORM_EPS)
    normed_one = inputs * scale_one
    h_one = (normed_one * gain_one).astype(low)
    grad_normed = grad_h_one * gain_one
    inner_mean = jnp.mean(grad_normed * normed_one, axis=-1, keepdims=True)
    grad_tokens_ref[...] += scale_one * (grad_normed - normed_one * inner_mean)
    copy = pltpu.make_async_copy(grad_tokens_ref, grad_tokens_out, done_sem.at[1])
    copy.start()
    waits.append(copy.wait)
    grad_small = grad_small + dot(
        (grad_h_one * normed_one).astype(low), (lane == route_cols).astype(low), TN
    )

    kept = []
    split = dp_ref.shape[2]

    def param_back(p, k, block):
        if p == 0:
            kept.append(block)
        else:
            block = block.at[:, pl.ds(0, split)]
            copy = remote(block, dp_ref.at[d], dp_send.at[p - 1], dp_recv.at[d], (k, r, c))
            copy.start()
            waits.append(copy.wait_send)

    params_plan = plan_reduce(
        dims,
        place,
        lambda col, k: part_ref.at[col, k],
        param_scratch[:3],
        param_scratch[3:],
        param_back,
        direct=True,
        lanes=(0, split),
    )
    first_plan = plan_dp_first(dims, place, param_scratch[0], params_plan.homes, split, first_scratch)
    finish([copy.wait_send for copy in tokens_plan.sent])
    blocked = part_ref.shape[1:4]
    for i in [*range(1, n_col), 0]:
        col = (c + i) % n_col
        qkv_cols = pl.ds(pl.multiple_of(col * wide_qkv, LANES), wide_qkv)
        out_cols = pl.ds(pl.multiple_of(col * wide_out, LANES), wide_out)
        part_ref[col, :, :, :, :wide_qkv] = (
            dot(h_one, grad_qkv_ref[:, qkv_cols], TN).astype(low).reshape(*blocked, wide_qkv)
        )
        part_ref[col, :, :, :, out_at:] = (
            dot(mixed_ref[...], grad_attn_ref[:, out_cols], TN)
            .astype(low)
            .reshape(*blocked, wide_out)
        )
        part_ref[col, :, :, :, wide_qkv:out_at] = grad_small.astype(low).reshape(*blocked, LANES)
        if i == n_col - 1:
            for t in range(n_dp):
                params_plan.send_cols(t)
    gather.pass_on(0)
    gather.pass_on(1)
    for t in range(n_dp):
        params_plan.sum_cols(t, False)
        first_plan.send_dp(t)
    for j in range(2, chunks * 2 // 3):
        gather.pass_on(j)
    for t in range(n_dp):
        params_plan.send_first(t)
    for j in range(chunks * 2 // 3, chunks):
        gather.pass_on(j)

    owner = r * n_col + c
    right_rows = right_sum_ref.shape[1]
    left_rows = left_sum_ref.shape[0]
    stores = []

    def store(m, kind, src, dst):
        copy = pltpu.make_async_copy(src, dst, store_sem.at[m, kind])
        copy.start()
        stores.append(copy)

    def shampoo_products(m):
        for j in range(m * chunks // 3, (m + 1) * chunks // 3):
            gather.last_arrivals(j)
        for j in range(m * chunks // 3, (m + 1) * chunks // 3):
            gather.wait_cols(j)
        span = pl.ds(m * D, D)
        home = pl.ds(pl.multiple_of(m * D + r * depth, 16), depth)
        for b in range(n_row):
            store(m, 3 + b, gathered_ref.at[c * n_row + b, home], block_out.at[m, b])
        root_loads[m].wait()
        lhs_ref[:right_rows] = gathered_ref[owner, span].T
        lhs_ref[right_rows:] = root_ref[m].astype(low)
        left_sum_ref[...] = jnp.zeros_like(left_sum_ref)

        @pl.loop(0, n_row * n_col, unroll=2)
        def _(q):
            cols = pl.ds(pl.multiple_of(q * slice_wide, slice_wide), slice_wide)
            block = gathered_ref[q, span]
            made = dot(lhs_ref[...], block)
            right_sum_ref[m, :, cols] = (0.5 * made[:right_rows]).astype(low)
            half_step_ref[:, cols] = made[right_rows:].astype(low)
            some = pl.ds(pl.multiple_of(m * D + owner * left_rows, 16), left_rows)
            left_sum_ref[...] += dot(gathered_ref[q, some], block, NT)

        left_low_ref[m] = (0.5 * left_sum_ref[...]).astype(low)
        store(m, 0, right_sum_ref.at[m], right_sum_out.at[m])
        store(m, 1, left_low_ref.at[m], left_sum_out.at[m])
        for t in range(tiles):
            n = m * tiles + t
            tile_loads[n].wait()
            step = dot(half_step_ref[...], tile_ref[n % held].astype(low), NT)
            step_ref[m, :, t * tile : (t + 1) * tile] = (SHAMPOO_RATE * step).astype(low)
            load_tile(n + held)
        store(m, 2, step_ref.at[m], step_out.at[m])

    shampoo_products(0)
    shampoo_products(1)
    for t in range(n_dp):
        params_plan.sum_rows(t, 0)
    first_plan.sum_dp()
    shampoo_products(2)
    for s in range(1, bits):
        for t in range(n_dp):
            params_plan.sum_rows(t, s)
    for s in range(bits):
        first_plan.sum_rows(s)
    sums = kept[0][:, :split].astype(jnp.float32)
    for p in range(1, n_dp):
        k = dp_order(d, p, n_dp)
        ref = dp_ref.at[k]
        remote(ref, ref, dp_send.at[p - 1], dp_recv.at[k], (d, r, c)).wait_recv()
        sums = sums + dp_ref[k].astype(jnp.float32)
    sum_ref[:, :split] = sums
    sum_ref[:, split:] = first_plan.total().astype(jnp.float32)
    for i in range(n_col):
        end_ref[i] = sum_ref[i * rows : (i + 1) * rows, :]
    for i in range(1, n_col):
        other = (c + i) % n_col
        copy = remote(
            end_ref.at[other], summed_ref.at[c], end_send.at[i], end_recv.at[i], (d, r, other)
        )
        copy.start()
        waits.append(copy.wait_send)
    summed_ref[pl.ds(c, 1)] = end_ref[pl.ds(c, 1)]
    for i in range(1, n_col):
        ref = summed_ref.at[(c + n_col - i) % n_col]
        remote(ref, ref, end_send.at[i], end_recv.at[i], (d, r, c)).wait_recv()
    waits += gather.sends()
    waits += [copy.wait for copy in stores]
    finish([copy.wait_send for copy in params_plan.sent + first_plan.sent])
    finish(waits)


def layer(
    lengths,
    routes,
    prev_logits,
    tokens,
    cotangent,
    w_qkv,
    w_out,
    route_w,
    gains,
    const_vec,
    weight_gu,
    weight_down,
    left_root_gu,
    right_root_down,
    right_root_gu,
    left_root_down,
    dims,
    widths,
):
    n_dp, n_row, n_col = dims
    low = jnp.bfloat16
    f32 = jnp.float32
    total = tokens.shape[0]
    rows = w_qkv.shape[0]
    wide = widths[0] + widths[1] + LANES
    num_ffn = prev_logits.shape[0] - 4
    depth, wide_col = weight_down.shape
    slice_wide = wide_col // n_row
    block_rows = n_col * rows
    wide_rows, wide_cols = left_root_down.shape
    right_rows = wide_cols // n_row // n_col
    left_rows = D // n_row // n_col
    tile = 2 * LANES
    split = wide // 2 // LANES * LANES
    chunks = 6
    dma = pltpu.SemaphoreType.DMA
    vmem = pl.BlockSpec(memory_space=pltpu.VMEM)
    hbm = pl.BlockSpec(memory_space=pl.ANY)
    whole = (n_col, n_dp, n_row, block_rows, wide)
    assert depth <= tile and 2 * wide_col <= wide_cols and wide >= 2 * D
    return pl.pallas_call(
        functools.partial(layer_kernel, (dims, num_ffn, *widths, chunks)),
        out_shape=[
            jax.ShapeDtypeStruct((total, D), low),
            jax.ShapeDtypeStruct((total, D), f32),
            jax.ShapeDtypeStruct((n_col, rows, wide), f32),
            jax.ShapeDtypeStruct((3, right_rows, wide_cols), low),
            jax.ShapeDtypeStruct((3, left_rows, D), low),
            jax.ShapeDtypeStruct((3, depth, wide_rows), low),
            jax.ShapeDtypeStruct((3, n_row, depth, slice_wide), low),
        ],
        in_specs=[pl.BlockSpec(memory_space=pltpu.SMEM)] + [vmem] * 9 + [hbm] * 6,
        out_specs=[hbm, hbm, vmem] + [hbm] * 4,
        scratch_shapes=[
            pltpu.VMEM((n_col, rows, wide), f32),
            pltpu.VMEM((LANES, LANES), f32),
            pltpu.VMEM((n_col, rows, wide), f32),
            pltpu.VMEM((block_rows, wide), f32),
            pltpu.VMEM(whole, low),
            pltpu.VMEM((n_row, 3, depth, slice_wide), low),
            pltpu.VMEM((3, n_row * depth, slice_wide), low),
            pltpu.VMEM((num_ffn, CAP, 2 * D), low),
            pltpu.VMEM((n_dp, n_col, n_row, CAP, 2 * D), low),
            pltpu.VMEM((n_dp, n_col * n_row * CAP, slice_wide), low),
            pltpu.VMEM((n_dp, n_col * n_row * CAP, 2 * slice_wide), low),
            pltpu.VMEM((3 * D, slice_wide), low),
            pltpu.VMEM((total, 3 * D), low),
            pltpu.VMEM((HEADS, total, total), f32),
            pltpu.VMEM((total, D), low),
            pltpu.VMEM((total, D), f32),
            pltpu.VMEM((n_dp, CAP, 2 * D), low),
            pltpu.VMEM((total, D), low),
            pltpu.VMEM((total, D), low),
            pltpu.VMEM((total, 3 * D), low),
            pltpu.VMEM(whole, low),
            pltpu.VMEM((n_dp, block_rows, split), low),
            pltpu.VMEM((n_col, rows, wide), f32),
            pltpu.VMEM((block_rows, wide), f32),
            pltpu.VMEM((n_col * n_row, 3 * D, slice_wide), low),
            pltpu.VMEM((3, depth, D), f32),
            pltpu.VMEM((2, tile, wide_cols), f32),
            pltpu.VMEM((depth, wide_cols), low),
            pltpu.VMEM((right_rows + depth, D), low),
            pltpu.VMEM((3, right_rows, wide_cols), low),
            pltpu.VMEM((left_rows, D), f32),
            pltpu.VMEM((3, left_rows, D), low),
            pltpu.VMEM((3, depth, wide_rows), low),
            pltpu.VMEM((total, D), low),
            pltpu.VMEM((total, D), f32),
            dma((n_col,)),
            dma((n_col,)),
            dma((3,)),
            dma((max(1, n_row - 1),)),
            dma((max(1, n_row - 1),)),
            dma((3,)),
            dma((3 * wide_rows // tile,)),
            dma((3, 3 + n_row)),
            dma((2,)),
            dma((n_dp,)),
            dma((n_dp,)),
            dma((n_dp,)),
            dma((n_dp,)),
            dma((n_col,)),
            dma((n_col,)),
            *spread_sems(dims, n_dp, copied=False),
            *spread_sems(dims, n_dp, copied=False),
            *spread_sems(dims, n_dp, copied=False),
            *spread_sems(dims, chunks),
            *reduce_scratch(dims, CAP, 2 * D, copied=False),
            *reduce_scratch(dims, block_rows, wide, copied=False, lanes=split),
            *dp_first_scratch(dims, block_rows, wide - split),
        ],
        compiler_params=pltpu.CompilerParams(
            collective_id=5, has_side_effects=True, vmem_limit_bytes=VMEM_BYTES
        ),
        name="layer",
    )(
        lengths,
        routes,
        prev_logits,
        tokens,
        cotangent,
        w_qkv,
        w_out,
        route_w,
        gains,
        const_vec,
        weight_gu,
        weight_down,
        left_root_gu,
        right_root_down,
        right_root_gu,
        left_root_down,
    )


def norm_forward(values, gain_vec):
    norm_scale = lax.rsqrt(jnp.mean(values * values, axis=-1, keepdims=True) + NORM_EPS)
    normed = values * norm_scale
    return (normed * gain_vec, normed, norm_scale)


def norm_backward(grad_out, normed, norm_scale, gain_vec):
    grad_normed = grad_out * gain_vec
    inner_mean = jnp.mean(grad_normed * normed, axis=-1, keepdims=True)
    return (norm_scale * (grad_normed - normed * inner_mean), jnp.sum(grad_out * normed, axis=0))


def attention_probs(queries, key_heads, allowed):
    scores = jnp.einsum(
        "qhd,khd->hqk", queries, key_heads, preferred_element_type=jnp.float32
    ) * HEAD ** (-0.5)
    scores = jnp.where(allowed[None], scores, -1e30)
    top_score = jnp.max(scores, axis=-1, keepdims=True)
    exp_scores = jnp.exp(scores - top_score)
    return exp_scores / jnp.sum(exp_scores, axis=-1, keepdims=True)


def diag_update(weight, grad, state, rate):
    new_state = 0.5 * state + 0.5 * grad * grad
    return (new_state, weight - rate * grad / (jnp.sqrt(new_state) + 1e-08))


def diagonal_updates(widths, n_col, summed_ref, in_refs, out_refs, turn_ref):
    wide_qkv, wide_out, route_cols = widths
    rows = summed_ref.shape[1]
    rates = (D ** (-0.5), HEAD ** (-0.5), (4 * D) ** (-0.5), 0.3, 0.5)

    def update(n, cols, grad):
        weight, state = in_refs[2 * n], in_refs[2 * n + 1]
        grad_ref, moment_ref, new_ref = out_refs[3 * n : 3 * n + 3]
        moment, new = diag_update(weight[:, cols], grad, state[:, cols], rates[n])
        grad_ref[:, cols] = grad
        moment_ref[:, cols] = moment
        new_ref[:, cols] = new

    for i in range(n_col):
        update(0, pl.ds(i * wide_qkv, wide_qkv), summed_ref[i, :, :wide_qkv])
        update(1, pl.ds(i * wide_out, wide_out), summed_ref[i, :, wide_qkv + LANES :])
    turn_ref[...] = jnp.zeros_like(turn_ref)
    turn_ref[:rows] = summed_ref[0, :, wide_qkv : wide_qkv + LANES]
    turned = turn_ref[...].T
    whole = pl.ds(0, rows)
    update(2, whole, turned[:route_cols, :rows])
    update(3, whole, turned[route_cols : route_cols + 2, :rows])
    update(4, whole, turned[route_cols + 2 : route_cols + 4, :rows])


def finish_kernel(sizes, *refs):
    n_col, widths = sizes
    refs, diag = [*refs[:13], *refs[38:]], refs[13:38]
    (
        right_sum,
        left_sum,
        step,
        block,
        left_gu,
        right_down,
        right_gu,
        left_down,
        weight_gu,
        weight_down,
        result,
        grad_tokens,
        summed,
        out_grad_gu,
        out_grad_down,
        out_left_gu,
        out_right_down,
        out_right_gu,
        out_left_down,
        out_weight_gu,
        out_weight_down,
        out_result,
        out_grad_tokens,
        right_sum_buf,
        left_sum_buf,
        step_buf,
        block_buf,
        right_buf,
        left_buf,
        weight_buf,
        grad_buf,
        result_buf,
        tokens_buf,
        turn_buf,
        *diag_buf,
        in_sem,
        out_sem,
        diag_sem,
    ) = refs
    pairs = zip([summed, *diag[:10]], diag_buf)
    small = [
        pltpu.make_async_copy(src, dst, diag_sem.at[n]) for n, (src, dst) in enumerate(pairs)
    ]
    for copy in small:
        copy.start()
    mats = range(3)
    f32 = jnp.float32
    n_row, _, slice_wide = block_buf.shape[1:]
    lefts = [left_gu.at[0], left_gu.at[1], right_down]
    rights = [right_gu.at[0], right_gu.at[1], left_down]
    weights = [weight_gu.at[:, 0], weight_gu.at[:, 1], weight_down]
    out_lefts = [out_left_gu.at[0], out_left_gu.at[1], out_right_down]
    out_rights = [out_right_gu.at[0], out_right_gu.at[1], out_left_down]
    out_weights = [out_weight_gu.at[:, 0], out_weight_gu.at[:, 1], out_weight_down]
    out_grads = [out_grad_gu.at[:, 0], out_grad_gu.at[:, 1], out_grad_down]
    loads = {}

    def load(m, kind, src, dst):
        copy = pltpu.make_async_copy(src, dst, in_sem.at[m, kind])
        copy.start()
        loads[m, kind] = copy

    stores = []

    def store(m, kind, src, dst):
        copy = pltpu.make_async_copy(src, dst, out_sem.at[m, kind])
        copy.start()
        stores.append(copy)

    for m in mats:
        load(m, 0, right_sum.at[m], right_sum_buf.at[m])
        load(m, 1, rights[m], right_buf.at[m])
        load(m, 2, block.at[m], block_buf.at[m])
        load(m, 3, step.at[m], step_buf.at[m])
        load(m, 4, weights[m], weight_buf.at[m])
        load(m, 5, left_sum.at[m], left_sum_buf.at[m])
        load(m, 6, lefts[m], left_buf.at[m])
    load(0, 7, result, result_buf)
    load(1, 7, grad_tokens, tokens_buf)
    for copy in small:
        copy.wait()
    diagonal_updates(widths, n_col, diag_buf[0], diag_buf[1:11], diag_buf[11:], turn_buf)
    for n, (src, dst) in enumerate(zip(diag_buf[11:], diag[10:])):
        copy = pltpu.make_async_copy(src, dst, diag_sem.at[11 + n])
        copy.start()
        stores.append(copy)
    for m in mats:
        loads[m, 0].wait()
        loads[m, 1].wait()
        right_buf[m] = 0.5 * right_buf[m] + right_sum_buf[m].astype(f32)
        store(m, 0, right_buf.at[m], out_rights[m])
        loads[m, 2].wait()
        for b in range(n_row):
            grad_buf[m, :, b * slice_wide : (b + 1) * slice_wide] = block_buf[m, b].astype(f32)
        store(m, 1, grad_buf.at[m], out_grads[m])
        loads[m, 3].wait()
        loads[m, 4].wait()
        weight_buf[m] = weight_buf[m] - step_buf[m].astype(f32)
        store(m, 2, weight_buf.at[m], out_weights[m])
        loads[m, 5].wait()
        loads[m, 6].wait()
        left_buf[m] = 0.5 * left_buf[m] + left_sum_buf[m].astype(f32)
        store(m, 3, left_buf.at[m], out_lefts[m])
    loads[0, 7].wait()
    store(0, 4, result_buf, out_result)
    loads[1, 7].wait()
    store(1, 4, tokens_buf, out_grad_tokens)
    for copy in stores:
        copy.wait()


def finish_update(
    products,
    left_gu,
    right_down,
    right_gu,
    left_down,
    weight_gu,
    weight_down,
    result,
    grad_tokens,
    summed,
    diag_in,
    n_col,
    widths,
):
    f32 = jnp.float32
    dma = pltpu.SemaphoreType.DMA
    hbm = pl.BlockSpec(memory_space=pl.ANY)
    right_sum, left_sum, step, block = products
    args = (
        *products,
        left_gu,
        right_down,
        right_gu,
        left_down,
        weight_gu,
        weight_down,
        result,
        grad_tokens,
        summed,
        *diag_in,
    )
    outs = [weight for weight in diag_in[::2] for _ in range(3)]
    outs += [weight_gu, weight_down, left_gu, right_down, right_gu, left_down]
    outs += [weight_gu, weight_down, result, grad_tokens]
    return pl.pallas_call(
        functools.partial(finish_kernel, (n_col, widths)),
        out_shape=[jax.ShapeDtypeStruct(like.shape, like.dtype) for like in outs],
        in_specs=[hbm] * 23,
        out_specs=[hbm] * 25,
        scratch_shapes=[
            pltpu.VMEM(right_sum.shape, right_sum.dtype),
            pltpu.VMEM(left_sum.shape, left_sum.dtype),
            pltpu.VMEM(step.shape, step.dtype),
            pltpu.VMEM(block.shape, block.dtype),
            pltpu.VMEM(right_sum.shape, f32),
            pltpu.VMEM(left_sum.shape, f32),
            pltpu.VMEM(step.shape, f32),
            pltpu.VMEM(step.shape, f32),
            pltpu.VMEM(result.shape, result.dtype),
            pltpu.VMEM(grad_tokens.shape, f32),
            pltpu.VMEM((LANES, LANES), f32),
            *[pltpu.VMEM(like.shape, f32) for like in (summed, *diag_in, *outs[:15])],
            dma((3, 8)),
            dma((3, 5)),
            dma((26,)),
        ],
        compiler_params=pltpu.CompilerParams(vmem_limit_bytes=VMEM_BYTES),
        name="finish",
    )(*args)


def shampoo_plain(
    grads,
    left_root_gu,
    right_root_down,
    right_root_gu,
    left_root_down,
    left_gu,
    right_down,
    right_gu,
    left_down,
    weight_gu,
    weight_down,
    n_row,
    n_col,
):
    low = jnp.bfloat16
    blocks, _, slice_wide = grads.shape
    model = left_root_gu.shape[2]
    r = lax.axis_index("row")
    c = lax.axis_index("col")
    owner = r * n_col + c
    left_rows = right_down.shape[0]
    right_rows = left_down.shape[0]
    product = functools.partial(jnp.einsum, preferred_element_type=jnp.float32)
    whole = grads.reshape(blocks, 3, model, slice_wide).transpose(1, 2, 0, 3).reshape(3, model, -1)
    mine_left = lax.dynamic_slice_in_dim(whole, owner * left_rows, left_rows, 1)
    mine_right = lax.dynamic_slice_in_dim(whole, owner * right_rows, right_rows, 2)
    left_sum = 0.5 * product("mif,mjf->mij", mine_left, whole)
    right_sum = 0.5 * product("mdi,mdj->mij", mine_right, whole)
    roots = jnp.concatenate([left_root_gu, right_root_down[None]]).astype(low)
    wides = jnp.concatenate([right_root_gu, left_root_down[None]]).astype(low)
    step = product("mid,mdf->mif", roots, whole).astype(low)
    step = SHAMPOO_RATE * product("mif,mjf->mij", step, wides)
    depth, wide_rows = weight_down.shape
    block = lax.dynamic_slice(whole, (0, r * depth, c * wide_rows), (3, depth, wide_rows))
    block = block.astype(jnp.float32)
    return (
        block[:2].transpose(1, 0, 2),
        block[2],
        0.5 * left_gu + left_sum[:2],
        0.5 * right_down + left_sum[2],
        0.5 * right_gu + right_sum[:2],
        0.5 * left_down + right_sum[2],
        weight_gu - step[:2].transpose(1, 0, 2),
        weight_down - step[2],
    )


def body_tiled(
    tokens,
    lengths,
    routes,
    prev_logits,
    cotangent,
    w_qkv,
    w_out,
    route_w,
    gains,
    const_vec,
    stat_qkv,
    stat_out,
    stat_route,
    stat_gains,
    stat_const,
    w_gate_up,
    w_down,
    left_gu,
    right_gu,
    left_down,
    right_down,
    left_root_gu,
    right_root_gu,
    left_root_down,
    right_root_down,
):
    dims = mesh_sizes()
    n_col = dims[2]
    wide_qkv = w_qkv.shape[1] // n_col
    wide_out = w_out.shape[1] // n_col
    widths = (wide_qkv, wide_out, route_w.shape[1])
    result, grad_input, summed, *products = layer(
        lengths,
        routes.T,
        prev_logits.T,
        tokens,
        cotangent,
        w_qkv,
        w_out,
        route_w.T,
        gains,
        const_vec,
        w_gate_up[0],
        w_down[0].T,
        left_root_gu[0],
        right_root_down[0],
        right_root_gu[0],
        left_root_down[0],
        dims,
        widths,
    )
    outs = finish_update(
        products,
        left_gu[0],
        right_down[0],
        right_gu[0],
        left_down[0],
        w_gate_up[0],
        w_down[0].T,
        result,
        grad_input,
        summed,
        [
            w_qkv,
            stat_qkv,
            w_out,
            stat_out,
            route_w.T,
            stat_route.T,
            gains,
            stat_gains,
            const_vec,
            stat_const,
        ],
        n_col,
        widths,
    )
    diag = list(outs[:15])
    diag[6:9] = [part.T for part in diag[6:9]]
    (
        grad_gate_up,
        grad_down,
        new_left_gu,
        new_right_down,
        new_right_gu,
        new_left_down,
        new_gate_up,
        new_down,
        result,
        grad_input,
    ) = outs[15:]
    return (
        result,
        grad_input,
        *diag,
        grad_gate_up[None],
        grad_down.T[None],
        new_left_gu[None],
        new_right_gu[None],
        new_left_down[None],
        new_right_down[None],
        new_gate_up[None],
        new_down.T[None],
    )


def body(
    tokens,
    lengths,
    routes,
    prev_logits,
    cotangent,
    w_qkv,
    w_out,
    route_w,
    gains,
    const_vec,
    stat_qkv,
    stat_out,
    stat_route,
    stat_gains,
    stat_const,
    w_gate_up,
    w_down,
    left_gu,
    right_gu,
    left_down,
    right_down,
    left_root_gu,
    right_root_gu,
    left_root_down,
    right_root_down,
):
    dims = mesh_sizes()
    n_dp, n_row, n_col = dims
    low = jnp.bfloat16
    row_total = tokens.shape[0]
    total_experts = prev_logits.shape[1]
    num_ffn = total_experts - 4
    seq_count = lengths.shape[1]
    shard_rows = w_qkv.shape[0]
    wide_qkv = w_qkv.shape[1] // n_col
    wide_out = w_out.shape[1] // n_col
    route_cols = route_w.shape[1]
    wide = wide_qkv + wide_out + LANES

    def by_col(matrix):
        return matrix.reshape(matrix.shape[0], n_col, -1).transpose(1, 0, 2)

    def small_block(route_part, gain_part, const_part):
        together = jnp.concatenate([route_part, gain_part.T, const_part.T], axis=1)
        return jnp.pad(together, ((0, 0), (0, LANES - together.shape[1])))

    small = small_block(route_w, gains, const_vec)
    shard = jnp.concatenate(
        [by_col(w_qkv), by_col(w_out), jnp.broadcast_to(small[None], (n_col, shard_rows, LANES))],
        axis=2,
    )
    whole = param_gather(shard, dims).reshape(n_col, D, wide)
    full_qkv = [whole[i, :, :wide_qkv] for i in range(n_col)]
    full_out = [whole[i, :, wide_qkv : wide_qkv + wide_out] for i in range(n_col)]
    full_small = whole[0, :, wide_qkv + wide_out :]
    full_route = full_small[:, :route_cols]
    row_vectors = full_small[:, route_cols : route_cols + 4].T.astype(jnp.float32)
    gain_one, gain_two, const_rows = row_vectors[0], row_vectors[1], row_vectors[2:4]

    row_depth = w_gate_up.shape[1]
    col_width = w_gate_up.shape[3]
    slice_wide = col_width // n_row
    gu_slices = w_gate_up[0].astype(low).reshape(row_depth, 2, n_row, slice_wide)
    gu_slices = gu_slices.transpose(2, 0, 1, 3)
    gu_own = lax.all_to_all(gu_slices, "row", split_axis=0, concat_axis=0, tiled=True)
    gu_own = gu_own.reshape(n_row * row_depth, 2 * slice_wide)
    down_slices = w_down[0].astype(low).reshape(n_row, slice_wide, row_depth)
    down_own = lax.all_to_all(down_slices, "row", split_axis=0, concat_axis=0, tiled=True)
    down_own = down_own.transpose(1, 0, 2).reshape(slice_wide, n_row * row_depth)

    positions = jnp.arange(row_total, dtype=jnp.int32)
    seq_ends = jnp.cumsum(lengths[0])
    doc_index = jnp.sum((positions[:, None] >= seq_ends[None, :]).astype(jnp.int32), axis=1)
    valid_rows = (doc_index < seq_count).astype(jnp.float32)[:, None]
    allowed = (doc_index[:, None] == doc_index[None, :]) & (
        positions[:, None] >= positions[None, :]
    )
    inputs = tokens.astype(jnp.float32)
    h_one, normed_one, scale_one = norm_forward(inputs, gain_one)
    h_one_low = h_one.astype(low)
    qkv_rows = jnp.concatenate([dot(h_one_low, part) for part in full_qkv], axis=1).astype(low)
    qkv_rows = qkv_rows.reshape(row_total, 3, HEADS, HEAD)
    queries, key_heads, values = (qkv_rows[:, 0], qkv_rows[:, 1], qkv_rows[:, 2])
    softmax_probs = attention_probs(queries, key_heads, allowed)
    probs_low = softmax_probs.astype(low)
    mixed_heads = jnp.einsum("hqk,khd->qhd", probs_low, values, preferred_element_type=jnp.float32)
    mixed_heads = mixed_heads.reshape(row_total, D).astype(low)
    attn_out = jnp.concatenate([dot(mixed_heads, part) for part in full_out], axis=1)
    first_sum = inputs + valid_rows * attn_out
    h_two, normed_two, scale_two = norm_forward(first_sum, gain_two)
    h_two_low = h_two.astype(low)
    logits_all = dot(h_two_low, full_route)
    logits = logits_all[:, :total_experts] + prev_logits
    pick_table = (
        routes[:, :, None] == jnp.arange(total_experts, dtype=jnp.int32)[None, None, :]
    ).astype(jnp.float32)
    chosen = jnp.sum(pick_table * logits[:, None, :], axis=-1)
    gate_weights = jax.nn.softmax(chosen, axis=-1)
    const_mix = jax.nn.softmax(logits_all[:, total_experts:].reshape(row_total, 2, 2), axis=-1)

    earlier = dot(
        (positions[:, None] > positions[None, :]).astype(low),
        jnp.sum(pick_table, axis=1).astype(low),
    )
    slot_index = jnp.sum(earlier[:, None, :] * pick_table, axis=-1).astype(jnp.int32)
    where_in = jnp.where(routes < num_ffn, routes * CAP + slot_index, -1)
    slot_ids = jnp.arange(num_ffn * CAP, dtype=jnp.int32)
    place_first = where_in[:, 0:1] == slot_ids[None, :]
    place_second = where_in[:, 1:2] == slot_ids[None, :]
    place_both = (place_first | place_second).astype(low)
    slot_gate = jnp.sum(
        place_first.astype(jnp.float32) * gate_weights[:, 0:1]
        + place_second.astype(jnp.float32) * gate_weights[:, 1:2],
        axis=0,
    )
    grad_y = cotangent.astype(jnp.float32) * valid_rows
    sent_rows = dot(place_both, h_two_low, TN).astype(low)
    grad_made = (slot_gate[:, None] * dot(place_both, grad_y.astype(low), TN)).astype(low)
    sent_both = jnp.concatenate(
        [sent_rows.reshape(num_ffn, CAP, D), grad_made.reshape(num_ffn, CAP, D)], axis=2
    )

    arrived = token_gather(sent_both, dims).reshape(-1, 2 * D)
    rows_in = arrived[:, :D]
    grads_in = arrived[:, D:]
    pre_act = dot(rows_in, gu_own)
    gate_part = pre_act[:, :slice_wide]
    up_part = pre_act[:, slice_wide:]
    sigma = jax.nn.sigmoid(gate_part)
    silu = gate_part * sigma
    hidden = (silu * up_part).astype(low)
    made_rows = dot(hidden, down_own).astype(low)
    grad_hidden = dot(grads_in, down_own, NT)
    grad_pre = jnp.concatenate(
        [
            grad_hidden * up_part * sigma * (1.0 + gate_part * (1.0 - sigma)),
            grad_hidden * silu,
        ],
        axis=1,
    ).astype(low)
    grad_rows = dot(grad_pre, gu_own, NT).astype(low)
    parts_back = jnp.concatenate([made_rows, grad_rows], axis=1)
    parts_back = parts_back.reshape(n_col, n_dp, n_row, CAP, 2 * D)
    came_back = token_reduce(parts_back, dims).reshape(num_ffn * CAP, 2 * D)
    expert_out = came_back[:, :D]
    grad_sent = came_back[:, D:]

    grad_gu_own = dot(rows_in, grad_pre, TN).astype(low)
    grad_down_own = dot(hidden, grads_in, TN).astype(low)
    grads_own = jnp.concatenate(
        [grad_gu_own[:, :slice_wide], grad_gu_own[:, slice_wide:], grad_down_own.T], axis=0
    )
    gathered = plane_gather(grads_own.reshape(4, -1, slice_wide), dims)
    gathered = gathered.reshape(n_col * n_row, 3 * D, slice_wide)

    is_ffn_first = dot(place_first.astype(low), expert_out)
    is_ffn_second = dot(place_second.astype(low), expert_out)
    picked = jnp.stack([is_ffn_first, is_ffn_second], axis=1)
    copy_sel = (routes == num_ffn + 1).astype(jnp.float32)
    const_sel = (
        routes[:, :, None] == num_ffn + 2 + jnp.arange(2, dtype=jnp.int32)[None, None, :]
    ).astype(jnp.float32)
    const_out = (
        const_mix[:, :, 0:1] * h_two[:, None, :] + const_mix[:, :, 1:2] * const_rows[None, :, :]
    )
    outputs = (
        picked
        + copy_sel[:, :, None] * h_two[:, None, :]
        + const_sel[:, :, 0:1] * const_out[:, None, 0, :]
        + const_sel[:, :, 1:2] * const_out[:, None, 1, :]
    )
    moe_out = valid_rows * jnp.sum(gate_weights[:, :, None] * outputs, axis=1)
    result = (first_sum + moe_out).astype(low)
    grad_gate = jnp.sum(grad_y[:, None, :] * outputs, axis=-1)
    grad_chosen = gate_weights * (
        grad_gate - jnp.sum(gate_weights * grad_gate, axis=-1, keepdims=True)
    )
    grad_logits = jnp.sum(grad_chosen[:, :, None] * pick_table, axis=1)
    const_weight = jnp.sum(const_sel * gate_weights[:, :, None], axis=1)
    mix_first = const_weight * jnp.sum(grad_y * h_two, axis=-1, keepdims=True)
    mix_second = const_weight * jnp.stack(
        [jnp.sum(grad_y * const_rows[0], axis=-1), jnp.sum(grad_y * const_rows[1], axis=-1)], axis=1
    )
    grad_mix = jnp.stack([mix_first, mix_second], axis=-1)
    grad_mix_logits = const_mix * (grad_mix - jnp.sum(const_mix * grad_mix, axis=-1, keepdims=True))
    grad_logits_all = jnp.concatenate(
        [grad_logits, grad_mix_logits.reshape(row_total, 4)], axis=1
    ).astype(low)
    grad_route_full = dot(h_two_low, grad_logits_all, TN)
    const_scale = const_weight * const_mix[:, :, 1]
    grad_const_full = jnp.stack(
        [
            jnp.sum(const_scale[:, 0:1] * grad_y, axis=0),
            jnp.sum(const_scale[:, 1:2] * grad_y, axis=0),
        ]
    )
    back_rows = dot(place_both, grad_sent)
    own_weight = jnp.sum(gate_weights * copy_sel, axis=1, keepdims=True) + jnp.sum(
        const_weight * const_mix[:, :, 0], axis=1, keepdims=True
    )
    grad_h_two = dot(grad_logits_all, full_route, NT) + back_rows + own_weight * grad_y
    grad_first, grad_gain_two = norm_backward(grad_h_two, normed_two, scale_two, gain_two)
    grad_first = grad_first + cotangent.astype(jnp.float32)
    grad_attn = (valid_rows * grad_first).astype(low)
    grad_mixed = functools.reduce(
        jnp.add,
        [
            dot(grad_attn[:, i * wide_out : (i + 1) * wide_out], part, NT)
            for i, part in enumerate(full_out)
        ],
    ).astype(low)
    grad_mixed = grad_mixed.reshape(row_total, HEADS, HEAD)
    grad_values = jnp.einsum(
        "hqk,qhd->khd", probs_low, grad_mixed, preferred_element_type=jnp.float32
    )
    grad_probs = jnp.einsum("qhd,khd->hqk", grad_mixed, values, preferred_element_type=jnp.float32)
    grad_scores = softmax_probs * (
        grad_probs - jnp.sum(softmax_probs * grad_probs, axis=-1, keepdims=True)
    )
    grad_scores = grad_scores.astype(low)
    grad_queries = jnp.einsum(
        "hqk,khd->qhd", grad_scores, key_heads, preferred_element_type=jnp.float32
    ) * HEAD ** (-0.5)
    grad_keys = jnp.einsum(
        "hqk,qhd->khd", grad_scores, queries, preferred_element_type=jnp.float32
    ) * HEAD ** (-0.5)
    grad_qkv_rows = (
        jnp.stack([grad_queries, grad_keys, grad_values], axis=1)
        .reshape(row_total, 3 * D)
        .astype(low)
    )
    grad_h_one = functools.reduce(
        jnp.add,
        [
            dot(grad_qkv_rows[:, i * wide_qkv : (i + 1) * wide_qkv], part, NT)
            for i, part in enumerate(full_qkv)
        ],
    )
    grad_input, grad_gain_one = norm_backward(grad_h_one, normed_one, scale_one, gain_one)
    grad_input = grad_input + grad_first
    grad_gains_full = jnp.stack([grad_gain_one, grad_gain_two])

    grad_small = small_block(grad_route_full, grad_gains_full, grad_const_full).astype(low)
    param_parts = jnp.stack(
        [
            jnp.concatenate(
                [
                    dot(h_one_low, grad_qkv_rows[:, i * wide_qkv : (i + 1) * wide_qkv], TN).astype(
                        low
                    ),
                    dot(mixed_heads, grad_attn[:, i * wide_out : (i + 1) * wide_out], TN).astype(
                        low
                    ),
                    grad_small,
                ],
                axis=1,
            )
            for i in range(n_col)
        ]
    )
    summed = param_reduce(
        param_parts.reshape(n_col, n_dp, n_row, n_col * shard_rows, wide), dims
    )

    def from_col(parts):
        return parts.transpose(1, 0, 2).reshape(parts.shape[1], -1)

    grad_qkv = from_col(summed[:, :, :wide_qkv])
    grad_attn_out = from_col(summed[:, :, wide_qkv : wide_qkv + wide_out])
    sum_small = summed[0, :, wide_qkv + wide_out :]
    grad_route = sum_small[:, :route_cols]
    grad_gains = sum_small[:, route_cols : route_cols + 2].T
    grad_const = sum_small[:, route_cols + 2 : route_cols + 4].T
    moment_qkv, new_qkv = diag_update(w_qkv, grad_qkv, stat_qkv, D ** (-0.5))
    moment_attn_out, new_attn_out = diag_update(w_out, grad_attn_out, stat_out, HEAD ** (-0.5))
    moment_route, new_route = diag_update(route_w, grad_route, stat_route, (4 * D) ** (-0.5))
    moment_gains, new_gains = diag_update(gains, grad_gains, stat_gains, 0.3)
    moment_const, new_const = diag_update(const_vec, grad_const, stat_const, 0.5)

    (
        grad_gate_up,
        grad_down,
        new_left_gu,
        new_right_down,
        new_right_gu,
        new_left_down,
        new_gate_up,
        new_down,
    ) = shampoo_plain(
        gathered,
        left_root_gu[0],
        right_root_down[0],
        right_root_gu[0],
        left_root_down[0],
        left_gu[0],
        right_down[0],
        right_gu[0],
        left_down[0],
        w_gate_up[0],
        w_down[0].T,
        n_row,
        n_col,
    )
    return (
        result,
        grad_input,
        grad_qkv,
        moment_qkv,
        new_qkv,
        grad_attn_out,
        moment_attn_out,
        new_attn_out,
        grad_route,
        moment_route,
        new_route,
        grad_gains,
        moment_gains,
        new_gains,
        grad_const,
        moment_const,
        new_const,
        grad_gate_up[None],
        grad_down.T[None],
        new_left_gu[None],
        new_right_gu[None],
        new_left_down[None],
        new_right_down[None],
        new_gate_up[None],
        new_down.T[None],
    )


def solution(mesh):
    placed = (
        P(("dp", "row", "col"), None),
        P(("dp", "row", "col"), None),
        P(("dp", "row", "col"), None),
        P(("dp", "row", "col"), None),
        P(("dp", "row", "col"), None),
        P(("dp", "row", "col"), None),
        P(("dp", "row", "col"), None),
        P(("dp", "row", "col"), None),
        P(None, ("dp", "row", "col")),
        P(None, ("dp", "row", "col")),
        P(("dp", "row", "col"), None),
        P(("dp", "row", "col"), None),
        P(("dp", "row", "col"), None),
        P(None, ("dp", "row", "col")),
        P(None, ("dp", "row", "col")),
        P("dp", "row", None, "col"),
        P("dp", "col", "row"),
        P("dp", None, ("row", "col"), None),
        P("dp", None, ("row", "col"), None),
        P("dp", ("row", "col"), None),
        P("dp", ("row", "col"), None),
        P("dp", None, "row", None),
        P("dp", None, "col", None),
        P("dp", "col", None),
        P("dp", "row", None),
    )
    tiled = 3 * D % (mesh.shape["col"] * LANES) == 0 and D % (mesh.shape["col"] * LANES) == 0
    tiled = tiled and D // mesh.shape["dp"] // mesh.shape["row"] % 16 == 0
    return jax.shard_map(
        body_tiled if tiled else body,
        mesh=mesh,
        in_specs=placed,
        out_specs=(
            P(("dp", "row", "col"), None),
            P(("dp", "row", "col"), None),
            P(("dp", "row", "col"), None),
            P(("dp", "row", "col"), None),
            P(("dp", "row", "col"), None),
            P(("dp", "row", "col"), None),
            P(("dp", "row", "col"), None),
            P(("dp", "row", "col"), None),
            P(("dp", "row", "col"), None),
            P(("dp", "row", "col"), None),
            P(("dp", "row", "col"), None),
            P(None, ("dp", "row", "col")),
            P(None, ("dp", "row", "col")),
            P(None, ("dp", "row", "col")),
            P(None, ("dp", "row", "col")),
            P(None, ("dp", "row", "col")),
            P(None, ("dp", "row", "col")),
            P("dp", "row", None, "col"),
            P("dp", "col", "row"),
            P("dp", None, ("row", "col"), None),
            P("dp", None, ("row", "col"), None),
            P("dp", ("row", "col"), None),
            P("dp", ("row", "col"), None),
            P("dp", "row", None, "col"),
            P("dp", "col", "row"),
        ),
        check_vma=False,
    )
```

```python
import functools
import types

import jax
import jax.numpy as jnp
from jax import lax
from jax.experimental import pallas as pl
from jax.experimental.pallas import tpu as pltpu
from jax.sharding import PartitionSpec as P

D = 768
HEADS = 12
HEAD = 64
CAP = 32
LANES = 128


NORM_EPS = 1e-06
SHAMPOO_RATE = 0.5
MESH = pl.DeviceIdType.MESH
VMEM_BYTES = 62 * 2**20


def dot(left, right, dims=(((1,), (0,)), ((), ()))):
    return lax.dot_general(left, right, dims, preferred_element_type=jnp.float32)


NT = (((1,), (1,)), ((), ()))
TN = (((0,), (0,)), ((), ()))


def flip(index, bit):
    return index + bit * (1 - 2 * ((index // bit) % 2))


def flip_all(index, mask, bits):
    for dim in range(bits):
        if mask & (1 << dim):
            index = flip(index, 1 << dim)
    return index


def dp_order(d, p, count):
    if p == 0:
        return d
    upper = d // max(1, count // 2)
    low_d = d + upper * (count - 1 - 2 * d)
    at = p - 1 + (p - 1 - low_d + count) // count
    return at + upper * (count - 1 - 2 * at)


def mesh_sizes():
    return tuple(lax.axis_size(name) for name in ("dp", "row", "col"))


def bits_of(count):
    bits = count.bit_length() - 1
    assert 1 << bits == count
    return bits


def greet(over_dp, dims, place, all_rows=False, wait=True):
    n_dp, n_row, n_col = dims
    d, r, c = place
    peers = []
    if over_dp:
        peers += [((d + j) % n_dp, r, c) for j in range(1, n_dp)]
    if all_rows:
        peers += [(d, (r + i) % n_row, c) for i in range(1, n_row)]
    else:
        peers += [(d, flip(r, 1 << dim), c) for dim in range(bits_of(n_row))]
    peers += [(d, r, (c + i) % n_col) for i in range(1, n_col)]
    barrier = pltpu.get_barrier_semaphore()
    for peer in peers:
        pl.semaphore_signal(barrier, inc=1, device_id=peer, device_id_type=MESH)
    if wait:
        pl.semaphore_wait(barrier, len(peers))
    return len(peers)


def remote(src, dst, send_sem, recv_sem, device):
    return pltpu.make_async_remote_copy(
        src_ref=src,
        dst_ref=dst,
        send_sem=send_sem,
        recv_sem=recv_sem,
        device_id=device,
        device_id_type=MESH,
    )


def plan_spread(dims, place, chunks, over_dp, own, dp_source, slot, sems, halves=False, totals=None):
    n_dp, n_row, n_col = dims
    d, r, c = place
    bits = bits_of(n_row)
    dp_send, dp_recv, row_send, row_recv, col_send, col_recv, own_sem = sems
    sent = []

    def of(sem, *at):
        return sem.at[tuple(0 for _ in at)] if totals else sem.at[at]


    def block(j, x):
        return slot(c, j, flip_all(r, x, bits))

    def to_row(j, src, x, bit):
        copy = remote(
            src,
            block(j, x),
            of(row_send, j, (x ^ bit) - 1),
            row_recv.at[j, (x ^ bit) - 1],
            (d, flip(r, bit), c),
        )
        copy.start()
        sent.append(copy)

    def to_cols(j, src, x):
        for i in range(1, n_col):
            copy = remote(
                src,
                block(j, x),
                of(col_send, j, x, i - 1),
                col_recv.at[j, x, i - 1],
                (d, r, (c + i) % n_col),
            )
            copy.start()
            sent.append(copy)

    def order(j):
        return [1 << ((j + s) % bits) for s in range(bits)]

    locals_ = {}

    def start(j):
        if over_dp and j > 0:
            src = block(j, 0)
            origin = dp_order(d, j, n_dp)
            remote(src, src, of(dp_send, j - 1), dp_recv.at[origin], (d, r, c)).wait_recv()
        elif own is None:
            src = block(j, 0)
        else:
            src = own(j)
            keep = pltpu.make_async_copy(src, block(j, 0), own_sem.at[j])
            keep.start()
            locals_[j] = keep
        for bit in order(j):
            to_row(j, src, 0, bit)
        to_cols(j, src, 0)

    def arrived(j, x, later_dims):
        ref = block(j, x)
        remote(ref, ref, of(row_send, j, x - 1), row_recv.at[j, x - 1], (d, r, c)).wait_recv()
        for later in later_dims:
            to_row(j, ref, x, later)
        to_cols(j, ref, x)

    def parts(ref):
        wide = ref.shape[-1]
        cut = (wide // LANES + 1) // 2 * LANES
        return [ref.at[:, pl.ds(0, cut)], ref.at[:, pl.ds(cut, wide - cut)]]

    def pass_halves(j):
        for x in order(j):
            arrived(j, x, [])
            half = x - 1
            part = parts(block(j, x))[half]
            copy = remote(
                part,
                part,
                of(row_send, j, 2 + half),
                row_recv.at[j, 2 + half],
                (d, flip(r, 3 - x), c),
            )
            copy.start()
            sent.append(copy)

    def last_halves(j):
        for half, part in enumerate(parts(block(j, 3))):
            remote(
                part, part, of(row_send, j, 2 + half), row_recv.at[j, 2 + half], (d, r, c)
            ).wait_recv()
        to_cols(j, block(j, 3), 3)

    def pass_on(j):
        have = [0]
        dim_order = order(j)
        for s, bit in enumerate(dim_order[:-1]):
            new = [x ^ bit for x in have]
            for x in new:
                arrived(j, x, dim_order[s + 1 :])
            have += new

    def last_arrivals(j):
        bit = order(j)[-1]
        for x in range(n_row):
            if x & bit:
                arrived(j, x, [])

    def send_dp():
        for j in range(1, n_dp):
            peer = dp_order(d, j, n_dp)
            copy = remote(
                dp_source(peer),
                slot(c, ("from", d), r),
                of(dp_send, j - 1),
                dp_recv.at[d],
                (peer, r, c),
            )
            copy.start()
            sent.append(copy)

    def wait_cols(j):
        for x in range(n_row):
            for i in range(1, n_col):
                ref = slot((c + n_col - i) % n_col, j, flip_all(r, x, bits))
                remote(
                    ref, ref, of(col_send, j, x, i - 1), col_recv.at[j, x, i - 1], (d, r, c)
                ).wait_recv()
        if j in locals_:
            locals_[j].wait()

    def sends():
        if totals is None:
            return [copy.wait_send for copy in sent]
        pairs = zip((dp_send, row_send, col_send), totals)
        return [
            remote(ref, ref, of(sem, *sem.shape), dp_recv.at[0], (d, r, c)).wait_send
            for sem, ref in pairs
            if ref is not None
        ]

    return types.SimpleNamespace(
        start=start,
        send_dp=send_dp,
        pass_on=pass_halves if halves else pass_on,
        last_arrivals=last_halves if halves else last_arrivals,
        wait_cols=wait_cols,
        sends=sends,
    )


def spread_blocks(dims, place, chunks, over_dp, own, dp_source, slot, sems, between=None):
    plan = plan_spread(dims, place, chunks, over_dp, own, dp_source, slot, sems)
    plan.start(0)
    if over_dp:
        plan.send_dp()
        for j in range(1, chunks):
            plan.start(j)
            plan.pass_on(j - 1)
        plan.pass_on(chunks - 1)
    else:
        for j in range(1, chunks):
            plan.start(j)
        for j in range(chunks):
            plan.pass_on(j)
    if between is not None:
        between()
    for j in range(chunks):
        plan.last_arrivals(j)
    for j in range(chunks):
        plan.wait_cols(j)
    return plan.sends()


def finish(waits):
    for wait in waits:
        wait()


def spread_sems(dims, chunks, copied=True, halves=False, shared=False):
    n_dp, n_row, n_col = dims
    pieces = max(1, n_row - 1) + halves
    dma = pltpu.SemaphoreType.DMA
    rows = (chunks, pieces)
    cols = (chunks, n_row, max(1, n_col - 1))
    return [
        dma((1,) if shared else (max(1, n_dp - 1),)),
        dma((n_dp,)),
        dma((1, 1) if shared else rows),
        dma(rows),
        dma((1, 1, 1) if shared else cols),
        dma(cols),
        dma((chunks if copied else 1,)),
    ]


def axis_place():
    return tuple(lax.axis_index(name) for name in ("dp", "row", "col"))


def param_gather_kernel(dims, shard_ref, out_ref, swap_ref, block_ref, swap_send, swap_recv, *sems):
    n_dp, n_row, n_col = dims
    place = axis_place()
    d, r, c = place
    rows = shard_ref.shape[1]
    greet(True, dims, place)
    copies = []
    for i in range(1, n_col):
        other = (c + i) % n_col
        copy = remote(
            shard_ref.at[other], swap_ref.at[c], swap_send.at[i], swap_recv.at[i], (d, r, other)
        )
        copy.start()
        copies.append(copy)
    swap_ref[pl.ds(c, 1)] = shard_ref[pl.ds(c, 1)]
    for copy in copies:
        copy.wait()
    for i in range(n_col):
        block_ref[i * rows : (i + 1) * rows, :] = swap_ref[i]
    low_ref = sems[-1]
    low_ref[...] = block_ref[...].astype(jnp.bfloat16)

    def slot(col, j, b):
        k = j[1] if isinstance(j, tuple) else dp_order(d, j, n_dp)
        return out_ref.at[col, k, b]

    finish(
        spread_blocks(
            dims, place, n_dp, True, lambda j: low_ref, lambda k: low_ref, slot, sems[:-1]
        )
    )


def param_gather(shard, dims):
    n_dp, n_row, n_col = dims
    _, rows, width = shard.shape
    dma = pltpu.SemaphoreType.DMA
    return pl.pallas_call(
        functools.partial(param_gather_kernel, dims),
        out_shape=jax.ShapeDtypeStruct((n_col, n_dp, n_row, n_col * rows, width), jnp.bfloat16),
        in_specs=[pl.BlockSpec(memory_space=pltpu.VMEM)],
        out_specs=pl.BlockSpec(memory_space=pl.ANY),
        scratch_shapes=[
            pltpu.VMEM((n_col, rows, width), jnp.float32),
            pltpu.VMEM((n_col * rows, width), jnp.float32),
            dma((n_col,)),
            dma((n_col,)),
            *spread_sems(dims, n_dp),
            pltpu.VMEM((n_col * rows, width), jnp.bfloat16),
        ],
        compiler_params=pltpu.CompilerParams(
            collective_id=0, has_side_effects=True, vmem_limit_bytes=VMEM_BYTES
        ),
        name="param_gather",
    )(shard)


def token_gather_kernel(dims, src_ref, out_ref, *sems):
    n_dp, n_row, n_col = dims
    place = axis_place()
    d = place[0]
    greet(True, dims, place)

    def slot(col, j, b):
        k = j[1] if isinstance(j, tuple) else dp_order(d, j, n_dp)
        return out_ref.at[col, k, b]

    finish(
        spread_blocks(
            dims,
            place,
            n_dp,
            True,
            lambda j: src_ref.at[d],
            lambda k: src_ref.at[k],
            slot,
            sems,
        )
    )


def token_gather(rows, dims):
    n_dp, n_row, n_col = dims
    _, slots, width = rows.shape
    return pl.pallas_call(
        functools.partial(token_gather_kernel, dims),
        out_shape=jax.ShapeDtypeStruct((n_col, n_dp, n_row, slots, width), rows.dtype),
        in_specs=[pl.BlockSpec(memory_space=pl.ANY)],
        out_specs=pl.BlockSpec(memory_space=pl.ANY),
        scratch_shapes=spread_sems(dims, n_dp),
        compiler_params=pltpu.CompilerParams(
            collective_id=1, has_side_effects=True, vmem_limit_bytes=VMEM_BYTES
        ),
        name="token_gather",
    )(rows)


def plane_gather_kernel(dims, src_ref, out_ref, *sems):
    place = axis_place()
    greet(False, dims, place)
    finish(
        spread_blocks(
            dims,
            place,
            src_ref.shape[0],
            False,
            lambda j: src_ref.at[j],
            None,
            lambda col, j, b: out_ref.at[col, b, j],
            sems,
        )
    )


def plane_gather(parts, dims):
    n_dp, n_row, n_col = dims
    chunks, rows, width = parts.shape
    return pl.pallas_call(
        functools.partial(plane_gather_kernel, dims),
        out_shape=jax.ShapeDtypeStruct((n_col, n_row, chunks, rows, width), parts.dtype),
        in_specs=[pl.BlockSpec(memory_space=pl.ANY)],
        out_specs=pl.BlockSpec(memory_space=pl.ANY),
        scratch_shapes=spread_sems(dims, chunks),
        compiler_params=pltpu.CompilerParams(
            collective_id=2, has_side_effects=True, vmem_limit_bytes=VMEM_BYTES
        ),
        name="plane_gather",
    )(parts)


def add_low(left, right):
    return (left.astype(jnp.float32) + right.astype(jnp.float32)).astype(jnp.bfloat16)


def plan_reduce(
    dims, place, part_at, bufs, sems, deliver, direct=False, far_first=True, lanes=None
):
    n_dp, n_row, n_col = dims
    d, r, c = place
    bits = bits_of(n_row)
    mine_ref, col_ref, row_ref = bufs
    mine_sem, col_send, col_recv, row_send, row_recv = sems
    steps = list(reversed(range(n_dp))) if far_first else list(range(n_dp))
    homes = [dp_order(d, p, n_dp) for p in steps]
    sent = [
        remote(ref, ref, sem.at[0], col_recv.at[0, 0], (d, r, c))
        for ref, sem in ((col_ref, col_send), (row_ref, row_send))
    ]
    held = []

    def send_cols(t):
        for i in range(1, n_col):
            other = (c + i) % n_col
            copy = remote(
                part_at(other, homes[t]),
                col_ref.at[t, i - 1],
                col_send.at[0],
                col_recv.at[t, i - 1],
                (d, r, other),
            )
            copy.start()

    def load_mine():
        for t in range(n_dp):
            keep = pltpu.make_async_copy(part_at(c, homes[t]), mine_ref.at[t], mine_sem.at[t])
            keep.start()
            held.append(keep)

    begin, width = lanes or (0, mine_ref.shape[-1])
    cut = (width // LANES + 1) // 2 * LANES
    spans = [pl.ds(begin, cut), pl.ds(begin + cut, width - cut)]
    marks = [pl.ds(0, cut), pl.ds(cut, width - cut)]

    def order(half):
        return [1 << ((half + s) % bits) for s in range(bits)]

    def send_half(t, half, s):
        dim_order = order(half)
        bit = dim_order[s]
        before = sum(dim_order[:s])
        span = spans[half]
        for x in range(n_row):
            if not x & before and x & bit:
                at = x ^ bit
                copy = remote(
                    mine_ref.at[t, flip_all(r, x, bits), :, span],
                    row_ref.at[t, slot_of(half, s, at), :, marks[half]],
                    row_send.at[0],
                    row_recv.at[t, half, slot_of(half, s, at)],
                    (d, flip(r, bit), c),
                )
                copy.start()

    def slot_of(half, s, at):
        places = []
        before = 0
        for step, bit in enumerate(order(half)):
            before += bit
            places += [(step, y) for y in range(n_row) if not y & before]
        return places.index((s, at))

    def sum_cols(t, send=True):
        if not direct:
            held[t].wait()
        for i in range(1, n_col):
            ref = col_ref.at[t, i - 1]
            remote(
                ref, ref, col_send.at[0], col_recv.at[t, i - 1], (d, r, c)
            ).wait_recv()
        k = homes[t]

        @pl.loop(0, n_row)
        def _(b):
            total = part_at(c, k)[b] if direct else mine_ref[t, b]
            total = total.astype(jnp.float32)
            for i in range(1, n_col):
                total = total + col_ref[t, i - 1, b].astype(jnp.float32)
            mine_ref[t, b] = total.astype(jnp.bfloat16)

        if send:
            send_first(t)

    def send_first(t):
        for half in range(2):
            send_half(t, half, 0)

    def sum_rows(t, s):
        for half in range(2):
            before = sum(order(half)[: s + 1])
            span = spans[half]
            for y in range(n_row):
                if not y & before:
                    slot = slot_of(half, s, y)
                    ref = row_ref.at[t, slot, :, marks[half]]
                    remote(
                        ref,
                        ref,
                        row_send.at[0],
                        row_recv.at[t, half, slot],
                        (d, r, c),
                    ).wait_recv()
                    b = flip_all(r, y, bits)
                    mine_ref[t, b, :, span] = add_low(mine_ref[t, b, :, span], ref[...])
            if s + 1 < bits:
                send_half(t, half, s + 1)
        if s + 1 == bits:
            deliver(steps[t], homes[t], mine_ref.at[t, r])

    def sum_all(between=None):
        ticks = n_dp + bits + 1
        for tick in range(ticks):
            if tick + 1 == ticks and between is not None:
                between()
            if tick < n_dp:
                sum_cols(tick)
            for s in reversed(range(bits)):
                t = tick - 2 - s
                if 0 <= t < n_dp:
                    sum_rows(t, s)

    return types.SimpleNamespace(
        send_cols=send_cols,
        load_mine=load_mine,
        sum_cols=sum_cols,
        send_first=send_first,
        homes=homes,
        sum_rows=sum_rows,
        sum_all=sum_all,
        sent=sent,
    )


def plan_dp_first(dims, place, mine_ref, homes, begin, scratch):
    n_dp, n_row, n_col = dims
    d, r, c = place
    bits = bits_of(n_row)
    in_ref, acc_ref, row_ref, dp_send, dp_recv, row_send, row_recv = scratch
    wide = acc_ref.shape[-1]
    cut = (wide // LANES + 1) // 2 * LANES
    spans = [pl.ds(0, cut), pl.ds(cut, wide - cut)]
    lanes = pl.ds(begin, wide)
    sent = [
        remote(ref, ref, sem.at[0], dp_recv.at[0], (d, r, c))
        for ref, sem in ((in_ref.at[pl.ds(0, n_dp - 1)], dp_send), (row_ref, row_send))
    ]

    def send_dp(t):
        p = n_dp - 1 - t
        if p:
            copy = remote(
                mine_ref.at[t, :, :, lanes],
                in_ref.at[d],
                dp_send.at[0],
                dp_recv.at[d],
                (homes[t], r, c),
            )
            copy.start()

    def order(half):
        return [1 << ((half + s) % bits) for s in range(bits)]

    def steps(half):
        before = 0
        places = []
        for bit in order(half):
            before += bit
            places.append([y for y in range(n_row) if not y & before])
        return places

    def slot_of(half, s, y):
        return sum(len(step) for step in steps(half)[:s]) + steps(half)[s].index(y)

    def send_half(half, s):
        bit = order(half)[s]
        for y in steps(half)[s]:
            slot = slot_of(half, s, y)
            copy = remote(
                acc_ref.at[flip_all(r, y ^ bit, bits), :, spans[half]],
                row_ref.at[slot, :, spans[half]],
                row_send.at[0],
                row_recv.at[half, slot],
                (d, flip(r, bit), c),
            )
            copy.start()

    def sum_dp():
        for p in range(1, n_dp):
            k = homes[n_dp - 1 - p]
            ref = in_ref.at[k]
            remote(ref, ref, dp_send.at[0], dp_recv.at[k], (d, r, c)).wait_recv()

        @pl.loop(0, n_row)
        def _(b):
            total = mine_ref[n_dp - 1, b, :, lanes].astype(jnp.float32)
            for p in range(1, n_dp):
                total = total + in_ref[homes[n_dp - 1 - p], b].astype(jnp.float32)
            acc_ref[b] = total.astype(jnp.bfloat16)

        for half in range(2):
            send_half(half, 0)

    def sum_rows(s):
        for half in range(2):
            for y in steps(half)[s]:
                slot = slot_of(half, s, y)
                ref = row_ref.at[slot, :, spans[half]]
                remote(
                    ref, ref, row_send.at[0], row_recv.at[half, slot], (d, r, c)
                ).wait_recv()
                b = flip_all(r, y, bits)
                acc_ref[b, :, spans[half]] = add_low(acc_ref[b, :, spans[half]], ref[...])
            if s + 1 < bits:
                send_half(half, s + 1)

    return types.SimpleNamespace(
        send_dp=send_dp, sum_dp=sum_dp, sum_rows=sum_rows, total=lambda: acc_ref[r], sent=sent
    )


def dp_first_scratch(dims, rows, width):
    n_dp, n_row, n_col = dims
    dma = pltpu.SemaphoreType.DMA
    low = jnp.bfloat16
    return [
        pltpu.VMEM((n_dp, n_row, rows, width), low),
        pltpu.VMEM((n_row, rows, width), low),
        pltpu.VMEM((max(1, n_row - 1), rows, width), low),
        dma((1,)),
        dma((n_dp,)),
        dma((1,)),
        dma((2, max(1, n_row - 1))),
    ]


def reduce_blocks(dims, place, part_ref, bufs, sems, deliver):
    plan = plan_reduce(dims, place, lambda col, k: part_ref.at[col, k], bufs, sems, deliver)
    for t in range(dims[0]):
        plan.send_cols(t)
    plan.load_mine()
    plan.sum_all()
    return plan.sent


def reduce_scratch(dims, rows, width, copied=True, lanes=None):
    n_dp, n_row, n_col = dims
    dma = pltpu.SemaphoreType.DMA
    low = jnp.bfloat16
    return [
        pltpu.VMEM((n_dp, n_row, rows, width), low),
        pltpu.VMEM((n_dp, max(1, n_col - 1), n_row, rows, width), low),
        pltpu.VMEM((n_dp, max(1, n_row - 1), rows, lanes or width), low),
        dma((n_dp if copied else 1,)),
        dma((1,)),
        dma((n_dp, max(1, n_col - 1))),
        dma((1,)),
        dma((n_dp, 2, max(1, n_row - 1))),
    ]


def token_reduce_kernel(dims, part_ref, out_ref, *scratch):
    n_dp, n_row, n_col = dims
    place = axis_place()
    d, r, c = place
    dp_send, dp_recv, own_sem = scratch[8:]
    greet(True, dims, place)
    late = []

    def deliver(p, k, block):
        if p == 0:
            keep = pltpu.make_async_copy(block, out_ref.at[d], own_sem)
            keep.start()
            late.append(keep.wait)
        else:
            copy = remote(block, out_ref.at[d], dp_send.at[p], dp_recv.at[d], (k, r, c))
            copy.start()
            late.append(copy.wait_send)

    sent = reduce_blocks(dims, place, part_ref, scratch[:3], scratch[3:8], deliver)
    for p in range(1, n_dp):
        k = dp_order(d, p, n_dp)
        ref = out_ref.at[k]
        remote(ref, ref, dp_send.at[p], dp_recv.at[k], (d, r, c)).wait_recv()
    for copy in sent:
        copy.wait_send()
    for wait in late:
        wait()


def token_reduce(parts, dims):
    n_dp = dims[0]
    slots, width = parts.shape[3:]
    dma = pltpu.SemaphoreType.DMA
    return pl.pallas_call(
        functools.partial(token_reduce_kernel, dims),
        out_shape=jax.ShapeDtypeStruct((n_dp, slots, width), jnp.bfloat16),
        in_specs=[pl.BlockSpec(memory_space=pl.ANY)],
        out_specs=pl.BlockSpec(memory_space=pl.ANY),
        scratch_shapes=[*reduce_scratch(dims, slots, width), dma((n_dp,)), dma((n_dp,)), dma],
        compiler_params=pltpu.CompilerParams(
            collective_id=3, has_side_effects=True, vmem_limit_bytes=VMEM_BYTES
        ),
        name="token_reduce",
    )(parts)


def param_reduce_kernel(dims, part_ref, out_ref, *scratch):
    n_dp, n_row, n_col = dims
    place = axis_place()
    d, r, c = place
    dp_send, dp_recv, dp_ref, swap_send, swap_recv, swap_ref, sum_ref = scratch[8:]
    rows = out_ref.shape[1]
    greet(True, dims, place)
    late = []
    kept = []

    def deliver(p, k, block):
        if p == 0:
            kept.append(block)
        else:
            copy = remote(block, dp_ref.at[d], dp_send.at[p], dp_recv.at[d], (k, r, c))
            copy.start()
            late.append(copy)

    sent = reduce_blocks(dims, place, part_ref, scratch[:3], scratch[3:8], deliver)
    total = kept[0][...].astype(jnp.float32)
    for p in range(1, n_dp):
        k = dp_order(d, p, n_dp)
        ref = dp_ref.at[k]
        remote(ref, ref, dp_send.at[p], dp_recv.at[k], (d, r, c)).wait_recv()
        total = total + dp_ref[k].astype(jnp.float32)
    sum_ref[...] = total
    for i in range(n_col):
        swap_ref[i] = sum_ref[i * rows : (i + 1) * rows, :]
    for i in range(1, n_col):
        other = (c + i) % n_col
        copy = remote(
            swap_ref.at[other], out_ref.at[c], swap_send.at[i], swap_recv.at[i], (d, r, other)
        )
        copy.start()
        late.append(copy)
    out_ref[pl.ds(c, 1)] = swap_ref[pl.ds(c, 1)]
    for i in range(1, n_col):
        ref = out_ref.at[(c + n_col - i) % n_col]
        remote(ref, ref, swap_send.at[i], swap_recv.at[i], (d, r, c)).wait_recv()
    for copy in sent:
        copy.wait_send()
    for copy in late:
        copy.wait_send()


def param_reduce(parts, dims):
    n_dp, n_row, n_col = dims
    block_rows, width = parts.shape[3:]
    rows = block_rows // n_col
    dma = pltpu.SemaphoreType.DMA
    return pl.pallas_call(
        functools.partial(param_reduce_kernel, dims),
        out_shape=jax.ShapeDtypeStruct((n_col, rows, width), jnp.float32),
        in_specs=[pl.BlockSpec(memory_space=pl.ANY)],
        out_specs=pl.BlockSpec(memory_space=pltpu.VMEM),
        scratch_shapes=[
            *reduce_scratch(dims, block_rows, width),
            dma((n_dp,)),
            dma((n_dp,)),
            pltpu.VMEM((n_dp, block_rows, width), jnp.bfloat16),
            dma((n_col,)),
            dma((n_col,)),
            pltpu.VMEM((n_col, rows, width), jnp.float32),
            pltpu.VMEM((block_rows, width), jnp.float32),
        ],
        compiler_params=pltpu.CompilerParams(
            collective_id=4, has_side_effects=True, vmem_limit_bytes=VMEM_BYTES
        ),
        name="param_reduce",
    )(parts)


def column(matrix, index):
    return matrix[:, index : index + 1]


def token_masks(lengths_ref, rows, seqs):
    down = lax.broadcasted_iota(jnp.int32, (rows, 1), 0)
    across = lax.broadcasted_iota(jnp.int32, (1, rows), 1)
    end = 0
    doc_down = jnp.zeros((rows, 1), jnp.int32)
    doc_across = jnp.zeros((1, rows), jnp.int32)
    for i in range(seqs):
        end = end + lengths_ref[0, i]
        doc_down = doc_down + (down >= end).astype(jnp.int32)
        doc_across = doc_across + (across >= end).astype(jnp.int32)
    valid = (doc_down < seqs).astype(jnp.float32)
    allowed = (doc_down == doc_across) & (down >= across)
    return valid, allowed


def row_vectors_of(small, first):
    shape = (8, small.shape[1])
    pick = lax.broadcasted_iota(jnp.int32, shape, 1) == first + lax.broadcasted_iota(
        jnp.int32, shape, 0
    )
    return dot(pick.astype(jnp.bfloat16), small, NT)


def half_mask(rows, half):
    return lax.broadcasted_iota(jnp.int32, (rows, LANES), 1) // HEAD == half


def attention_forward(qkv_ref, probs_ref, mixed_ref, allowed, first, last):
    rows = qkv_ref.shape[0]
    low = jnp.bfloat16

    @pl.loop(first, last, unroll=3)
    def _(pair):
        def cols(base):
            return pl.ds(pl.multiple_of(base + pair * LANES, LANES), LANES)

        queries = qkv_ref[:, cols(0)]
        key_heads = qkv_ref[:, cols(D)]
        values = qkv_ref[:, cols(2 * D)]
        mixed = jnp.zeros((rows, LANES), jnp.float32)
        for half in range(LANES // HEAD):
            mask = half_mask(rows, half)
            scores = dot(jnp.where(mask, queries, 0), key_heads, NT) * HEAD ** (-0.5)
            scores = jnp.where(allowed, scores, -1e30)
            top_score = jnp.max(scores, axis=-1, keepdims=True)
            exp_scores = jnp.exp(scores - top_score)
            probs = exp_scores / jnp.sum(exp_scores, axis=-1, keepdims=True)
            probs_ref[pair * (LANES // HEAD) + half] = probs
            mixed = mixed + dot(probs.astype(low), jnp.where(mask, values, 0))
        mixed_ref[:, cols(0)] = mixed.astype(low)


def two_way(first, second):
    top = jnp.maximum(first, second)
    exp_first = jnp.exp(first - top)
    exp_second = jnp.exp(second - top)
    total = exp_first + exp_second
    return exp_first / total, exp_second / total


def attention_backward(qkv_ref, probs_ref, grad_mixed_ref, grad_qkv_ref):
    rows = qkv_ref.shape[0]
    low = jnp.bfloat16

    @pl.loop(0, HEADS * HEAD // LANES, unroll=2)
    def _(pair):
        def cols(base):
            return pl.ds(pl.multiple_of(base + pair * LANES, LANES), LANES)

        queries = qkv_ref[:, cols(0)]
        key_heads = qkv_ref[:, cols(D)]
        values = qkv_ref[:, cols(2 * D)]
        grad_mixed = grad_mixed_ref[:, cols(0)]
        grad_queries = jnp.zeros((rows, LANES), jnp.float32)
        grad_keys = jnp.zeros((rows, LANES), jnp.float32)
        grad_values = jnp.zeros((rows, LANES), jnp.float32)
        for half in range(LANES // HEAD):
            mask = half_mask(rows, half)
            probs = probs_ref[pair * (LANES // HEAD) + half]
            grad_part = jnp.where(mask, grad_mixed, 0)
            grad_values = grad_values + dot(probs.astype(low), grad_part, TN)
            grad_probs = dot(grad_part, values, NT)
            grad_scores = probs * (
                grad_probs - jnp.sum(probs * grad_probs, axis=-1, keepdims=True)
            )
            grad_scores = grad_scores.astype(low)
            grad_queries = grad_queries + dot(grad_scores, jnp.where(mask, key_heads, 0))
            grad_keys = grad_keys + dot(grad_scores, jnp.where(mask, queries, 0), TN)
        grad_qkv_ref[:, cols(0)] = (grad_queries * HEAD ** (-0.5)).astype(low)
        grad_qkv_ref[:, cols(D)] = (grad_keys * HEAD ** (-0.5)).astype(low)
        grad_qkv_ref[:, cols(2 * D)] = grad_values.astype(low)


def layer_kernel(sizes, *refs):
    dims, num_ffn, wide_qkv, wide_out, route_cols, chunks = sizes
    n_dp, n_row, n_col = dims
    low = jnp.bfloat16
    (
        lengths_ref,
        routes_ref,
        prev_ref,
        tokens_ref,
        cotangent_ref,
        w_qkv_ref,
        w_out_ref,
        route_w_ref,
        gains_ref,
        const_ref,
        weight_gu,
        weight_down,
        left_root_gu,
        right_root_down,
        right_root_gu,
        left_root_down,
        result_out,
        grad_tokens_out,
        summed_ref,
        right_sum_out,
        left_sum_out,
        step_out,
        block_out,
        shard_ref,
        turn_ref,
        swap_ref,
        block_ref,
        whole_ref,
        pack_ref,
        expert_ref,
        stage_ref,
        arrived_ref,
        hidden_ref,
        pre_ref,
        qkv_ref,
        probs_ref,
        mixed_ref,
        first_ref,
        came_ref,
        grad_attn_ref,
        grad_mixed_ref,
        grad_qkv_ref,
        part_ref,
        dp_ref,
        end_ref,
        sum_ref,
        gathered_ref,
        root_ref,
        tile_ref,
        half_step_ref,
        lhs_ref,
        right_sum_ref,
        left_sum_ref,
        left_low_ref,
        step_ref,
        result_ref,
        grad_tokens_ref,
        swap_send,
        swap_recv,
        load_sem,
        expert_send,
        expert_recv,
        root_sem,
        tile_sem,
        store_sem,
        done_sem,
        came_send,
        came_recv,
        dp_send,
        dp_recv,
        end_send,
        end_recv,
        *more,
    ) = refs
    halves = n_row == 4
    param_sems, out_sems, token_sems, gather_sems = (more[7 * n : 7 * n + 7] for n in range(4))
    token_scratch, param_scratch, first_scratch = more[28:36], more[36:44], more[44:]
    place = axis_place()
    d, r, c = place
    rows = shard_ref.shape[1]
    depth, slice_wide = pack_ref.shape[2:]
    held, tile = tile_ref.shape[:2]
    wide_col = n_row * slice_wide
    greeted = greet(True, dims, place, all_rows=True, wait=False)
    staged = []
    loads = []
    for m, src in enumerate([weight_gu.at[:, 0], weight_gu.at[:, 1], weight_down]):
        begin = m % 2 * wide_col
        staged.append((m // 2, begin))
        dst = tile_ref.at[m // 2, pl.ds(0, depth), pl.ds(begin, wide_col)]
        copy = pltpu.make_async_copy(src, dst, load_sem.at[m])
        copy.start()
        loads.append(copy)
    roots = [left_root_gu.at[0], left_root_gu.at[1], right_root_down]
    root_loads = []
    for m in range(3):
        copy = pltpu.make_async_copy(roots[m], root_ref.at[m], root_sem.at[m])
        copy.start()
        root_loads.append(copy)
    turn_ref[...] = jnp.zeros_like(turn_ref)
    out_at = wide_qkv + LANES
    at = 0
    for ref in (route_w_ref, gains_ref, const_ref):
        turn_ref[at : at + ref.shape[0], : ref.shape[1]] = ref[...]
        at += ref.shape[0]
    small_shard = turn_ref[...].T[:rows]
    for i in range(n_col):
        shard_ref[i, :, :wide_qkv] = w_qkv_ref[:, i * wide_qkv : (i + 1) * wide_qkv]
        shard_ref[i, :, wide_qkv:out_at] = small_shard
        shard_ref[i, :, out_at:] = w_out_ref[:, i * wide_out : (i + 1) * wide_out]
    pl.semaphore_wait(pltpu.get_barrier_semaphore(), greeted)

    copies = []
    for i in range(1, n_col):
        other = (c + i) % n_col
        copy = remote(
            shard_ref.at[other], swap_ref.at[c], swap_send.at[i], swap_recv.at[i], (d, r, other)
        )
        copy.start()
        copies.append(copy)
    swap_ref[pl.ds(c, 1)] = shard_ref[pl.ds(c, 1)]
    for copy in copies:
        copy.wait()
    for i in range(n_col):
        block_ref[i * rows : (i + 1) * rows, :] = swap_ref[i]
    whole_ref[c, d, r] = block_ref[...].astype(low)

    def plan_params(begin, wide, sems):
        span = pl.ds(begin, wide)

        def slot(col, j, b):
            k = j[1] if isinstance(j, tuple) else dp_order(d, j, n_dp)
            return whole_ref.at[col, k, b, :, span]

        own = whole_ref.at[c, d, r, :, span]
        totals = (
            whole_ref.at[0, pl.ds(0, n_dp - 1), 0, :, span],
            whole_ref.at[0, :, pl.ds(0, n_row - 1), :, span],
            whole_ref.at[pl.ds(0, n_col - 1), :, :, :, span],
        )
        return plan_spread(
            dims, place, n_dp, True, None, lambda k: own, slot, sems, halves, totals
        )

    qkv_plan = plan_params(0, out_at, param_sems)
    out_plan = plan_params(out_at, wide_out, out_sems)
    waits = []

    bits = bits_of(n_row)
    near = [1 << dim for dim in range(bits)]

    def pack_experts():
        for copy in loads:
            copy.wait()
        for m, (slot, begin) in enumerate(staged):
            for b in range(n_row):
                at = begin + b * slice_wide
                pack_ref[b, m] = tile_ref[slot, :depth, at : at + slice_wide].astype(low)
        expert_ref[:, pl.ds(pl.multiple_of(r * depth, 16), depth)] = pack_ref[r]

    def send_experts(masks):
        home = pl.ds(pl.multiple_of(r * depth, 16), depth)
        for x in masks:
            other = flip_all(r, x, bits)
            copy = remote(
                pack_ref.at[other],
                expert_ref.at[:, home],
                expert_send.at[x - 1],
                expert_recv.at[x - 1],
                (d, other, c),
            )
            copy.start()
            waits.append(copy.wait_send)

    for plan in (qkv_plan, out_plan):
        plan.start(0)
        plan.send_dp()
    pack_experts()
    send_experts(near)
    for j in range(1, n_dp):
        qkv_plan.start(j)
        qkv_plan.pass_on(j - 1)
    for j in range(1, n_dp):
        out_plan.start(j)
    qkv_plan.pass_on(n_dp - 1)
    for j in range(n_dp):
        out_plan.pass_on(j)
    send_experts([x for x in range(1, n_row) if x not in near])
    for j in range(n_dp):
        qkv_plan.last_arrivals(j)
    for j in range(n_dp):
        qkv_plan.wait_cols(j)

    def whole_cols(col, begin, wide):
        return whole_ref[col, :, :, :, begin : begin + wide].reshape(D, wide)

    total = tokens_ref.shape[0]
    valid, allowed = token_masks(lengths_ref, total, lengths_ref.shape[1])
    small = whole_cols(0, wide_qkv, LANES)
    vectors = row_vectors_of(small, route_cols)
    inputs = tokens_ref[...].astype(jnp.float32)
    scale_one = lax.rsqrt(jnp.mean(inputs * inputs, axis=-1, keepdims=True) + NORM_EPS)
    h_one = (inputs * scale_one * vectors[0:1]).astype(low)
    for i in range(n_col):
        qkv_ref[:, i * wide_qkv : (i + 1) * wide_qkv] = dot(h_one, whole_cols(i, 0, wide_qkv)).astype(
            low
        )
    pairs = HEADS * HEAD // LANES
    attention_forward(qkv_ref, probs_ref, mixed_ref, allowed, 0, pairs // 2)
    for j in range(n_dp):
        out_plan.last_arrivals(j)
    attention_forward(qkv_ref, probs_ref, mixed_ref, allowed, pairs // 2, pairs)
    for j in range(n_dp):
        out_plan.wait_cols(j)
    waits += qkv_plan.sends() + out_plan.sends()
    for i in range(n_col):
        cols = slice(i * wide_out, (i + 1) * wide_out)
        attn_out = dot(mixed_ref[...], whole_cols(i, out_at, wide_out))
        first_ref[:, cols] = tokens_ref[:, cols].astype(jnp.float32) + valid * attn_out
    first_sum = first_ref[...]
    scale_two = lax.rsqrt(jnp.mean(first_sum * first_sum, axis=-1, keepdims=True) + NORM_EPS)
    h_two = (first_sum * scale_two * vectors[1:2]).astype(low)
    experts = prev_ref.shape[0]
    turn_ref[...] = jnp.zeros_like(turn_ref)
    turn_ref[:experts] = prev_ref[...]
    turn_ref[experts : experts + 2] = routes_ref[...].astype(jnp.float32)
    turned = turn_ref[...].T
    logits_all = dot(h_two, small)
    lane = lax.broadcasted_iota(jnp.int32, (total, LANES), 1)
    logits = logits_all + jnp.where(lane < experts, turned, 0.0)
    route_first = column(turned, experts).astype(jnp.int32)
    route_second = column(turned, experts + 1).astype(jnp.int32)
    pick_first = (lane == route_first).astype(jnp.float32)
    pick_second = (lane == route_second).astype(jnp.float32)
    gates = two_way(
        jnp.sum(pick_first * logits, axis=-1, keepdims=True),
        jnp.sum(pick_second * logits, axis=-1, keepdims=True),
    )
    mix_base = num_ffn + 4
    mixes = []
    for i in range(2):
        mixes += two_way(
            column(logits_all, mix_base + 2 * i), column(logits_all, mix_base + 2 * i + 1)
        )
    before = lax.broadcasted_iota(jnp.int32, (total, total), 0) > lax.broadcasted_iota(
        jnp.int32, (total, total), 1
    )
    earlier = dot(before.astype(low), (pick_first + pick_second).astype(low))
    in_slots = []
    for route, pick in ((route_first, pick_first), (route_second, pick_second)):
        slot_index = jnp.sum(earlier * pick, axis=-1, keepdims=True)
        where_in = (route * CAP).astype(jnp.float32) + slot_index
        in_slots.append(jnp.where(route < num_ffn, where_in, -1.0))
    slots = num_ffn * CAP
    slot_lane = lax.broadcasted_iota(jnp.int32, (total, slots), 1).astype(jnp.float32)
    places = [(slot_lane == where_in).astype(low) for where_in in in_slots]
    grad_y = cotangent_ref[...].astype(jnp.float32) * valid
    sent = dot(places[0] + places[1], h_two, TN).astype(low)
    made = dot(places[0], (gates[0] * grad_y).astype(low), TN) + dot(
        places[1], (gates[1] * grad_y).astype(low), TN
    )
    stage_ref[:, :, :D] = sent.reshape(num_ffn, CAP, D)
    stage_ref[:, :, D:] = made.astype(low).reshape(num_ffn, CAP, D)

    def token_slot(col, j, b):
        k = j[1] if isinstance(j, tuple) else dp_order(d, j, n_dp)
        return arrived_ref.at[k, col, b]

    arrived_ref[d, c, r] = stage_ref[d]
    rows_plan = plan_spread(
        dims,
        place,
        n_dp,
        True,
        None,
        lambda k: stage_ref.at[k],
        token_slot,
        token_sems,
        halves,
        (
            arrived_ref.at[pl.ds(0, n_dp - 1), 0, 0],
            arrived_ref.at[:, 0, pl.ds(0, n_row - 1)],
            arrived_ref.at[:, pl.ds(0, n_col - 1)],
        ),
    )
    rows_plan.start(0)
    rows_plan.send_dp()
    rows_plan.start(1)
    rows_plan.pass_on(0)

    wides = [right_root_gu.at[0], right_root_gu.at[1], left_root_down]
    tiles = left_root_down.shape[0] // tile
    tile_loads = []

    def load_tile(n):
        if n < 3 * tiles:
            copy = pltpu.make_async_copy(
                wides[n // tiles].at[pl.ds(n % tiles * tile, tile)],
                tile_ref.at[n % held],
                tile_sem.at[n],
            )
            copy.start()
            tile_loads.append(copy)

    for n in range(held):
        load_tile(n)

    def token_back(p, k, block):
        if p == 0:
            came_ref[d] = block[...]
        else:
            copy = remote(block, came_ref.at[d], came_send.at[p - 1], came_recv.at[d], (k, r, c))
            copy.start()
            waits.append(copy.wait_send)

    tokens_plan = plan_reduce(
        dims,
        place,
        lambda col, k: part_ref.at[col, k, :, pl.ds(0, CAP), pl.ds(0, 2 * D)],
        token_scratch[:3],
        token_scratch[3:],
        token_back,
        direct=True,
        far_first=False,
    )

    tall = n_col * n_row * CAP

    def expert_rows(p):
        k = dp_order(d, p, n_dp)
        some = arrived_ref[k].reshape(tall, 2 * D)
        rows_in = some[:, :D]
        grads_in = some[:, D:]
        gate_part = dot(rows_in, expert_ref[0])
        up_part = dot(rows_in, expert_ref[1])
        grad_hidden = dot(grads_in, expert_ref[2])
        sigma = jax.nn.sigmoid(gate_part)
        silu = gate_part * sigma
        hidden = (silu * up_part).astype(low)
        grad_gate = (grad_hidden * up_part * sigma * (1.0 + gate_part * (1.0 - sigma))).astype(low)
        grad_up = (grad_hidden * silu).astype(low)
        hidden_ref[k] = hidden
        pre_ref[k, :, :slice_wide] = grad_gate
        pre_ref[k, :, slice_wide:] = grad_up
        made_rows = dot(hidden, expert_ref[2], NT).astype(low)
        grad_rows = (dot(grad_gate, expert_ref[0], NT) + dot(grad_up, expert_ref[1], NT)).astype(low)
        for col in range(n_col):
            span = slice(col * n_row * CAP, (col + 1) * n_row * CAP)
            part_ref[col, k, :, :CAP, :D] = made_rows[span].reshape(n_row, CAP, D)
            part_ref[col, k, :, :CAP, D : 2 * D] = grad_rows[span].reshape(n_row, CAP, D)
        tokens_plan.send_cols(p)

    def chunk_in(p):
        if p + 2 < n_dp:
            rows_plan.start(p + 2)
        if p + 1 < n_dp:
            rows_plan.pass_on(p + 1)
        if p == 0:
            for x in range(1, n_row):
                home = pl.ds(pl.multiple_of(flip_all(r, x, bits) * depth, 16), depth)
                ref = expert_ref.at[:, home]
                remote(
                    ref, ref, expert_send.at[x - 1], expert_recv.at[x - 1], (d, r, c)
                ).wait_recv()
        rows_plan.last_arrivals(p)
        rows_plan.wait_cols(p)
        expert_rows(p)

    def sums_before(t):
        for s in range(bits):
            if 0 <= t - 1 - s:
                tokens_plan.sum_rows(t - 1 - s, s)

    chunk_in(0)
    for t in range(n_dp - 1):
        if t < n_dp - 2:
            chunk_in(t + 1)
        tokens_plan.sum_cols(t)
        sums_before(t)
    if n_dp > 1:
        chunk_in(n_dp - 1)
    tokens_plan.sum_cols(n_dp - 1)
    sums_before(n_dp - 1)
    waits += rows_plan.sends()
    all_count = n_dp * tall
    all_rows = arrived_ref[:, :, :, :, :D].reshape(all_count, D)
    all_grads = arrived_ref[:, :, :, :, D:].reshape(all_count, D)
    for m in range(2):
        gathered_ref[c * n_row + r, m * D : (m + 1) * D] = dot(
            all_rows,
            pre_ref[:, :, m * slice_wide : (m + 1) * slice_wide].reshape(all_count, slice_wide),
            TN,
        ).astype(low)
    gathered_ref[c * n_row + r, 2 * D :] = dot(
        all_grads, hidden_ref[...].reshape(all_count, slice_wide), TN
    ).astype(low)
    tall = gathered_ref.shape[1] // chunks
    gather = plan_spread(
        dims,
        place,
        chunks,
        False,
        None,
        None,
        lambda col, j, b: gathered_ref.at[col * n_row + b, pl.ds(j * tall, tall)],
        gather_sems,
        halves,
        (
            None,
            gathered_ref.at[pl.ds(0, n_row - 1)],
            gathered_ref.at[pl.ds(0, (n_col - 1) * n_row)],
        ),
    )
    gather.start(0)
    for t in range(n_dp, n_dp + bits):
        for s in range(bits):
            if 0 <= t - 1 - s < n_dp:
                tokens_plan.sum_rows(t - 1 - s, s)
        if t == n_dp + bits - 2:
            for j in range(1, chunks):
                gather.start(j)

    gain_one, gain_two = vectors[0:1], vectors[1:2]
    const_rows = [vectors[2:3], vectors[3:4]]
    mixes = [mixes[:2], mixes[2:]]
    routes = [route_first, route_second]
    picks = [pick_first, pick_second]
    cotangent = cotangent_ref[...].astype(jnp.float32)
    grad_y = cotangent * valid
    grad_y_low = grad_y.astype(low)
    first_sum = first_ref[...]
    scale_two = lax.rsqrt(jnp.mean(first_sum * first_sum, axis=-1, keepdims=True) + NORM_EPS)
    normed_two = first_sum * scale_two
    h_two = normed_two * gain_two
    h_two_low = h_two.astype(low)
    const_sel = [
        [(route == num_ffn + 2 + n).astype(jnp.float32) for n in range(2)] for route in routes
    ]
    for p in range(1, n_dp):
        k = dp_order(d, p, n_dp)
        ref = came_ref.at[k]
        remote(ref, ref, came_send.at[p - 1], came_recv.at[k], (d, r, c)).wait_recv()
    expert_out = came_ref[:, :, :D].reshape(slots, D)
    grad_sent = came_ref[:, :, D:].reshape(slots, D)
    moe_out = jnp.zeros_like(first_sum)
    grad_gates = []
    own_weight = jnp.zeros((total, 1), jnp.float32)
    for n in range(2):
        own = (routes[n] == num_ffn + 1).astype(jnp.float32)
        for i in range(2):
            own = own + const_sel[n][i] * mixes[i][0]
        output = dot(places[n], expert_out) + own * h_two
        for i in range(2):
            output = output + const_sel[n][i] * mixes[i][1] * const_rows[i]
        moe_out = moe_out + gates[n] * output
        grad_gates.append(jnp.sum(grad_y * output, axis=-1, keepdims=True))
        own_weight = own_weight + gates[n] * own
    result_ref[...] = (first_sum + valid * moe_out).astype(low)
    copy = pltpu.make_async_copy(result_ref, result_out, done_sem.at[0])
    copy.start()
    waits.append(copy.wait)
    mean_gate = gates[0] * grad_gates[0] + gates[1] * grad_gates[1]
    grad_logits = sum(gates[n] * (grad_gates[n] - mean_gate) * picks[n] for n in range(2))
    grad_own = jnp.sum(grad_y * h_two, axis=-1, keepdims=True)
    const_lanes = jnp.zeros((total, LANES), jnp.float32)
    for i in range(2):
        weight = const_sel[0][i] * gates[0] + const_sel[1][i] * gates[1]
        mix_grads = [
            weight * grad_own,
            weight * jnp.sum(grad_y * const_rows[i], axis=-1, keepdims=True),
        ]
        mean_mix = mixes[i][0] * mix_grads[0] + mixes[i][1] * mix_grads[1]
        for n in range(2):
            grad_mix = mixes[i][n] * (mix_grads[n] - mean_mix)
            grad_logits = jnp.where(lane == num_ffn + 4 + 2 * i + n, grad_mix, grad_logits)
        const_lanes = jnp.where(lane == route_cols + 2 + i, weight * mixes[i][1], const_lanes)
    grad_logits = grad_logits.astype(low)

    grad_h_two = (
        dot(grad_logits, small, NT) + dot(places[0] + places[1], grad_sent) + own_weight * grad_y
    )
    grad_normed = grad_h_two * gain_two
    inner_mean = jnp.mean(grad_normed * normed_two, axis=-1, keepdims=True)
    grad_first = scale_two * (grad_normed - normed_two * inner_mean) + cotangent
    grad_tokens_ref[...] = grad_first
    grad_attn_ref[...] = (valid * grad_first).astype(low)
    grad_small = (
        dot(h_two_low, grad_logits, TN)
        + dot(grad_y_low, const_lanes.astype(low), TN)
        + dot((grad_h_two * normed_two).astype(low), (lane == route_cols + 1).astype(low), TN)
    )
    grad_mixed = jnp.zeros((total, D), jnp.float32)
    for i in range(n_col):
        grad_mixed = grad_mixed + dot(
            grad_attn_ref[:, i * wide_out : (i + 1) * wide_out],
            whole_cols(i, out_at, wide_out),
            NT,
        )
    grad_mixed_ref[...] = grad_mixed.astype(low)
    attention_backward(qkv_ref, probs_ref, grad_mixed_ref, grad_qkv_ref)
    grad_h_one = jnp.zeros((total, D), jnp.float32)
    for i in range(n_col):
        grad_h_one = grad_h_one + dot(
            grad_qkv_ref[:, i * wide_qkv : (i + 1) * wide_qkv], whole_cols(i, 0, wide_qkv), NT
        )
    inputs = tokens_ref[...].astype(jnp.float32)
    scale_one = lax.rsqrt(jnp.mean(inputs * inputs, axis=-1, keepdims=True) + NORM_EPS)
    normed_one = inputs * scale_one
    h_one = (normed_one * gain_one).astype(low)
    grad_normed = grad_h_one * gain_one
    inner_mean = jnp.mean(grad_normed * normed_one, axis=-1, keepdims=True)
    grad_tokens_ref[...] += scale_one * (grad_normed - normed_one * inner_mean)
    copy = pltpu.make_async_copy(grad_tokens_ref, grad_tokens_out, done_sem.at[1])
    copy.start()
    waits.append(copy.wait)
    grad_small = grad_small + dot(
        (grad_h_one * normed_one).astype(low), (lane == route_cols).astype(low), TN
    )

    kept = []
    split = dp_ref.shape[2]

    def param_back(p, k, block):
        if p == 0:
            kept.append(block)
        else:
            block = block.at[:, pl.ds(0, split)]
            copy = remote(block, dp_ref.at[d], dp_send.at[p - 1], dp_recv.at[d], (k, r, c))
            copy.start()
            waits.append(copy.wait_send)

    params_plan = plan_reduce(
        dims,
        place,
        lambda col, k: part_ref.at[col, k],
        param_scratch[:3],
        param_scratch[3:],
        param_back,
        direct=True,
        lanes=(0, split),
    )
    first_plan = plan_dp_first(dims, place, param_scratch[0], params_plan.homes, split, first_scratch)
    finish([copy.wait_send for copy in tokens_plan.sent])
    blocked = part_ref.shape[1:4]
    for i in [*range(1, n_col), 0]:
        col = (c + i) % n_col
        qkv_cols = pl.ds(pl.multiple_of(col * wide_qkv, LANES), wide_qkv)
        out_cols = pl.ds(pl.multiple_of(col * wide_out, LANES), wide_out)
        part_ref[col, :, :, :, :wide_qkv] = (
            dot(h_one, grad_qkv_ref[:, qkv_cols], TN).astype(low).reshape(*blocked, wide_qkv)
        )
        part_ref[col, :, :, :, out_at:] = (
            dot(mixed_ref[...], grad_attn_ref[:, out_cols], TN)
            .astype(low)
            .reshape(*blocked, wide_out)
        )
        part_ref[col, :, :, :, wide_qkv:out_at] = grad_small.astype(low).reshape(*blocked, LANES)
        if i == n_col - 1:
            for t in range(n_dp):
                params_plan.send_cols(t)
    gather.pass_on(0)
    gather.pass_on(1)
    for t in range(n_dp):
        params_plan.sum_cols(t, False)
        first_plan.send_dp(t)
    for j in range(2, chunks * 2 // 3):
        gather.pass_on(j)
    for t in range(n_dp):
        params_plan.send_first(t)
    for j in range(chunks * 2 // 3, chunks):
        gather.pass_on(j)

    owner = r * n_col + c
    right_rows = right_sum_ref.shape[1]
    left_rows = left_sum_ref.shape[0]
    stores = []

    def store(m, kind, src, dst):
        copy = pltpu.make_async_copy(src, dst, store_sem.at[m, kind])
        copy.start()
        stores.append(copy)

    def shampoo_products(m):
        for j in range(m * chunks // 3, (m + 1) * chunks // 3):
            gather.last_arrivals(j)
        for j in range(m * chunks // 3, (m + 1) * chunks // 3):
            gather.wait_cols(j)
        span = pl.ds(m * D, D)
        home = pl.ds(pl.multiple_of(m * D + r * depth, 16), depth)
        for b in range(n_row):
            store(m, 3 + b, gathered_ref.at[c * n_row + b, home], block_out.at[m, b])
        root_loads[m].wait()
        lhs_ref[:right_rows] = gathered_ref[owner, span].T
        lhs_ref[right_rows:] = root_ref[m].astype(low)
        left_sum_ref[...] = jnp.zeros_like(left_sum_ref)

        @pl.loop(0, n_row * n_col, unroll=2)
        def _(q):
            cols = pl.ds(pl.multiple_of(q * slice_wide, slice_wide), slice_wide)
            block = gathered_ref[q, span]
            made = dot(lhs_ref[...], block)
            right_sum_ref[m, :, cols] = (0.5 * made[:right_rows]).astype(low)
            half_step_ref[:, cols] = made[right_rows:].astype(low)
            some = pl.ds(pl.multiple_of(m * D + owner * left_rows, 16), left_rows)
            left_sum_ref[...] += dot(gathered_ref[q, some], block, NT)

        left_low_ref[m] = (0.5 * left_sum_ref[...]).astype(low)
        store(m, 0, right_sum_ref.at[m], right_sum_out.at[m])
        store(m, 1, left_low_ref.at[m], left_sum_out.at[m])
        for t in range(tiles):
            n = m * tiles + t
            tile_loads[n].wait()
            step = dot(half_step_ref[...], tile_ref[n % held].astype(low), NT)
            step_ref[m, :, t * tile : (t + 1) * tile] = (SHAMPOO_RATE * step).astype(low)
            load_tile(n + held)
        store(m, 2, step_ref.at[m], step_out.at[m])

    shampoo_products(0)
    shampoo_products(1)
    for t in range(n_dp):
        params_plan.sum_rows(t, 0)
    first_plan.sum_dp()
    shampoo_products(2)
    for s in range(1, bits):
        for t in range(n_dp):
            params_plan.sum_rows(t, s)
    for s in range(bits):
        first_plan.sum_rows(s)
    sums = kept[0][:, :split].astype(jnp.float32)
    for p in range(1, n_dp):
        k = dp_order(d, p, n_dp)
        ref = dp_ref.at[k]
        remote(ref, ref, dp_send.at[p - 1], dp_recv.at[k], (d, r, c)).wait_recv()
        sums = sums + dp_ref[k].astype(jnp.float32)
    sum_ref[:, :split] = sums
    sum_ref[:, split:] = first_plan.total().astype(jnp.float32)
    for i in range(n_col):
        end_ref[i] = sum_ref[i * rows : (i + 1) * rows, :]
    for i in range(1, n_col):
        other = (c + i) % n_col
        copy = remote(
            end_ref.at[other], summed_ref.at[c], end_send.at[i], end_recv.at[i], (d, r, other)
        )
        copy.start()
        waits.append(copy.wait_send)
    summed_ref[pl.ds(c, 1)] = end_ref[pl.ds(c, 1)]
    for i in range(1, n_col):
        ref = summed_ref.at[(c + n_col - i) % n_col]
        remote(ref, ref, end_send.at[i], end_recv.at[i], (d, r, c)).wait_recv()
    waits += gather.sends()
    waits += [copy.wait for copy in stores]
    finish([copy.wait_send for copy in params_plan.sent + first_plan.sent])
    finish(waits)


def layer(
    lengths,
    routes,
    prev_logits,
    tokens,
    cotangent,
    w_qkv,
    w_out,
    route_w,
    gains,
    const_vec,
    weight_gu,
    weight_down,
    left_root_gu,
    right_root_down,
    right_root_gu,
    left_root_down,
    dims,
    widths,
):
    n_dp, n_row, n_col = dims
    low = jnp.bfloat16
    f32 = jnp.float32
    total = tokens.shape[0]
    rows = w_qkv.shape[0]
    wide = widths[0] + widths[1] + LANES
    num_ffn = prev_logits.shape[0] - 4
    depth, wide_col = weight_down.shape
    slice_wide = wide_col // n_row
    block_rows = n_col * rows
    wide_rows, wide_cols = left_root_down.shape
    right_rows = wide_cols // n_row // n_col
    left_rows = D // n_row // n_col
    tile = 2 * LANES
    split = wide // 2 // LANES * LANES
    chunks = 6
    dma = pltpu.SemaphoreType.DMA
    vmem = pl.BlockSpec(memory_space=pltpu.VMEM)
    hbm = pl.BlockSpec(memory_space=pl.ANY)
    whole = (n_col, n_dp, n_row, block_rows, wide)
    assert depth <= tile and 2 * wide_col <= wide_cols and wide >= 2 * D
    return pl.pallas_call(
        functools.partial(layer_kernel, (dims, num_ffn, *widths, chunks)),
        out_shape=[
            jax.ShapeDtypeStruct((total, D), low),
            jax.ShapeDtypeStruct((total, D), f32),
            jax.ShapeDtypeStruct((n_col, rows, wide), f32),
            jax.ShapeDtypeStruct((3, right_rows, wide_cols), low),
            jax.ShapeDtypeStruct((3, left_rows, D), low),
            jax.ShapeDtypeStruct((3, depth, wide_rows), low),
            jax.ShapeDtypeStruct((3, n_row, depth, slice_wide), low),
        ],
        in_specs=[pl.BlockSpec(memory_space=pltpu.SMEM)] + [vmem] * 9 + [hbm] * 6,
        out_specs=[hbm, hbm, vmem] + [hbm] * 4,
        scratch_shapes=[
            pltpu.VMEM((n_col, rows, wide), f32),
            pltpu.VMEM((LANES, LANES), f32),
            pltpu.VMEM((n_col, rows, wide), f32),
            pltpu.VMEM((block_rows, wide), f32),
            pltpu.VMEM(whole, low),
            pltpu.VMEM((n_row, 3, depth, slice_wide), low),
            pltpu.VMEM((3, n_row * depth, slice_wide), low),
            pltpu.VMEM((num_ffn, CAP, 2 * D), low),
            pltpu.VMEM((n_dp, n_col, n_row, CAP, 2 * D), low),
            pltpu.VMEM((n_dp, n_col * n_row * CAP, slice_wide), low),
            pltpu.VMEM((n_dp, n_col * n_row * CAP, 2 * slice_wide), low),
            pltpu.VMEM((total, 3 * D), low),
            pltpu.VMEM((HEADS, total, total), f32),
            pltpu.VMEM((total, D), low),
            pltpu.VMEM((total, D), f32),
            pltpu.VMEM((n_dp, CAP, 2 * D), low),
            pltpu.VMEM((total, D), low),
            pltpu.VMEM((total, D), low),
            pltpu.VMEM((total, 3 * D), low),
            pltpu.VMEM(whole, low),
            pltpu.VMEM((n_dp, block_rows, split), low),
            pltpu.VMEM((n_col, rows, wide), f32),
            pltpu.VMEM((block_rows, wide), f32),
            pltpu.VMEM((n_col * n_row, 3 * D, slice_wide), low),
            pltpu.VMEM((3, depth, D), f32),
            pltpu.VMEM((2, tile, wide_cols), f32),
            pltpu.VMEM((depth, wide_cols), low),
            pltpu.VMEM((right_rows + depth, D), low),
            pltpu.VMEM((3, right_rows, wide_cols), low),
            pltpu.VMEM((left_rows, D), f32),
            pltpu.VMEM((3, left_rows, D), low),
            pltpu.VMEM((3, depth, wide_rows), low),
            pltpu.VMEM((total, D), low),
            pltpu.VMEM((total, D), f32),
            dma((n_col,)),
            dma((n_col,)),
            dma((3,)),
            dma((max(1, n_row - 1),)),
            dma((max(1, n_row - 1),)),
            dma((3,)),
            dma((3 * wide_rows // tile,)),
            dma((3, 3 + n_row)),
            dma((2,)),
            dma((n_dp,)),
            dma((n_dp,)),
            dma((n_dp,)),
            dma((n_dp,)),
            dma((n_col,)),
            dma((n_col,)),
            *spread_sems(dims, n_dp, False, n_row == 4, True),
            *spread_sems(dims, n_dp, False, n_row == 4, True),
            *spread_sems(dims, n_dp, False, n_row == 4, True),
            *spread_sems(dims, chunks, False, n_row == 4, True),
            *reduce_scratch(dims, CAP, 2 * D, copied=False),
            *reduce_scratch(dims, block_rows, wide, copied=False, lanes=split),
            *dp_first_scratch(dims, block_rows, wide - split),
        ],
        compiler_params=pltpu.CompilerParams(
            collective_id=5, has_side_effects=True, vmem_limit_bytes=VMEM_BYTES
        ),
        name="layer",
    )(
        lengths,
        routes,
        prev_logits,
        tokens,
        cotangent,
        w_qkv,
        w_out,
        route_w,
        gains,
        const_vec,
        weight_gu,
        weight_down,
        left_root_gu,
        right_root_down,
        right_root_gu,
        left_root_down,
    )


def norm_forward(values, gain_vec):
    norm_scale = lax.rsqrt(jnp.mean(values * values, axis=-1, keepdims=True) + NORM_EPS)
    normed = values * norm_scale
    return (normed * gain_vec, normed, norm_scale)


def norm_backward(grad_out, normed, norm_scale, gain_vec):
    grad_normed = grad_out * gain_vec
    inner_mean = jnp.mean(grad_normed * normed, axis=-1, keepdims=True)
    return (norm_scale * (grad_normed - normed * inner_mean), jnp.sum(grad_out * normed, axis=0))


def attention_probs(queries, key_heads, allowed):
    scores = jnp.einsum(
        "qhd,khd->hqk", queries, key_heads, preferred_element_type=jnp.float32
    ) * HEAD ** (-0.5)
    scores = jnp.where(allowed[None], scores, -1e30)
    top_score = jnp.max(scores, axis=-1, keepdims=True)
    exp_scores = jnp.exp(scores - top_score)
    return exp_scores / jnp.sum(exp_scores, axis=-1, keepdims=True)


def diag_update(weight, grad, state, rate):
    new_state = 0.5 * state + 0.5 * grad * grad
    return (new_state, weight - rate * grad / (jnp.sqrt(new_state) + 1e-08))


def diagonal_updates(widths, n_col, summed_ref, in_refs, out_refs, turn_ref):
    wide_qkv, wide_out, route_cols = widths
    rows = summed_ref.shape[1]
    rates = (D ** (-0.5), HEAD ** (-0.5), (4 * D) ** (-0.5), 0.3, 0.5)

    def update(n, cols, grad):
        weight, state = in_refs[2 * n], in_refs[2 * n + 1]
        grad_ref, moment_ref, new_ref = out_refs[3 * n : 3 * n + 3]
        moment, new = diag_update(weight[:, cols], grad, state[:, cols], rates[n])
        grad_ref[:, cols] = grad
        moment_ref[:, cols] = moment
        new_ref[:, cols] = new

    for i in range(n_col):
        update(0, pl.ds(i * wide_qkv, wide_qkv), summed_ref[i, :, :wide_qkv])
        update(1, pl.ds(i * wide_out, wide_out), summed_ref[i, :, wide_qkv + LANES :])
    turn_ref[...] = jnp.zeros_like(turn_ref)
    turn_ref[:rows] = summed_ref[0, :, wide_qkv : wide_qkv + LANES]
    turned = turn_ref[...].T
    whole = pl.ds(0, rows)
    update(2, whole, turned[:route_cols, :rows])
    update(3, whole, turned[route_cols : route_cols + 2, :rows])
    update(4, whole, turned[route_cols + 2 : route_cols + 4, :rows])


def finish_kernel(sizes, *refs):
    n_col, widths = sizes
    refs, diag = [*refs[:13], *refs[38:]], refs[13:38]
    (
        right_sum,
        left_sum,
        step,
        block,
        left_gu,
        right_down,
        right_gu,
        left_down,
        weight_gu,
        weight_down,
        result,
        grad_tokens,
        summed,
        out_grad_gu,
        out_grad_down,
        out_left_gu,
        out_right_down,
        out_right_gu,
        out_left_down,
        out_weight_gu,
        out_weight_down,
        out_result,
        out_grad_tokens,
        right_sum_buf,
        left_sum_buf,
        step_buf,
        block_buf,
        right_buf,
        left_buf,
        weight_buf,
        grad_buf,
        result_buf,
        tokens_buf,
        turn_buf,
        *diag_buf,
        in_sem,
        out_sem,
        diag_sem,
    ) = refs
    pairs = zip([summed, *diag[:10]], diag_buf)
    small = [
        pltpu.make_async_copy(src, dst, diag_sem.at[n]) for n, (src, dst) in enumerate(pairs)
    ]
    for copy in small:
        copy.start()
    mats = range(3)
    f32 = jnp.float32
    n_row, _, slice_wide = block_buf.shape[1:]
    lefts = [left_gu.at[0], left_gu.at[1], right_down]
    rights = [right_gu.at[0], right_gu.at[1], left_down]
    weights = [weight_gu.at[:, 0], weight_gu.at[:, 1], weight_down]
    out_lefts = [out_left_gu.at[0], out_left_gu.at[1], out_right_down]
    out_rights = [out_right_gu.at[0], out_right_gu.at[1], out_left_down]
    out_weights = [out_weight_gu.at[:, 0], out_weight_gu.at[:, 1], out_weight_down]
    out_grads = [out_grad_gu.at[:, 0], out_grad_gu.at[:, 1], out_grad_down]
    loads = {}

    def load(m, kind, src, dst):
        copy = pltpu.make_async_copy(src, dst, in_sem.at[m, kind])
        copy.start()
        loads[m, kind] = copy

    stores = []

    def store(m, kind, src, dst):
        copy = pltpu.make_async_copy(src, dst, out_sem.at[m, kind])
        copy.start()
        stores.append(copy)

    for m in mats:
        load(m, 0, right_sum.at[m], right_sum_buf.at[m])
        load(m, 1, rights[m], right_buf.at[m])
        load(m, 2, block.at[m], block_buf.at[m])
        load(m, 3, step.at[m], step_buf.at[m])
        load(m, 4, weights[m], weight_buf.at[m])
        load(m, 5, left_sum.at[m], left_sum_buf.at[m])
        load(m, 6, lefts[m], left_buf.at[m])
    load(0, 7, result, result_buf)
    load(1, 7, grad_tokens, tokens_buf)
    for copy in small:
        copy.wait()
    diagonal_updates(widths, n_col, diag_buf[0], diag_buf[1:11], diag_buf[11:], turn_buf)
    for n, (src, dst) in enumerate(zip(diag_buf[11:], diag[10:])):
        copy = pltpu.make_async_copy(src, dst, diag_sem.at[11 + n])
        copy.start()
        stores.append(copy)
    for m in mats:
        loads[m, 0].wait()
        loads[m, 1].wait()
        right_buf[m] = 0.5 * right_buf[m] + right_sum_buf[m].astype(f32)
        store(m, 0, right_buf.at[m], out_rights[m])
        loads[m, 2].wait()
        for b in range(n_row):
            grad_buf[m, :, b * slice_wide : (b + 1) * slice_wide] = block_buf[m, b].astype(f32)
        store(m, 1, grad_buf.at[m], out_grads[m])
        loads[m, 3].wait()
        loads[m, 4].wait()
        weight_buf[m] = weight_buf[m] - step_buf[m].astype(f32)
        store(m, 2, weight_buf.at[m], out_weights[m])
        loads[m, 5].wait()
        loads[m, 6].wait()
        left_buf[m] = 0.5 * left_buf[m] + left_sum_buf[m].astype(f32)
        store(m, 3, left_buf.at[m], out_lefts[m])
    loads[0, 7].wait()
    store(0, 4, result_buf, out_result)
    loads[1, 7].wait()
    store(1, 4, tokens_buf, out_grad_tokens)
    for copy in stores:
        copy.wait()


def finish_update(
    products,
    left_gu,
    right_down,
    right_gu,
    left_down,
    weight_gu,
    weight_down,
    result,
    grad_tokens,
    summed,
    diag_in,
    n_col,
    widths,
):
    f32 = jnp.float32
    dma = pltpu.SemaphoreType.DMA
    hbm = pl.BlockSpec(memory_space=pl.ANY)
    right_sum, left_sum, step, block = products
    args = (
        *products,
        left_gu,
        right_down,
        right_gu,
        left_down,
        weight_gu,
        weight_down,
        result,
        grad_tokens,
        summed,
        *diag_in,
    )
    outs = [weight for weight in diag_in[::2] for _ in range(3)]
    outs += [weight_gu, weight_down, left_gu, right_down, right_gu, left_down]
    outs += [weight_gu, weight_down, result, grad_tokens]
    return pl.pallas_call(
        functools.partial(finish_kernel, (n_col, widths)),
        out_shape=[jax.ShapeDtypeStruct(like.shape, like.dtype) for like in outs],
        in_specs=[hbm] * 23,
        out_specs=[hbm] * 25,
        scratch_shapes=[
            pltpu.VMEM(right_sum.shape, right_sum.dtype),
            pltpu.VMEM(left_sum.shape, left_sum.dtype),
            pltpu.VMEM(step.shape, step.dtype),
            pltpu.VMEM(block.shape, block.dtype),
            pltpu.VMEM(right_sum.shape, f32),
            pltpu.VMEM(left_sum.shape, f32),
            pltpu.VMEM(step.shape, f32),
            pltpu.VMEM(step.shape, f32),
            pltpu.VMEM(result.shape, result.dtype),
            pltpu.VMEM(grad_tokens.shape, f32),
            pltpu.VMEM((LANES, LANES), f32),
            *[pltpu.VMEM(like.shape, f32) for like in (summed, *diag_in, *outs[:15])],
            dma((3, 8)),
            dma((3, 5)),
            dma((26,)),
        ],
        compiler_params=pltpu.CompilerParams(vmem_limit_bytes=VMEM_BYTES),
        name="finish",
    )(*args)


def shampoo_plain(
    grads,
    left_root_gu,
    right_root_down,
    right_root_gu,
    left_root_down,
    left_gu,
    right_down,
    right_gu,
    left_down,
    weight_gu,
    weight_down,
    n_row,
    n_col,
):
    low = jnp.bfloat16
    blocks, _, slice_wide = grads.shape
    model = left_root_gu.shape[2]
    r = lax.axis_index("row")
    c = lax.axis_index("col")
    owner = r * n_col + c
    left_rows = right_down.shape[0]
    right_rows = left_down.shape[0]
    product = functools.partial(jnp.einsum, preferred_element_type=jnp.float32)
    whole = grads.reshape(blocks, 3, model, slice_wide).transpose(1, 2, 0, 3).reshape(3, model, -1)
    mine_left = lax.dynamic_slice_in_dim(whole, owner * left_rows, left_rows, 1)
    mine_right = lax.dynamic_slice_in_dim(whole, owner * right_rows, right_rows, 2)
    left_sum = 0.5 * product("mif,mjf->mij", mine_left, whole)
    right_sum = 0.5 * product("mdi,mdj->mij", mine_right, whole)
    roots = jnp.concatenate([left_root_gu, right_root_down[None]]).astype(low)
    wides = jnp.concatenate([right_root_gu, left_root_down[None]]).astype(low)
    step = product("mid,mdf->mif", roots, whole).astype(low)
    step = SHAMPOO_RATE * product("mif,mjf->mij", step, wides)
    depth, wide_rows = weight_down.shape
    block = lax.dynamic_slice(whole, (0, r * depth, c * wide_rows), (3, depth, wide_rows))
    block = block.astype(jnp.float32)
    return (
        block[:2].transpose(1, 0, 2),
        block[2],
        0.5 * left_gu + left_sum[:2],
        0.5 * right_down + left_sum[2],
        0.5 * right_gu + right_sum[:2],
        0.5 * left_down + right_sum[2],
        weight_gu - step[:2].transpose(1, 0, 2),
        weight_down - step[2],
    )


def body_tiled(
    tokens,
    lengths,
    routes,
    prev_logits,
    cotangent,
    w_qkv,
    w_out,
    route_w,
    gains,
    const_vec,
    stat_qkv,
    stat_out,
    stat_route,
    stat_gains,
    stat_const,
    w_gate_up,
    w_down,
    left_gu,
    right_gu,
    left_down,
    right_down,
    left_root_gu,
    right_root_gu,
    left_root_down,
    right_root_down,
):
    dims = mesh_sizes()
    n_col = dims[2]
    wide_qkv = w_qkv.shape[1] // n_col
    wide_out = w_out.shape[1] // n_col
    widths = (wide_qkv, wide_out, route_w.shape[1])
    result, grad_input, summed, *products = layer(
        lengths,
        routes.T,
        prev_logits.T,
        tokens,
        cotangent,
        w_qkv,
        w_out,
        route_w.T,
        gains,
        const_vec,
        w_gate_up[0],
        w_down[0].T,
        left_root_gu[0],
        right_root_down[0],
        right_root_gu[0],
        left_root_down[0],
        dims,
        widths,
    )
    outs = finish_update(
        products,
        left_gu[0],
        right_down[0],
        right_gu[0],
        left_down[0],
        w_gate_up[0],
        w_down[0].T,
        result,
        grad_input,
        summed,
        [
            w_qkv,
            stat_qkv,
            w_out,
            stat_out,
            route_w.T,
            stat_route.T,
            gains,
            stat_gains,
            const_vec,
            stat_const,
        ],
        n_col,
        widths,
    )
    diag = list(outs[:15])
    diag[6:9] = [part.T for part in diag[6:9]]
    (
        grad_gate_up,
        grad_down,
        new_left_gu,
        new_right_down,
        new_right_gu,
        new_left_down,
        new_gate_up,
        new_down,
        result,
        grad_input,
    ) = outs[15:]
    return (
        result,
        grad_input,
        *diag,
        grad_gate_up[None],
        grad_down.T[None],
        new_left_gu[None],
        new_right_gu[None],
        new_left_down[None],
        new_right_down[None],
        new_gate_up[None],
        new_down.T[None],
    )


def body(
    tokens,
    lengths,
    routes,
    prev_logits,
    cotangent,
    w_qkv,
    w_out,
    route_w,
    gains,
    const_vec,
    stat_qkv,
    stat_out,
    stat_route,
    stat_gains,
    stat_const,
    w_gate_up,
    w_down,
    left_gu,
    right_gu,
    left_down,
    right_down,
    left_root_gu,
    right_root_gu,
    left_root_down,
    right_root_down,
):
    dims = mesh_sizes()
    n_dp, n_row, n_col = dims
    low = jnp.bfloat16
    row_total = tokens.shape[0]
    total_experts = prev_logits.shape[1]
    num_ffn = total_experts - 4
    seq_count = lengths.shape[1]
    shard_rows = w_qkv.shape[0]
    wide_qkv = w_qkv.shape[1] // n_col
    wide_out = w_out.shape[1] // n_col
    route_cols = route_w.shape[1]
    wide = wide_qkv + wide_out + LANES

    def by_col(matrix):
        return matrix.reshape(matrix.shape[0], n_col, -1).transpose(1, 0, 2)

    def small_block(route_part, gain_part, const_part):
        together = jnp.concatenate([route_part, gain_part.T, const_part.T], axis=1)
        return jnp.pad(together, ((0, 0), (0, LANES - together.shape[1])))

    small = small_block(route_w, gains, const_vec)
    shard = jnp.concatenate(
        [by_col(w_qkv), by_col(w_out), jnp.broadcast_to(small[None], (n_col, shard_rows, LANES))],
        axis=2,
    )
    whole = param_gather(shard, dims).reshape(n_col, D, wide)
    full_qkv = [whole[i, :, :wide_qkv] for i in range(n_col)]
    full_out = [whole[i, :, wide_qkv : wide_qkv + wide_out] for i in range(n_col)]
    full_small = whole[0, :, wide_qkv + wide_out :]
    full_route = full_small[:, :route_cols]
    row_vectors = full_small[:, route_cols : route_cols + 4].T.astype(jnp.float32)
    gain_one, gain_two, const_rows = row_vectors[0], row_vectors[1], row_vectors[2:4]

    row_depth = w_gate_up.shape[1]
    col_width = w_gate_up.shape[3]
    slice_wide = col_width // n_row
    gu_slices = w_gate_up[0].astype(low).reshape(row_depth, 2, n_row, slice_wide)
    gu_slices = gu_slices.transpose(2, 0, 1, 3)
    gu_own = lax.all_to_all(gu_slices, "row", split_axis=0, concat_axis=0, tiled=True)
    gu_own = gu_own.reshape(n_row * row_depth, 2 * slice_wide)
    down_slices = w_down[0].astype(low).reshape(n_row, slice_wide, row_depth)
    down_own = lax.all_to_all(down_slices, "row", split_axis=0, concat_axis=0, tiled=True)
    down_own = down_own.transpose(1, 0, 2).reshape(slice_wide, n_row * row_depth)

    positions = jnp.arange(row_total, dtype=jnp.int32)
    seq_ends = jnp.cumsum(lengths[0])
    doc_index = jnp.sum((positions[:, None] >= seq_ends[None, :]).astype(jnp.int32), axis=1)
    valid_rows = (doc_index < seq_count).astype(jnp.float32)[:, None]
    allowed = (doc_index[:, None] == doc_index[None, :]) & (
        positions[:, None] >= positions[None, :]
    )
    inputs = tokens.astype(jnp.float32)
    h_one, normed_one, scale_one = norm_forward(inputs, gain_one)
    h_one_low = h_one.astype(low)
    qkv_rows = jnp.concatenate([dot(h_one_low, part) for part in full_qkv], axis=1).astype(low)
    qkv_rows = qkv_rows.reshape(row_total, 3, HEADS, HEAD)
    queries, key_heads, values = (qkv_rows[:, 0], qkv_rows[:, 1], qkv_rows[:, 2])
    softmax_probs = attention_probs(queries, key_heads, allowed)
    probs_low = softmax_probs.astype(low)
    mixed_heads = jnp.einsum("hqk,khd->qhd", probs_low, values, preferred_element_type=jnp.float32)
    mixed_heads = mixed_heads.reshape(row_total, D).astype(low)
    attn_out = jnp.concatenate([dot(mixed_heads, part) for part in full_out], axis=1)
    first_sum = inputs + valid_rows * attn_out
    h_two, normed_two, scale_two = norm_forward(first_sum, gain_two)
    h_two_low = h_two.astype(low)
    logits_all = dot(h_two_low, full_route)
    logits = logits_all[:, :total_experts] + prev_logits
    pick_table = (
        routes[:, :, None] == jnp.arange(total_experts, dtype=jnp.int32)[None, None, :]
    ).astype(jnp.float32)
    chosen = jnp.sum(pick_table * logits[:, None, :], axis=-1)
    gate_weights = jax.nn.softmax(chosen, axis=-1)
    const_mix = jax.nn.softmax(logits_all[:, total_experts:].reshape(row_total, 2, 2), axis=-1)

    earlier = dot(
        (positions[:, None] > positions[None, :]).astype(low),
        jnp.sum(pick_table, axis=1).astype(low),
    )
    slot_index = jnp.sum(earlier[:, None, :] * pick_table, axis=-1).astype(jnp.int32)
    where_in = jnp.where(routes < num_ffn, routes * CAP + slot_index, -1)
    slot_ids = jnp.arange(num_ffn * CAP, dtype=jnp.int32)
    place_first = where_in[:, 0:1] == slot_ids[None, :]
    place_second = where_in[:, 1:2] == slot_ids[None, :]
    place_both = (place_first | place_second).astype(low)
    slot_gate = jnp.sum(
        place_first.astype(jnp.float32) * gate_weights[:, 0:1]
        + place_second.astype(jnp.float32) * gate_weights[:, 1:2],
        axis=0,
    )
    grad_y = cotangent.astype(jnp.float32) * valid_rows
    sent_rows = dot(place_both, h_two_low, TN).astype(low)
    grad_made = (slot_gate[:, None] * dot(place_both, grad_y.astype(low), TN)).astype(low)
    sent_both = jnp.concatenate(
        [sent_rows.reshape(num_ffn, CAP, D), grad_made.reshape(num_ffn, CAP, D)], axis=2
    )

    arrived = token_gather(sent_both, dims).reshape(-1, 2 * D)
    rows_in = arrived[:, :D]
    grads_in = arrived[:, D:]
    pre_act = dot(rows_in, gu_own)
    gate_part = pre_act[:, :slice_wide]
    up_part = pre_act[:, slice_wide:]
    sigma = jax.nn.sigmoid(gate_part)
    silu = gate_part * sigma
    hidden = (silu * up_part).astype(low)
    made_rows = dot(hidden, down_own).astype(low)
    grad_hidden = dot(grads_in, down_own, NT)
    grad_pre = jnp.concatenate(
        [
            grad_hidden * up_part * sigma * (1.0 + gate_part * (1.0 - sigma)),
            grad_hidden * silu,
        ],
        axis=1,
    ).astype(low)
    grad_rows = dot(grad_pre, gu_own, NT).astype(low)
    parts_back = jnp.concatenate([made_rows, grad_rows], axis=1)
    parts_back = parts_back.reshape(n_col, n_dp, n_row, CAP, 2 * D)
    came_back = token_reduce(parts_back, dims).reshape(num_ffn * CAP, 2 * D)
    expert_out = came_back[:, :D]
    grad_sent = came_back[:, D:]

    grad_gu_own = dot(rows_in, grad_pre, TN).astype(low)
    grad_down_own = dot(hidden, grads_in, TN).astype(low)
    grads_own = jnp.concatenate(
        [grad_gu_own[:, :slice_wide], grad_gu_own[:, slice_wide:], grad_down_own.T], axis=0
    )
    gathered = plane_gather(grads_own.reshape(4, -1, slice_wide), dims)
    gathered = gathered.reshape(n_col * n_row, 3 * D, slice_wide)

    is_ffn_first = dot(place_first.astype(low), expert_out)
    is_ffn_second = dot(place_second.astype(low), expert_out)
    picked = jnp.stack([is_ffn_first, is_ffn_second], axis=1)
    copy_sel = (routes == num_ffn + 1).astype(jnp.float32)
    const_sel = (
        routes[:, :, None] == num_ffn + 2 + jnp.arange(2, dtype=jnp.int32)[None, None, :]
    ).astype(jnp.float32)
    const_out = (
        const_mix[:, :, 0:1] * h_two[:, None, :] + const_mix[:, :, 1:2] * const_rows[None, :, :]
    )
    outputs = (
        picked
        + copy_sel[:, :, None] * h_two[:, None, :]
        + const_sel[:, :, 0:1] * const_out[:, None, 0, :]
        + const_sel[:, :, 1:2] * const_out[:, None, 1, :]
    )
    moe_out = valid_rows * jnp.sum(gate_weights[:, :, None] * outputs, axis=1)
    result = (first_sum + moe_out).astype(low)
    grad_gate = jnp.sum(grad_y[:, None, :] * outputs, axis=-1)
    grad_chosen = gate_weights * (
        grad_gate - jnp.sum(gate_weights * grad_gate, axis=-1, keepdims=True)
    )
    grad_logits = jnp.sum(grad_chosen[:, :, None] * pick_table, axis=1)
    const_weight = jnp.sum(const_sel * gate_weights[:, :, None], axis=1)
    mix_first = const_weight * jnp.sum(grad_y * h_two, axis=-1, keepdims=True)
    mix_second = const_weight * jnp.stack(
        [jnp.sum(grad_y * const_rows[0], axis=-1), jnp.sum(grad_y * const_rows[1], axis=-1)], axis=1
    )
    grad_mix = jnp.stack([mix_first, mix_second], axis=-1)
    grad_mix_logits = const_mix * (grad_mix - jnp.sum(const_mix * grad_mix, axis=-1, keepdims=True))
    grad_logits_all = jnp.concatenate(
        [grad_logits, grad_mix_logits.reshape(row_total, 4)], axis=1
    ).astype(low)
    grad_route_full = dot(h_two_low, grad_logits_all, TN)
    const_scale = const_weight * const_mix[:, :, 1]
    grad_const_full = jnp.stack(
        [
            jnp.sum(const_scale[:, 0:1] * grad_y, axis=0),
            jnp.sum(const_scale[:, 1:2] * grad_y, axis=0),
        ]
    )
    back_rows = dot(place_both, grad_sent)
    own_weight = jnp.sum(gate_weights * copy_sel, axis=1, keepdims=True) + jnp.sum(
        const_weight * const_mix[:, :, 0], axis=1, keepdims=True
    )
    grad_h_two = dot(grad_logits_all, full_route, NT) + back_rows + own_weight * grad_y
    grad_first, grad_gain_two = norm_backward(grad_h_two, normed_two, scale_two, gain_two)
    grad_first = grad_first + cotangent.astype(jnp.float32)
    grad_attn = (valid_rows * grad_first).astype(low)
    grad_mixed = functools.reduce(
        jnp.add,
        [
            dot(grad_attn[:, i * wide_out : (i + 1) * wide_out], part, NT)
            for i, part in enumerate(full_out)
        ],
    ).astype(low)
    grad_mixed = grad_mixed.reshape(row_total, HEADS, HEAD)
    grad_values = jnp.einsum(
        "hqk,qhd->khd", probs_low, grad_mixed, preferred_element_type=jnp.float32
    )
    grad_probs = jnp.einsum("qhd,khd->hqk", grad_mixed, values, preferred_element_type=jnp.float32)
    grad_scores = softmax_probs * (
        grad_probs - jnp.sum(softmax_probs * grad_probs, axis=-1, keepdims=True)
    )
    grad_scores = grad_scores.astype(low)
    grad_queries = jnp.einsum(
        "hqk,khd->qhd", grad_scores, key_heads, preferred_element_type=jnp.float32
    ) * HEAD ** (-0.5)
    grad_keys = jnp.einsum(
        "hqk,qhd->khd", grad_scores, queries, preferred_element_type=jnp.float32
    ) * HEAD ** (-0.5)
    grad_qkv_rows = (
        jnp.stack([grad_queries, grad_keys, grad_values], axis=1)
        .reshape(row_total, 3 * D)
        .astype(low)
    )
    grad_h_one = functools.reduce(
        jnp.add,
        [
            dot(grad_qkv_rows[:, i * wide_qkv : (i + 1) * wide_qkv], part, NT)
            for i, part in enumerate(full_qkv)
        ],
    )
    grad_input, grad_gain_one = norm_backward(grad_h_one, normed_one, scale_one, gain_one)
    grad_input = grad_input + grad_first
    grad_gains_full = jnp.stack([grad_gain_one, grad_gain_two])

    grad_small = small_block(grad_route_full, grad_gains_full, grad_const_full).astype(low)
    param_parts = jnp.stack(
        [
            jnp.concatenate(
                [
                    dot(h_one_low, grad_qkv_rows[:, i * wide_qkv : (i + 1) * wide_qkv], TN).astype(
                        low
                    ),
                    dot(mixed_heads, grad_attn[:, i * wide_out : (i + 1) * wide_out], TN).astype(
                        low
                    ),
                    grad_small,
                ],
                axis=1,
            )
            for i in range(n_col)
        ]
    )
    summed = param_reduce(
        param_parts.reshape(n_col, n_dp, n_row, n_col * shard_rows, wide), dims
    )

    def from_col(parts):
        return parts.transpose(1, 0, 2).reshape(parts.shape[1], -1)

    grad_qkv = from_col(summed[:, :, :wide_qkv])
    grad_attn_out = from_col(summed[:, :, wide_qkv : wide_qkv + wide_out])
    sum_small = summed[0, :, wide_qkv + wide_out :]
    grad_route = sum_small[:, :route_cols]
    grad_gains = sum_small[:, route_cols : route_cols + 2].T
    grad_const = sum_small[:, route_cols + 2 : route_cols + 4].T
    moment_qkv, new_qkv = diag_update(w_qkv, grad_qkv, stat_qkv, D ** (-0.5))
    moment_attn_out, new_attn_out = diag_update(w_out, grad_attn_out, stat_out, HEAD ** (-0.5))
    moment_route, new_route = diag_update(route_w, grad_route, stat_route, (4 * D) ** (-0.5))
    moment_gains, new_gains = diag_update(gains, grad_gains, stat_gains, 0.3)
    moment_const, new_const = diag_update(const_vec, grad_const, stat_const, 0.5)

    (
        grad_gate_up,
        grad_down,
        new_left_gu,
        new_right_down,
        new_right_gu,
        new_left_down,
        new_gate_up,
        new_down,
    ) = shampoo_plain(
        gathered,
        left_root_gu[0],
        right_root_down[0],
        right_root_gu[0],
        left_root_down[0],
        left_gu[0],
        right_down[0],
        right_gu[0],
        left_down[0],
        w_gate_up[0],
        w_down[0].T,
        n_row,
        n_col,
    )
    return (
        result,
        grad_input,
        grad_qkv,
        moment_qkv,
        new_qkv,
        grad_attn_out,
        moment_attn_out,
        new_attn_out,
        grad_route,
        moment_route,
        new_route,
        grad_gains,
        moment_gains,
        new_gains,
        grad_const,
        moment_const,
        new_const,
        grad_gate_up[None],
        grad_down.T[None],
        new_left_gu[None],
        new_right_gu[None],
        new_left_down[None],
        new_right_down[None],
        new_gate_up[None],
        new_down.T[None],
    )


def solution(mesh):
    placed = (
        P(("dp", "row", "col"), None),
        P(("dp", "row", "col"), None),
        P(("dp", "row", "col"), None),
        P(("dp", "row", "col"), None),
        P(("dp", "row", "col"), None),
        P(("dp", "row", "col"), None),
        P(("dp", "row", "col"), None),
        P(("dp", "row", "col"), None),
        P(None, ("dp", "row", "col")),
        P(None, ("dp", "row", "col")),
        P(("dp", "row", "col"), None),
        P(("dp", "row", "col"), None),
        P(("dp", "row", "col"), None),
        P(None, ("dp", "row", "col")),
        P(None, ("dp", "row", "col")),
        P("dp", "row", None, "col"),
        P("dp", "col", "row"),
        P("dp", None, ("row", "col"), None),
        P("dp", None, ("row", "col"), None),
        P("dp", ("row", "col"), None),
        P("dp", ("row", "col"), None),
        P("dp", None, "row", None),
        P("dp", None, "col", None),
        P("dp", "col", None),
        P("dp", "row", None),
    )
    tiled = 3 * D % (mesh.shape["col"] * LANES) == 0 and D % (mesh.shape["col"] * LANES) == 0
    tiled = tiled and D // mesh.shape["dp"] // mesh.shape["row"] % 16 == 0
    return jax.shard_map(
        body_tiled if tiled else body,
        mesh=mesh,
        in_specs=placed,
        out_specs=(
            P(("dp", "row", "col"), None),
            P(("dp", "row", "col"), None),
            P(("dp", "row", "col"), None),
            P(("dp", "row", "col"), None),
            P(("dp", "row", "col"), None),
            P(("dp", "row", "col"), None),
            P(("dp", "row", "col"), None),
            P(("dp", "row", "col"), None),
            P(("dp", "row", "col"), None),
            P(("dp", "row", "col"), None),
            P(("dp", "row", "col"), None),
            P(None, ("dp", "row", "col")),
            P(None, ("dp", "row", "col")),
            P(None, ("dp", "row", "col")),
            P(None, ("dp", "row", "col")),
            P(None, ("dp", "row", "col")),
            P(None, ("dp", "row", "col")),
            P("dp", "row", None, "col"),
            P("dp", "col", "row"),
            P("dp", None, ("row", "col"), None),
            P("dp", None, ("row", "col"), None),
            P("dp", ("row", "col"), None),
            P("dp", ("row", "col"), None),
            P("dp", "row", None, "col"),
            P("dp", "col", "row"),
        ),
        check_vma=False,
    )
```

```python
import functools
import types

import jax
import jax.numpy as jnp
from jax import lax
from jax.experimental import pallas as pl
from jax.experimental.pallas import tpu as pltpu
from jax.sharding import PartitionSpec as P

D = 768
HEADS = 12
HEAD = 64
CAP = 32
LANES = 128


NORM_EPS = 1e-06
SHAMPOO_RATE = 0.5
MESH = pl.DeviceIdType.MESH
VMEM_BYTES = 62 * 2**20


def dot(left, right, dims=(((1,), (0,)), ((), ()))):
    return lax.dot_general(left, right, dims, preferred_element_type=jnp.float32)


NT = (((1,), (1,)), ((), ()))
TN = (((0,), (0,)), ((), ()))


def flip(index, bit):
    return index + bit * (1 - 2 * ((index // bit) % 2))


def flip_all(index, mask, bits):
    for dim in range(bits):
        if mask & (1 << dim):
            index = flip(index, 1 << dim)
    return index


def dp_order(d, p, count):
    if p == 0:
        return d
    upper = d // max(1, count // 2)
    low_d = d + upper * (count - 1 - 2 * d)
    at = p - 1 + (p - 1 - low_d + count) // count
    return at + upper * (count - 1 - 2 * at)


def mesh_sizes():
    return tuple(lax.axis_size(name) for name in ("dp", "row", "col"))


def bits_of(count):
    bits = count.bit_length() - 1
    assert 1 << bits == count
    return bits


def greet(over_dp, dims, place, all_rows=False, wait=True):
    n_dp, n_row, n_col = dims
    d, r, c = place
    peers = []
    if over_dp:
        peers += [((d + j) % n_dp, r, c) for j in range(1, n_dp)]
    if all_rows:
        peers += [(d, (r + i) % n_row, c) for i in range(1, n_row)]
    else:
        peers += [(d, flip(r, 1 << dim), c) for dim in range(bits_of(n_row))]
    peers += [(d, r, (c + i) % n_col) for i in range(1, n_col)]
    barrier = pltpu.get_barrier_semaphore()
    for peer in peers:
        pl.semaphore_signal(barrier, inc=1, device_id=peer, device_id_type=MESH)
    if wait:
        pl.semaphore_wait(barrier, len(peers))
    return len(peers)


def remote(src, dst, send_sem, recv_sem, device):
    return pltpu.make_async_remote_copy(
        src_ref=src,
        dst_ref=dst,
        send_sem=send_sem,
        recv_sem=recv_sem,
        device_id=device,
        device_id_type=MESH,
    )


def plan_spread(
    dims, place, chunks, over_dp, own, dp_source, slot, sems, halves=False, totals=None, size=1, landed=None
):
    n_dp, n_row, n_col = dims
    d, r, c = place
    bits = bits_of(n_row)
    dp_send, dp_recv, row_send, row_recv, col_send, col_recv, own_sem = sems
    sent = []

    def of(sem, *at):
        return sem.at[tuple(0 for _ in at)] if totals else sem.at[at]


    def block(j, x):
        return slot(c, j, flip_all(r, x, bits))

    def to_row(j, src, x, bit):
        copy = remote(
            src,
            block(j, x),
            of(row_send, j, (x ^ bit) - 1),
            row_recv.at[j, (x ^ bit) - 1],
            (d, flip(r, bit), c),
        )
        copy.start()
        sent.append(copy)

    def to_cols(j, src, x):
        for i in range(1, n_col):
            copy = remote(
                src,
                block(j, x),
                of(col_send, j, x, i - 1),
                col_recv.at[(j // size, i - 1) if landed else (j, x, i - 1)],
                (d, r, (c + i) % n_col),
            )
            copy.start()
            sent.append(copy)

    def order(j):
        return [1 << ((j + s) % bits) for s in range(bits)]

    locals_ = {}

    def start(j):
        if over_dp and j > 0:
            src = block(j, 0)
            origin = dp_order(d, j, n_dp)
            remote(src, src, of(dp_send, j - 1), dp_recv.at[origin], (d, r, c)).wait_recv()
        elif own is None:
            src = block(j, 0)
        else:
            src = own(j)
            keep = pltpu.make_async_copy(src, block(j, 0), own_sem.at[j])
            keep.start()
            locals_[j] = keep
        for bit in order(j):
            to_row(j, src, 0, bit)
        to_cols(j, src, 0)

    def arrived(j, x, later_dims):
        ref = block(j, x)
        remote(ref, ref, of(row_send, j, x - 1), row_recv.at[j, x - 1], (d, r, c)).wait_recv()
        for later in later_dims:
            to_row(j, ref, x, later)
        to_cols(j, ref, x)

    def parts(ref):
        wide = ref.shape[-1]
        cut = (wide // LANES + 1) // 2 * LANES
        return [ref.at[:, pl.ds(0, cut)], ref.at[:, pl.ds(cut, wide - cut)]]

    def pass_halves(j):
        for x in order(j):
            arrived(j, x, [])
            half = x - 1
            part = parts(block(j, x))[half]
            copy = remote(
                part,
                part,
                of(row_send, j, 2 + half),
                row_recv.at[j, 2 + half],
                (d, flip(r, 3 - x), c),
            )
            copy.start()
            sent.append(copy)

    def last_halves(j):
        for half, part in enumerate(parts(block(j, 3))):
            remote(
                part, part, of(row_send, j, 2 + half), row_recv.at[j, 2 + half], (d, r, c)
            ).wait_recv()
        to_cols(j, block(j, 3), 3)

    def pass_on(j):
        have = [0]
        dim_order = order(j)
        for s, bit in enumerate(dim_order[:-1]):
            new = [x ^ bit for x in have]
            for x in new:
                arrived(j, x, dim_order[s + 1 :])
            have += new

    def last_arrivals(j):
        bit = order(j)[-1]
        for x in range(n_row):
            if x & bit:
                arrived(j, x, [])

    def send_dp():
        for j in range(1, n_dp):
            peer = dp_order(d, j, n_dp)
            copy = remote(
                dp_source(peer),
                slot(c, ("from", d), r),
                of(dp_send, j - 1),
                dp_recv.at[d],
                (peer, r, c),
            )
            copy.start()
            sent.append(copy)

    def wait_cols(j):
        if landed is not None:
            if (j + 1) % size == 0:
                for i in range(1, n_col):
                    ref = landed((c + n_col - i) % n_col, j // size)
                    sem = col_recv.at[j // size, i - 1]
                    remote(ref, ref, of(col_send, 0, 0, 0), sem, (d, r, c)).wait_recv()
            return
        for x in range(n_row):
            for i in range(1, n_col):
                ref = slot((c + n_col - i) % n_col, j, flip_all(r, x, bits))
                remote(
                    ref, ref, of(col_send, j, x, i - 1), col_recv.at[j, x, i - 1], (d, r, c)
                ).wait_recv()
        if j in locals_:
            locals_[j].wait()

    def sends():
        if totals is None:
            return [copy.wait_send for copy in sent]
        pairs = zip((dp_send, row_send, col_send), totals)
        return [
            remote(ref, ref, of(sem, *sem.shape), dp_recv.at[0], (d, r, c)).wait_send
            for sem, ref in pairs
            if ref is not None
        ]

    return types.SimpleNamespace(
        start=start,
        send_dp=send_dp,
        pass_on=pass_halves if halves else pass_on,
        last_arrivals=last_halves if halves else last_arrivals,
        wait_cols=wait_cols,
        sends=sends,
    )


def spread_blocks(dims, place, chunks, over_dp, own, dp_source, slot, sems, between=None):
    plan = plan_spread(dims, place, chunks, over_dp, own, dp_source, slot, sems)
    plan.start(0)
    if over_dp:
        plan.send_dp()
        for j in range(1, chunks):
            plan.start(j)
            plan.pass_on(j - 1)
        plan.pass_on(chunks - 1)
    else:
        for j in range(1, chunks):
            plan.start(j)
        for j in range(chunks):
            plan.pass_on(j)
    if between is not None:
        between()
    for j in range(chunks):
        plan.last_arrivals(j)
    for j in range(chunks):
        plan.wait_cols(j)
    return plan.sends()


def finish(waits):
    for wait in waits:
        wait()


def spread_sems(dims, chunks, copied=True, halves=False, shared=False, groups=None):
    n_dp, n_row, n_col = dims
    pieces = max(1, n_row - 1) + halves
    dma = pltpu.SemaphoreType.DMA
    rows = (chunks, pieces)
    cols = (chunks, n_row, max(1, n_col - 1))
    return [
        dma((1,) if shared else (max(1, n_dp - 1),)),
        dma((n_dp,)),
        dma((1, 1) if shared else rows),
        dma(rows),
        dma((1, 1, 1) if shared else cols),
        dma((groups, max(1, n_col - 1)) if groups else cols),
        dma((chunks if copied else 1,)),
    ]


def axis_place():
    return tuple(lax.axis_index(name) for name in ("dp", "row", "col"))


def param_gather_kernel(dims, shard_ref, out_ref, swap_ref, block_ref, swap_send, swap_recv, *sems):
    n_dp, n_row, n_col = dims
    place = axis_place()
    d, r, c = place
    rows = shard_ref.shape[1]
    greet(True, dims, place)
    copies = []
    for i in range(1, n_col):
        other = (c + i) % n_col
        copy = remote(
            shard_ref.at[other], swap_ref.at[c], swap_send.at[i], swap_recv.at[i], (d, r, other)
        )
        copy.start()
        copies.append(copy)
    swap_ref[pl.ds(c, 1)] = shard_ref[pl.ds(c, 1)]
    for copy in copies:
        copy.wait()
    for i in range(n_col):
        block_ref[i * rows : (i + 1) * rows, :] = swap_ref[i]
    low_ref = sems[-1]
    low_ref[...] = block_ref[...].astype(jnp.bfloat16)

    def slot(col, j, b):
        k = j[1] if isinstance(j, tuple) else dp_order(d, j, n_dp)
        return out_ref.at[col, k, b]

    finish(
        spread_blocks(
            dims, place, n_dp, True, lambda j: low_ref, lambda k: low_ref, slot, sems[:-1]
        )
    )


def param_gather(shard, dims):
    n_dp, n_row, n_col = dims
    _, rows, width = shard.shape
    dma = pltpu.SemaphoreType.DMA
    return pl.pallas_call(
        functools.partial(param_gather_kernel, dims),
        out_shape=jax.ShapeDtypeStruct((n_col, n_dp, n_row, n_col * rows, width), jnp.bfloat16),
        in_specs=[pl.BlockSpec(memory_space=pltpu.VMEM)],
        out_specs=pl.BlockSpec(memory_space=pl.ANY),
        scratch_shapes=[
            pltpu.VMEM((n_col, rows, width), jnp.float32),
            pltpu.VMEM((n_col * rows, width), jnp.float32),
            dma((n_col,)),
            dma((n_col,)),
            *spread_sems(dims, n_dp),
            pltpu.VMEM((n_col * rows, width), jnp.bfloat16),
        ],
        compiler_params=pltpu.CompilerParams(
            collective_id=0, has_side_effects=True, vmem_limit_bytes=VMEM_BYTES
        ),
        name="param_gather",
    )(shard)


def token_gather_kernel(dims, src_ref, out_ref, *sems):
    n_dp, n_row, n_col = dims
    place = axis_place()
    d = place[0]
    greet(True, dims, place)

    def slot(col, j, b):
        k = j[1] if isinstance(j, tuple) else dp_order(d, j, n_dp)
        return out_ref.at[col, k, b]

    finish(
        spread_blocks(
            dims,
            place,
            n_dp,
            True,
            lambda j: src_ref.at[d],
            lambda k: src_ref.at[k],
            slot,
            sems,
        )
    )


def token_gather(rows, dims):
    n_dp, n_row, n_col = dims
    _, slots, width = rows.shape
    return pl.pallas_call(
        functools.partial(token_gather_kernel, dims),
        out_shape=jax.ShapeDtypeStruct((n_col, n_dp, n_row, slots, width), rows.dtype),
        in_specs=[pl.BlockSpec(memory_space=pl.ANY)],
        out_specs=pl.BlockSpec(memory_space=pl.ANY),
        scratch_shapes=spread_sems(dims, n_dp),
        compiler_params=pltpu.CompilerParams(
            collective_id=1, has_side_effects=True, vmem_limit_bytes=VMEM_BYTES
        ),
        name="token_gather",
    )(rows)


def plane_gather_kernel(dims, src_ref, out_ref, *sems):
    place = axis_place()
    greet(False, dims, place)
    finish(
        spread_blocks(
            dims,
            place,
            src_ref.shape[0],
            False,
            lambda j: src_ref.at[j],
            None,
            lambda col, j, b: out_ref.at[col, b, j],
            sems,
        )
    )


def plane_gather(parts, dims):
    n_dp, n_row, n_col = dims
    chunks, rows, width = parts.shape
    return pl.pallas_call(
        functools.partial(plane_gather_kernel, dims),
        out_shape=jax.ShapeDtypeStruct((n_col, n_row, chunks, rows, width), parts.dtype),
        in_specs=[pl.BlockSpec(memory_space=pl.ANY)],
        out_specs=pl.BlockSpec(memory_space=pl.ANY),
        scratch_shapes=spread_sems(dims, chunks),
        compiler_params=pltpu.CompilerParams(
            collective_id=2, has_side_effects=True, vmem_limit_bytes=VMEM_BYTES
        ),
        name="plane_gather",
    )(parts)


def add_low(left, right):
    return (left.astype(jnp.float32) + right.astype(jnp.float32)).astype(jnp.bfloat16)


def plan_reduce(
    dims, place, part_at, bufs, sems, deliver, direct=False, far_first=True, lanes=None
):
    n_dp, n_row, n_col = dims
    d, r, c = place
    bits = bits_of(n_row)
    mine_ref, col_ref, row_ref = bufs
    mine_sem, col_send, col_recv, row_send, row_recv = sems
    steps = list(reversed(range(n_dp))) if far_first else list(range(n_dp))
    homes = [dp_order(d, p, n_dp) for p in steps]
    sent = [
        remote(ref, ref, sem.at[0], col_recv.at[0, 0], (d, r, c))
        for ref, sem in ((col_ref, col_send), (row_ref, row_send))
    ]
    held = []

    def send_cols(t):
        for i in range(1, n_col):
            other = (c + i) % n_col
            copy = remote(
                part_at(other, homes[t]),
                col_ref.at[t, i - 1],
                col_send.at[0],
                col_recv.at[t, i - 1],
                (d, r, other),
            )
            copy.start()

    def load_mine():
        for t in range(n_dp):
            keep = pltpu.make_async_copy(part_at(c, homes[t]), mine_ref.at[t], mine_sem.at[t])
            keep.start()
            held.append(keep)

    begin, width = lanes or (0, mine_ref.shape[-1])
    cut = (width // LANES + 1) // 2 * LANES
    spans = [pl.ds(begin, cut), pl.ds(begin + cut, width - cut)]
    marks = [pl.ds(0, cut), pl.ds(cut, width - cut)]

    def order(half):
        return [1 << ((half + s) % bits) for s in range(bits)]

    def send_half(t, half, s):
        dim_order = order(half)
        bit = dim_order[s]
        before = sum(dim_order[:s])
        span = spans[half]
        for x in range(n_row):
            if not x & before and x & bit:
                at = x ^ bit
                copy = remote(
                    mine_ref.at[t, flip_all(r, x, bits), :, span],
                    row_ref.at[t, slot_of(half, s, at), :, marks[half]],
                    row_send.at[0],
                    row_recv.at[t, half, slot_of(half, s, at)],
                    (d, flip(r, bit), c),
                )
                copy.start()

    def slot_of(half, s, at):
        places = []
        before = 0
        for step, bit in enumerate(order(half)):
            before += bit
            places += [(step, y) for y in range(n_row) if not y & before]
        return places.index((s, at))

    def sum_cols(t, send=True):
        if not direct:
            held[t].wait()
        for i in range(1, n_col):
            ref = col_ref.at[t, i - 1]
            remote(
                ref, ref, col_send.at[0], col_recv.at[t, i - 1], (d, r, c)
            ).wait_recv()
        k = homes[t]

        @pl.loop(0, n_row)
        def _(b):
            total = part_at(c, k)[b] if direct else mine_ref[t, b]
            total = total.astype(jnp.float32)
            for i in range(1, n_col):
                total = total + col_ref[t, i - 1, b].astype(jnp.float32)
            mine_ref[t, b] = total.astype(jnp.bfloat16)

        if send:
            send_first(t)

    def send_first(t):
        for half in range(2):
            send_half(t, half, 0)

    def sum_rows(t, s):
        for half in range(2):
            before = sum(order(half)[: s + 1])
            span = spans[half]
            for y in range(n_row):
                if not y & before:
                    slot = slot_of(half, s, y)
                    ref = row_ref.at[t, slot, :, marks[half]]
                    remote(
                        ref,
                        ref,
                        row_send.at[0],
                        row_recv.at[t, half, slot],
                        (d, r, c),
                    ).wait_recv()
                    b = flip_all(r, y, bits)
                    mine_ref[t, b, :, span] = add_low(mine_ref[t, b, :, span], ref[...])
            if s + 1 < bits:
                send_half(t, half, s + 1)
        if s + 1 == bits:
            deliver(steps[t], homes[t], mine_ref.at[t, r])

    def sum_all(between=None):
        ticks = n_dp + bits + 1
        for tick in range(ticks):
            if tick + 1 == ticks and between is not None:
                between()
            if tick < n_dp:
                sum_cols(tick)
            for s in reversed(range(bits)):
                t = tick - 2 - s
                if 0 <= t < n_dp:
                    sum_rows(t, s)

    return types.SimpleNamespace(
        send_cols=send_cols,
        load_mine=load_mine,
        sum_cols=sum_cols,
        send_first=send_first,
        homes=homes,
        sum_rows=sum_rows,
        sum_all=sum_all,
        sent=sent,
    )


def plan_dp_first(dims, place, mine_ref, homes, begin, scratch):
    n_dp, n_row, n_col = dims
    d, r, c = place
    bits = bits_of(n_row)
    in_ref, acc_ref, row_ref, dp_send, dp_recv, row_send, row_recv = scratch
    wide = acc_ref.shape[-1]
    cut = (wide // LANES + 1) // 2 * LANES
    spans = [pl.ds(0, cut), pl.ds(cut, wide - cut)]
    lanes = pl.ds(begin, wide)
    sent = [
        remote(ref, ref, sem.at[0], dp_recv.at[0], (d, r, c))
        for ref, sem in ((in_ref.at[pl.ds(0, n_dp - 1)], dp_send), (row_ref, row_send))
    ]

    def send_dp(t):
        p = n_dp - 1 - t
        if p:
            copy = remote(
                mine_ref.at[t, :, :, lanes],
                in_ref.at[d],
                dp_send.at[0],
                dp_recv.at[d],
                (homes[t], r, c),
            )
            copy.start()

    def order(half):
        return [1 << ((half + s) % bits) for s in range(bits)]

    def steps(half):
        before = 0
        places = []
        for bit in order(half):
            before += bit
            places.append([y for y in range(n_row) if not y & before])
        return places

    def slot_of(half, s, y):
        return sum(len(step) for step in steps(half)[:s]) + steps(half)[s].index(y)

    def send_half(half, s):
        bit = order(half)[s]
        for y in steps(half)[s]:
            slot = slot_of(half, s, y)
            copy = remote(
                acc_ref.at[flip_all(r, y ^ bit, bits), :, spans[half]],
                row_ref.at[slot, :, spans[half]],
                row_send.at[0],
                row_recv.at[half, slot],
                (d, flip(r, bit), c),
            )
            copy.start()

    def sum_dp():
        for p in range(1, n_dp):
            k = homes[n_dp - 1 - p]
            ref = in_ref.at[k]
            remote(ref, ref, dp_send.at[0], dp_recv.at[k], (d, r, c)).wait_recv()

        @pl.loop(0, n_row)
        def _(b):
            total = mine_ref[n_dp - 1, b, :, lanes].astype(jnp.float32)
            for p in range(1, n_dp):
                total = total + in_ref[homes[n_dp - 1 - p], b].astype(jnp.float32)
            acc_ref[b] = total.astype(jnp.bfloat16)

        for half in range(2):
            send_half(half, 0)

    def sum_rows(s):
        for half in range(2):
            for y in steps(half)[s]:
                slot = slot_of(half, s, y)
                ref = row_ref.at[slot, :, spans[half]]
                remote(
                    ref, ref, row_send.at[0], row_recv.at[half, slot], (d, r, c)
                ).wait_recv()
                b = flip_all(r, y, bits)
                acc_ref[b, :, spans[half]] = add_low(acc_ref[b, :, spans[half]], ref[...])
            if s + 1 < bits:
                send_half(half, s + 1)

    return types.SimpleNamespace(
        send_dp=send_dp, sum_dp=sum_dp, sum_rows=sum_rows, total=lambda: acc_ref[r], sent=sent
    )


def dp_first_scratch(dims, rows, width):
    n_dp, n_row, n_col = dims
    dma = pltpu.SemaphoreType.DMA
    low = jnp.bfloat16
    return [
        pltpu.VMEM((n_dp, n_row, rows, width), low),
        pltpu.VMEM((n_row, rows, width), low),
        pltpu.VMEM((max(1, n_row - 1), rows, width), low),
        dma((1,)),
        dma((n_dp,)),
        dma((1,)),
        dma((2, max(1, n_row - 1))),
    ]


def reduce_blocks(dims, place, part_ref, bufs, sems, deliver):
    plan = plan_reduce(dims, place, lambda col, k: part_ref.at[col, k], bufs, sems, deliver)
    for t in range(dims[0]):
        plan.send_cols(t)
    plan.load_mine()
    plan.sum_all()
    return plan.sent


def reduce_scratch(dims, rows, width, copied=True, lanes=None):
    n_dp, n_row, n_col = dims
    dma = pltpu.SemaphoreType.DMA
    low = jnp.bfloat16
    return [
        pltpu.VMEM((n_dp, n_row, rows, width), low),
        pltpu.VMEM((n_dp, max(1, n_col - 1), n_row, rows, width), low),
        pltpu.VMEM((n_dp, max(1, n_row - 1), rows, lanes or width), low),
        dma((n_dp if copied else 1,)),
        dma((1,)),
        dma((n_dp, max(1, n_col - 1))),
        dma((1,)),
        dma((n_dp, 2, max(1, n_row - 1))),
    ]


def token_reduce_kernel(dims, part_ref, out_ref, *scratch):
    n_dp, n_row, n_col = dims
    place = axis_place()
    d, r, c = place
    dp_send, dp_recv, own_sem = scratch[8:]
    greet(True, dims, place)
    late = []

    def deliver(p, k, block):
        if p == 0:
            keep = pltpu.make_async_copy(block, out_ref.at[d], own_sem)
            keep.start()
            late.append(keep.wait)
        else:
            copy = remote(block, out_ref.at[d], dp_send.at[p], dp_recv.at[d], (k, r, c))
            copy.start()
            late.append(copy.wait_send)

    sent = reduce_blocks(dims, place, part_ref, scratch[:3], scratch[3:8], deliver)
    for p in range(1, n_dp):
        k = dp_order(d, p, n_dp)
        ref = out_ref.at[k]
        remote(ref, ref, dp_send.at[p], dp_recv.at[k], (d, r, c)).wait_recv()
    for copy in sent:
        copy.wait_send()
    for wait in late:
        wait()


def token_reduce(parts, dims):
    n_dp = dims[0]
    slots, width = parts.shape[3:]
    dma = pltpu.SemaphoreType.DMA
    return pl.pallas_call(
        functools.partial(token_reduce_kernel, dims),
        out_shape=jax.ShapeDtypeStruct((n_dp, slots, width), jnp.bfloat16),
        in_specs=[pl.BlockSpec(memory_space=pl.ANY)],
        out_specs=pl.BlockSpec(memory_space=pl.ANY),
        scratch_shapes=[*reduce_scratch(dims, slots, width), dma((n_dp,)), dma((n_dp,)), dma],
        compiler_params=pltpu.CompilerParams(
            collective_id=3, has_side_effects=True, vmem_limit_bytes=VMEM_BYTES
        ),
        name="token_reduce",
    )(parts)


def param_reduce_kernel(dims, part_ref, out_ref, *scratch):
    n_dp, n_row, n_col = dims
    place = axis_place()
    d, r, c = place
    dp_send, dp_recv, dp_ref, swap_send, swap_recv, swap_ref, sum_ref = scratch[8:]
    rows = out_ref.shape[1]
    greet(True, dims, place)
    late = []
    kept = []

    def deliver(p, k, block):
        if p == 0:
            kept.append(block)
        else:
            copy = remote(block, dp_ref.at[d], dp_send.at[p], dp_recv.at[d], (k, r, c))
            copy.start()
            late.append(copy)

    sent = reduce_blocks(dims, place, part_ref, scratch[:3], scratch[3:8], deliver)
    total = kept[0][...].astype(jnp.float32)
    for p in range(1, n_dp):
        k = dp_order(d, p, n_dp)
        ref = dp_ref.at[k]
        remote(ref, ref, dp_send.at[p], dp_recv.at[k], (d, r, c)).wait_recv()
        total = total + dp_ref[k].astype(jnp.float32)
    sum_ref[...] = total
    for i in range(n_col):
        swap_ref[i] = sum_ref[i * rows : (i + 1) * rows, :]
    for i in range(1, n_col):
        other = (c + i) % n_col
        copy = remote(
            swap_ref.at[other], out_ref.at[c], swap_send.at[i], swap_recv.at[i], (d, r, other)
        )
        copy.start()
        late.append(copy)
    out_ref[pl.ds(c, 1)] = swap_ref[pl.ds(c, 1)]
    for i in range(1, n_col):
        ref = out_ref.at[(c + n_col - i) % n_col]
        remote(ref, ref, swap_send.at[i], swap_recv.at[i], (d, r, c)).wait_recv()
    for copy in sent:
        copy.wait_send()
    for copy in late:
        copy.wait_send()


def param_reduce(parts, dims):
    n_dp, n_row, n_col = dims
    block_rows, width = parts.shape[3:]
    rows = block_rows // n_col
    dma = pltpu.SemaphoreType.DMA
    return pl.pallas_call(
        functools.partial(param_reduce_kernel, dims),
        out_shape=jax.ShapeDtypeStruct((n_col, rows, width), jnp.float32),
        in_specs=[pl.BlockSpec(memory_space=pl.ANY)],
        out_specs=pl.BlockSpec(memory_space=pltpu.VMEM),
        scratch_shapes=[
            *reduce_scratch(dims, block_rows, width),
            dma((n_dp,)),
            dma((n_dp,)),
            pltpu.VMEM((n_dp, block_rows, width), jnp.bfloat16),
            dma((n_col,)),
            dma((n_col,)),
            pltpu.VMEM((n_col, rows, width), jnp.float32),
            pltpu.VMEM((block_rows, width), jnp.float32),
        ],
        compiler_params=pltpu.CompilerParams(
            collective_id=4, has_side_effects=True, vmem_limit_bytes=VMEM_BYTES
        ),
        name="param_reduce",
    )(parts)


def column(matrix, index):
    return matrix[:, index : index + 1]


def token_masks(lengths_ref, rows, seqs):
    down = lax.broadcasted_iota(jnp.int32, (rows, 1), 0)
    across = lax.broadcasted_iota(jnp.int32, (1, rows), 1)
    end = 0
    doc_down = jnp.zeros((rows, 1), jnp.int32)
    doc_across = jnp.zeros((1, rows), jnp.int32)
    for i in range(seqs):
        end = end + lengths_ref[0, i]
        doc_down = doc_down + (down >= end).astype(jnp.int32)
        doc_across = doc_across + (across >= end).astype(jnp.int32)
    valid = (doc_down < seqs).astype(jnp.float32)
    allowed = (doc_down == doc_across) & (down >= across)
    return valid, allowed


def row_vectors_of(small, first):
    shape = (8, small.shape[1])
    pick = lax.broadcasted_iota(jnp.int32, shape, 1) == first + lax.broadcasted_iota(
        jnp.int32, shape, 0
    )
    return dot(pick.astype(jnp.bfloat16), small, NT)


def half_mask(rows, half):
    return lax.broadcasted_iota(jnp.int32, (rows, LANES), 1) // HEAD == half


def attention_forward(qkv_ref, probs_ref, mixed_ref, allowed, first, last):
    rows = qkv_ref.shape[0]
    low = jnp.bfloat16

    @pl.loop(first, last, unroll=3)
    def _(pair):
        def cols(base):
            return pl.ds(pl.multiple_of(base + pair * LANES, LANES), LANES)

        queries = qkv_ref[:, cols(0)]
        key_heads = qkv_ref[:, cols(D)]
        values = qkv_ref[:, cols(2 * D)]
        mixed = jnp.zeros((rows, LANES), jnp.float32)
        for half in range(LANES // HEAD):
            mask = half_mask(rows, half)
            scores = dot(jnp.where(mask, queries, 0), key_heads, NT) * HEAD ** (-0.5)
            scores = jnp.where(allowed, scores, -1e30)
            top_score = jnp.max(scores, axis=-1, keepdims=True)
            exp_scores = jnp.exp(scores - top_score)
            probs = exp_scores / jnp.sum(exp_scores, axis=-1, keepdims=True)
            probs_ref[pair * (LANES // HEAD) + half] = probs
            mixed = mixed + dot(probs.astype(low), jnp.where(mask, values, 0))
        mixed_ref[:, cols(0)] = mixed.astype(low)


def two_way(first, second):
    top = jnp.maximum(first, second)
    exp_first = jnp.exp(first - top)
    exp_second = jnp.exp(second - top)
    total = exp_first + exp_second
    return exp_first / total, exp_second / total


def attention_backward(qkv_ref, probs_ref, grad_mixed_ref, grad_qkv_ref):
    rows = qkv_ref.shape[0]
    low = jnp.bfloat16

    @pl.loop(0, HEADS * HEAD // LANES, unroll=3)
    def _(pair):
        def cols(base):
            return pl.ds(pl.multiple_of(base + pair * LANES, LANES), LANES)

        queries = qkv_ref[:, cols(0)]
        key_heads = qkv_ref[:, cols(D)]
        values = qkv_ref[:, cols(2 * D)]
        grad_mixed = grad_mixed_ref[:, cols(0)]
        grad_queries = jnp.zeros((rows, LANES), jnp.float32)
        grad_keys = jnp.zeros((rows, LANES), jnp.float32)
        grad_values = jnp.zeros((rows, LANES), jnp.float32)
        for half in range(LANES // HEAD):
            mask = half_mask(rows, half)
            probs = probs_ref[pair * (LANES // HEAD) + half]
            grad_part = jnp.where(mask, grad_mixed, 0)
            grad_values = grad_values + dot(probs.astype(low), grad_part, TN)
            grad_probs = dot(grad_part, values, NT)
            grad_scores = probs * (
                grad_probs - jnp.sum(probs * grad_probs, axis=-1, keepdims=True)
            )
            grad_scores = grad_scores.astype(low)
            grad_queries = grad_queries + dot(grad_scores, jnp.where(mask, key_heads, 0))
            grad_keys = grad_keys + dot(grad_scores, jnp.where(mask, queries, 0), TN)
        grad_qkv_ref[:, cols(0)] = (grad_queries * HEAD ** (-0.5)).astype(low)
        grad_qkv_ref[:, cols(D)] = (grad_keys * HEAD ** (-0.5)).astype(low)
        grad_qkv_ref[:, cols(2 * D)] = grad_values.astype(low)


def layer_kernel(sizes, *refs):
    dims, num_ffn, wide_qkv, wide_out, route_cols, chunks = sizes
    n_dp, n_row, n_col = dims
    low = jnp.bfloat16
    (
        lengths_ref,
        routes_ref,
        prev_ref,
        tokens_ref,
        cotangent_ref,
        w_qkv_ref,
        w_out_ref,
        route_w_ref,
        gains_ref,
        const_ref,
        weight_gu,
        weight_down,
        left_root_gu,
        right_root_down,
        right_root_gu,
        left_root_down,
        result_out,
        grad_tokens_out,
        summed_ref,
        right_sum_out,
        left_sum_out,
        step_out,
        block_out,
        shard_ref,
        turn_ref,
        swap_ref,
        block_ref,
        whole_ref,
        pack_ref,
        expert_ref,
        stage_ref,
        arrived_ref,
        hidden_ref,
        pre_ref,
        qkv_ref,
        probs_ref,
        mixed_ref,
        first_ref,
        came_ref,
        grad_attn_ref,
        grad_mixed_ref,
        grad_qkv_ref,
        part_ref,
        dp_ref,
        end_ref,
        sum_ref,
        gathered_ref,
        root_ref,
        tile_ref,
        half_step_ref,
        lhs_ref,
        right_sum_ref,
        left_sum_ref,
        left_low_ref,
        step_ref,
        result_ref,
        grad_tokens_ref,
        swap_send,
        swap_recv,
        load_sem,
        expert_send,
        expert_recv,
        root_sem,
        tile_sem,
        store_sem,
        done_sem,
        came_send,
        came_recv,
        dp_send,
        dp_recv,
        end_send,
        end_recv,
        *more,
    ) = refs
    halves = n_row == 4
    param_sems, out_sems, token_sems, gather_sems = (more[7 * n : 7 * n + 7] for n in range(4))
    token_scratch, param_scratch, first_scratch = more[28:36], more[36:44], more[44:]
    place = axis_place()
    d, r, c = place
    rows = shard_ref.shape[1]
    depth, slice_wide = pack_ref.shape[2:]
    held, tile = tile_ref.shape[:2]
    wide_col = n_row * slice_wide
    greeted = greet(True, dims, place, all_rows=True, wait=False)
    staged = []
    loads = []
    for m, src in enumerate([weight_gu.at[:, 0], weight_gu.at[:, 1], weight_down]):
        begin = m % 2 * wide_col
        staged.append((m // 2, begin))
        dst = tile_ref.at[m // 2, pl.ds(0, depth), pl.ds(begin, wide_col)]
        copy = pltpu.make_async_copy(src, dst, load_sem.at[m])
        copy.start()
        loads.append(copy)
    roots = [left_root_gu.at[0], left_root_gu.at[1], right_root_down]
    root_loads = []
    for m in range(3):
        copy = pltpu.make_async_copy(roots[m], root_ref.at[m], root_sem.at[m])
        copy.start()
        root_loads.append(copy)
    turn_ref[...] = jnp.zeros_like(turn_ref)
    out_at = wide_qkv + LANES
    at = 0
    for ref in (route_w_ref, gains_ref, const_ref):
        turn_ref[at : at + ref.shape[0], : ref.shape[1]] = ref[...]
        at += ref.shape[0]
    small_shard = turn_ref[...].T[:rows]
    for i in range(n_col):
        shard_ref[i, :, :wide_qkv] = w_qkv_ref[:, i * wide_qkv : (i + 1) * wide_qkv]
        shard_ref[i, :, wide_qkv:out_at] = small_shard
        shard_ref[i, :, out_at:] = w_out_ref[:, i * wide_out : (i + 1) * wide_out]
    pl.semaphore_wait(pltpu.get_barrier_semaphore(), greeted)

    copies = []
    for i in range(1, n_col):
        other = (c + i) % n_col
        copy = remote(
            shard_ref.at[other], swap_ref.at[c], swap_send.at[i], swap_recv.at[i], (d, r, other)
        )
        copy.start()
        copies.append(copy)
    swap_ref[pl.ds(c, 1)] = shard_ref[pl.ds(c, 1)]
    for copy in copies:
        copy.wait()
    for i in range(n_col):
        block_ref[i * rows : (i + 1) * rows, :] = swap_ref[i]
    whole_ref[c, d, r] = block_ref[...].astype(low)

    def plan_params(begin, wide, sems):
        span = pl.ds(begin, wide)

        def slot(col, j, b):
            k = j[1] if isinstance(j, tuple) else dp_order(d, j, n_dp)
            return whole_ref.at[col, k, b, :, span]

        own = whole_ref.at[c, d, r, :, span]
        totals = (
            whole_ref.at[0, pl.ds(0, n_dp - 1), 0, :, span],
            whole_ref.at[0, :, pl.ds(0, n_row - 1), :, span],
            whole_ref.at[pl.ds(0, n_col - 1), :, :, :, span],
        )
        return plan_spread(
            dims,
            place,
            n_dp,
            True,
            None,
            lambda k: own,
            slot,
            sems,
            halves,
            totals,
            n_dp,
            lambda col, g: whole_ref.at[col, :, :, :, span],
        )

    qkv_plan = plan_params(0, out_at, param_sems)
    out_plan = plan_params(out_at, wide_out, out_sems)
    waits = []

    bits = bits_of(n_row)
    near = [1 << dim for dim in range(bits)]

    def pack_experts():
        for copy in loads:
            copy.wait()
        for m, (slot, begin) in enumerate(staged):
            for b in range(n_row):
                at = begin + b * slice_wide
                pack_ref[b, m] = tile_ref[slot, :depth, at : at + slice_wide].astype(low)
        expert_ref[:, pl.ds(pl.multiple_of(r * depth, 16), depth)] = pack_ref[r]

    def send_experts(masks):
        home = pl.ds(pl.multiple_of(r * depth, 16), depth)
        for x in masks:
            other = flip_all(r, x, bits)
            copy = remote(
                pack_ref.at[other],
                expert_ref.at[:, home],
                expert_send.at[x - 1],
                expert_recv.at[x - 1],
                (d, other, c),
            )
            copy.start()
            waits.append(copy.wait_send)

    for plan in (qkv_plan, out_plan):
        plan.start(0)
        plan.send_dp()
    pack_experts()
    send_experts(near)
    for j in range(1, n_dp):
        qkv_plan.start(j)
        qkv_plan.pass_on(j - 1)
    for j in range(1, n_dp):
        out_plan.start(j)
    qkv_plan.pass_on(n_dp - 1)
    for j in range(n_dp):
        out_plan.pass_on(j)
    send_experts([x for x in range(1, n_row) if x not in near])
    for j in range(n_dp):
        qkv_plan.last_arrivals(j)
    for j in range(n_dp):
        qkv_plan.wait_cols(j)

    def whole_cols(col, begin, wide):
        return whole_ref[col, :, :, :, begin : begin + wide].reshape(D, wide)

    total = tokens_ref.shape[0]
    valid, allowed = token_masks(lengths_ref, total, lengths_ref.shape[1])
    small = whole_cols(0, wide_qkv, LANES)
    vectors = row_vectors_of(small, route_cols)
    inputs = tokens_ref[...].astype(jnp.float32)
    scale_one = lax.rsqrt(jnp.mean(inputs * inputs, axis=-1, keepdims=True) + NORM_EPS)
    h_one = (inputs * scale_one * vectors[0:1]).astype(low)
    for i in range(n_col):
        qkv_ref[:, i * wide_qkv : (i + 1) * wide_qkv] = dot(h_one, whole_cols(i, 0, wide_qkv)).astype(
            low
        )
    pairs = HEADS * HEAD // LANES
    attention_forward(qkv_ref, probs_ref, mixed_ref, allowed, 0, pairs // 2)
    for j in range(n_dp):
        out_plan.last_arrivals(j)
    attention_forward(qkv_ref, probs_ref, mixed_ref, allowed, pairs // 2, pairs)
    for j in range(n_dp):
        out_plan.wait_cols(j)
    waits += qkv_plan.sends() + out_plan.sends()
    for i in range(n_col):
        cols = slice(i * wide_out, (i + 1) * wide_out)
        attn_out = dot(mixed_ref[...], whole_cols(i, out_at, wide_out))
        first_ref[:, cols] = tokens_ref[:, cols].astype(jnp.float32) + valid * attn_out
    first_sum = first_ref[...]
    scale_two = lax.rsqrt(jnp.mean(first_sum * first_sum, axis=-1, keepdims=True) + NORM_EPS)
    h_two = (first_sum * scale_two * vectors[1:2]).astype(low)
    experts = prev_ref.shape[0]
    turn_ref[...] = jnp.zeros_like(turn_ref)
    turn_ref[:experts] = prev_ref[...]
    turn_ref[experts : experts + 2] = routes_ref[...].astype(jnp.float32)
    turned = turn_ref[...].T
    logits_all = dot(h_two, small)
    lane = lax.broadcasted_iota(jnp.int32, (total, LANES), 1)
    logits = logits_all + jnp.where(lane < experts, turned, 0.0)
    route_first = column(turned, experts).astype(jnp.int32)
    route_second = column(turned, experts + 1).astype(jnp.int32)
    pick_first = (lane == route_first).astype(jnp.float32)
    pick_second = (lane == route_second).astype(jnp.float32)
    gates = two_way(
        jnp.sum(pick_first * logits, axis=-1, keepdims=True),
        jnp.sum(pick_second * logits, axis=-1, keepdims=True),
    )
    mix_base = num_ffn + 4
    mixes = []
    for i in range(2):
        mixes += two_way(
            column(logits_all, mix_base + 2 * i), column(logits_all, mix_base + 2 * i + 1)
        )
    before = lax.broadcasted_iota(jnp.int32, (total, total), 0) > lax.broadcasted_iota(
        jnp.int32, (total, total), 1
    )
    earlier = dot(before.astype(low), (pick_first + pick_second).astype(low))
    in_slots = []
    for route, pick in ((route_first, pick_first), (route_second, pick_second)):
        slot_index = jnp.sum(earlier * pick, axis=-1, keepdims=True)
        where_in = (route * CAP).astype(jnp.float32) + slot_index
        in_slots.append(jnp.where(route < num_ffn, where_in, -1.0))
    slots = num_ffn * CAP
    slot_lane = lax.broadcasted_iota(jnp.int32, (total, slots), 1).astype(jnp.float32)
    places = [(slot_lane == where_in).astype(low) for where_in in in_slots]
    grad_y = cotangent_ref[...].astype(jnp.float32) * valid
    sent = dot(places[0] + places[1], h_two, TN).astype(low)
    made = dot(places[0], (gates[0] * grad_y).astype(low), TN) + dot(
        places[1], (gates[1] * grad_y).astype(low), TN
    )
    stage_ref[:, :, :D] = sent.reshape(num_ffn, CAP, D)
    stage_ref[:, :, D:] = made.astype(low).reshape(num_ffn, CAP, D)

    def token_slot(col, j, b):
        k = j[1] if isinstance(j, tuple) else dp_order(d, j, n_dp)
        return arrived_ref.at[k, col, b]

    arrived_ref[d, c, r] = stage_ref[d]
    rows_plan = plan_spread(
        dims,
        place,
        n_dp,
        True,
        None,
        lambda k: stage_ref.at[k],
        token_slot,
        token_sems,
        halves,
        (
            arrived_ref.at[pl.ds(0, n_dp - 1), 0, 0],
            arrived_ref.at[:, 0, pl.ds(0, n_row - 1)],
            arrived_ref.at[:, pl.ds(0, n_col - 1)],
        ),
        1,
        lambda col, g: arrived_ref.at[dp_order(d, g, n_dp), col],
    )
    rows_plan.start(0)
    rows_plan.send_dp()
    rows_plan.start(1)
    rows_plan.pass_on(0)

    wides = [right_root_gu.at[0], right_root_gu.at[1], left_root_down]
    tiles = left_root_down.shape[0] // tile
    tile_loads = []

    def load_tile(n):
        if n < 3 * tiles:
            copy = pltpu.make_async_copy(
                wides[n // tiles].at[pl.ds(n % tiles * tile, tile)],
                tile_ref.at[n % held],
                tile_sem.at[n],
            )
            copy.start()
            tile_loads.append(copy)

    for n in range(held):
        load_tile(n)

    def token_back(p, k, block):
        if p == 0:
            came_ref[d] = block[...]
        else:
            copy = remote(block, came_ref.at[d], came_send.at[p - 1], came_recv.at[d], (k, r, c))
            copy.start()
            waits.append(copy.wait_send)

    tokens_plan = plan_reduce(
        dims,
        place,
        lambda col, k: part_ref.at[col, k, :, pl.ds(0, CAP), pl.ds(0, 2 * D)],
        token_scratch[:3],
        token_scratch[3:],
        token_back,
        direct=True,
        far_first=False,
    )

    tall = n_col * n_row * CAP

    def expert_rows(p):
        k = dp_order(d, p, n_dp)
        some = arrived_ref[k].reshape(tall, 2 * D)
        rows_in = some[:, :D]
        grads_in = some[:, D:]
        gate_part = dot(rows_in, expert_ref[0])
        up_part = dot(rows_in, expert_ref[1])
        grad_hidden = dot(grads_in, expert_ref[2])
        sigma = jax.nn.sigmoid(gate_part)
        silu = gate_part * sigma
        hidden = (silu * up_part).astype(low)
        grad_gate = (grad_hidden * up_part * sigma * (1.0 + gate_part * (1.0 - sigma))).astype(low)
        grad_up = (grad_hidden * silu).astype(low)
        hidden_ref[k] = hidden
        pre_ref[k, :, :slice_wide] = grad_gate
        pre_ref[k, :, slice_wide:] = grad_up
        made_rows = dot(hidden, expert_ref[2], NT).astype(low)
        grad_rows = (dot(grad_gate, expert_ref[0], NT) + dot(grad_up, expert_ref[1], NT)).astype(low)
        for col in range(n_col):
            span = slice(col * n_row * CAP, (col + 1) * n_row * CAP)
            part_ref[col, k, :, :CAP, :D] = made_rows[span].reshape(n_row, CAP, D)
            part_ref[col, k, :, :CAP, D : 2 * D] = grad_rows[span].reshape(n_row, CAP, D)
        tokens_plan.send_cols(p)

    def chunk_in(p):
        if p + 2 < n_dp:
            rows_plan.start(p + 2)
        if p + 1 < n_dp:
            rows_plan.pass_on(p + 1)
        if p == 0:
            for x in range(1, n_row):
                home = pl.ds(pl.multiple_of(flip_all(r, x, bits) * depth, 16), depth)
                ref = expert_ref.at[:, home]
                remote(
                    ref, ref, expert_send.at[x - 1], expert_recv.at[x - 1], (d, r, c)
                ).wait_recv()
        rows_plan.last_arrivals(p)
        rows_plan.wait_cols(p)
        expert_rows(p)

    def sums_before(t):
        for s in range(bits):
            if 0 <= t - 1 - s:
                tokens_plan.sum_rows(t - 1 - s, s)

    chunk_in(0)
    for t in range(n_dp - 1):
        if t < n_dp - 2:
            chunk_in(t + 1)
        tokens_plan.sum_cols(t)
        sums_before(t)
    if n_dp > 1:
        chunk_in(n_dp - 1)
    tokens_plan.sum_cols(n_dp - 1)
    sums_before(n_dp - 1)
    waits += rows_plan.sends()
    all_count = n_dp * tall
    all_rows = arrived_ref[:, :, :, :, :D].reshape(all_count, D)
    all_grads = arrived_ref[:, :, :, :, D:].reshape(all_count, D)
    for m in range(2):
        gathered_ref[c * n_row + r, m * D : (m + 1) * D] = dot(
            all_rows,
            pre_ref[:, :, m * slice_wide : (m + 1) * slice_wide].reshape(all_count, slice_wide),
            TN,
        ).astype(low)
    gathered_ref[c * n_row + r, 2 * D :] = dot(
        all_grads, hidden_ref[...].reshape(all_count, slice_wide), TN
    ).astype(low)
    tall = gathered_ref.shape[1] // chunks
    gather = plan_spread(
        dims,
        place,
        chunks,
        False,
        None,
        None,
        lambda col, j, b: gathered_ref.at[col * n_row + b, pl.ds(j * tall, tall)],
        gather_sems,
        halves,
        (
            None,
            gathered_ref.at[pl.ds(0, n_row - 1)],
            gathered_ref.at[pl.ds(0, (n_col - 1) * n_row)],
        ),
        chunks // 3,
        lambda col, g: gathered_ref.at[pl.ds(col * n_row, n_row), pl.ds(g * D, D)],
    )
    gather.start(0)
    for t in range(n_dp, n_dp + bits):
        for s in range(bits):
            if 0 <= t - 1 - s < n_dp:
                tokens_plan.sum_rows(t - 1 - s, s)
        if t == n_dp + bits - 2:
            for j in range(1, chunks):
                gather.start(j)

    gain_one, gain_two = vectors[0:1], vectors[1:2]
    const_rows = [vectors[2:3], vectors[3:4]]
    mixes = [mixes[:2], mixes[2:]]
    routes = [route_first, route_second]
    picks = [pick_first, pick_second]
    cotangent = cotangent_ref[...].astype(jnp.float32)
    grad_y = cotangent * valid
    grad_y_low = grad_y.astype(low)
    first_sum = first_ref[...]
    scale_two = lax.rsqrt(jnp.mean(first_sum * first_sum, axis=-1, keepdims=True) + NORM_EPS)
    normed_two = first_sum * scale_two
    h_two = normed_two * gain_two
    h_two_low = h_two.astype(low)
    const_sel = [
        [(route == num_ffn + 2 + n).astype(jnp.float32) for n in range(2)] for route in routes
    ]
    for p in range(1, n_dp):
        k = dp_order(d, p, n_dp)
        ref = came_ref.at[k]
        remote(ref, ref, came_send.at[p - 1], came_recv.at[k], (d, r, c)).wait_recv()
    expert_out = came_ref[:, :, :D].reshape(slots, D)
    grad_sent = came_ref[:, :, D:].reshape(slots, D)
    moe_out = jnp.zeros_like(first_sum)
    grad_gates = []
    own_weight = jnp.zeros((total, 1), jnp.float32)
    for n in range(2):
        own = (routes[n] == num_ffn + 1).astype(jnp.float32)
        for i in range(2):
            own = own + const_sel[n][i] * mixes[i][0]
        output = dot(places[n], expert_out) + own * h_two
        for i in range(2):
            output = output + const_sel[n][i] * mixes[i][1] * const_rows[i]
        moe_out = moe_out + gates[n] * output
        grad_gates.append(jnp.sum(grad_y * output, axis=-1, keepdims=True))
        own_weight = own_weight + gates[n] * own
    result_ref[...] = (first_sum + valid * moe_out).astype(low)
    copy = pltpu.make_async_copy(result_ref, result_out, done_sem.at[0])
    copy.start()
    waits.append(copy.wait)
    mean_gate = gates[0] * grad_gates[0] + gates[1] * grad_gates[1]
    grad_logits = sum(gates[n] * (grad_gates[n] - mean_gate) * picks[n] for n in range(2))
    grad_own = jnp.sum(grad_y * h_two, axis=-1, keepdims=True)
    const_lanes = jnp.zeros((total, LANES), jnp.float32)
    for i in range(2):
        weight = const_sel[0][i] * gates[0] + const_sel[1][i] * gates[1]
        mix_grads = [
            weight * grad_own,
            weight * jnp.sum(grad_y * const_rows[i], axis=-1, keepdims=True),
        ]
        mean_mix = mixes[i][0] * mix_grads[0] + mixes[i][1] * mix_grads[1]
        for n in range(2):
            grad_mix = mixes[i][n] * (mix_grads[n] - mean_mix)
            grad_logits = jnp.where(lane == num_ffn + 4 + 2 * i + n, grad_mix, grad_logits)
        const_lanes = jnp.where(lane == route_cols + 2 + i, weight * mixes[i][1], const_lanes)
    grad_logits = grad_logits.astype(low)

    grad_h_two = (
        dot(grad_logits, small, NT) + dot(places[0] + places[1], grad_sent) + own_weight * grad_y
    )
    grad_normed = grad_h_two * gain_two
    inner_mean = jnp.mean(grad_normed * normed_two, axis=-1, keepdims=True)
    grad_first = scale_two * (grad_normed - normed_two * inner_mean) + cotangent
    grad_tokens_ref[...] = grad_first
    grad_attn_ref[...] = (valid * grad_first).astype(low)
    grad_small = (
        dot(h_two_low, grad_logits, TN)
        + dot(grad_y_low, const_lanes.astype(low), TN)
        + dot((grad_h_two * normed_two).astype(low), (lane == route_cols + 1).astype(low), TN)
    )
    grad_mixed = jnp.zeros((total, D), jnp.float32)
    for i in range(n_col):
        grad_mixed = grad_mixed + dot(
            grad_attn_ref[:, i * wide_out : (i + 1) * wide_out],
            whole_cols(i, out_at, wide_out),
            NT,
        )
    grad_mixed_ref[...] = grad_mixed.astype(low)
    attention_backward(qkv_ref, probs_ref, grad_mixed_ref, grad_qkv_ref)
    grad_h_one = jnp.zeros((total, D), jnp.float32)
    for i in range(n_col):
        grad_h_one = grad_h_one + dot(
            grad_qkv_ref[:, i * wide_qkv : (i + 1) * wide_qkv], whole_cols(i, 0, wide_qkv), NT
        )
    inputs = tokens_ref[...].astype(jnp.float32)
    scale_one = lax.rsqrt(jnp.mean(inputs * inputs, axis=-1, keepdims=True) + NORM_EPS)
    normed_one = inputs * scale_one
    h_one = (normed_one * gain_one).astype(low)
    grad_normed = grad_h_one * gain_one
    inner_mean = jnp.mean(grad_normed * normed_one, axis=-1, keepdims=True)
    grad_tokens_ref[...] += scale_one * (grad_normed - normed_one * inner_mean)
    copy = pltpu.make_async_copy(grad_tokens_ref, grad_tokens_out, done_sem.at[1])
    copy.start()
    waits.append(copy.wait)
    grad_small = grad_small + dot(
        (grad_h_one * normed_one).astype(low), (lane == route_cols).astype(low), TN
    )

    kept = []
    split = dp_ref.shape[2]

    def param_back(p, k, block):
        if p == 0:
            kept.append(block)
        else:
            block = block.at[:, pl.ds(0, split)]
            copy = remote(block, dp_ref.at[d], dp_send.at[p - 1], dp_recv.at[d], (k, r, c))
            copy.start()
            waits.append(copy.wait_send)

    params_plan = plan_reduce(
        dims,
        place,
        lambda col, k: part_ref.at[col, k],
        param_scratch[:3],
        param_scratch[3:],
        param_back,
        direct=True,
        lanes=(0, split),
    )
    first_plan = plan_dp_first(dims, place, param_scratch[0], params_plan.homes, split, first_scratch)
    finish([copy.wait_send for copy in tokens_plan.sent])
    blocked = part_ref.shape[1:4]
    for i in [*range(1, n_col), 0]:
        col = (c + i) % n_col
        qkv_cols = pl.ds(pl.multiple_of(col * wide_qkv, LANES), wide_qkv)
        out_cols = pl.ds(pl.multiple_of(col * wide_out, LANES), wide_out)
        part_ref[col, :, :, :, :wide_qkv] = (
            dot(h_one, grad_qkv_ref[:, qkv_cols], TN).astype(low).reshape(*blocked, wide_qkv)
        )
        part_ref[col, :, :, :, out_at:] = (
            dot(mixed_ref[...], grad_attn_ref[:, out_cols], TN)
            .astype(low)
            .reshape(*blocked, wide_out)
        )
        part_ref[col, :, :, :, wide_qkv:out_at] = grad_small.astype(low).reshape(*blocked, LANES)
        if i == n_col - 1:
            for t in range(n_dp):
                params_plan.send_cols(t)
    gather.pass_on(0)
    gather.pass_on(1)
    for t in range(n_dp):
        params_plan.sum_cols(t, False)
        first_plan.send_dp(t)
    for j in range(2, chunks * 2 // 3):
        gather.pass_on(j)
    for t in range(n_dp):
        params_plan.send_first(t)
    for j in range(chunks * 2 // 3, chunks):
        gather.pass_on(j)

    owner = r * n_col + c
    right_rows = right_sum_ref.shape[1]
    left_rows = left_sum_ref.shape[0]
    stores = []

    def store(m, kind, src, dst):
        copy = pltpu.make_async_copy(src, dst, store_sem.at[m, kind])
        copy.start()
        stores.append(copy)

    def shampoo_products(m):
        for j in range(m * chunks // 3, (m + 1) * chunks // 3):
            gather.last_arrivals(j)
        for j in range(m * chunks // 3, (m + 1) * chunks // 3):
            gather.wait_cols(j)
        span = pl.ds(m * D, D)
        home = pl.ds(pl.multiple_of(m * D + r * depth, 16), depth)
        for b in range(n_row):
            store(m, 3 + b, gathered_ref.at[c * n_row + b, home], block_out.at[m, b])
        root_loads[m].wait()
        lhs_ref[:right_rows] = gathered_ref[owner, span].T
        lhs_ref[right_rows:] = root_ref[m].astype(low)
        left_sum_ref[...] = jnp.zeros_like(left_sum_ref)

        @pl.loop(0, n_row * n_col, unroll=2)
        def _(q):
            cols = pl.ds(pl.multiple_of(q * slice_wide, slice_wide), slice_wide)
            block = gathered_ref[q, span]
            made = dot(lhs_ref[...], block)
            right_sum_ref[m, :, cols] = (0.5 * made[:right_rows]).astype(low)
            half_step_ref[:, cols] = made[right_rows:].astype(low)
            some = pl.ds(pl.multiple_of(m * D + owner * left_rows, 16), left_rows)
            left_sum_ref[...] += dot(gathered_ref[q, some], block, NT)

        left_low_ref[m] = (0.5 * left_sum_ref[...]).astype(low)
        store(m, 0, right_sum_ref.at[m], right_sum_out.at[m])
        store(m, 1, left_low_ref.at[m], left_sum_out.at[m])
        for t in range(tiles):
            n = m * tiles + t
            tile_loads[n].wait()
            step = dot(half_step_ref[...], tile_ref[n % held].astype(low), NT)
            step_ref[m, :, t * tile : (t + 1) * tile] = (SHAMPOO_RATE * step).astype(low)
            load_tile(n + held)
        store(m, 2, step_ref.at[m], step_out.at[m])

    shampoo_products(0)
    shampoo_products(1)
    for t in range(n_dp):
        params_plan.sum_rows(t, 0)
    first_plan.sum_dp()
    shampoo_products(2)
    for s in range(1, bits):
        for t in range(n_dp):
            params_plan.sum_rows(t, s)
    for s in range(bits):
        first_plan.sum_rows(s)
    sums = kept[0][:, :split].astype(jnp.float32)
    for p in range(1, n_dp):
        k = dp_order(d, p, n_dp)
        ref = dp_ref.at[k]
        remote(ref, ref, dp_send.at[p - 1], dp_recv.at[k], (d, r, c)).wait_recv()
        sums = sums + dp_ref[k].astype(jnp.float32)
    sum_ref[:, :split] = sums
    sum_ref[:, split:] = first_plan.total().astype(jnp.float32)
    for i in range(n_col):
        end_ref[i] = sum_ref[i * rows : (i + 1) * rows, :]
    for i in range(1, n_col):
        other = (c + i) % n_col
        copy = remote(
            end_ref.at[other], summed_ref.at[c], end_send.at[i], end_recv.at[i], (d, r, other)
        )
        copy.start()
        waits.append(copy.wait_send)
    summed_ref[pl.ds(c, 1)] = end_ref[pl.ds(c, 1)]
    for i in range(1, n_col):
        ref = summed_ref.at[(c + n_col - i) % n_col]
        remote(ref, ref, end_send.at[i], end_recv.at[i], (d, r, c)).wait_recv()
    waits += gather.sends()
    waits += [copy.wait for copy in stores]
    finish([copy.wait_send for copy in params_plan.sent + first_plan.sent])
    finish(waits)


def layer(
    lengths,
    routes,
    prev_logits,
    tokens,
    cotangent,
    w_qkv,
    w_out,
    route_w,
    gains,
    const_vec,
    weight_gu,
    weight_down,
    left_root_gu,
    right_root_down,
    right_root_gu,
    left_root_down,
    dims,
    widths,
):
    n_dp, n_row, n_col = dims
    low = jnp.bfloat16
    f32 = jnp.float32
    total = tokens.shape[0]
    rows = w_qkv.shape[0]
    wide = widths[0] + widths[1] + LANES
    num_ffn = prev_logits.shape[0] - 4
    depth, wide_col = weight_down.shape
    slice_wide = wide_col // n_row
    block_rows = n_col * rows
    wide_rows, wide_cols = left_root_down.shape
    right_rows = wide_cols // n_row // n_col
    left_rows = D // n_row // n_col
    tile = 2 * LANES
    split = wide // 2 // LANES * LANES
    chunks = 6
    dma = pltpu.SemaphoreType.DMA
    vmem = pl.BlockSpec(memory_space=pltpu.VMEM)
    hbm = pl.BlockSpec(memory_space=pl.ANY)
    whole = (n_col, n_dp, n_row, block_rows, wide)
    assert depth <= tile and 2 * wide_col <= wide_cols and wide >= 2 * D
    return pl.pallas_call(
        functools.partial(layer_kernel, (dims, num_ffn, *widths, chunks)),
        out_shape=[
            jax.ShapeDtypeStruct((total, D), low),
            jax.ShapeDtypeStruct((total, D), f32),
            jax.ShapeDtypeStruct((n_col, rows, wide), f32),
            jax.ShapeDtypeStruct((3, right_rows, wide_cols), low),
            jax.ShapeDtypeStruct((3, left_rows, D), low),
            jax.ShapeDtypeStruct((3, depth, wide_rows), low),
            jax.ShapeDtypeStruct((3, n_row, depth, slice_wide), low),
        ],
        in_specs=[pl.BlockSpec(memory_space=pltpu.SMEM)] + [vmem] * 9 + [hbm] * 6,
        out_specs=[hbm, hbm, vmem] + [hbm] * 4,
        scratch_shapes=[
            pltpu.VMEM((n_col, rows, wide), f32),
            pltpu.VMEM((LANES, LANES), f32),
            pltpu.VMEM((n_col, rows, wide), f32),
            pltpu.VMEM((block_rows, wide), f32),
            pltpu.VMEM(whole, low),
            pltpu.VMEM((n_row, 3, depth, slice_wide), low),
            pltpu.VMEM((3, n_row * depth, slice_wide), low),
            pltpu.VMEM((num_ffn, CAP, 2 * D), low),
            pltpu.VMEM((n_dp, n_col, n_row, CAP, 2 * D), low),
            pltpu.VMEM((n_dp, n_col * n_row * CAP, slice_wide), low),
            pltpu.VMEM((n_dp, n_col * n_row * CAP, 2 * slice_wide), low),
            pltpu.VMEM((total, 3 * D), low),
            pltpu.VMEM((HEADS, total, total), f32),
            pltpu.VMEM((total, D), low),
            pltpu.VMEM((total, D), f32),
            pltpu.VMEM((n_dp, CAP, 2 * D), low),
            pltpu.VMEM((total, D), low),
            pltpu.VMEM((total, D), low),
            pltpu.VMEM((total, 3 * D), low),
            pltpu.VMEM(whole, low),
            pltpu.VMEM((n_dp, block_rows, split), low),
            pltpu.VMEM((n_col, rows, wide), f32),
            pltpu.VMEM((block_rows, wide), f32),
            pltpu.VMEM((n_col * n_row, 3 * D, slice_wide), low),
            pltpu.VMEM((3, depth, D), f32),
            pltpu.VMEM((2, tile, wide_cols), f32),
            pltpu.VMEM((depth, wide_cols), low),
            pltpu.VMEM((right_rows + depth, D), low),
            pltpu.VMEM((3, right_rows, wide_cols), low),
            pltpu.VMEM((left_rows, D), f32),
            pltpu.VMEM((3, left_rows, D), low),
            pltpu.VMEM((3, depth, wide_rows), low),
            pltpu.VMEM((total, D), low),
            pltpu.VMEM((total, D), f32),
            dma((n_col,)),
            dma((n_col,)),
            dma((3,)),
            dma((max(1, n_row - 1),)),
            dma((max(1, n_row - 1),)),
            dma((3,)),
            dma((3 * wide_rows // tile,)),
            dma((3, 3 + n_row)),
            dma((2,)),
            dma((n_dp,)),
            dma((n_dp,)),
            dma((n_dp,)),
            dma((n_dp,)),
            dma((n_col,)),
            dma((n_col,)),
            *spread_sems(dims, n_dp, False, n_row == 4, True, 1),
            *spread_sems(dims, n_dp, False, n_row == 4, True, 1),
            *spread_sems(dims, n_dp, False, n_row == 4, True, n_dp),
            *spread_sems(dims, chunks, False, n_row == 4, True, 3),
            *reduce_scratch(dims, CAP, 2 * D, copied=False),
            *reduce_scratch(dims, block_rows, wide, copied=False, lanes=split),
            *dp_first_scratch(dims, block_rows, wide - split),
        ],
        compiler_params=pltpu.CompilerParams(
            collective_id=5, has_side_effects=True, vmem_limit_bytes=VMEM_BYTES
        ),
        name="layer",
    )(
        lengths,
        routes,
        prev_logits,
        tokens,
        cotangent,
        w_qkv,
        w_out,
        route_w,
        gains,
        const_vec,
        weight_gu,
        weight_down,
        left_root_gu,
        right_root_down,
        right_root_gu,
        left_root_down,
    )


def norm_forward(values, gain_vec):
    norm_scale = lax.rsqrt(jnp.mean(values * values, axis=-1, keepdims=True) + NORM_EPS)
    normed = values * norm_scale
    return (normed * gain_vec, normed, norm_scale)


def norm_backward(grad_out, normed, norm_scale, gain_vec):
    grad_normed = grad_out * gain_vec
    inner_mean = jnp.mean(grad_normed * normed, axis=-1, keepdims=True)
    return (norm_scale * (grad_normed - normed * inner_mean), jnp.sum(grad_out * normed, axis=0))


def attention_probs(queries, key_heads, allowed):
    scores = jnp.einsum(
        "qhd,khd->hqk", queries, key_heads, preferred_element_type=jnp.float32
    ) * HEAD ** (-0.5)
    scores = jnp.where(allowed[None], scores, -1e30)
    top_score = jnp.max(scores, axis=-1, keepdims=True)
    exp_scores = jnp.exp(scores - top_score)
    return exp_scores / jnp.sum(exp_scores, axis=-1, keepdims=True)


def diag_update(weight, grad, state, rate):
    new_state = 0.5 * state + 0.5 * grad * grad
    return (new_state, weight - rate * grad / (jnp.sqrt(new_state) + 1e-08))


def diagonal_updates(widths, n_col, summed_ref, in_refs, out_refs, turn_ref):
    wide_qkv, wide_out, route_cols = widths
    rows = summed_ref.shape[1]
    rates = (D ** (-0.5), HEAD ** (-0.5), (4 * D) ** (-0.5), 0.3, 0.5)

    def update(n, cols, grad):
        weight, state = in_refs[2 * n], in_refs[2 * n + 1]
        grad_ref, moment_ref, new_ref = out_refs[3 * n : 3 * n + 3]
        moment, new = diag_update(weight[:, cols], grad, state[:, cols], rates[n])
        grad_ref[:, cols] = grad
        moment_ref[:, cols] = moment
        new_ref[:, cols] = new

    for i in range(n_col):
        update(0, pl.ds(i * wide_qkv, wide_qkv), summed_ref[i, :, :wide_qkv])
        update(1, pl.ds(i * wide_out, wide_out), summed_ref[i, :, wide_qkv + LANES :])
    turn_ref[...] = jnp.zeros_like(turn_ref)
    turn_ref[:rows] = summed_ref[0, :, wide_qkv : wide_qkv + LANES]
    turned = turn_ref[...].T
    whole = pl.ds(0, rows)
    update(2, whole, turned[:route_cols, :rows])
    update(3, whole, turned[route_cols : route_cols + 2, :rows])
    update(4, whole, turned[route_cols + 2 : route_cols + 4, :rows])


def finish_kernel(sizes, *refs):
    n_col, widths = sizes
    refs, diag = [*refs[:13], *refs[38:]], refs[13:38]
    (
        right_sum,
        left_sum,
        step,
        block,
        left_gu,
        right_down,
        right_gu,
        left_down,
        weight_gu,
        weight_down,
        result,
        grad_tokens,
        summed,
        out_grad_gu,
        out_grad_down,
        out_left_gu,
        out_right_down,
        out_right_gu,
        out_left_down,
        out_weight_gu,
        out_weight_down,
        out_result,
        out_grad_tokens,
        right_sum_buf,
        left_sum_buf,
        step_buf,
        block_buf,
        right_buf,
        left_buf,
        weight_buf,
        grad_buf,
        result_buf,
        tokens_buf,
        turn_buf,
        *diag_buf,
        in_sem,
        out_sem,
        diag_sem,
    ) = refs
    pairs = zip([summed, *diag[:10]], diag_buf)
    small = [
        pltpu.make_async_copy(src, dst, diag_sem.at[n]) for n, (src, dst) in enumerate(pairs)
    ]
    for copy in small:
        copy.start()
    mats = range(3)
    f32 = jnp.float32
    n_row, _, slice_wide = block_buf.shape[1:]
    lefts = [left_gu.at[0], left_gu.at[1], right_down]
    rights = [right_gu.at[0], right_gu.at[1], left_down]
    weights = [weight_gu.at[:, 0], weight_gu.at[:, 1], weight_down]
    out_lefts = [out_left_gu.at[0], out_left_gu.at[1], out_right_down]
    out_rights = [out_right_gu.at[0], out_right_gu.at[1], out_left_down]
    out_weights = [out_weight_gu.at[:, 0], out_weight_gu.at[:, 1], out_weight_down]
    out_grads = [out_grad_gu.at[:, 0], out_grad_gu.at[:, 1], out_grad_down]
    loads = {}

    def load(m, kind, src, dst):
        copy = pltpu.make_async_copy(src, dst, in_sem.at[m, kind])
        copy.start()
        loads[m, kind] = copy

    stores = []

    def store(m, kind, src, dst):
        copy = pltpu.make_async_copy(src, dst, out_sem.at[m, kind])
        copy.start()
        stores.append(copy)

    for m in mats:
        load(m, 0, right_sum.at[m], right_sum_buf.at[m])
        load(m, 1, rights[m], right_buf.at[m])
        load(m, 2, block.at[m], block_buf.at[m])
        load(m, 3, step.at[m], step_buf.at[m])
        load(m, 4, weights[m], weight_buf.at[m])
        load(m, 5, left_sum.at[m], left_sum_buf.at[m])
        load(m, 6, lefts[m], left_buf.at[m])
    load(0, 7, result, result_buf)
    load(1, 7, grad_tokens, tokens_buf)
    for copy in small:
        copy.wait()
    diagonal_updates(widths, n_col, diag_buf[0], diag_buf[1:11], diag_buf[11:], turn_buf)
    for n, (src, dst) in enumerate(zip(diag_buf[11:], diag[10:])):
        copy = pltpu.make_async_copy(src, dst, diag_sem.at[11 + n])
        copy.start()
        stores.append(copy)
    for m in mats:
        loads[m, 0].wait()
        loads[m, 1].wait()
        right_buf[m] = 0.5 * right_buf[m] + right_sum_buf[m].astype(f32)
        store(m, 0, right_buf.at[m], out_rights[m])
        loads[m, 2].wait()
        for b in range(n_row):
            grad_buf[m, :, b * slice_wide : (b + 1) * slice_wide] = block_buf[m, b].astype(f32)
        store(m, 1, grad_buf.at[m], out_grads[m])
        loads[m, 3].wait()
        loads[m, 4].wait()
        weight_buf[m] = weight_buf[m] - step_buf[m].astype(f32)
        store(m, 2, weight_buf.at[m], out_weights[m])
        loads[m, 5].wait()
        loads[m, 6].wait()
        left_buf[m] = 0.5 * left_buf[m] + left_sum_buf[m].astype(f32)
        store(m, 3, left_buf.at[m], out_lefts[m])
    loads[0, 7].wait()
    store(0, 4, result_buf, out_result)
    loads[1, 7].wait()
    store(1, 4, tokens_buf, out_grad_tokens)
    for copy in stores:
        copy.wait()


def finish_update(
    products,
    left_gu,
    right_down,
    right_gu,
    left_down,
    weight_gu,
    weight_down,
    result,
    grad_tokens,
    summed,
    diag_in,
    n_col,
    widths,
):
    f32 = jnp.float32
    dma = pltpu.SemaphoreType.DMA
    hbm = pl.BlockSpec(memory_space=pl.ANY)
    right_sum, left_sum, step, block = products
    args = (
        *products,
        left_gu,
        right_down,
        right_gu,
        left_down,
        weight_gu,
        weight_down,
        result,
        grad_tokens,
        summed,
        *diag_in,
    )
    outs = [weight for weight in diag_in[::2] for _ in range(3)]
    outs += [weight_gu, weight_down, left_gu, right_down, right_gu, left_down]
    outs += [weight_gu, weight_down, result, grad_tokens]
    return pl.pallas_call(
        functools.partial(finish_kernel, (n_col, widths)),
        out_shape=[jax.ShapeDtypeStruct(like.shape, like.dtype) for like in outs],
        in_specs=[hbm] * 23,
        out_specs=[hbm] * 25,
        scratch_shapes=[
            pltpu.VMEM(right_sum.shape, right_sum.dtype),
            pltpu.VMEM(left_sum.shape, left_sum.dtype),
            pltpu.VMEM(step.shape, step.dtype),
            pltpu.VMEM(block.shape, block.dtype),
            pltpu.VMEM(right_sum.shape, f32),
            pltpu.VMEM(left_sum.shape, f32),
            pltpu.VMEM(step.shape, f32),
            pltpu.VMEM(step.shape, f32),
            pltpu.VMEM(result.shape, result.dtype),
            pltpu.VMEM(grad_tokens.shape, f32),
            pltpu.VMEM((LANES, LANES), f32),
            *[pltpu.VMEM(like.shape, f32) for like in (summed, *diag_in, *outs[:15])],
            dma((3, 8)),
            dma((3, 5)),
            dma((26,)),
        ],
        compiler_params=pltpu.CompilerParams(vmem_limit_bytes=VMEM_BYTES),
        name="finish",
    )(*args)


def shampoo_plain(
    grads,
    left_root_gu,
    right_root_down,
    right_root_gu,
    left_root_down,
    left_gu,
    right_down,
    right_gu,
    left_down,
    weight_gu,
    weight_down,
    n_row,
    n_col,
):
    low = jnp.bfloat16
    blocks, _, slice_wide = grads.shape
    model = left_root_gu.shape[2]
    r = lax.axis_index("row")
    c = lax.axis_index("col")
    owner = r * n_col + c
    left_rows = right_down.shape[0]
    right_rows = left_down.shape[0]
    product = functools.partial(jnp.einsum, preferred_element_type=jnp.float32)
    whole = grads.reshape(blocks, 3, model, slice_wide).transpose(1, 2, 0, 3).reshape(3, model, -1)
    mine_left = lax.dynamic_slice_in_dim(whole, owner * left_rows, left_rows, 1)
    mine_right = lax.dynamic_slice_in_dim(whole, owner * right_rows, right_rows, 2)
    left_sum = 0.5 * product("mif,mjf->mij", mine_left, whole)
    right_sum = 0.5 * product("mdi,mdj->mij", mine_right, whole)
    roots = jnp.concatenate([left_root_gu, right_root_down[None]]).astype(low)
    wides = jnp.concatenate([right_root_gu, left_root_down[None]]).astype(low)
    step = product("mid,mdf->mif", roots, whole).astype(low)
    step = SHAMPOO_RATE * product("mif,mjf->mij", step, wides)
    depth, wide_rows = weight_down.shape
    block = lax.dynamic_slice(whole, (0, r * depth, c * wide_rows), (3, depth, wide_rows))
    block = block.astype(jnp.float32)
    return (
        block[:2].transpose(1, 0, 2),
        block[2],
        0.5 * left_gu + left_sum[:2],
        0.5 * right_down + left_sum[2],
        0.5 * right_gu + right_sum[:2],
        0.5 * left_down + right_sum[2],
        weight_gu - step[:2].transpose(1, 0, 2),
        weight_down - step[2],
    )


def body_tiled(
    tokens,
    lengths,
    routes,
    prev_logits,
    cotangent,
    w_qkv,
    w_out,
    route_w,
    gains,
    const_vec,
    stat_qkv,
    stat_out,
    stat_route,
    stat_gains,
    stat_const,
    w_gate_up,
    w_down,
    left_gu,
    right_gu,
    left_down,
    right_down,
    left_root_gu,
    right_root_gu,
    left_root_down,
    right_root_down,
):
    dims = mesh_sizes()
    n_col = dims[2]
    wide_qkv = w_qkv.shape[1] // n_col
    wide_out = w_out.shape[1] // n_col
    widths = (wide_qkv, wide_out, route_w.shape[1])
    result, grad_input, summed, *products = layer(
        lengths,
        routes.T,
        prev_logits.T,
        tokens,
        cotangent,
        w_qkv,
        w_out,
        route_w.T,
        gains,
        const_vec,
        w_gate_up[0],
        w_down[0].T,
        left_root_gu[0],
        right_root_down[0],
        right_root_gu[0],
        left_root_down[0],
        dims,
        widths,
    )
    outs = finish_update(
        products,
        left_gu[0],
        right_down[0],
        right_gu[0],
        left_down[0],
        w_gate_up[0],
        w_down[0].T,
        result,
        grad_input,
        summed,
        [
            w_qkv,
            stat_qkv,
            w_out,
            stat_out,
            route_w.T,
            stat_route.T,
            gains,
            stat_gains,
            const_vec,
            stat_const,
        ],
        n_col,
        widths,
    )
    diag = list(outs[:15])
    diag[6:9] = [part.T for part in diag[6:9]]
    (
        grad_gate_up,
        grad_down,
        new_left_gu,
        new_right_down,
        new_right_gu,
        new_left_down,
        new_gate_up,
        new_down,
        result,
        grad_input,
    ) = outs[15:]
    return (
        result,
        grad_input,
        *diag,
        grad_gate_up[None],
        grad_down.T[None],
        new_left_gu[None],
        new_right_gu[None],
        new_left_down[None],
        new_right_down[None],
        new_gate_up[None],
        new_down.T[None],
    )


def body(
    tokens,
    lengths,
    routes,
    prev_logits,
    cotangent,
    w_qkv,
    w_out,
    route_w,
    gains,
    const_vec,
    stat_qkv,
    stat_out,
    stat_route,
    stat_gains,
    stat_const,
    w_gate_up,
    w_down,
    left_gu,
    right_gu,
    left_down,
    right_down,
    left_root_gu,
    right_root_gu,
    left_root_down,
    right_root_down,
):
    dims = mesh_sizes()
    n_dp, n_row, n_col = dims
    low = jnp.bfloat16
    row_total = tokens.shape[0]
    total_experts = prev_logits.shape[1]
    num_ffn = total_experts - 4
    seq_count = lengths.shape[1]
    shard_rows = w_qkv.shape[0]
    wide_qkv = w_qkv.shape[1] // n_col
    wide_out = w_out.shape[1] // n_col
    route_cols = route_w.shape[1]
    wide = wide_qkv + wide_out + LANES

    def by_col(matrix):
        return matrix.reshape(matrix.shape[0], n_col, -1).transpose(1, 0, 2)

    def small_block(route_part, gain_part, const_part):
        together = jnp.concatenate([route_part, gain_part.T, const_part.T], axis=1)
        return jnp.pad(together, ((0, 0), (0, LANES - together.shape[1])))

    small = small_block(route_w, gains, const_vec)
    shard = jnp.concatenate(
        [by_col(w_qkv), by_col(w_out), jnp.broadcast_to(small[None], (n_col, shard_rows, LANES))],
        axis=2,
    )
    whole = param_gather(shard, dims).reshape(n_col, D, wide)
    full_qkv = [whole[i, :, :wide_qkv] for i in range(n_col)]
    full_out = [whole[i, :, wide_qkv : wide_qkv + wide_out] for i in range(n_col)]
    full_small = whole[0, :, wide_qkv + wide_out :]
    full_route = full_small[:, :route_cols]
    row_vectors = full_small[:, route_cols : route_cols + 4].T.astype(jnp.float32)
    gain_one, gain_two, const_rows = row_vectors[0], row_vectors[1], row_vectors[2:4]

    row_depth = w_gate_up.shape[1]
    col_width = w_gate_up.shape[3]
    slice_wide = col_width // n_row
    gu_slices = w_gate_up[0].astype(low).reshape(row_depth, 2, n_row, slice_wide)
    gu_slices = gu_slices.transpose(2, 0, 1, 3)
    gu_own = lax.all_to_all(gu_slices, "row", split_axis=0, concat_axis=0, tiled=True)
    gu_own = gu_own.reshape(n_row * row_depth, 2 * slice_wide)
    down_slices = w_down[0].astype(low).reshape(n_row, slice_wide, row_depth)
    down_own = lax.all_to_all(down_slices, "row", split_axis=0, concat_axis=0, tiled=True)
    down_own = down_own.transpose(1, 0, 2).reshape(slice_wide, n_row * row_depth)

    positions = jnp.arange(row_total, dtype=jnp.int32)
    seq_ends = jnp.cumsum(lengths[0])
    doc_index = jnp.sum((positions[:, None] >= seq_ends[None, :]).astype(jnp.int32), axis=1)
    valid_rows = (doc_index < seq_count).astype(jnp.float32)[:, None]
    allowed = (doc_index[:, None] == doc_index[None, :]) & (
        positions[:, None] >= positions[None, :]
    )
    inputs = tokens.astype(jnp.float32)
    h_one, normed_one, scale_one = norm_forward(inputs, gain_one)
    h_one_low = h_one.astype(low)
    qkv_rows = jnp.concatenate([dot(h_one_low, part) for part in full_qkv], axis=1).astype(low)
    qkv_rows = qkv_rows.reshape(row_total, 3, HEADS, HEAD)
    queries, key_heads, values = (qkv_rows[:, 0], qkv_rows[:, 1], qkv_rows[:, 2])
    softmax_probs = attention_probs(queries, key_heads, allowed)
    probs_low = softmax_probs.astype(low)
    mixed_heads = jnp.einsum("hqk,khd->qhd", probs_low, values, preferred_element_type=jnp.float32)
    mixed_heads = mixed_heads.reshape(row_total, D).astype(low)
    attn_out = jnp.concatenate([dot(mixed_heads, part) for part in full_out], axis=1)
    first_sum = inputs + valid_rows * attn_out
    h_two, normed_two, scale_two = norm_forward(first_sum, gain_two)
    h_two_low = h_two.astype(low)
    logits_all = dot(h_two_low, full_route)
    logits = logits_all[:, :total_experts] + prev_logits
    pick_table = (
        routes[:, :, None] == jnp.arange(total_experts, dtype=jnp.int32)[None, None, :]
    ).astype(jnp.float32)
    chosen = jnp.sum(pick_table * logits[:, None, :], axis=-1)
    gate_weights = jax.nn.softmax(chosen, axis=-1)
    const_mix = jax.nn.softmax(logits_all[:, total_experts:].reshape(row_total, 2, 2), axis=-1)

    earlier = dot(
        (positions[:, None] > positions[None, :]).astype(low),
        jnp.sum(pick_table, axis=1).astype(low),
    )
    slot_index = jnp.sum(earlier[:, None, :] * pick_table, axis=-1).astype(jnp.int32)
    where_in = jnp.where(routes < num_ffn, routes * CAP + slot_index, -1)
    slot_ids = jnp.arange(num_ffn * CAP, dtype=jnp.int32)
    place_first = where_in[:, 0:1] == slot_ids[None, :]
    place_second = where_in[:, 1:2] == slot_ids[None, :]
    place_both = (place_first | place_second).astype(low)
    slot_gate = jnp.sum(
        place_first.astype(jnp.float32) * gate_weights[:, 0:1]
        + place_second.astype(jnp.float32) * gate_weights[:, 1:2],
        axis=0,
    )
    grad_y = cotangent.astype(jnp.float32) * valid_rows
    sent_rows = dot(place_both, h_two_low, TN).astype(low)
    grad_made = (slot_gate[:, None] * dot(place_both, grad_y.astype(low), TN)).astype(low)
    sent_both = jnp.concatenate(
        [sent_rows.reshape(num_ffn, CAP, D), grad_made.reshape(num_ffn, CAP, D)], axis=2
    )

    arrived = token_gather(sent_both, dims).reshape(-1, 2 * D)
    rows_in = arrived[:, :D]
    grads_in = arrived[:, D:]
    pre_act = dot(rows_in, gu_own)
    gate_part = pre_act[:, :slice_wide]
    up_part = pre_act[:, slice_wide:]
    sigma = jax.nn.sigmoid(gate_part)
    silu = gate_part * sigma
    hidden = (silu * up_part).astype(low)
    made_rows = dot(hidden, down_own).astype(low)
    grad_hidden = dot(grads_in, down_own, NT)
    grad_pre = jnp.concatenate(
        [
            grad_hidden * up_part * sigma * (1.0 + gate_part * (1.0 - sigma)),
            grad_hidden * silu,
        ],
        axis=1,
    ).astype(low)
    grad_rows = dot(grad_pre, gu_own, NT).astype(low)
    parts_back = jnp.concatenate([made_rows, grad_rows], axis=1)
    parts_back = parts_back.reshape(n_col, n_dp, n_row, CAP, 2 * D)
    came_back = token_reduce(parts_back, dims).reshape(num_ffn * CAP, 2 * D)
    expert_out = came_back[:, :D]
    grad_sent = came_back[:, D:]

    grad_gu_own = dot(rows_in, grad_pre, TN).astype(low)
    grad_down_own = dot(hidden, grads_in, TN).astype(low)
    grads_own = jnp.concatenate(
        [grad_gu_own[:, :slice_wide], grad_gu_own[:, slice_wide:], grad_down_own.T], axis=0
    )
    gathered = plane_gather(grads_own.reshape(4, -1, slice_wide), dims)
    gathered = gathered.reshape(n_col * n_row, 3 * D, slice_wide)

    is_ffn_first = dot(place_first.astype(low), expert_out)
    is_ffn_second = dot(place_second.astype(low), expert_out)
    picked = jnp.stack([is_ffn_first, is_ffn_second], axis=1)
    copy_sel = (routes == num_ffn + 1).astype(jnp.float32)
    const_sel = (
        routes[:, :, None] == num_ffn + 2 + jnp.arange(2, dtype=jnp.int32)[None, None, :]
    ).astype(jnp.float32)
    const_out = (
        const_mix[:, :, 0:1] * h_two[:, None, :] + const_mix[:, :, 1:2] * const_rows[None, :, :]
    )
    outputs = (
        picked
        + copy_sel[:, :, None] * h_two[:, None, :]
        + const_sel[:, :, 0:1] * const_out[:, None, 0, :]
        + const_sel[:, :, 1:2] * const_out[:, None, 1, :]
    )
    moe_out = valid_rows * jnp.sum(gate_weights[:, :, None] * outputs, axis=1)
    result = (first_sum + moe_out).astype(low)
    grad_gate = jnp.sum(grad_y[:, None, :] * outputs, axis=-1)
    grad_chosen = gate_weights * (
        grad_gate - jnp.sum(gate_weights * grad_gate, axis=-1, keepdims=True)
    )
    grad_logits = jnp.sum(grad_chosen[:, :, None] * pick_table, axis=1)
    const_weight = jnp.sum(const_sel * gate_weights[:, :, None], axis=1)
    mix_first = const_weight * jnp.sum(grad_y * h_two, axis=-1, keepdims=True)
    mix_second = const_weight * jnp.stack(
        [jnp.sum(grad_y * const_rows[0], axis=-1), jnp.sum(grad_y * const_rows[1], axis=-1)], axis=1
    )
    grad_mix = jnp.stack([mix_first, mix_second], axis=-1)
    grad_mix_logits = const_mix * (grad_mix - jnp.sum(const_mix * grad_mix, axis=-1, keepdims=True))
    grad_logits_all = jnp.concatenate(
        [grad_logits, grad_mix_logits.reshape(row_total, 4)], axis=1
    ).astype(low)
    grad_route_full = dot(h_two_low, grad_logits_all, TN)
    const_scale = const_weight * const_mix[:, :, 1]
    grad_const_full = jnp.stack(
        [
            jnp.sum(const_scale[:, 0:1] * grad_y, axis=0),
            jnp.sum(const_scale[:, 1:2] * grad_y, axis=0),
        ]
    )
    back_rows = dot(place_both, grad_sent)
    own_weight = jnp.sum(gate_weights * copy_sel, axis=1, keepdims=True) + jnp.sum(
        const_weight * const_mix[:, :, 0], axis=1, keepdims=True
    )
    grad_h_two = dot(grad_logits_all, full_route, NT) + back_rows + own_weight * grad_y
    grad_first, grad_gain_two = norm_backward(grad_h_two, normed_two, scale_two, gain_two)
    grad_first = grad_first + cotangent.astype(jnp.float32)
    grad_attn = (valid_rows * grad_first).astype(low)
    grad_mixed = functools.reduce(
        jnp.add,
        [
            dot(grad_attn[:, i * wide_out : (i + 1) * wide_out], part, NT)
            for i, part in enumerate(full_out)
        ],
    ).astype(low)
    grad_mixed = grad_mixed.reshape(row_total, HEADS, HEAD)
    grad_values = jnp.einsum(
        "hqk,qhd->khd", probs_low, grad_mixed, preferred_element_type=jnp.float32
    )
    grad_probs = jnp.einsum("qhd,khd->hqk", grad_mixed, values, preferred_element_type=jnp.float32)
    grad_scores = softmax_probs * (
        grad_probs - jnp.sum(softmax_probs * grad_probs, axis=-1, keepdims=True)
    )
    grad_scores = grad_scores.astype(low)
    grad_queries = jnp.einsum(
        "hqk,khd->qhd", grad_scores, key_heads, preferred_element_type=jnp.float32
    ) * HEAD ** (-0.5)
    grad_keys = jnp.einsum(
        "hqk,qhd->khd", grad_scores, queries, preferred_element_type=jnp.float32
    ) * HEAD ** (-0.5)
    grad_qkv_rows = (
        jnp.stack([grad_queries, grad_keys, grad_values], axis=1)
        .reshape(row_total, 3 * D)
        .astype(low)
    )
    grad_h_one = functools.reduce(
        jnp.add,
        [
            dot(grad_qkv_rows[:, i * wide_qkv : (i + 1) * wide_qkv], part, NT)
            for i, part in enumerate(full_qkv)
        ],
    )
    grad_input, grad_gain_one = norm_backward(grad_h_one, normed_one, scale_one, gain_one)
    grad_input = grad_input + grad_first
    grad_gains_full = jnp.stack([grad_gain_one, grad_gain_two])

    grad_small = small_block(grad_route_full, grad_gains_full, grad_const_full).astype(low)
    param_parts = jnp.stack(
        [
            jnp.concatenate(
                [
                    dot(h_one_low, grad_qkv_rows[:, i * wide_qkv : (i + 1) * wide_qkv], TN).astype(
                        low
                    ),
                    dot(mixed_heads, grad_attn[:, i * wide_out : (i + 1) * wide_out], TN).astype(
                        low
                    ),
                    grad_small,
                ],
                axis=1,
            )
            for i in range(n_col)
        ]
    )
    summed = param_reduce(
        param_parts.reshape(n_col, n_dp, n_row, n_col * shard_rows, wide), dims
    )

    def from_col(parts):
        return parts.transpose(1, 0, 2).reshape(parts.shape[1], -1)

    grad_qkv = from_col(summed[:, :, :wide_qkv])
    grad_attn_out = from_col(summed[:, :, wide_qkv : wide_qkv + wide_out])
    sum_small = summed[0, :, wide_qkv + wide_out :]
    grad_route = sum_small[:, :route_cols]
    grad_gains = sum_small[:, route_cols : route_cols + 2].T
    grad_const = sum_small[:, route_cols + 2 : route_cols + 4].T
    moment_qkv, new_qkv = diag_update(w_qkv, grad_qkv, stat_qkv, D ** (-0.5))
    moment_attn_out, new_attn_out = diag_update(w_out, grad_attn_out, stat_out, HEAD ** (-0.5))
    moment_route, new_route = diag_update(route_w, grad_route, stat_route, (4 * D) ** (-0.5))
    moment_gains, new_gains = diag_update(gains, grad_gains, stat_gains, 0.3)
    moment_const, new_const = diag_update(const_vec, grad_const, stat_const, 0.5)

    (
        grad_gate_up,
        grad_down,
        new_left_gu,
        new_right_down,
        new_right_gu,
        new_left_down,
        new_gate_up,
        new_down,
    ) = shampoo_plain(
        gathered,
        left_root_gu[0],
        right_root_down[0],
        right_root_gu[0],
        left_root_down[0],
        left_gu[0],
        right_down[0],
        right_gu[0],
        left_down[0],
        w_gate_up[0],
        w_down[0].T,
        n_row,
        n_col,
    )
    return (
        result,
        grad_input,
        grad_qkv,
        moment_qkv,
        new_qkv,
        grad_attn_out,
        moment_attn_out,
        new_attn_out,
        grad_route,
        moment_route,
        new_route,
        grad_gains,
        moment_gains,
        new_gains,
        grad_const,
        moment_const,
        new_const,
        grad_gate_up[None],
        grad_down.T[None],
        new_left_gu[None],
        new_right_gu[None],
        new_left_down[None],
        new_right_down[None],
        new_gate_up[None],
        new_down.T[None],
    )


def solution(mesh):
    placed = (
        P(("dp", "row", "col"), None),
        P(("dp", "row", "col"), None),
        P(("dp", "row", "col"), None),
        P(("dp", "row", "col"), None),
        P(("dp", "row", "col"), None),
        P(("dp", "row", "col"), None),
        P(("dp", "row", "col"), None),
        P(("dp", "row", "col"), None),
        P(None, ("dp", "row", "col")),
        P(None, ("dp", "row", "col")),
        P(("dp", "row", "col"), None),
        P(("dp", "row", "col"), None),
        P(("dp", "row", "col"), None),
        P(None, ("dp", "row", "col")),
        P(None, ("dp", "row", "col")),
        P("dp", "row", None, "col"),
        P("dp", "col", "row"),
        P("dp", None, ("row", "col"), None),
        P("dp", None, ("row", "col"), None),
        P("dp", ("row", "col"), None),
        P("dp", ("row", "col"), None),
        P("dp", None, "row", None),
        P("dp", None, "col", None),
        P("dp", "col", None),
        P("dp", "row", None),
    )
    tiled = 3 * D % (mesh.shape["col"] * LANES) == 0 and D % (mesh.shape["col"] * LANES) == 0
    tiled = tiled and D // mesh.shape["dp"] // mesh.shape["row"] % 16 == 0
    return jax.shard_map(
        body_tiled if tiled else body,
        mesh=mesh,
        in_specs=placed,
        out_specs=(
            P(("dp", "row", "col"), None),
            P(("dp", "row", "col"), None),
            P(("dp", "row", "col"), None),
            P(("dp", "row", "col"), None),
            P(("dp", "row", "col"), None),
            P(("dp", "row", "col"), None),
            P(("dp", "row", "col"), None),
            P(("dp", "row", "col"), None),
            P(("dp", "row", "col"), None),
            P(("dp", "row", "col"), None),
            P(("dp", "row", "col"), None),
            P(None, ("dp", "row", "col")),
            P(None, ("dp", "row", "col")),
            P(None, ("dp", "row", "col")),
            P(None, ("dp", "row", "col")),
            P(None, ("dp", "row", "col")),
            P(None, ("dp", "row", "col")),
            P("dp", "row", None, "col"),
            P("dp", "col", "row"),
            P("dp", None, ("row", "col"), None),
            P("dp", None, ("row", "col"), None),
            P("dp", ("row", "col"), None),
            P("dp", ("row", "col"), None),
            P("dp", "row", None, "col"),
            P("dp", "col", "row"),
        ),
        check_vma=False,
    )
```
